32 devices in a mesh: space: 8 (over y, x, core), filt: 4 (over z).
Axes of the slice: x: 2, y: 2, z: 4, core: 2. Of those that a mesh axis runs over, the one named last changes fastest.
Arguments:
- volume: bfloat16 [32, 64, 16, 128], P('space', 'filt'), may hold values from -6 to 6
- w_early: bfloat16 [27, 128, 128], replicated, may hold values from -0.109375 to 0.109375
- w_deep: bfloat16 [27, 128, 256], P(None, None, 'filt'), may hold values from -0.109375 to 0.109375
- cotangent: bfloat16 [16, 32, 8, 256], P('space', None, None, 'filt'), may hold values from -6 to 6
Outputs:
- block_out: bfloat16 [16, 32, 8, 256], P('space', None, None, 'filt')
- grad_early: float32 [27, 128, 128], replicated
- grad_deep: float32 [27, 128, 256], P(None, None, 'filt')
The draws below stay inside these ranges and needn't reach their ends.
All inputs are finite; a program needn't handle non-finite values.
Results may differ from the reference program's by a relative error of at most 0.0059.
Values may be sent and summed in bfloat16 or wider, within the bound.
No kernel may reach another device: no remote copies, remote signals or barrier semaphores. Data moves between devices by JAX's collectives and lax.ppermute only.
A program may use at most 128 MiB of HBM per device.

```python
import math
import jax
import jax.numpy as jnp
from jax import lax

C0 = 128
C1 = 128
C2 = 256
NZ = 16
NX = 32
NY = 64


def levels(stream_key, extent, pieces, least, top_value):
    factor_of = 1.0
    for position, parts in pieces:
        draws = jax.random.uniform(jax.random.fold_in(jax.random.fold_in(stream_key, 6), position), (parts,), jnp.float32, least / len(pieces), top_value / len(pieces))
        factor_of = factor_of * jnp.repeat(jnp.exp(draws), extent[position] // parts).reshape((-1,) + (1,) * (len(extent) - 1 - position))
    return factor_of


def noise(key, extent, scale, bound, split=(), held_as=jnp.bfloat16):
    drawn = jax.random.normal(key, extent, jnp.float32) * scale
    if len(split) > 0:
        drawn = levels(key, extent, split, -0.22, 0.18) * drawn
    return jnp.clip(drawn, min=-bound, max=bound).astype(held_as)


def setup_inputs(seed: int = 0) -> dict:
    keys = jax.random.split(jax.random.key(seed), 5)
    return {
        "volume": noise(keys[0], (NX, NY, NZ, C0), 1.0, 6.0, ((0, 8), (1, 4))),
        "w_early": noise(keys[1], (27, C0, C1), (27 * C0) ** -0.5, 0.109375),
        "w_deep": noise(keys[2], (27, C1, C2), (27 * C1) ** -0.5, 0.109375, ((2, 4),)),
        "cotangent": noise(keys[3], (NX // 2, NY // 2, NZ // 2, C2), 1.0, 6.0, ((0, 8), (3, 4))),
    }


def silu_grad(value):
    sig = jax.nn.sigmoid(value)
    return sig * (1.0 + value * (1.0 - sig))

def convolve(field, kernel):
    cin = kernel.shape[1]
    cout = kernel.shape[2]
    result = lax.conv_general_dilated(field[None], kernel.reshape(3, 3, 3, cin, cout), (1, 1, 1), 'SAME', dimension_numbers=('NDHWC', 'DHWIO', 'NDHWC'), precision=lax.Precision.HIGHEST)
    return result[0]

def reference(volume, w_early, w_deep, cotangent):
    field = volume.astype(jnp.float32)
    kernel_one = w_early.astype(jnp.float32)
    kernel_two = w_deep.astype(jnp.float32)
    pre_early = convolve(field, kernel_one)
    size_x, size_y, size_z, width = pre_early.shape
    pooled = jax.nn.silu(pre_early).reshape(size_x // 2, 2, size_y // 2, 2, size_z // 2, 2, width).mean(axis=(1, 3, 5)).astype(jnp.bfloat16)
    pooled_f = lax.optimization_barrier(pooled).astype(jnp.float32)
    pre_deep = convolve(pooled_f, kernel_two)
    block_out = jax.nn.silu(pre_deep).astype(jnp.bfloat16)
    grad_pre_deep = (cotangent.astype(jnp.float32) * silu_grad(pre_deep)).astype(jnp.bfloat16)
    grad_pre_deep = lax.optimization_barrier(grad_pre_deep).astype(jnp.float32)
    unused, pull_deep = jax.vjp(convolve, pooled_f, kernel_two)
    grad_pooled, grad_deep = pull_deep(grad_pre_deep)
    grad_pooled = lax.optimization_barrier(grad_pooled.astype(jnp.bfloat16)).astype(jnp.float32)
    spread = jnp.repeat(jnp.repeat(jnp.repeat(grad_pooled, 2, axis=0), 2, axis=1), 2, axis=2) / 8.0
    grad_pre_early = (spread * silu_grad(pre_early)).astype(jnp.bfloat16)
    grad_pre_early = lax.optimization_barrier(grad_pre_early).astype(jnp.float32)
    unused_two, pull_early = jax.vjp(lambda kernel: convolve(field, kernel), kernel_one)
    grad_early = pull_early(grad_pre_early)[0]
    total = size_x * size_y * size_z
    grad_early = grad_early / math.sqrt(total)
    grad_deep = grad_deep / math.sqrt(total // 8)
    return (block_out, grad_early, grad_deep)
```

```python
import functools
import math

import jax
import jax.numpy as jnp
from jax import lax
from jax.experimental import pallas as pl
from jax.experimental.pallas import tpu as pltpu
from jax.sharding import PartitionSpec as P

F32 = jnp.float32
BF16 = jnp.bfloat16
VMEM_LIMIT = 40 * 1024 * 1024
SMEM = pl.BlockSpec(memory_space=pltpu.SMEM)
VMEM = pl.BlockSpec(memory_space=pltpu.VMEM)


def call(body, name, out_shape, ids, operands, scratch=(), flops=0, moved=1 << 20):
    return pl.pallas_call(
        body,
        name=name,
        out_shape=out_shape,
        in_specs=[SMEM] + [VMEM] * len(operands),
        out_specs=jax.tree.map(lambda _: VMEM, out_shape),
        scratch_shapes=list(scratch),
        compiler_params=pltpu.CompilerParams(vmem_limit_bytes=VMEM_LIMIT),
        cost_estimate=pl.CostEstimate(flops=flops, bytes_accessed=moved, transcendentals=0),
    )(ids, *operands)


def struct(shape, dtype=BF16):
    return jax.ShapeDtypeStruct(shape, dtype)


def ceil_to(value, step):
    return -(-value // step) * step


def sigmoid(value):
    return 1.0 / (1.0 + jnp.exp(-value))


def early_body(space, ids, center, xlo, xhi, ylo, yhi, w, windows, sg, pooled, field, wide):
    nx, ny, nz, cin = center.shape
    cout = w.shape[2]
    half = nz // 2
    rows = ny * half
    ext = nx + 6
    field[:, :, 0:8] = jnp.zeros((ext, ny + 2, 8, cin), F32)
    field[:, :, 8 + nz : 16 + nz] = jnp.zeros((ext, ny + 2, 8, cin), F32)
    field[0:3, 1 : ny + 1, 8 : 8 + nz] = xlo[...].astype(F32)
    field[3 : nx + 3, 1 : ny + 1, 8 : 8 + nz] = center[...].astype(F32)
    field[nx + 3 : ext, 1 : ny + 1, 8 : 8 + nz] = xhi[...].astype(F32)
    field[:, 0:1, 8 : 8 + nz] = ylo[...].astype(F32)
    field[:, ny + 1 : ny + 2, 8 : 8 + nz] = yhi[...].astype(F32)
    for ab in range(9):
        for group in range(4):
            for side in range(2):
                tap = group - side
                value = (
                    w[3 * ab + tap] if 0 <= tap <= 2 else jnp.zeros((cin, cout), BF16)
                )
                wide[
                    ab, group * cin : (group + 1) * cin, side * cout : (side + 1) * cout
                ] = value
    for x in range(ext):
        for group in range(4):
            plane = field[x, :, pl.ds(7 + group, half, stride=2), :]
            for b in range(3):
                windows[b, x, :, group * cin : (group + 1) * cin] = (
                    plane[b : b + ny].reshape(rows, cin).astype(BF16)
                )
    low = jnp.where(ids[0] > 0, 1.0, 0.0).astype(F32)
    high = jnp.where(ids[0] < space - 1, 1.0, 0.0).astype(F32)
    for chunk in range(nx // 2 + 2):
        start = 2 * chunk
        acc = jnp.zeros((2 * rows, 2 * cout), F32)
        for ab in range(9):
            a, b = ab // 3, ab % 3
            left = windows[b, start + a : start + a + 2].reshape(2 * rows, 4 * cin)
            acc = acc + jnp.dot(left, wide[ab], preferred_element_type=F32)
        sig = sigmoid(acc)
        keep = 0.125
        if chunk == 0:
            keep = 0.125 * low
        if chunk == nx // 2 + 1:
            keep = 0.125 * high
        sg[start : start + 2] = (sig * (1.0 + acc * (1.0 - sig)) * keep).reshape(
            2, rows, 2 * cout
        )
        act = acc * sig
        act = act[:rows] + act[rows:]
        act = act[:, :cout] + act[:, cout:]
        act = act.reshape(ny // 2, 2, half, cout)
        act = (act[:, 0] + act[:, 1]) * keep
        pooled[chunk] = act.reshape(rows // 2, cout).astype(BF16)


def transpose_body(ids, windows, turned):
    for b in range(windows.shape[0]):
        rows = windows.shape[2]
        for x in range(windows.shape[1]):
            turned[b, :, x * rows : (x + 1) * rows] = windows[b, x].T


def roll_z(value, shift):
    size = value.shape[-2]
    rolled = pltpu.roll(value, shift % size, value.ndim - 2)
    spot = lax.broadcasted_iota(jnp.int32, value.shape, value.ndim - 2)
    edge = 0 if shift == 1 else size - 1
    return jnp.where(spot == edge, 0.0, rolled)


def deep_body(parts_n, ids, *refs):
    parts = refs[:parts_n]
    wt, cot = refs[parts_n : parts_n + 2]
    block_out, grad, windows = refs[parts_n + 2 : parts_n + 5]
    sends = refs[parts_n + 5 : 2 * parts_n + 5]
    field, wide, terms = refs[2 * parts_n + 5 :]
    nx, ny, nz, filters = cot.shape
    width = wt.shape[2]
    rows = ny * nz
    py = ny // parts_n
    mine = ids[1]
    for ab in range(9):
        for c in range(3):
            wide[ab, :, c * width : (c + 1) * width] = wt[3 * ab + c]
    field[:, 0:1] = jnp.zeros((nx + 2, 1, nz, width), F32)
    field[:, ny + 1 : ny + 2] = jnp.zeros((nx + 2, 1, nz, width), F32)
    for j in range(parts_n):
        spot = lax.rem(mine + (parts_n - j), parts_n) * py + 1
        field[:, pl.ds(spot, py)] = parts[j][...].astype(F32).reshape(nx + 2, py, nz, width)
    for x in range(nx + 2):
        plane = field[x]
        for c in range(3):
            moved = plane if c == 1 else roll_z(plane, 1 - c)
            for b in range(3):
                windows[b, x, :, c * width : (c + 1) * width] = (
                    moved[b : b + ny].reshape(rows, width).astype(BF16)
                )
    for x in range(nx):
        acc = jnp.zeros((rows, filters), F32)
        for ab in range(9):
            a, b = ab // 3, ab % 3
            acc = acc + lax.dot_general(
                windows[b, x + a], wide[ab], (((1,), (1,)), ((), ())), preferred_element_type=F32
            )
        sig = sigmoid(acc)
        block_out[x] = (acc * sig).reshape(ny, nz, filters).astype(BF16)
        slope = sig * (1.0 + acc * (1.0 - sig))
        grad[x] = (cot[x].astype(F32).reshape(rows, filters) * slope).astype(BF16)
    terms[...] = jnp.zeros(terms.shape, F32)
    for ab in range(9):
        a, b = ab // 3, ab % 3
        for x in range(nx):
            part = jnp.dot(grad[x], wide[ab], preferred_element_type=F32)
            terms[x + a, b : b + ny] += part.reshape(ny, nz, 3 * width)
    for j in range(parts_n):
        spot = lax.rem(mine + j, parts_n) * py + 1
        value = terms[:, pl.ds(spot, py)]
        total = value[..., width : 2 * width]
        total = total + roll_z(value[..., :width], -1) + roll_z(value[..., 2 * width :], 1)
        sends[j][...] = total.reshape(nx + 2, py * nz, width).astype(BF16)


def deep_grad_body(ids, windows, grad, out, held):
    nx, rows, filters = grad.shape
    width = windows.shape[3] // 3
    turned = grad[...].reshape(nx * rows, filters).astype(F32).T.astype(BF16)
    pieces, piece_rows, _ = out.shape
    total = 27 * filters
    if pieces * piece_rows > total:
        held[total:] = jnp.zeros((pieces * piece_rows - total, width), F32)
    for ab in range(9):
        a, b = ab // 3, ab % 3
        value = jnp.dot(
            turned,
            windows[b, a : a + nx].reshape(nx * rows, 3 * width),
            preferred_element_type=F32,
        )
        for c in range(3):
            spot = (3 * ab + c) * filters
            held[spot : spot + filters] = value[:, c * width : (c + 1) * width]
    for s in range(pieces):
        out[s] = held[s * piece_rows : (s + 1) * piece_rows].astype(BF16)


def early_grad_body(parts_n, nz, ids, *refs):
    parts = refs[:parts_n]
    sg, turned, out, grad, held = refs[parts_n:]
    ext, rows, wide = sg.shape
    width = wide // 2
    total = parts[0][...].astype(F32)
    for j in range(1, parts_n):
        total = total + parts[j][...].astype(F32)
    px, prow, _ = total.shape
    py = prow // nz
    total = jnp.concatenate([total, total], axis=2).reshape(px, py, 1, nz, wide)
    total = jnp.broadcast_to(total, (px, py, 2, nz, wide)).reshape(px, rows, wide)
    for x in range(ext):
        grad[x] = (total[x // 2] * sg[x]).astype(BF16)
    cin = turned.shape[1] // 4
    right = grad[...].reshape(ext * rows, wide)
    for ab in range(9):
        a, b = ab // 3, ab % 3
        value = jnp.dot(
            turned[b, :, a * rows : (a + ext) * rows], right, preferred_element_type=F32
        )
        for c in range(3):
            held[(3 * ab + c) * cin : (3 * ab + c + 1) * cin] = (
                value[c * cin : (c + 1) * cin, :width]
                + value[(c + 1) * cin : (c + 2) * cin, width:]
            )
    for s in range(out.shape[0]):
        out[s] = held[s * out.shape[1] : (s + 1) * out.shape[1]].astype(BF16)


def sum_spread_body(parts_n, ids, pieces, *refs):
    outs, held = refs[:parts_n], refs[parts_n]
    total = pieces[0].astype(F32)
    for s in range(1, pieces.shape[0]):
        total = total + pieces[s].astype(F32)
    rows = total.shape[0]
    held[0:rows] = total
    size = outs[0].shape[0]
    if size * parts_n > rows:
        held[rows:] = jnp.zeros((size * parts_n - rows, total.shape[1]), F32)
    for j in range(parts_n):
        spot = pl.multiple_of(lax.rem(ids[1] + j, parts_n) * size, 8)
        outs[j][...] = held[pl.ds(spot, size)].astype(BF16)


def sum_body(ids, *refs):
    total = refs[0][...].astype(F32)
    for ref in refs[1:-1]:
        total = total + ref[...].astype(F32)
    refs[-1][...] = total.astype(BF16)


def line_up_body(parts_n, ids, *refs):
    out = refs[parts_n]
    size = refs[0].shape[0]
    for j in range(parts_n):
        spot = lax.rem(ids[1] + (parts_n - j), parts_n)
        for s in range(out.shape[0]):
            out[s, spot] = refs[j][...]


def sum_copies_body(ids, pieces, out):
    total = pieces[0].astype(F32)
    for s in range(1, pieces.shape[0]):
        total = total + pieces[s].astype(F32)
    total = total.astype(BF16)
    for s in range(pieces.shape[0]):
        out[s] = total


def finish_body(scale, step, ids, pieces, out):
    rows = out.shape[0]
    for s in range(pieces.shape[0]):
        count = min(step, rows - s * step)
        if count > 0:
            out[s * step : s * step + count] = pieces[s, :count].astype(F32) * scale


def from_others(value, axis):
    count = lax.axis_size(axis)
    return [value] + [
        lax.ppermute(value, axis, [(i, (i + j) % count) for i in range(count)])
        for j in range(1, count)
    ]


def to_others(values, axis):
    count = lax.axis_size(axis)
    return [values[0]] + [
        lax.ppermute(values[j], axis, [(i, (i + j) % count) for i in range(count)])
        for j in range(1, count)
    ]


def both_sides(low, high, axis):
    count = lax.axis_size(axis)
    forward = [(i, i + 1) for i in range(count - 1)]
    backward = [(i + 1, i) for i in range(count - 1)]
    return lax.ppermute(high, axis, forward), lax.ppermute(low, axis, backward)


def shards(volume, w_early, w_deep, cotangent):
    nx, ny, nz, cin = volume.shape
    width = w_early.shape[2]
    filters = w_deep.shape[2]
    space = lax.axis_size("space")
    filt = lax.axis_size("filt")
    half = nz // 2
    ids = jnp.stack([lax.axis_index("space"), lax.axis_index("filt")]).astype(jnp.int32)
    xlo, xhi = both_sides(volume[:3], volume[nx - 3 :], "space")
    first = jnp.concatenate([xlo[:, :1], volume[:, :1], xhi[:, :1]], axis=0)
    last = jnp.concatenate([xlo[:, ny - 1 :], volume[:, ny - 1 :], xhi[:, ny - 1 :]], axis=0)
    ylo, yhi = both_sides(first, last, "filt")
    ext = nx + 6
    rows = ny * half
    windows, sg, pooled = call(
        functools.partial(early_body, space),
        "early_conv",
        (
            struct((3, ext, rows, 4 * cin)),
            struct((nx + 4, rows, 2 * width), F32),
            struct((nx // 2 + 2, rows // 2, width)),
        ),
        ids,
        (volume, xlo, xhi, ylo, yhi, w_early),
        [
            pltpu.VMEM((ext, ny + 2, nz + 16, cin), F32),
            pltpu.VMEM((9, 4 * cin, 2 * width), BF16),
        ],
        flops=2 * (nx + 4) * rows * 36 * cin * 2 * width,
    )
    parts = from_others(pooled, "filt")
    turned = call(
        transpose_body,
        "turn_windows",
        struct((3, 4 * cin, ext * rows)),
        ids,
        (windows,),
        flops=1 << 30,
    )
    dx, dy, dz, _ = cotangent.shape
    px = dx + 2
    prow = rows // 2
    deep = call(
        functools.partial(deep_body, filt),
        "deep_conv",
        [
            struct(cotangent.shape),
            struct((dx, dy * dz, filters)),
            struct((3, px, dy * dz, 3 * width)),
        ]
        + [struct((px, prow, width))] * filt,
        ids,
        (*parts, jnp.swapaxes(w_deep, 1, 2), cotangent),
        [
            pltpu.VMEM((px, dy + 2, dz, width), F32),
            pltpu.VMEM((9, filters, 3 * width), BF16),
            pltpu.VMEM((px, dy + 2, dz, 3 * width), F32),
        ],
        flops=4 * dx * dy * dz * 27 * width * filters,
    )
    block_out, grad, deep_windows = deep[:3]
    terms = to_others(deep[3:], "filt")

    deep_rows = ceil_to(-(-27 * filters // space), 16)
    deep_pieces = call(
        deep_grad_body,
        "deep_grad",
        struct((space, deep_rows, width)),
        ids,
        (deep_windows, grad),
        [pltpu.VMEM((space * deep_rows, width), F32)],
        flops=2 * dx * dy * dz * 27 * width * filters,
    )
    deep_pieces = lax.all_to_all(deep_pieces, "space", 0, 0, tiled=True)
    deep_pieces = call(
        sum_copies_body, "deep_sum", struct(deep_pieces.shape), ids, (deep_pieces,)
    )
    deep_pieces = lax.all_to_all(deep_pieces, "space", 0, 0, tiled=True)
    deep_total = dx * dy * dz * space
    grad_deep = call(
        functools.partial(finish_body, 1.0 / math.sqrt(deep_total), deep_rows),
        "deep_finish",
        struct((27 * filters, width), F32),
        ids,
        (deep_pieces,),
    )
    grad_deep = jnp.swapaxes(grad_deep.reshape(27, filters, width), 1, 2)

    early_rows = 27 * cin // space
    pieces = call(
        functools.partial(early_grad_body, filt, half),
        "early_grad",
        struct((space, early_rows, width)),
        ids,
        (*terms, sg, turned),
        [
            pltpu.VMEM((nx + 4, rows, 2 * width), BF16),
            pltpu.VMEM((27 * cin, width), F32),
        ],
        flops=2 * (nx + 4) * rows * 36 * cin * 2 * width,
    )
    pieces = lax.all_to_all(pieces, "space", 0, 0, tiled=True)
    small = ceil_to(-(-early_rows // filt), 16)
    shares = call(
        functools.partial(sum_spread_body, filt),
        "early_sum",
        [struct((small, width))] * filt,
        ids,
        (pieces,),
        [pltpu.VMEM((small * filt, width), F32)],
    )
    share = call(sum_body, "early_share", struct((small, width)), ids, to_others(shares, "filt"))
    copies = call(
        functools.partial(line_up_body, filt),
        "early_copies",
        struct((space, filt, small, width)),
        ids,
        from_others(share, "filt"),
    )
    copies = lax.all_to_all(
        copies.reshape(space, filt * small, width), "space", 0, 0, tiled=True
    )
    early_total = nx * ny * nz * space * filt
    grad_early = call(
        functools.partial(finish_body, 1.0 / math.sqrt(early_total), early_rows),
        "early_finish",
        struct((27 * cin, width), F32),
        ids,
        (copies,),
    ).reshape(27, cin, width)
    return (block_out, grad_early, grad_deep)


def solution(mesh):
    return jax.shard_map(
        shards,
        mesh=mesh,
        in_specs=(
            P("space", "filt", None, None),
            P(),
            P(None, None, "filt"),
            P("space", None, None, "filt"),
        ),
        out_specs=(P("space", None, None, "filt"), P(), P(None, None, "filt")),
        check_vma=False,
    )
```

```python
import functools
import math

import jax
import jax.numpy as jnp
from jax import lax
from jax.experimental import pallas as pl
from jax.experimental.pallas import tpu as pltpu
from jax.sharding import PartitionSpec as P

F32 = jnp.float32
BF16 = jnp.bfloat16
VMEM_LIMIT = 24 * 1024 * 1024
SMEM = pl.BlockSpec(memory_space=pltpu.SMEM)
VMEM = pl.BlockSpec(memory_space=pltpu.VMEM)


def call(body, name, out_shape, ids, operands, scratch=(), flops=0, moved=1 << 20):
    return pl.pallas_call(
        body,
        name=name,
        out_shape=out_shape,
        in_specs=[SMEM] + [VMEM] * len(operands),
        out_specs=jax.tree.map(lambda _: VMEM, out_shape),
        scratch_shapes=list(scratch),
        compiler_params=pltpu.CompilerParams(vmem_limit_bytes=VMEM_LIMIT),
        cost_estimate=pl.CostEstimate(flops=flops, bytes_accessed=moved, transcendentals=0),
    )(ids, *operands)


def struct(shape, dtype=BF16):
    return jax.ShapeDtypeStruct(shape, dtype)


def ceil_to(value, step):
    return -(-value // step) * step


def sigmoid(value):
    return 1.0 / (1.0 + jnp.exp(-value))


def edges_body(ids, center, xlo, xhi, first, last):
    nx, ny, _, _ = center.shape
    for out, spot in ((first, 0), (last, ny - 1)):
        out[0:3] = xlo[nx - 3 :, spot : spot + 1]
        out[3 : nx + 3] = center[:, spot : spot + 1]
        out[nx + 3 :] = xhi[:3, spot : spot + 1]


def widen_body(ids, w, wt, early, deep):
    _, cin, cout = w.shape
    width = wt.shape[2]
    for ab in range(9):
        for group in range(4):
            for side in range(2):
                tap = group - side
                value = w[3 * ab + tap] if 0 <= tap <= 2 else jnp.zeros((cin, cout), BF16)
                early[
                    ab, group * cin : (group + 1) * cin, side * cout : (side + 1) * cout
                ] = value
        for c in range(3):
            deep[ab, :, c * width : (c + 1) * width] = wt[3 * ab + c]


def early_body(space, ids, center, xlo, xhi, ylo, yhi, wide, windows, sg, pooled, field):
    nx, ny, nz, cin = center.shape
    cout = wide.shape[2] // 2
    half = nz // 2
    rows = ny * half
    ext = nx + 6
    field[:, :, 0:8] = jnp.zeros((ext, ny + 2, 8, cin), F32)
    field[:, :, 8 + nz : 16 + nz] = jnp.zeros((ext, ny + 2, 8, cin), F32)
    field[0:3, 1 : ny + 1, 8 : 8 + nz] = xlo[nx - 3 :].astype(F32)
    field[3 : nx + 3, 1 : ny + 1, 8 : 8 + nz] = center[...].astype(F32)
    field[nx + 3 : ext, 1 : ny + 1, 8 : 8 + nz] = xhi[:3].astype(F32)
    field[:, 0:1, 8 : 8 + nz] = ylo[...].astype(F32)
    field[:, ny + 1 : ny + 2, 8 : 8 + nz] = yhi[...].astype(F32)
    for x in range(ext):
        for group in range(4):
            plane = field[x, :, pl.ds(7 + group, half, stride=2), :]
            for b in range(3):
                windows[b, x, :, group * cin : (group + 1) * cin] = (
                    plane[b : b + ny].reshape(rows, cin).astype(BF16)
                )
    low = jnp.where(ids[0] > 0, 1.0, 0.0).astype(F32)
    high = jnp.where(ids[0] < space - 1, 1.0, 0.0).astype(F32)
    for chunk in range(nx // 2 + 2):
        start = 2 * chunk
        acc = jnp.zeros((2 * rows, 2 * cout), F32)
        for ab in range(9):
            a, b = ab // 3, ab % 3
            left = windows[b, start + a : start + a + 2].reshape(2 * rows, 4 * cin)
            acc = acc + jnp.dot(left, wide[ab], preferred_element_type=F32)
        sig = sigmoid(acc)
        keep = 0.125
        if chunk == 0:
            keep = 0.125 * low
        if chunk == nx // 2 + 1:
            keep = 0.125 * high
        sg[start : start + 2] = (sig * (1.0 + acc * (1.0 - sig)) * keep).reshape(
            2, rows, 2 * cout
        )
        act = acc * sig
        act = act[:rows] + act[rows:]
        act = act[:, :cout] + act[:, cout:]
        act = act.reshape(ny // 2, 2, half, cout)
        act = (act[:, 0] + act[:, 1]) * keep
        pooled[chunk] = act.reshape(rows // 2, cout).astype(BF16)


def transpose_body(ids, windows, turned):
    rows = windows.shape[2]
    part = turned.shape[2] // 4
    for b in range(windows.shape[0]):
        for x in range(windows.shape[1]):
            value = windows[b, x].T
            for group in range(4):
                for side in range(2):
                    spot = (2 * group + side) * part
                    turned[
                        b, side, group * part : (group + 1) * part, x * rows : (x + 1) * rows
                    ] = value[spot : spot + part]


def roll_z(value, shift):
    size = value.shape[-2]
    rolled = pltpu.roll(value, shift % size, value.ndim - 2)
    spot = lax.broadcasted_iota(jnp.int32, value.shape, value.ndim - 2)
    edge = 0 if shift == 1 else size - 1
    return jnp.where(spot == edge, 0.0, rolled)


def deep_body(parts_n, ids, *refs):
    parts = refs[:parts_n]
    wide, cot = refs[parts_n : parts_n + 2]
    block_out, grad, windows = refs[parts_n + 2 : parts_n + 5]
    sends = refs[parts_n + 5 : 2 * parts_n + 5]
    field, terms = refs[2 * parts_n + 5 :]
    nx, ny, nz, filters = cot.shape
    width = wide.shape[2] // 3
    rows = ny * nz
    py = ny // parts_n
    mine = ids[1]
    field[:, 0:1] = jnp.zeros((nx + 2, 1, nz, width), F32)
    field[:, ny + 1 : ny + 2] = jnp.zeros((nx + 2, 1, nz, width), F32)
    for j in range(parts_n):
        spot = lax.bitwise_xor(mine, j) * py + 1
        field[:, pl.ds(spot, py)] = parts[j][...].astype(F32).reshape(nx + 2, py, nz, width)
    for x in range(nx + 2):
        plane = field[x]
        for c in range(3):
            moved = plane if c == 1 else roll_z(plane, 1 - c)
            for b in range(3):
                windows[b, x, :, c * width : (c + 1) * width] = (
                    moved[b : b + ny].reshape(rows, width).astype(BF16)
                )
    for x in range(nx):
        acc = jnp.zeros((rows, filters), F32)
        for ab in range(9):
            a, b = ab // 3, ab % 3
            acc = acc + lax.dot_general(
                windows[b, x + a], wide[ab], (((1,), (1,)), ((), ())), preferred_element_type=F32
            )
        sig = sigmoid(acc)
        block_out[x] = (acc * sig).reshape(ny, nz, filters).astype(BF16)
        slope = sig * (1.0 + acc * (1.0 - sig))
        grad[x] = (cot[x].astype(F32).reshape(rows, filters) * slope).astype(BF16)
    terms[...] = jnp.zeros(terms.shape, F32)
    for ab in range(9):
        a, b = ab // 3, ab % 3
        for x in range(nx):
            part = jnp.dot(grad[x], wide[ab], preferred_element_type=F32)
            terms[x + a, b : b + ny] += part.reshape(ny, nz, 3 * width)
    for j in range(parts_n):
        spot = lax.bitwise_xor(mine, j) * py + 1
        value = terms[:, pl.ds(spot, py)]
        total = value[..., width : 2 * width]
        total = total + roll_z(value[..., :width], -1) + roll_z(value[..., 2 * width :], 1)
        sends[j][...] = total.reshape(nx + 2, py * nz, width).astype(sends[j].dtype)


def deep_grad_body(ids, windows, grad, theirs, mine, held):
    nx, rows, filters = grad.shape
    width = windows.shape[3] // 3
    turned = grad[...].reshape(nx * rows, filters).astype(F32).T.astype(BF16)
    chips, step, _ = mine.shape
    part = filters // 2
    total = 27 * part
    if chips * step > total:
        held[:, total:] = jnp.zeros((2, chips * step - total, width), F32)
    for ab in range(9):
        a, b = ab // 3, ab % 3
        value = jnp.dot(
            turned,
            windows[b, a : a + nx].reshape(nx * rows, 3 * width),
            preferred_element_type=F32,
        )
        for c in range(3):
            spot = (3 * ab + c) * part
            for side in range(2):
                held[side, spot : spot + part] = value[
                    side * part : (side + 1) * part, c * width : (c + 1) * width
                ]
    core = lax.rem(ids[0], 2)
    for q in range(chips):
        theirs[q] = held[1 - core, q * step : (q + 1) * step].astype(theirs.dtype)
        mine[q] = held[core, q * step : (q + 1) * step]


def early_grad_body(nz, ids, *refs):
    parts, (sg, turned, deep, out, grad, held) = refs[:-6], refs[-6:]
    ext, rows, wide = sg.shape
    total = parts[0][...]
    for part in parts[1:]:
        total = total + part[...].astype(F32)
    px, prow, _ = total.shape
    py = prow // nz
    total = jnp.concatenate([total, total], axis=2).reshape(px, py, 1, nz, wide)
    total = jnp.broadcast_to(total, (px, py, 2, nz, wide)).reshape(px, rows, wide)
    for x in range(ext):
        grad[x] = (total[x // 2] * sg[x]).astype(BF16)
    early_grad_half(1 - lax.rem(ids[0], 2), grad, turned, deep, out, held)


def early_grad_rest_body(ids, grad, turned, deep, out, held):
    early_grad_half(lax.rem(ids[0], 2), grad, turned, deep, out, held)


def early_grad_half(side, grad, turned, deep, out, held):
    ext, rows, wide = grad.shape
    width = wide // 2
    part = turned.shape[2] // 4
    right = grad[...].reshape(ext * rows, wide)
    for ab in range(9):
        a, b = ab // 3, ab % 3
        value = jnp.dot(
            turned[b, side, :, a * rows : (a + ext) * rows], right, preferred_element_type=F32
        )
        for c in range(3):
            spot = (3 * ab + c) * part
            held[spot : spot + part] = (
                value[c * part : (c + 1) * part, :width]
                + value[(c + 1) * part : (c + 2) * part, width:]
            )
    step = held.shape[0] // out.shape[0]
    for q in range(out.shape[0]):
        out[q, :step] = held[q * step : (q + 1) * step].astype(out.dtype)
        out[q, step:] = deep[q].astype(out.dtype)


def core_sum_body(ids, mine, other, *outs):
    chip = lax.div(ids[0], 2)
    for j, out in enumerate(outs):
        q = lax.bitwise_xor(chip, j)
        out[...] = (mine[q] + other[q].astype(F32)).astype(out.dtype)


def chip_sum_body(count, step, ids, *refs):
    others, (deep, *outs, held) = refs[:count], refs[count:]
    total = others[0][...]
    for ref in others[1:]:
        total = total + ref[...].astype(F32)
    held[:step] = total[:step]
    if held.shape[0] > step:
        held[step:] = jnp.zeros((held.shape[0] - step, total.shape[1]), F32)
    deep[...] = total[step:].astype(BF16)
    size = outs[0].shape[0]
    for j, out in enumerate(outs):
        spot = pl.multiple_of(lax.bitwise_xor(ids[1], j) * size, 8)
        out[...] = held[pl.ds(spot, size)].astype(out.dtype)


def sum_body(ids, *refs):
    total = refs[0][...]
    for ref in refs[1:-1]:
        total = total + ref[...].astype(F32)
    refs[-1][...] = total.astype(BF16)


def line_up_body(ids, *refs):
    shares, deep, out = refs[:-2], refs[-2], refs[-1]
    size = shares[0].shape[0]
    for j, share in enumerate(shares):
        spot = pl.multiple_of(lax.bitwise_xor(ids[1], j) * size, 16)
        out[pl.ds(spot, size)] = share[...]
    out[size * len(shares) :] = deep[...]


def stack_body(ids, *refs):
    out = refs[-1]
    chip = lax.div(ids[0], 2)
    for j, ref in enumerate(refs[:-1]):
        out[lax.bitwise_xor(chip, j)] = ref[...]


def finish_body(early_scale, deep_scale, early_rows, ids, mine, other, early, deep):
    core = lax.rem(ids[0], 2)
    chips, rows, _ = mine.shape
    deep_rows = (27 * deep.shape[1] // 2 + chips - 1) // chips
    deep_rows = ceil_to(deep_rows, 16)
    for piece, side in ((mine, core), (other, 1 - core)):
        for out, first, step, scale in (
            (early, 0, early_rows, early_scale),
            (deep, rows - deep_rows, deep_rows, deep_scale),
        ):
            part = out.shape[1] // 2
            base = pl.multiple_of(side * part, 8)
            for q in range(chips):
                row = q * step
                while row < min((q + 1) * step, 27 * part):
                    tap, inner = row // part, row % part
                    size = min(part - inner, (q + 1) * step - row)
                    here = first + row - q * step
                    out[tap, pl.ds(base + inner, size)] = (
                        piece[q, here : here + size].astype(F32) * scale
                    )
                    row += size


def paired(values, axis, step=1):
    count = lax.axis_size(axis)
    return [values[0]] + [
        lax.ppermute(values[j], axis, [(i, i ^ (step * j)) for i in range(count)])
        for j in range(1, len(values))
    ]


def both_sides(low, high, axis):
    count = lax.axis_size(axis)
    forward = [(i, i + 1) for i in range(count - 1)]
    backward = [(i + 1, i) for i in range(count - 1)]
    return lax.ppermute(high, axis, forward), lax.ppermute(low, axis, backward)


def shards(volume, w_early, w_deep, cotangent):
    nx, ny, nz, cin = volume.shape
    width = w_early.shape[2]
    filters = w_deep.shape[2]
    space = lax.axis_size("space")
    filt = lax.axis_size("filt")
    chips = space // 2
    half = nz // 2
    ids = jnp.stack([lax.axis_index("space"), lax.axis_index("filt")]).astype(jnp.int32)
    xlo, xhi = both_sides(volume, volume, "space")
    ext = nx + 6
    rows = ny * half
    first, last = call(
        edges_body, "edges", [struct((ext, 1, nz, cin))] * 2, ids, (volume, xlo, xhi)
    )
    ylo, yhi = both_sides(first, last, "filt")
    early_wide, deep_wide = call(
        widen_body,
        "widen_weights",
        [struct((9, 4 * cin, 2 * width)), struct((9, filters, 3 * width))],
        ids,
        (w_early, jnp.swapaxes(w_deep, 1, 2)),
    )
    windows, sg, pooled = call(
        functools.partial(early_body, space),
        "early_conv",
        (
            struct((3, ext, rows, 4 * cin)),
            struct((nx + 4, rows, 2 * width), F32),
            struct((nx // 2 + 2, rows // 2, width)),
        ),
        ids,
        (volume, xlo, xhi, ylo, yhi, early_wide),
        [pltpu.VMEM((ext, ny + 2, nz + 16, cin), F32)],
        flops=2 * (nx + 4) * rows * 36 * cin * 2 * width,
    )
    parts = paired([pooled] * filt, "filt")
    turned = call(
        transpose_body,
        "turn_windows",
        struct((3, 2, 2 * cin, ext * rows)),
        ids,
        (windows,),
        flops=1 << 30,
    )
    *parts, turned = lax.optimization_barrier((*parts, turned))
    dx, dy, dz, _ = cotangent.shape
    px = dx + 2
    prow = rows // 2
    deep = call(
        functools.partial(deep_body, filt),
        "deep_conv",
        [
            struct(cotangent.shape),
            struct((dx, dy * dz, filters)),
            struct((3, px, dy * dz, 3 * width)),
            struct((px, prow, width), F32),
        ]
        + [struct((px, prow, width))] * (filt - 1),
        ids,
        (*parts, deep_wide, cotangent),
        [
            pltpu.VMEM((px, dy + 2, dz, width), F32),
            pltpu.VMEM((px, dy + 2, dz, 3 * width), F32),
        ],
        flops=4 * dx * dy * dz * 27 * width * filters,
    )
    block_out, grad, deep_windows = deep[:3]
    terms = paired(deep[3:], "filt")

    early_rows = 27 * cin // space
    deep_rows = ceil_to(-(-27 * filters // space), 16)
    deep_first, deep_second = call(
        deep_grad_body,
        "deep_grad",
        [struct((chips, deep_rows, width)), struct((chips, deep_rows, width), F32)],
        ids,
        (deep_windows, grad),
        [pltpu.VMEM((2, chips * deep_rows, width), F32)],
        flops=2 * dx * dy * dz * 27 * width * filters,
    )
    piece = (chips, early_rows + deep_rows, width)
    held = pltpu.VMEM((27 * cin // 2, width), F32)
    flops = (nx + 4) * rows * 36 * cin * 2 * width
    theirs, grad = call(
        functools.partial(early_grad_body, half),
        "early_grad",
        [struct(piece), struct((nx + 4, rows, 2 * width))],
        ids,
        (*terms, sg, turned, deep_first),
        [held],
        flops=flops,
    )
    theirs = lax.ppermute(theirs, "space", [(i, i ^ 1) for i in range(space)])
    mine = call(
        early_grad_rest_body,
        "early_grad_rest",
        struct(piece, F32),
        ids,
        (grad, turned, deep_second),
        [held],
        flops=flops,
    )
    sums = call(
        core_sum_body,
        "core_sum",
        [struct(piece[1:], F32)] + [struct(piece[1:])] * (chips - 1),
        ids,
        (mine, theirs),
    )
    sums = paired(sums, "space", 2)
    small = ceil_to(-(-early_rows // filt), 16)
    deep_sum, *shares = call(
        functools.partial(chip_sum_body, chips, early_rows),
        "chip_sum",
        [struct((deep_rows, width)), struct((small, width), F32)]
        + [struct((small, width))] * (filt - 1),
        ids,
        sums,
        [pltpu.VMEM((small * filt, width), F32)],
    )
    share = call(sum_body, "filt_sum", struct((small, width)), ids, paired(shares, "filt"))
    shares = paired([share] * filt, "filt")
    final_rows = small * filt + deep_rows
    final = call(line_up_body, "line_up", struct((final_rows, width)), ids, (*shares, deep_sum))
    finals = paired([final] * chips, "space", 2)
    own = call(stack_body, "stack", struct((chips, final_rows, width)), ids, finals)
    other = lax.ppermute(own, "space", [(i, i ^ 1) for i in range(space)])
    early_total = nx * ny * nz * space * filt
    deep_total = dx * dy * dz * space
    grad_early, grad_deep = call(
        functools.partial(
            finish_body, 1.0 / math.sqrt(early_total), 1.0 / math.sqrt(deep_total), early_rows
        ),
        "finish",
        [struct((27, cin, width), F32), struct((27, filters, width), F32)],
        ids,
        (own, other),
    )
    return (block_out, grad_early, jnp.swapaxes(grad_deep, 1, 2))


def solution(mesh):
    return jax.shard_map(
        shards,
        mesh=mesh,
        in_specs=(
            P("space", "filt", None, None),
            P(),
            P(None, None, "filt"),
            P("space", None, None, "filt"),
        ),
        out_specs=(P("space", None, None, "filt"), P(), P(None, None, "filt")),
        check_vma=False,
    )
```

```python
import functools
import math

import jax
import jax.numpy as jnp
from jax import lax
from jax.experimental import pallas as pl
from jax.experimental.pallas import tpu as pltpu
from jax.sharding import PartitionSpec as P

F32 = jnp.float32
BF16 = jnp.bfloat16
VMEM_LIMIT = 24 * 1024 * 1024
VMEM = pl.BlockSpec(memory_space=pltpu.VMEM)
HBM = pl.BlockSpec(memory_space=pltpu.HBM)
DMA = pltpu.SemaphoreType.DMA


def call(
    body, name, out_shape, operands, scratch=(), flops=0, moved=1 << 20, hbm=(), outs=VMEM, alias=()
):
    return pl.pallas_call(
        body,
        name=name,
        out_shape=out_shape,
        in_specs=[HBM if i in hbm else VMEM for i in range(len(operands))],
        out_specs=jax.tree.map(lambda _: outs, out_shape),
        scratch_shapes=list(scratch),
        input_output_aliases=dict(alias),
        compiler_params=pltpu.CompilerParams(vmem_limit_bytes=VMEM_LIMIT),
        cost_estimate=pl.CostEstimate(flops=flops, bytes_accessed=moved, transcendentals=0),
    )(*operands)


def struct(shape, dtype=BF16):
    return jax.ShapeDtypeStruct(shape, dtype)


def ceil_to(value, step):
    return -(-value // step) * step


def sigmoid(value):
    return 1.0 / (1.0 + jnp.exp(-value))


def sides_body(ylo, yhi, sides):
    sides[:, 0:1] = ylo[...]
    sides[:, 1:2] = yhi[...]


def early_body(
    volume, xlo, xhi, ylo, yhi, clo, chi, w, windows, sg, pooled, center, field, wide, sem, wsem
):
    nx, ny, nz, cin = volume.shape
    cout = w.shape[3]
    half = nz // 2
    rows = ny * half
    ext = nx + 6
    space = lax.axis_size("space")
    fetch = pltpu.make_async_copy(volume, center, sem.at[0])
    fetch.start()
    weights = [
        pltpu.make_async_copy(
            w.at[pl.ds(3 * a, 3), tap],
            wide.at[
                pl.ds(3 * a, 3),
                pl.ds((tap + side) * cin, cin),
                pl.ds(side * cout, cout),
            ],
            wsem.at[a, 2 * tap + side],
        )
        for a in range(3)
        for tap in range(3)
        for side in range(2)
    ]
    for copy in weights:
        copy.start()
    wide[:, 0:cin, cout:] = jnp.zeros((9, cin, cout), BF16)
    wide[:, 3 * cin :, :cout] = jnp.zeros((9, cin, cout), BF16)
    field[:, :, 0:8] = jnp.zeros((ext, ny + 2, 8, cin), F32)
    field[:, :, 8 + nz : 16 + nz] = jnp.zeros((ext, ny + 2, 8, cin), F32)
    cells = slice(8, 8 + nz)
    for top, size, main, sides in ((0, 3, xlo, clo), (nx + 3, 3, xhi, chi)):
        first = nx - 3 if top == 0 else 0
        field[top : top + size, 1 : ny + 1, cells] = main[first : first + size].astype(F32)
        field[top : top + size, 0:1, cells] = sides[first : first + size, 0:1].astype(F32)
        field[top : top + size, ny + 1 :, cells] = sides[first : first + size, 1:2].astype(F32)
    field[3 : nx + 3, 0:1, cells] = ylo[...].astype(F32)
    field[3 : nx + 3, ny + 1 :, cells] = yhi[...].astype(F32)
    fetch.wait()
    field[3 : nx + 3, 1 : ny + 1, cells] = center[...].astype(F32)
    for x in range(ext):
        for group in range(4):
            plane = field[x, :, pl.ds(7 + group, half, stride=2), :]
            for b in range(3):
                windows[b, x, :, group * cin : (group + 1) * cin] = (
                    plane[b : b + ny].reshape(rows, cin).astype(BF16)
                )
    low = jnp.where(lax.axis_index("space") > 0, 1.0, 0.0).astype(F32)
    high = jnp.where(lax.axis_index("space") < space - 1, 1.0, 0.0).astype(F32)
    for chunk in range(nx // 2 + 2):
        start = 2 * chunk
        acc = jnp.zeros((2 * rows, 2 * cout), F32)
        for ab in range(9):
            a, b = ab // 3, ab % 3
            if chunk == 0 and b == 0:
                for copy in weights[6 * a : 6 * a + 6]:
                    copy.wait()
            left = windows[b, start + a : start + a + 2].reshape(2 * rows, 4 * cin)
            acc = acc + jnp.dot(left, wide[ab], preferred_element_type=F32)
        sig = sigmoid(acc)
        keep = 0.125
        if chunk == 0:
            keep = 0.125 * low
        if chunk == nx // 2 + 1:
            keep = 0.125 * high
        sg[start : start + 2] = (sig * (1.0 + acc * (1.0 - sig)) * keep).reshape(
            2, rows, 2 * cout
        )
        act = acc * sig
        act = act[:rows] + act[rows:]
        act = act[:, :cout] + act[:, cout:]
        act = act.reshape(ny // 2, 2, half, cout)
        act = (act[:, 0] + act[:, 1]) * keep
        pooled[chunk] = act.reshape(rows // 2, cout).astype(BF16)


def transpose_body(windows, turned):
    rows = windows.shape[2]
    part = turned.shape[2] // 4
    for b in range(windows.shape[0]):
        for x in range(windows.shape[1]):
            value = windows[b, x].T
            for group in range(4):
                for side in range(2):
                    spot = (2 * group + side) * part
                    turned[
                        b, side, group * part : (group + 1) * part, x * rows : (x + 1) * rows
                    ] = value[spot : spot + part]


def roll_z(value, shift):
    size = value.shape[-2]
    rolled = pltpu.roll(value, shift % size, value.ndim - 2)
    spot = lax.broadcasted_iota(jnp.int32, value.shape, value.ndim - 2)
    edge = 0 if shift == 1 else size - 1
    return jnp.where(spot == edge, 0.0, rolled)


def deep_body(parts_n, *refs):
    parts = refs[:parts_n]
    wt, cotangent = refs[parts_n : parts_n + 2]
    block_out, grad, windows = refs[parts_n + 2 : parts_n + 5]
    sends = refs[parts_n + 5 : 2 * parts_n + 5]
    field, terms, wide, cot, sem = refs[2 * parts_n + 5 :]
    nx, ny, nz, filters = cot.shape
    width = wt.shape[3]
    copies = [
        pltpu.make_async_copy(wt.at[:, c], wide.at[:, :, pl.ds(c * width, width)], sem.at[c])
        for c in range(3)
    ] + [pltpu.make_async_copy(cotangent, cot, sem.at[3])]
    for copy in copies:
        copy.start()
    rows = ny * nz
    py = ny // parts_n
    mine = lax.axis_index("filt")
    field[:, 0:1] = jnp.zeros((nx + 2, 1, nz, width), F32)
    field[:, ny + 1 : ny + 2] = jnp.zeros((nx + 2, 1, nz, width), F32)
    for j in range(parts_n):
        spot = lax.bitwise_xor(mine, j) * py + 1
        field[:, pl.ds(spot, py)] = parts[j][...].astype(F32).reshape(nx + 2, py, nz, width)
    for x in range(nx + 2):
        plane = field[x]
        for c in range(3):
            moved = plane if c == 1 else roll_z(plane, 1 - c)
            for b in range(3):
                windows[b, x, :, c * width : (c + 1) * width] = (
                    moved[b : b + ny].reshape(rows, width).astype(BF16)
                )
    for copy in copies:
        copy.wait()
    for x in range(nx):
        acc = jnp.zeros((rows, filters), F32)
        for ab in range(9):
            a, b = ab // 3, ab % 3
            acc = acc + lax.dot_general(
                windows[b, x + a], wide[ab], (((1,), (1,)), ((), ())), preferred_element_type=F32
            )
        sig = sigmoid(acc)
        block_out[x] = (acc * sig).reshape(ny, nz, filters).astype(BF16)
        slope = sig * (1.0 + acc * (1.0 - sig))
        grad[x] = (cot[x].astype(F32).reshape(rows, filters) * slope).astype(BF16)
    terms[...] = jnp.zeros(terms.shape, F32)
    for ab in range(9):
        a, b = ab // 3, ab % 3
        for x in range(nx):
            part = jnp.dot(grad[x], wide[ab], preferred_element_type=F32)
            terms[x + a, b : b + ny] += part.reshape(ny, nz, 3 * width)
    for j in range(parts_n):
        spot = lax.bitwise_xor(mine, j) * py + 1
        value = terms[:, pl.ds(spot, py)]
        total = value[..., width : 2 * width]
        total = total + roll_z(value[..., :width], -1) + roll_z(value[..., 2 * width :], 1)
        sends[j][...] = total.reshape(nx + 2, py * nz, width).astype(sends[j].dtype)


def deep_grad_body(windows, grad, theirs, mine, held):
    nx, rows, filters = grad.shape
    width = windows.shape[3] // 3
    turned = grad[...].reshape(nx * rows, filters).astype(F32).T.astype(BF16)
    chips, step, _ = mine.shape
    part = filters // 2
    total = 27 * part
    if chips * step > total:
        held[:, total:] = jnp.zeros((2, chips * step - total, width), F32)
    for ab in range(9):
        a, b = ab // 3, ab % 3
        value = jnp.dot(
            turned,
            windows[b, a : a + nx].reshape(nx * rows, 3 * width),
            preferred_element_type=F32,
        )
        for c in range(3):
            spot = (3 * ab + c) * part
            for side in range(2):
                held[side, spot : spot + part] = value[
                    side * part : (side + 1) * part, c * width : (c + 1) * width
                ]
    core = lax.rem(lax.axis_index("space"), 2)
    for q in range(chips):
        theirs[q] = held[1 - core, q * step : (q + 1) * step].astype(theirs.dtype)
        mine[q] = held[core, q * step : (q + 1) * step]


def early_grad_body(nz, *refs):
    parts, (sg, turned, deep, out, grad, held) = refs[:-6], refs[-6:]
    ext, rows, wide = sg.shape
    total = parts[0][...]
    for part in parts[1:]:
        total = total + part[...].astype(F32)
    px, prow, _ = total.shape
    py = prow // nz
    total = jnp.concatenate([total, total], axis=2).reshape(px, py, 1, nz, wide)
    total = jnp.broadcast_to(total, (px, py, 2, nz, wide)).reshape(px, rows, wide)
    for x in range(ext):
        grad[x] = (total[x // 2] * sg[x]).astype(BF16)
    early_grad_half(1 - lax.rem(lax.axis_index("space"), 2), grad, turned, deep, out, held)


def early_grad_rest_body(grad, turned, deep, out, held):
    early_grad_half(lax.rem(lax.axis_index("space"), 2), grad, turned, deep, out, held)


def early_grad_half(side, grad, turned, deep, out, held):
    ext, rows, wide = grad.shape
    width = wide // 2
    part = turned.shape[2] // 4
    right = grad[...].reshape(ext * rows, wide)
    for ab in range(9):
        a, b = ab // 3, ab % 3
        value = jnp.dot(
            turned[b, side, :, a * rows : (a + ext) * rows], right, preferred_element_type=F32
        )
        for c in range(3):
            spot = (3 * ab + c) * part
            held[spot : spot + part] = (
                value[c * part : (c + 1) * part, :width]
                + value[(c + 1) * part : (c + 2) * part, width:]
            )
    step = held.shape[0] // out.shape[0]
    for q in range(out.shape[0]):
        out[q, :step] = held[q * step : (q + 1) * step].astype(out.dtype)
        out[q, step:] = deep[q].astype(out.dtype)


def core_sum_body(mine, other, *outs):
    chip = lax.div(lax.axis_index("space"), 2)
    for j, out in enumerate(outs):
        q = lax.bitwise_xor(chip, j)
        out[...] = (mine[q] + other[q].astype(F32)).astype(out.dtype)


def chip_sum_body(count, step, *refs):
    others, (deep, *outs, held) = refs[:count], refs[count:]
    total = others[0][...]
    for ref in others[1:]:
        total = total + ref[...].astype(F32)
    held[:step] = total[:step]
    if held.shape[0] > step:
        held[step:] = jnp.zeros((held.shape[0] - step, total.shape[1]), F32)
    deep[...] = total[step:].astype(BF16)
    size = outs[0].shape[0]
    for j, out in enumerate(outs):
        spot = pl.multiple_of(lax.bitwise_xor(lax.axis_index("filt"), j) * size, 8)
        out[...] = held[pl.ds(spot, size)].astype(out.dtype)


def sum_body(*refs):
    total = refs[0][...]
    for ref in refs[1:-1]:
        total = total + ref[...].astype(F32)
    refs[-1][...] = total.astype(BF16)


def line_up_body(*refs):
    shares, deep, out = refs[:-2], refs[-2], refs[-1]
    size = shares[0].shape[0]
    for j, share in enumerate(shares):
        spot = pl.multiple_of(lax.bitwise_xor(lax.axis_index("filt"), j) * size, 16)
        out[pl.ds(spot, size)] = share[...]
    out[size * len(shares) :] = deep[...]


def stack_body(*refs):
    out = refs[-1]
    chip = lax.div(lax.axis_index("space"), 2)
    for j, ref in enumerate(refs[:-1]):
        out[lax.bitwise_xor(chip, j)] = ref[...]


def finish_body(own, early_scale, deep_scale, early_rows, deep_rows, pieces, *refs):
    early, deep, early_held, deep_held, sem = refs[-5:]
    core = lax.rem(lax.axis_index("space"), 2)
    side = core if own else 1 - core
    copies = []
    for out, held, first, step, scale in (
        (early, early_held, 0, early_rows, early_scale),
        (deep, deep_held, pieces.shape[1] - deep_rows, deep_rows, deep_scale),
    ):
        part = held.shape[1]
        for tap in range(27):
            row = tap * part
            while row < (tap + 1) * part:
                q, inner = row // step, row % step
                size = min(step - inner, (tap + 1) * part - row)
                spot = row - tap * part
                held[tap, spot : spot + size] = (
                    pieces[q, first + inner : first + inner + size].astype(F32) * scale
                )
                row += size
            if tap % 9 == 8:
                taps = pl.ds(tap - 8, 9)
                copy = pltpu.make_async_copy(
                    held.at[taps], out.at[taps, pl.ds(side * part, part)], sem.at[len(copies)]
                )
                copy.start()
                copies.append(copy)
    for copy in copies:
        copy.wait()


def paired(values, axis, step=1):
    count = lax.axis_size(axis)
    got = {
        j: lax.ppermute(values[j], axis, [(i, i ^ (step * j)) for i in range(count)])
        for j in reversed(range(1, len(values)))
    }
    return [values[0]] + [got[j] for j in range(1, len(values))]


def backward(values):
    return [values[0]] + values[:0:-1]


def both_sides(low, high, axis):
    count = lax.axis_size(axis)
    forward = [(i, i + 1) for i in range(count - 1)]
    backward = [(i + 1, i) for i in range(count - 1)]
    return lax.ppermute(high, axis, forward), lax.ppermute(low, axis, backward)


def shards(volume, w_early, w_deep, cotangent):
    nx, ny, nz, cin = volume.shape
    width = w_early.shape[2]
    filters = w_deep.shape[2]
    space = lax.axis_size("space")
    filt = lax.axis_size("filt")
    chips = space // 2
    half = nz // 2
    ext = nx + 6
    rows = ny * half
    ylo, yhi = both_sides(volume[:, :1], volume[:, ny - 1 :], "filt")
    xlo, xhi = both_sides(volume, volume, "space")
    sides = call(
        sides_body,
        "sides",
        struct((nx, 2, nz, cin)),
        (ylo, yhi),
        flops=1 << 32,
        moved=1 << 24,
    )
    clo, chi = both_sides(sides, sides, "space")
    windows, sg, pooled = call(
        early_body,
        "early_conv",
        (
            struct((3, ext, rows, 4 * cin)),
            struct((nx + 4, rows, 2 * width), F32),
            struct((nx // 2 + 2, rows // 2, width)),
        ),
        (volume, xlo, xhi, ylo, yhi, clo, chi, w_early.reshape(9, 3, cin, width)),
        [
            pltpu.VMEM(volume.shape, BF16),
            pltpu.VMEM((ext, ny + 2, nz + 16, cin), F32),
            pltpu.VMEM((9, 4 * cin, 2 * width), BF16),
            DMA((1,)),
            DMA((3, 6)),
        ],
        flops=2 * (nx + 4) * rows * 36 * cin * 2 * width,
        hbm=(0, 7),
    )
    parts = paired([pooled] * filt, "filt")
    turned = call(
        transpose_body,
        "turn_windows",
        struct((3, 2, 2 * cin, ext * rows)),
        (windows,),
        flops=1 << 30,
    )
    *parts, turned = lax.optimization_barrier((*parts, turned))
    dx, dy, dz, _ = cotangent.shape
    px = dx + 2
    prow = rows // 2
    deep = call(
        functools.partial(deep_body, filt),
        "deep_conv",
        [
            struct(cotangent.shape),
            struct((dx, dy * dz, filters)),
            struct((3, px, dy * dz, 3 * width)),
            struct((px, prow, width), F32),
        ]
        + [struct((px, prow, width))] * (filt - 1),
        (*parts, jnp.swapaxes(w_deep, 1, 2).reshape(9, 3, filters, width), cotangent),
        [
            pltpu.VMEM((px, dy + 2, dz, width), F32),
            pltpu.VMEM((px, dy + 2, dz, 3 * width), F32),
            pltpu.VMEM((9, filters, 3 * width), BF16),
            pltpu.VMEM(cotangent.shape, BF16),
            DMA((4,)),
        ],
        hbm=(filt, filt + 1),
        flops=4 * dx * dy * dz * 27 * width * filters,
    )
    block_out, grad, deep_windows = deep[:3]
    terms = paired(deep[3:], "filt")

    early_rows = 27 * cin // space
    deep_rows = ceil_to(-(-27 * filters // space), 16)
    deep_first, deep_second = call(
        deep_grad_body,
        "deep_grad",
        [struct((chips, deep_rows, width)), struct((chips, deep_rows, width), F32)],
        (deep_windows, grad),
        [pltpu.VMEM((2, chips * deep_rows, width), F32)],
        flops=2 * dx * dy * dz * 27 * width * filters,
    )
    piece = (chips, early_rows + deep_rows, width)
    held = pltpu.VMEM((27 * cin // 2, width), F32)
    flops = (nx + 4) * rows * 36 * cin * 2 * width
    theirs, grad = call(
        functools.partial(early_grad_body, half),
        "early_grad",
        [struct(piece), struct((nx + 4, rows, 2 * width))],
        (*backward(terms), sg, turned, deep_first),
        [held],
        flops=flops,
    )
    theirs = lax.ppermute(theirs, "space", [(i, i ^ 1) for i in range(space)])
    mine = call(
        early_grad_rest_body,
        "early_grad_rest",
        struct(piece, F32),
        (grad, turned, deep_second),
        [held],
        flops=flops,
    )
    sums = call(
        core_sum_body,
        "core_sum",
        [struct(piece[1:], F32)] + [struct(piece[1:])] * (chips - 1),
        (mine, theirs),
    )
    sums = backward(paired(sums, "space", 2))
    small = ceil_to(-(-early_rows // filt), 16)
    deep_sum, *shares = call(
        functools.partial(chip_sum_body, chips, early_rows),
        "chip_sum",
        [struct((deep_rows, width)), struct((small, width), F32)]
        + [struct((small, width))] * (filt - 1),
        sums,
        [pltpu.VMEM((small * filt, width), F32)],
    )
    share = call(sum_body, "filt_sum", struct((small, width)), backward(paired(shares, "filt")))
    shares = paired([share] * filt, "filt")
    final_rows = small * filt + deep_rows
    final = call(line_up_body, "line_up", struct((final_rows, width)), (*shares, deep_sum))
    finals = paired([final] * chips, "space", 2)
    own = call(stack_body, "stack", struct((chips, final_rows, width)), finals)
    other = lax.ppermute(own, "space", [(i, i ^ 1) for i in range(space)])
    early_total = nx * ny * nz * space * filt
    deep_total = dx * dy * dz * space
    results = [struct((27, cin, width), F32), struct((27, filters, width), F32)]
    scales = (1.0 / math.sqrt(early_total), 1.0 / math.sqrt(deep_total), early_rows, deep_rows)
    scratch = [
        pltpu.VMEM((27, cin // 2, width), F32),
        pltpu.VMEM((27, filters // 2, width), F32),
        DMA((6,)),
    ]
    results = call(
        functools.partial(finish_body, True, *scales),
        "finish_own",
        results,
        (own,),
        scratch,
        outs=HBM,
    )
    grad_early, grad_deep = call(
        functools.partial(finish_body, False, *scales),
        "finish_other",
        [struct(value.shape, F32) for value in results],
        (other, *results),
        scratch,
        hbm=(1, 2),
        outs=HBM,
        alias=((1, 0), (2, 1)),
    )
    return (block_out, grad_early, jnp.swapaxes(grad_deep, 1, 2))


def solution(mesh):
    return jax.shard_map(
        shards,
        mesh=mesh,
        in_specs=(
            P("space", "filt", None, None),
            P(),
            P(None, None, "filt"),
            P("space", None, None, "filt"),
        ),
        out_specs=(P("space", None, None, "filt"), P(), P(None, None, "filt")),
        check_vma=False,
    )
```

```python
import functools
import math

import jax
import jax.numpy as jnp
from jax import lax
from jax.experimental import pallas as pl
from jax.experimental.pallas import tpu as pltpu
from jax.sharding import PartitionSpec as P

F32 = jnp.float32
BF16 = jnp.bfloat16
VMEM_LIMIT = 24 * 1024 * 1024
VMEM = pl.BlockSpec(memory_space=pltpu.VMEM)
HBM = pl.BlockSpec(memory_space=pltpu.HBM)
DMA = pltpu.SemaphoreType.DMA


def call(
    body, name, out_shape, operands, scratch=(), flops=0, moved=1 << 20, hbm=(), outs=VMEM, alias=()
):
    return pl.pallas_call(
        body,
        name=name,
        out_shape=out_shape,
        in_specs=[HBM if i in hbm else VMEM for i in range(len(operands))],
        out_specs=jax.tree.map(lambda _: outs, out_shape),
        scratch_shapes=list(scratch),
        input_output_aliases=dict(alias),
        compiler_params=pltpu.CompilerParams(vmem_limit_bytes=VMEM_LIMIT),
        cost_estimate=pl.CostEstimate(flops=flops, bytes_accessed=moved, transcendentals=0),
    )(*operands)


def struct(shape, dtype=BF16):
    return jax.ShapeDtypeStruct(shape, dtype)


def ceil_to(value, step):
    return -(-value // step) * step


def sigmoid(value):
    return 1.0 / (1.0 + jnp.exp(-value))


def sides_body(even_pair, odd_pair, sides):
    even = lax.rem(lax.axis_index("filt"), 2) == 0
    sides[:, 0:1] = jnp.where(even, odd_pair[:, 1:2], even_pair[:, 1:2])
    sides[:, 1:2] = jnp.where(even, even_pair[:, 0:1], odd_pair[:, 0:1])


def early_body(center, xeven, xodd, mid, ceven, codd, w, windows, sg, pooled, field, wide):
    nx, ny, nz, cin = center.shape
    cout = w.shape[2]
    half = nz // 2
    rows = ny * half
    ext = nx + 6
    space = lax.axis_size("space")
    for ab in range(9):
        for group in range(4):
            for side in range(2):
                tap = group - side
                value = w[3 * ab + tap] if 0 <= tap <= 2 else jnp.zeros((cin, cout), BF16)
                wide[
                    ab, group * cin : (group + 1) * cin, side * cout : (side + 1) * cout
                ] = value
    field[:, :, 0:8] = jnp.zeros((ext, ny + 2, 8, cin), F32)
    field[:, :, 8 + nz : 16 + nz] = jnp.zeros((ext, ny + 2, 8, cin), F32)
    cells = slice(8, 8 + nz)
    even = lax.rem(lax.axis_index("space"), 2) == 0
    for top, first, main, edge in (
        (0, nx - 3, (xodd, xeven), (codd, ceven)),
        (nx + 3, 0, (xeven, xodd), (ceven, codd)),
    ):
        take = slice(first, first + 3)
        field[top : top + 3, 1 : ny + 1, cells] = jnp.where(
            even, main[0][take].astype(F32), main[1][take].astype(F32)
        )
        beside = jnp.where(even, edge[0][take].astype(F32), edge[1][take].astype(F32))
        field[top : top + 3, 0:1, cells] = beside[:, 0:1]
        field[top : top + 3, ny + 1 :, cells] = beside[:, 1:2]
    field[3 : nx + 3, 0:1, cells] = mid[:, 0:1].astype(F32)
    field[3 : nx + 3, ny + 1 :, cells] = mid[:, 1:2].astype(F32)
    field[3 : nx + 3, 1 : ny + 1, cells] = center[...].astype(F32)
    for x in range(ext):
        for group in range(4):
            plane = field[x, :, pl.ds(7 + group, half, stride=2), :]
            for b in range(3):
                windows[b, x, :, group * cin : (group + 1) * cin] = (
                    plane[b : b + ny].reshape(rows, cin).astype(BF16)
                )
    low = jnp.where(lax.axis_index("space") > 0, 1.0, 0.0).astype(F32)
    high = jnp.where(lax.axis_index("space") < space - 1, 1.0, 0.0).astype(F32)
    for chunk in range(nx // 2 + 2):
        start = 2 * chunk
        acc = jnp.zeros((2 * rows, 2 * cout), F32)
        for ab in range(9):
            a, b = ab // 3, ab % 3
            left = windows[b, start + a : start + a + 2].reshape(2 * rows, 4 * cin)
            acc = acc + jnp.dot(left, wide[ab], preferred_element_type=F32)
        sig = sigmoid(acc)
        keep = 0.125
        if chunk == 0:
            keep = 0.125 * low
        if chunk == nx // 2 + 1:
            keep = 0.125 * high
        sg[start : start + 2] = (sig * (1.0 + acc * (1.0 - sig)) * keep).reshape(
            2, rows, 2 * cout
        )
        act = acc * sig
        act = act[:rows] + act[rows:]
        act = act[:, :cout] + act[:, cout:]
        act = act.reshape(ny // 2, 2, half, cout)
        act = (act[:, 0] + act[:, 1]) * keep
        pooled[chunk] = act.reshape(rows // 2, cout).astype(BF16)


def transpose_body(windows, turned):
    rows = windows.shape[2]
    part = turned.shape[2] // 4
    for b in range(windows.shape[0]):
        for x in range(windows.shape[1]):
            value = windows[b, x].T
            for group in range(4):
                for side in range(2):
                    spot = (2 * group + side) * part
                    turned[
                        b, side, group * part : (group + 1) * part, x * rows : (x + 1) * rows
                    ] = value[spot : spot + part]


def roll_z(value, shift):
    size = value.shape[-2]
    rolled = pltpu.roll(value, shift % size, value.ndim - 2)
    spot = lax.broadcasted_iota(jnp.int32, value.shape, value.ndim - 2)
    edge = 0 if shift == 1 else size - 1
    return jnp.where(spot == edge, 0.0, rolled)


def deep_body(parts_n, *refs):
    parts = refs[:parts_n]
    wt, cot = refs[parts_n : parts_n + 2]
    block_out, grad, windows = refs[parts_n + 2 : parts_n + 5]
    sends = refs[parts_n + 5 : 2 * parts_n + 5]
    field, wide, slopes, turned, terms = refs[2 * parts_n + 5 :]
    nx, ny, nz, filters = cot.shape
    width = wt.shape[2]
    rows = ny * nz
    py = ny // parts_n
    mine = lax.axis_index("filt")
    for ab in range(9):
        for c in range(3):
            wide[ab, :, c * width : (c + 1) * width] = wt[
                ab, c * filters : (c + 1) * filters
            ]
    field[:, 0:1] = jnp.zeros((nx + 2, 1, nz, width), F32)
    field[:, ny + 1 : ny + 2] = jnp.zeros((nx + 2, 1, nz, width), F32)
    for j in range(parts_n):
        spot = lax.bitwise_xor(mine, j) * py + 1
        field[:, pl.ds(spot, py)] = parts[j][...].astype(F32).reshape(nx + 2, py, nz, width)
    for x in range(nx + 2):
        plane = field[x]
        for c in range(3):
            moved = plane if c == 1 else roll_z(plane, 1 - c)
            for b in range(3):
                windows[b, x, :, c * width : (c + 1) * width] = (
                    moved[b : b + ny].reshape(rows, width).astype(BF16)
                )
    slopes[:, 0:1] = jnp.zeros((nx, 1, nz, filters), F32)
    slopes[:, ny + 1 :] = jnp.zeros((nx, 1, nz, filters), F32)
    for x in range(nx):
        acc = jnp.zeros((rows, filters), F32)
        for ab in range(9):
            a, b = ab // 3, ab % 3
            acc = acc + lax.dot_general(
                windows[b, x + a], wide[ab], (((1,), (1,)), ((), ())), preferred_element_type=F32
            )
        sig = sigmoid(acc)
        block_out[x] = (acc * sig).reshape(ny, nz, filters).astype(BF16)
        slope = sig * (1.0 + acc * (1.0 - sig))
        value = (cot[x].astype(F32).reshape(rows, filters) * slope).astype(BF16)
        grad[x] = value
        slopes[x, 1 : ny + 1] = value.astype(F32).reshape(ny, nz, filters)
    for x in range(nx):
        plane = slopes[x]
        plane = jnp.concatenate([roll_z(plane, -1), plane, roll_z(plane, 1)], axis=2)
        for b in range(3):
            turned[b, x] = (
                plane[2 - b : 2 - b + ny].reshape(rows, 3 * filters).astype(BF16)
            )
    for r in range(nx + 2):
        total = jnp.zeros((rows, width), F32)
        for ab in range(9):
            a, b = ab // 3, ab % 3
            if 0 <= r - a < nx:
                total = total + jnp.dot(turned[b, r - a], wt[ab], preferred_element_type=F32)
        terms[r] = total.reshape(ny, nz, width)
    for j in range(parts_n):
        spot = lax.bitwise_xor(mine, j) * py
        value = terms[:, pl.ds(spot, py)]
        sends[j][...] = value.reshape(nx + 2, py * nz, width).astype(sends[j].dtype)


def deep_grad_body(windows, grad, theirs, mine, held):
    nx, rows, filters = grad.shape
    width = windows.shape[3] // 3
    turned = grad[...].reshape(nx * rows, filters).astype(F32).T.astype(BF16)
    chips, step, _ = mine.shape
    part = filters // 2
    total = 27 * part
    if chips * step > total:
        held[:, total:] = jnp.zeros((2, chips * step - total, width), F32)
    for ab in range(9):
        a, b = ab // 3, ab % 3
        value = jnp.dot(
            turned,
            windows[b, a : a + nx].reshape(nx * rows, 3 * width),
            preferred_element_type=F32,
        )
        for c in range(3):
            spot = (3 * ab + c) * part
            for side in range(2):
                held[side, spot : spot + part] = value[
                    side * part : (side + 1) * part, c * width : (c + 1) * width
                ]
    core = lax.rem(lax.axis_index("space"), 2)
    for q in range(chips):
        theirs[q] = held[1 - core, q * step : (q + 1) * step].astype(theirs.dtype)
        mine[q] = held[core, q * step : (q + 1) * step]


def early_grad_body(nz, *refs):
    parts, (sg, turned, deep, out, grad, held) = refs[:-6], refs[-6:]
    ext, rows, wide = sg.shape
    total = parts[0][...]
    for part in parts[1:]:
        total = total + part[...].astype(F32)
    px, prow, _ = total.shape
    py = prow // nz
    total = jnp.concatenate([total, total], axis=2).reshape(px, py, 1, nz, wide)
    total = jnp.broadcast_to(total, (px, py, 2, nz, wide)).reshape(px, rows, wide)
    for x in range(ext):
        grad[x] = (total[x // 2] * sg[x]).astype(BF16)
    early_grad_half(1 - lax.rem(lax.axis_index("space"), 2), grad, turned, deep, out, held)


def early_grad_rest_body(grad, turned, deep, out, held):
    early_grad_half(lax.rem(lax.axis_index("space"), 2), grad, turned, deep, out, held)


def early_grad_half(side, grad, turned, deep, out, held):
    ext, rows, wide = grad.shape
    width = wide // 2
    part = turned.shape[2] // 4
    right = grad[...].reshape(ext * rows, wide)
    for ab in range(9):
        a, b = ab // 3, ab % 3
        value = jnp.dot(
            turned[b, side, :, a * rows : (a + ext) * rows], right, preferred_element_type=F32
        )
        for c in range(3):
            spot = (3 * ab + c) * part
            held[spot : spot + part] = (
                value[c * part : (c + 1) * part, :width]
                + value[(c + 1) * part : (c + 2) * part, width:]
            )
    step = held.shape[0] // out.shape[0]
    for q in range(out.shape[0]):
        out[q, :step] = held[q * step : (q + 1) * step].astype(out.dtype)
        out[q, step:] = deep[q].astype(out.dtype)


def core_sum_body(mine, other, *outs):
    chip = lax.div(lax.axis_index("space"), 2)
    for j, out in enumerate(outs):
        q = lax.bitwise_xor(chip, j)
        out[...] = (mine[q] + other[q].astype(F32)).astype(out.dtype)


def chip_sum_body(count, step, *refs):
    others, (deep, *outs, held) = refs[:count], refs[count:]
    total = others[0][...]
    for ref in others[1:]:
        total = total + ref[...].astype(F32)
    held[:step] = total[:step]
    if held.shape[0] > step:
        held[step:] = jnp.zeros((held.shape[0] - step, total.shape[1]), F32)
    deep[...] = total[step:].astype(BF16)
    size = outs[0].shape[0]
    for j, out in enumerate(outs):
        spot = pl.multiple_of(lax.bitwise_xor(lax.axis_index("filt"), j) * size, 8)
        out[...] = held[pl.ds(spot, size)].astype(out.dtype)


def sum_body(*refs):
    total = refs[0][...]
    for ref in refs[1:-1]:
        total = total + ref[...].astype(F32)
    refs[-1][...] = total.astype(BF16)


def line_up_body(*refs):
    shares, deep, out = refs[:-2], refs[-2], refs[-1]
    size = shares[0].shape[0]
    for j, share in enumerate(shares):
        spot = pl.multiple_of(lax.bitwise_xor(lax.axis_index("filt"), j) * size, 16)
        out[pl.ds(spot, size)] = share[...]
    out[size * len(shares) :] = deep[...]


def stack_body(*refs):
    out = refs[-1]
    chip = lax.div(lax.axis_index("space"), 2)
    for j, ref in enumerate(refs[:-1]):
        out[lax.bitwise_xor(chip, j)] = ref[...]


def finish_body(own, early_scale, deep_scale, early_rows, deep_rows, pieces, *refs):
    early, deep, early_held, deep_held, sem = refs[-5:]
    core = lax.rem(lax.axis_index("space"), 2)
    side = core if own else 1 - core
    copies = []
    for out, held, first, step, scale in (
        (early, early_held, 0, early_rows, early_scale),
        (deep, deep_held, pieces.shape[1] - deep_rows, deep_rows, deep_scale),
    ):
        part = held.shape[1]
        for tap in range(27):
            row = tap * part
            while row < (tap + 1) * part:
                q, inner = row // step, row % step
                size = min(step - inner, (tap + 1) * part - row)
                spot = row - tap * part
                held[tap, spot : spot + size] = (
                    pieces[q, first + inner : first + inner + size].astype(F32) * scale
                )
                row += size
            if tap % 9 == 8:
                taps = pl.ds(tap - 8, 9)
                copy = pltpu.make_async_copy(
                    held.at[taps], out.at[taps, pl.ds(side * part, part)], sem.at[len(copies)]
                )
                copy.start()
                copies.append(copy)
    for copy in copies:
        copy.wait()


def paired(values, axis, step=1):
    count = lax.axis_size(axis)
    got = {
        j: lax.ppermute(values[j], axis, [(i, i ^ (step * j)) for i in range(count)])
        for j in reversed(range(1, len(values)))
    }
    return [values[0]] + [got[j] for j in range(1, len(values))]


def backward(values):
    return [values[0]] + values[:0:-1]


def neighbours(value, axis):
    count = lax.axis_size(axis)
    return [
        lax.ppermute(
            value,
            axis,
            [pair for i in range(first, count - 1, 2) for pair in ((i, i + 1), (i + 1, i))],
        )
        for first in (0, 1)
    ]


def shards(volume, w_early, w_deep, cotangent):
    nx, ny, nz, cin = volume.shape
    width = w_early.shape[2]
    filters = w_deep.shape[2]
    space = lax.axis_size("space")
    filt = lax.axis_size("filt")
    chips = space // 2
    half = nz // 2
    ext = nx + 6
    rows = ny * half
    edges = jnp.concatenate([volume[:, :1], volume[:, ny - 1 :]], axis=1)
    yeven, yodd = neighbours(edges, "filt")
    xeven, xodd = neighbours(volume, "space")
    sides = call(
        sides_body,
        "sides",
        struct((nx, 2, nz, cin)),
        (yeven, yodd),
        flops=1 << 32,
        moved=1 << 24,
    )
    ceven, codd = neighbours(sides, "space")
    windows, sg, pooled = call(
        early_body,
        "early_conv",
        (
            struct((3, ext, rows, 4 * cin)),
            struct((nx + 4, rows, 2 * width), F32),
            struct((nx // 2 + 2, rows // 2, width)),
        ),
        (volume, xeven, xodd, sides, ceven, codd, w_early),
        [
            pltpu.VMEM((ext, ny + 2, nz + 16, cin), F32),
            pltpu.VMEM((9, 4 * cin, 2 * width), BF16),
        ],
        flops=2 * (nx + 4) * rows * 36 * cin * 2 * width,
    )
    parts = paired([pooled] * filt, "filt")
    turned = call(
        transpose_body,
        "turn_windows",
        struct((3, 2, 2 * cin, ext * rows)),
        (windows,),
        flops=1 << 30,
    )
    *parts, turned = lax.optimization_barrier((*parts, turned))
    dx, dy, dz, _ = cotangent.shape
    px = dx + 2
    prow = rows // 2
    deep = call(
        functools.partial(deep_body, filt),
        "deep_conv",
        [
            struct(cotangent.shape),
            struct((dx, dy * dz, filters)),
            struct((3, px, dy * dz, 3 * width)),
            struct((px, prow, width), F32),
        ]
        + [struct((px, prow, width))] * (filt - 1),
        (*parts, jnp.swapaxes(w_deep, 1, 2).reshape(9, 3 * filters, width), cotangent),
        [
            pltpu.VMEM((px, dy + 2, dz, width), F32),
            pltpu.VMEM((9, filters, 3 * width), BF16),
            pltpu.VMEM((dx, dy + 2, dz, filters), F32),
            pltpu.VMEM((3, dx, dy * dz, 3 * filters), BF16),
            pltpu.VMEM((px, dy, dz, width), F32),
        ],
        flops=4 * dx * dy * dz * 27 * width * filters,
    )
    block_out, grad, deep_windows = deep[:3]
    terms = paired(deep[3:], "filt")

    early_rows = 27 * cin // space
    deep_rows = ceil_to(-(-27 * filters // space), 16)
    deep_first, deep_second = call(
        deep_grad_body,
        "deep_grad",
        [struct((chips, deep_rows, width)), struct((chips, deep_rows, width), F32)],
        (deep_windows, grad),
        [pltpu.VMEM((2, chips * deep_rows, width), F32)],
        flops=2 * dx * dy * dz * 27 * width * filters,
    )
    piece = (chips, early_rows + deep_rows, width)
    held = pltpu.VMEM((27 * cin // 2, width), F32)
    flops = (nx + 4) * rows * 36 * cin * 2 * width
    theirs, grad = call(
        functools.partial(early_grad_body, half),
        "early_grad",
        [struct(piece), struct((nx + 4, rows, 2 * width))],
        (*backward(terms), sg, turned, deep_first),
        [held],
        flops=flops,
    )
    theirs = lax.ppermute(theirs, "space", [(i, i ^ 1) for i in range(space)])
    mine = call(
        early_grad_rest_body,
        "early_grad_rest",
        struct(piece, F32),
        (grad, turned, deep_second),
        [held],
        flops=flops,
    )
    sums = call(
        core_sum_body,
        "core_sum",
        [struct(piece[1:], F32)] + [struct(piece[1:])] * (chips - 1),
        (mine, theirs),
    )
    sums = backward(paired(sums, "space", 2))
    small = ceil_to(-(-early_rows // filt), 16)
    deep_sum, *shares = call(
        functools.partial(chip_sum_body, chips, early_rows),
        "chip_sum",
        [struct((deep_rows, width)), struct((small, width), F32)]
        + [struct((small, width))] * (filt - 1),
        sums,
        [pltpu.VMEM((small * filt, width), F32)],
    )
    share = call(sum_body, "filt_sum", struct((small, width)), backward(paired(shares, "filt")))
    shares = paired([share] * filt, "filt")
    final_rows = small * filt + deep_rows
    final = call(line_up_body, "line_up", struct((final_rows, width)), (*shares, deep_sum))
    finals = paired([final] * chips, "space", 2)
    own = call(stack_body, "stack", struct((chips, final_rows, width)), finals)
    other = lax.ppermute(own, "space", [(i, i ^ 1) for i in range(space)])
    early_total = nx * ny * nz * space * filt
    deep_total = dx * dy * dz * space
    results = [struct((27, cin, width), F32), struct((27, filters, width), F32)]
    scales = (1.0 / math.sqrt(early_total), 1.0 / math.sqrt(deep_total), early_rows, deep_rows)
    scratch = [
        pltpu.VMEM((27, cin // 2, width), F32),
        pltpu.VMEM((27, filters // 2, width), F32),
        DMA((6,)),
    ]
    results = call(
        functools.partial(finish_body, True, *scales),
        "finish_own",
        results,
        (own,),
        scratch,
        outs=HBM,
    )
    grad_early, grad_deep = call(
        functools.partial(finish_body, False, *scales),
        "finish_other",
        [struct(value.shape, F32) for value in results],
        (other, *results),
        scratch,
        hbm=(1, 2),
        outs=HBM,
        alias=((1, 0), (2, 1)),
    )
    return (block_out, grad_early, jnp.swapaxes(grad_deep, 1, 2))


def solution(mesh):
    return jax.shard_map(
        shards,
        mesh=mesh,
        in_specs=(
            P("space", "filt", None, None),
            P(),
            P(None, None, "filt"),
            P("space", None, None, "filt"),
        ),
        out_specs=(P("space", None, None, "filt"), P(), P(None, None, "filt")),
        check_vma=False,
    )
```

```python
import functools
import math

import jax
import jax.numpy as jnp
from jax import lax
from jax.experimental import pallas as pl
from jax.experimental.pallas import tpu as pltpu
from jax.sharding import PartitionSpec as P

F32 = jnp.float32
BF16 = jnp.bfloat16
VMEM_LIMIT = 24 * 1024 * 1024
VMEM = pl.BlockSpec(memory_space=pltpu.VMEM)
HBM = pl.BlockSpec(memory_space=pltpu.HBM)
DMA = pltpu.SemaphoreType.DMA


def call(
    body, name, out_shape, operands, scratch=(), flops=0, moved=1 << 20, hbm=(), outs=VMEM, alias=()
):
    return pl.pallas_call(
        body,
        name=name,
        out_shape=out_shape,
        in_specs=[HBM if i in hbm else VMEM for i in range(len(operands))],
        out_specs=jax.tree.map(lambda _: outs, out_shape),
        scratch_shapes=list(scratch),
        input_output_aliases=dict(alias),
        compiler_params=pltpu.CompilerParams(vmem_limit_bytes=VMEM_LIMIT),
        cost_estimate=pl.CostEstimate(flops=flops, bytes_accessed=moved, transcendentals=0),
    )(*operands)


def struct(shape, dtype=BF16):
    return jax.ShapeDtypeStruct(shape, dtype)


def ceil_to(value, step):
    return -(-value // step) * step


def sigmoid(value):
    return 1.0 / (1.0 + jnp.exp(-value))


def sides_body(even_pair, odd_pair, sides):
    even = lax.rem(lax.axis_index("filt"), 2) == 0
    sides[:, 0:1] = jnp.where(even, odd_pair[:, 1:2], even_pair[:, 1:2])
    sides[:, 1:2] = jnp.where(even, even_pair[:, 0:1], odd_pair[:, 0:1])


def windows_body(center, xeven, xodd, windows, field):
    nx, ny, nz, cin = center.shape
    half = nz // 2
    rows = ny * half
    ext = nx + 6
    cells = slice(8, 8 + nz)
    field[:, :, 0:8] = jnp.zeros((ext, ny + 2, 8, cin), F32)
    field[:, :, 8 + nz : 16 + nz] = jnp.zeros((ext, ny + 2, 8, cin), F32)
    field[:, 0:1, cells] = jnp.zeros((ext, 1, nz, cin), F32)
    field[:, ny + 1 :, cells] = jnp.zeros((ext, 1, nz, cin), F32)
    field[3 : nx + 3, 1 : ny + 1, cells] = center[...].astype(F32)
    even = lax.rem(lax.axis_index("space"), 2) == 0
    far = xodd[...].astype(F32)
    field[0:3, 1 : ny + 1, cells] = jnp.where(even, far, xeven[nx - 3 :].astype(F32))
    field[nx + 3 :, 1 : ny + 1, cells] = jnp.where(even, xeven[:3].astype(F32), far)
    for x in range(ext):
        for group in range(4):
            plane = field[x, :, pl.ds(7 + group, half, stride=2), :]
            for b in range(3):
                windows[b, x, :, group * cin : (group + 1) * cin] = (
                    plane[b : b + ny].reshape(rows, cin).astype(BF16)
                )


def early_body(windows, mid, ceven, codd, w, sg, pooled, edges, field, wide):
    nx, _, nz, cin = mid.shape
    cout = w.shape[2]
    half = nz // 2
    rows = windows.shape[2]
    ny = rows // half
    ext = nx + 6
    space = lax.axis_size("space")
    for ab in range(9):
        for group in range(4):
            for side in range(2):
                tap = group - side
                value = w[3 * ab + tap] if 0 <= tap <= 2 else jnp.zeros((cin, cout), BF16)
                wide[
                    ab, group * cin : (group + 1) * cin, side * cout : (side + 1) * cout
                ] = value
    cells = slice(8, 8 + nz)
    field[:, :, 0:8] = jnp.zeros((ext, 2, 8, cin), F32)
    field[:, :, 8 + nz : 16 + nz] = jnp.zeros((ext, 2, 8, cin), F32)
    even = lax.rem(lax.axis_index("space"), 2) == 0
    field[0:3, :, cells] = jnp.where(
        even, codd[nx - 3 :].astype(F32), ceven[nx - 3 :].astype(F32)
    )
    field[3 : nx + 3, :, cells] = mid[...].astype(F32)
    field[nx + 3 :, :, cells] = jnp.where(even, ceven[:3].astype(F32), codd[:3].astype(F32))
    for group in range(4):
        plane = field[:, :, pl.ds(7 + group, half, stride=2), :]
        for side in range(2):
            edges[side, :, :, group * cin : (group + 1) * cin] = plane[:, side]
    corner = []
    for side in range(2):
        total = jnp.zeros(((nx + 4) * half, 2 * cout), F32)
        for a in range(3):
            left = edges[side, a : a + nx + 4].reshape((nx + 4) * half, 4 * cin).astype(BF16)
            total = total + jnp.dot(left, wide[3 * a + 2 * side], preferred_element_type=F32)
        corner.append(total.reshape(nx + 4, 1, half, 2 * cout))
    low = jnp.where(lax.axis_index("space") > 0, 1.0, 0.0).astype(F32)
    high = jnp.where(lax.axis_index("space") < space - 1, 1.0, 0.0).astype(F32)
    for chunk in range(nx // 2 + 2):
        start = 2 * chunk
        acc = jnp.zeros((2 * rows, 2 * cout), F32)
        for ab in range(9):
            a, b = ab // 3, ab % 3
            left = windows[b, start + a : start + a + 2].reshape(2 * rows, 4 * cin)
            acc = acc + jnp.dot(left, wide[ab], preferred_element_type=F32)
        acc = acc.reshape(2, ny, half, 2 * cout)
        acc = jnp.concatenate(
            [
                acc[:, :1] + corner[0][start : start + 2],
                acc[:, 1 : ny - 1],
                acc[:, ny - 1 :] + corner[1][start : start + 2],
            ],
            axis=1,
        ).reshape(2 * rows, 2 * cout)
        sig = sigmoid(acc)
        keep = 0.125
        if chunk == 0:
            keep = 0.125 * low
        if chunk == nx // 2 + 1:
            keep = 0.125 * high
        sg[start : start + 2] = (sig * (1.0 + acc * (1.0 - sig)) * keep).reshape(
            2, rows, 2 * cout
        )
        act = acc * sig
        act = act[:rows] + act[rows:]
        act = act[:, :cout] + act[:, cout:]
        act = act.reshape(ny // 2, 2, half, cout)
        act = (act[:, 0] + act[:, 1]) * keep
        pooled[chunk] = act.reshape(rows // 2, cout).astype(BF16)


def transpose_body(windows, edges, turned):
    rows = windows.shape[2]
    part = turned.shape[2] // 4
    for b in range(windows.shape[0]):
        for x in range(windows.shape[1]):
            value = windows[b, x]
            if b != 1:
                beside = edges[b // 2, x]
                value = value.astype(F32)
                if b == 0:
                    value = jnp.concatenate([beside, value[beside.shape[0] :]], axis=0)
                else:
                    value = jnp.concatenate([value[: rows - beside.shape[0]], beside], axis=0)
                value = value.astype(BF16)
            value = value.T
            for group in range(4):
                for side in range(2):
                    spot = (2 * group + side) * part
                    turned[
                        b, side, group * part : (group + 1) * part, x * rows : (x + 1) * rows
                    ] = value[spot : spot + part]


def roll_z(value, shift):
    size = value.shape[-2]
    rolled = pltpu.roll(value, shift % size, value.ndim - 2)
    spot = lax.broadcasted_iota(jnp.int32, value.shape, value.ndim - 2)
    edge = 0 if shift == 1 else size - 1
    return jnp.where(spot == edge, 0.0, rolled)


def deep_body(parts_n, *refs):
    parts = refs[:parts_n]
    wt, cot = refs[parts_n : parts_n + 2]
    block_out, grad, windows = refs[parts_n + 2 : parts_n + 5]
    sends = refs[parts_n + 5 : 2 * parts_n + 5]
    field, wide, slopes, turned, terms = refs[2 * parts_n + 5 :]
    nx, ny, nz, filters = cot.shape
    width = wt.shape[2]
    rows = ny * nz
    py = ny // parts_n
    mine = lax.axis_index("filt")
    for ab in range(9):
        for c in range(3):
            wide[ab, :, c * width : (c + 1) * width] = wt[
                ab, c * filters : (c + 1) * filters
            ]
    field[:, 0:1] = jnp.zeros((nx + 2, 1, nz, width), F32)
    field[:, ny + 1 : ny + 2] = jnp.zeros((nx + 2, 1, nz, width), F32)
    for j in range(parts_n):
        spot = lax.bitwise_xor(mine, j) * py + 1
        field[:, pl.ds(spot, py)] = parts[j][...].astype(F32).reshape(nx + 2, py, nz, width)
    for x in range(nx + 2):
        plane = field[x]
        for c in range(3):
            moved = plane if c == 1 else roll_z(plane, 1 - c)
            for b in range(3):
                windows[b, x, :, c * width : (c + 1) * width] = (
                    moved[b : b + ny].reshape(rows, width).astype(BF16)
                )
    slopes[:, 0:1] = jnp.zeros((nx, 1, nz, filters), F32)
    slopes[:, ny + 1 :] = jnp.zeros((nx, 1, nz, filters), F32)
    for x in range(nx):
        acc = jnp.zeros((rows, filters), F32)
        for ab in range(9):
            a, b = ab // 3, ab % 3
            acc = acc + lax.dot_general(
                windows[b, x + a], wide[ab], (((1,), (1,)), ((), ())), preferred_element_type=F32
            )
        sig = sigmoid(acc)
        block_out[x] = (acc * sig).reshape(ny, nz, filters).astype(BF16)
        slope = sig * (1.0 + acc * (1.0 - sig))
        value = (cot[x].astype(F32).reshape(rows, filters) * slope).astype(BF16)
        grad[x] = value
        slopes[x, 1 : ny + 1] = value.astype(F32).reshape(ny, nz, filters)
    for x in range(nx):
        plane = slopes[x]
        plane = jnp.concatenate([roll_z(plane, -1), plane, roll_z(plane, 1)], axis=2)
        for b in range(3):
            turned[b, x] = (
                plane[2 - b : 2 - b + ny].reshape(rows, 3 * filters).astype(BF16)
            )
    for r in range(nx + 2):
        total = jnp.zeros((rows, width), F32)
        for ab in range(9):
            a, b = ab // 3, ab % 3
            if 0 <= r - a < nx:
                total = total + jnp.dot(turned[b, r - a], wt[ab], preferred_element_type=F32)
        terms[r] = total.reshape(ny, nz, width)
    for j in range(parts_n):
        spot = lax.bitwise_xor(mine, j) * py
        value = terms[:, pl.ds(spot, py)]
        sends[j][...] = value.reshape(nx + 2, py * nz, width).astype(sends[j].dtype)


def deep_grad_body(windows, grad, theirs, mine, held):
    nx, rows, filters = grad.shape
    width = windows.shape[3] // 3
    turned = grad[...].reshape(nx * rows, filters).astype(F32).T.astype(BF16)
    chips, step, _ = mine.shape
    part = filters // 2
    total = 27 * part
    if chips * step > total:
        held[:, total:] = jnp.zeros((2, chips * step - total, width), F32)
    for ab in range(9):
        a, b = ab // 3, ab % 3
        value = jnp.dot(
            turned,
            windows[b, a : a + nx].reshape(nx * rows, 3 * width),
            preferred_element_type=F32,
        )
        for c in range(3):
            spot = (3 * ab + c) * part
            for side in range(2):
                held[side, spot : spot + part] = value[
                    side * part : (side + 1) * part, c * width : (c + 1) * width
                ]
    core = lax.rem(lax.axis_index("space"), 2)
    for q in range(chips):
        theirs[q] = held[1 - core, q * step : (q + 1) * step].astype(theirs.dtype)
        mine[q] = held[core, q * step : (q + 1) * step]


def early_grad_body(nz, *refs):
    parts, (sg, turned, deep, out, grad, held) = refs[:-6], refs[-6:]
    ext, rows, wide = sg.shape
    total = parts[0][...]
    for part in parts[1:]:
        total = total + part[...].astype(F32)
    px, prow, _ = total.shape
    py = prow // nz
    total = jnp.concatenate([total, total], axis=2).reshape(px, py, 1, nz, wide)
    total = jnp.broadcast_to(total, (px, py, 2, nz, wide)).reshape(px, rows, wide)
    for x in range(ext):
        grad[x] = (total[x // 2] * sg[x]).astype(BF16)
    early_grad_half(1 - lax.rem(lax.axis_index("space"), 2), grad, turned, deep, out, held)


def early_grad_rest_body(grad, turned, deep, out, held):
    early_grad_half(lax.rem(lax.axis_index("space"), 2), grad, turned, deep, out, held)


def early_grad_half(side, grad, turned, deep, out, held):
    ext, rows, wide = grad.shape
    width = wide // 2
    part = turned.shape[2] // 4
    right = grad[...].reshape(ext * rows, wide)
    for ab in range(9):
        a, b = ab // 3, ab % 3
        value = jnp.dot(
            turned[b, side, :, a * rows : (a + ext) * rows], right, preferred_element_type=F32
        )
        for c in range(3):
            spot = (3 * ab + c) * part
            held[spot : spot + part] = (
                value[c * part : (c + 1) * part, :width]
                + value[(c + 1) * part : (c + 2) * part, width:]
            )
    step = held.shape[0] // out.shape[0]
    for q in range(out.shape[0]):
        out[q, :step] = held[q * step : (q + 1) * step].astype(out.dtype)
        out[q, step:] = deep[q].astype(out.dtype)


def core_sum_body(mine, other, *outs):
    chip = lax.div(lax.axis_index("space"), 2)
    for j, out in enumerate(outs):
        q = lax.bitwise_xor(chip, j)
        out[...] = (mine[q] + other[q].astype(F32)).astype(out.dtype)


def chip_sum_body(count, step, *refs):
    others, (deep, *outs, held) = refs[:count], refs[count:]
    total = others[0][...]
    for ref in others[1:]:
        total = total + ref[...].astype(F32)
    held[:step] = total[:step]
    if held.shape[0] > step:
        held[step:] = jnp.zeros((held.shape[0] - step, total.shape[1]), F32)
    deep[...] = total[step:].astype(BF16)
    size = outs[0].shape[0]
    for j, out in enumerate(outs):
        spot = pl.multiple_of(lax.bitwise_xor(lax.axis_index("filt"), j) * size, 8)
        out[...] = held[pl.ds(spot, size)].astype(out.dtype)


def sum_body(*refs):
    total = refs[0][...]
    for ref in refs[1:-1]:
        total = total + ref[...].astype(F32)
    refs[-1][...] = total.astype(BF16)


def line_up_body(*refs):
    shares, deep, out = refs[:-2], refs[-2], refs[-1]
    size = shares[0].shape[0]
    for j, share in enumerate(shares):
        spot = pl.multiple_of(lax.bitwise_xor(lax.axis_index("filt"), j) * size, 16)
        out[pl.ds(spot, size)] = share[...]
    out[size * len(shares) :] = deep[...]


def stack_body(*refs):
    out = refs[-1]
    chip = lax.div(lax.axis_index("space"), 2)
    for j, ref in enumerate(refs[:-1]):
        out[lax.bitwise_xor(chip, j)] = ref[...]


def finish_body(own, early_scale, deep_scale, early_rows, deep_rows, pieces, *refs):
    early, deep, early_held, deep_held, sem = refs[-5:]
    core = lax.rem(lax.axis_index("space"), 2)
    side = core if own else 1 - core
    copies = []
    for out, held, first, step, scale in (
        (early, early_held, 0, early_rows, early_scale),
        (deep, deep_held, pieces.shape[1] - deep_rows, deep_rows, deep_scale),
    ):
        part = held.shape[1]
        for tap in range(27):
            row = tap * part
            while row < (tap + 1) * part:
                q, inner = row // step, row % step
                size = min(step - inner, (tap + 1) * part - row)
                spot = row - tap * part
                held[tap, spot : spot + size] = (
                    pieces[q, first + inner : first + inner + size].astype(F32) * scale
                )
                row += size
            if tap % 9 == 8:
                taps = pl.ds(tap - 8, 9)
                copy = pltpu.make_async_copy(
                    held.at[taps], out.at[taps, pl.ds(side * part, part)], sem.at[len(copies)]
                )
                copy.start()
                copies.append(copy)
    for copy in copies:
        copy.wait()


def paired(values, axis, step=1):
    count = lax.axis_size(axis)
    got = {
        j: lax.ppermute(values[j], axis, [(i, i ^ (step * j)) for i in range(count)])
        for j in reversed(range(1, len(values)))
    }
    return [values[0]] + [got[j] for j in range(1, len(values))]


def backward(values):
    return [values[0]] + values[:0:-1]


def swap(value, axis, first):
    count = lax.axis_size(axis)
    pairs = [pair for i in range(first, count - 1, 2) for pair in ((i, i + 1), (i + 1, i))]
    return lax.ppermute(value, axis, pairs)


def shards(volume, w_early, w_deep, cotangent):
    nx, ny, nz, cin = volume.shape
    width = w_early.shape[2]
    filters = w_deep.shape[2]
    space = lax.axis_size("space")
    filt = lax.axis_size("filt")
    chips = space // 2
    half = nz // 2
    ext = nx + 6
    rows = ny * half
    odd = lax.rem(lax.axis_index("space"), 2)
    far = lax.dynamic_slice_in_dim(volume, odd * (nx - 3), 3, 0)
    edges = jnp.concatenate([volume[:, :1], volume[:, ny - 1 :]], axis=1)
    far, edges = lax.optimization_barrier((far, edges))
    xodd = swap(far, "space", 1)
    yeven, yodd = swap(edges, "filt", 0), swap(edges, "filt", 1)
    xeven = swap(volume, "space", 0)
    sides = call(
        sides_body,
        "sides",
        struct((nx, 2, nz, cin)),
        (yeven, yodd),
        flops=3 << 28,
        moved=0,
    )
    ceven, codd = swap(sides, "space", 0), swap(sides, "space", 1)
    windows = call(
        windows_body,
        "windows",
        struct((3, ext, rows, 4 * cin)),
        (volume, xeven, xodd),
        [pltpu.VMEM((ext, ny + 2, nz + 16, cin), F32)],
        flops=1 << 33,
    )
    sg, pooled, beside = call(
        early_body,
        "early_conv",
        (
            struct((nx + 4, rows, 2 * width), F32),
            struct((nx // 2 + 2, rows // 2, width)),
            struct((2, ext, half, 4 * cin), F32),
        ),
        (windows, sides, ceven, codd, w_early),
        [
            pltpu.VMEM((ext, 2, nz + 16, cin), F32),
            pltpu.VMEM((9, 4 * cin, 2 * width), BF16),
        ],
        flops=2 * (nx + 4) * rows * 36 * cin * 2 * width,
    )
    parts = paired([pooled] * filt, "filt")
    turned = call(
        transpose_body,
        "turn_windows",
        struct((3, 2, 2 * cin, ext * rows)),
        (windows, beside),
        flops=1 << 30,
    )
    *parts, turned = lax.optimization_barrier((*parts, turned))
    dx, dy, dz, _ = cotangent.shape
    px = dx + 2
    prow = rows // 2
    deep = call(
        functools.partial(deep_body, filt),
        "deep_conv",
        [
            struct(cotangent.shape),
            struct((dx, dy * dz, filters)),
            struct((3, px, dy * dz, 3 * width)),
            struct((px, prow, width), F32),
        ]
        + [struct((px, prow, width))] * (filt - 1),
        (*parts, jnp.swapaxes(w_deep, 1, 2).reshape(9, 3 * filters, width), cotangent),
        [
            pltpu.VMEM((px, dy + 2, dz, width), F32),
            pltpu.VMEM((9, filters, 3 * width), BF16),
            pltpu.VMEM((dx, dy + 2, dz, filters), F32),
            pltpu.VMEM((3, dx, dy * dz, 3 * filters), BF16),
            pltpu.VMEM((px, dy, dz, width), F32),
        ],
        flops=4 * dx * dy * dz * 27 * width * filters,
    )
    block_out, grad, deep_windows = deep[:3]
    terms = paired(deep[3:], "filt")

    early_rows = 27 * cin // space
    deep_rows = ceil_to(-(-27 * filters // space), 16)
    deep_first, deep_second = call(
        deep_grad_body,
        "deep_grad",
        [struct((chips, deep_rows, width)), struct((chips, deep_rows, width), F32)],
        (deep_windows, grad),
        [pltpu.VMEM((2, chips * deep_rows, width), F32)],
        flops=2 * dx * dy * dz * 27 * width * filters,
    )
    piece = (chips, early_rows + deep_rows, width)
    held = pltpu.VMEM((27 * cin // 2, width), F32)
    flops = (nx + 4) * rows * 36 * cin * 2 * width
    theirs, grad = call(
        functools.partial(early_grad_body, half),
        "early_grad",
        [struct(piece), struct((nx + 4, rows, 2 * width))],
        (*backward(terms), sg, turned, deep_first),
        [held],
        flops=flops,
    )
    theirs = lax.ppermute(theirs, "space", [(i, i ^ 1) for i in range(space)])
    mine = call(
        early_grad_rest_body,
        "early_grad_rest",
        struct(piece, F32),
        (grad, turned, deep_second),
        [held],
        flops=flops,
    )
    sums = call(
        core_sum_body,
        "core_sum",
        [struct(piece[1:], F32)] + [struct(piece[1:])] * (chips - 1),
        (mine, theirs),
    )
    sums = backward(paired(sums, "space", 2))
    small = ceil_to(-(-early_rows // filt), 16)
    deep_sum, *shares = call(
        functools.partial(chip_sum_body, chips, early_rows),
        "chip_sum",
        [struct((deep_rows, width)), struct((small, width), F32)]
        + [struct((small, width))] * (filt - 1),
        sums,
        [pltpu.VMEM((small * filt, width), F32)],
    )
    share = call(sum_body, "filt_sum", struct((small, width)), backward(paired(shares, "filt")))
    shares = paired([share] * filt, "filt")
    final_rows = small * filt + deep_rows
    final = call(line_up_body, "line_up", struct((final_rows, width)), (*shares, deep_sum))
    finals = paired([final] * chips, "space", 2)
    own = call(stack_body, "stack", struct((chips, final_rows, width)), finals)
    other = lax.ppermute(own, "space", [(i, i ^ 1) for i in range(space)])
    early_total = nx * ny * nz * space * filt
    deep_total = dx * dy * dz * space
    results = [struct((27, cin, width), F32), struct((27, filters, width), F32)]
    scales = (1.0 / math.sqrt(early_total), 1.0 / math.sqrt(deep_total), early_rows, deep_rows)
    scratch = [
        pltpu.VMEM((27, cin // 2, width), F32),
        pltpu.VMEM((27, filters // 2, width), F32),
        DMA((6,)),
    ]
    results = call(
        functools.partial(finish_body, True, *scales),
        "finish_own",
        results,
        (own,),
        scratch,
        outs=HBM,
    )
    grad_early, grad_deep = call(
        functools.partial(finish_body, False, *scales),
        "finish_other",
        [struct(value.shape, F32) for value in results],
        (other, *results),
        scratch,
        hbm=(1, 2),
        outs=HBM,
        alias=((1, 0), (2, 1)),
    )
    return (block_out, grad_early, jnp.swapaxes(grad_deep, 1, 2))


def solution(mesh):
    return jax.shard_map(
        shards,
        mesh=mesh,
        in_specs=(
            P("space", "filt", None, None),
            P(),
            P(None, None, "filt"),
            P("space", None, None, "filt"),
        ),
        out_specs=(P("space", None, None, "filt"), P(), P(None, None, "filt")),
        check_vma=False,
    )
```

```python
import functools
import math

import jax
import jax.numpy as jnp
from jax import lax
from jax.experimental import pallas as pl
from jax.experimental.pallas import tpu as pltpu
from jax.sharding import PartitionSpec as P

F32 = jnp.float32
BF16 = jnp.bfloat16
VMEM_LIMIT = 24 * 1024 * 1024
VMEM = pl.BlockSpec(memory_space=pltpu.VMEM)
HBM = pl.BlockSpec(memory_space=pltpu.HBM)
DMA = pltpu.SemaphoreType.DMA


def call(
    body, name, out_shape, operands, scratch=(), flops=0, moved=1 << 20, hbm=(), outs=VMEM, alias=()
):
    return pl.pallas_call(
        body,
        name=name,
        out_shape=out_shape,
        in_specs=[HBM if i in hbm else VMEM for i in range(len(operands))],
        out_specs=jax.tree.map(lambda _: outs, out_shape),
        scratch_shapes=list(scratch),
        input_output_aliases=dict(alias),
        compiler_params=pltpu.CompilerParams(vmem_limit_bytes=VMEM_LIMIT),
        cost_estimate=pl.CostEstimate(flops=flops, bytes_accessed=moved, transcendentals=0),
    )(*operands)


def struct(shape, dtype=BF16):
    return jax.ShapeDtypeStruct(shape, dtype)


def ceil_to(value, step):
    return -(-value // step) * step


def sigmoid(value):
    return 1.0 / (1.0 + jnp.exp(-value))


def is_even(axis):
    return lax.rem(lax.axis_index(axis), 2) == 0


def edges_body(center, edges, copied):
    ny = center.shape[1]
    edges[:, 0:1] = center[:, 0:1]
    edges[:, 1:2] = center[:, ny - 1 :]
    copied[...] = center[...]


def spread_body(center, yeven, yodd, sides, near, far):
    nx, ny, _, _ = center.shape
    even = is_even("filt")
    sides[:, 0:1] = jnp.where(even, yodd[:, 1:2], yeven[:, 1:2])
    sides[:, 1:2] = jnp.where(even, yeven[:, 0:1], yodd[:, 0:1])
    odd = lax.rem(lax.axis_index("space"), 2)
    for out, start in ((near, (1 - odd) * (nx - 3)), (far, odd * (nx - 3))):
        rows = pl.ds(start, 3)
        out[:, 0:1] = sides[rows, 0:1]
        out[:, 1 : ny + 1] = center[rows]
        out[:, ny + 1 :] = sides[rows, 1:2]


def fill_windows(field, windows):
    count, wide_y, _, cin = field.shape
    ny = wide_y - 2
    half = windows.shape[2] // ny
    for x in range(count):
        for group in range(4):
            plane = field[x, :, pl.ds(7 + group, half, stride=2), :]
            for b in range(3):
                windows[b, x, :, group * cin : (group + 1) * cin] = (
                    plane[b : b + ny].reshape(ny * half, cin).astype(BF16)
                )


def clear_ends(field, nz):
    count, wide_y, _, cin = field.shape
    field[:, :, 0:8] = jnp.zeros((count, wide_y, 8, cin), F32)
    field[:, :, 8 + nz : 16 + nz] = jnp.zeros((count, wide_y, 8, cin), F32)


def early_rows_of(windows, start, wide, ny, keep):
    rows = windows.shape[2]
    cout = wide.shape[2] // 2
    acc = jnp.zeros((2 * rows, 2 * cout), F32)
    for ab in range(9):
        a, b = ab // 3, ab % 3
        left = windows[b, pl.ds(start + a, 2)].reshape(2 * rows, windows.shape[3])
        acc = acc + jnp.dot(left, wide[ab], preferred_element_type=F32)
    sig = sigmoid(acc)
    slope = (sig * (1.0 + acc * (1.0 - sig)) * keep).reshape(2, rows, 2 * cout)
    act = acc * sig
    act = act[:rows] + act[rows:]
    act = act[:, :cout] + act[:, cout:]
    act = act.reshape(ny // 2, 2, rows // ny, cout)
    act = (act[:, 0] + act[:, 1]) * keep
    return slope, act.reshape(rows // 2, cout).astype(BF16)


def near_body(center, sides, near, w, windows, sg, pooled, wide, field):
    nx, ny, nz, cin = center.shape
    cout = w.shape[2]
    for ab in range(9):
        for group in range(4):
            for side in range(2):
                tap = group - side
                value = w[3 * ab + tap] if 0 <= tap <= 2 else jnp.zeros((cin, cout), BF16)
                wide[
                    ab, group * cin : (group + 1) * cin, side * cout : (side + 1) * cout
                ] = value
    odd = lax.rem(lax.axis_index("space"), 2)
    clear_ends(field, nz)
    cells = slice(8, 8 + nz)
    own = pl.ds(3 * odd, nx)
    field[own, 1 : ny + 1, cells] = center[...].astype(F32)
    field[own, 0:1, cells] = sides[:, 0:1].astype(F32)
    field[own, ny + 1 :, cells] = sides[:, 1:2].astype(F32)
    field[pl.ds((1 - odd) * nx, 3), :, cells] = near[...].astype(F32)
    fill_windows(field, windows)
    for chunk in range(nx // 2):
        slope, pool = early_rows_of(windows, 1 - odd + 2 * chunk, wide, ny, 0.125)
        sg[2 * chunk : 2 * chunk + 2] = slope
        pooled[chunk] = pool


def far_body(windows, far, wide, near_pooled, far_windows, sg, pooled, field, held):
    _, wide_y, nz, _ = far.shape
    odd = lax.rem(lax.axis_index("space"), 2)
    clear_ends(field, nz)
    field[:, :, 8 : 8 + nz] = far[...].astype(F32)
    fill_windows(field, far_windows)
    for b in range(3):
        held[b, pl.ds(3 * odd, 3)] = far_windows[b]
        held[b, pl.ds(3 - 3 * odd, 3)] = windows[b, pl.ds(4 * odd, 3)]
    here = lax.axis_index("space")
    inside = jnp.where((here > 0) & (here < lax.axis_size("space") - 1), 1.0, 0.0)
    first = jnp.where(odd == 0, inside, 1.0).astype(F32)
    second = jnp.where(odd == 1, inside, 1.0).astype(F32)
    count = near_pooled.shape[0]
    for chunk, flag in enumerate((first, second)):
        slope, pool = early_rows_of(held, 2 * chunk, wide, wide_y - 2, 0.125 * flag)
        sg[2 * chunk : 2 * chunk + 2] = slope
        pooled[count * odd + chunk] = pool
        pooled[count * (1 - odd) + chunk] = near_pooled[chunk]


def transpose_body(windows, far_windows, turned):
    rows = windows.shape[2]
    part = turned.shape[2] // 4
    odd = lax.rem(lax.axis_index("space"), 2)
    for source, first in ((windows, 3 * (1 - odd)), (far_windows, windows.shape[1] * odd)):
        for b in range(3):
            for x in range(source.shape[1]):
                value = source[b, x].T
                spot = pl.multiple_of((first + x) * rows, rows)
                for group in range(4):
                    for side in range(2):
                        row = (2 * group + side) * part
                        turned[
                            b, side, group * part : (group + 1) * part, pl.ds(spot, rows)
                        ] = value[row : row + part]


def roll_z(value, shift):
    size = value.shape[-2]
    rolled = pltpu.roll(value, shift % size, value.ndim - 2)
    spot = lax.broadcasted_iota(jnp.int32, value.shape, value.ndim - 2)
    edge = 0 if shift == 1 else size - 1
    return jnp.where(spot == edge, 0.0, rolled)


def deep_body(parts_n, *refs):
    parts = refs[:parts_n]
    wt, cot = refs[parts_n : parts_n + 2]
    block_out, grad, windows = refs[parts_n + 2 : parts_n + 5]
    sends = refs[parts_n + 5 : 2 * parts_n + 5]
    field, wide, slopes, turned, terms = refs[2 * parts_n + 5 :]
    nx, ny, nz, filters = cot.shape
    width = wt.shape[2]
    rows = ny * nz
    py = ny // parts_n
    mine = lax.axis_index("filt")
    for ab in range(9):
        for c in range(3):
            wide[ab, :, c * width : (c + 1) * width] = wt[
                ab, c * filters : (c + 1) * filters
            ]
    field[:, 0:1] = jnp.zeros((nx + 2, 1, nz, width), F32)
    field[:, ny + 1 : ny + 2] = jnp.zeros((nx + 2, 1, nz, width), F32)
    for j in range(parts_n):
        spot = lax.bitwise_xor(mine, j) * py + 1
        field[:, pl.ds(spot, py)] = parts[j][...].astype(F32).reshape(nx + 2, py, nz, width)
    for x in range(nx + 2):
        plane = field[x]
        for c in range(3):
            moved = plane if c == 1 else roll_z(plane, 1 - c)
            for b in range(3):
                windows[b, x, :, c * width : (c + 1) * width] = (
                    moved[b : b + ny].reshape(rows, width).astype(BF16)
                )
    slopes[:, 0:1] = jnp.zeros((nx, 1, nz, filters), F32)
    slopes[:, ny + 1 :] = jnp.zeros((nx, 1, nz, filters), F32)
    for x in range(nx):
        acc = jnp.zeros((rows, filters), F32)
        for ab in range(9):
            a, b = ab // 3, ab % 3
            acc = acc + lax.dot_general(
                windows[b, x + a], wide[ab], (((1,), (1,)), ((), ())), preferred_element_type=F32
            )
        sig = sigmoid(acc)
        block_out[x] = (acc * sig).reshape(ny, nz, filters).astype(BF16)
        slope = sig * (1.0 + acc * (1.0 - sig))
        value = (cot[x].astype(F32).reshape(rows, filters) * slope).astype(BF16)
        grad[x] = value
        slopes[x, 1 : ny + 1] = value.astype(F32).reshape(ny, nz, filters)
    for x in range(nx):
        plane = slopes[x]
        plane = jnp.concatenate([roll_z(plane, -1), plane, roll_z(plane, 1)], axis=2)
        for b in range(3):
            turned[b, x] = (
                plane[2 - b : 2 - b + ny].reshape(rows, 3 * filters).astype(BF16)
            )
    for r in range(nx + 2):
        total = jnp.zeros((rows, width), F32)
        for ab in range(9):
            a, b = ab // 3, ab % 3
            if 0 <= r - a < nx:
                total = total + jnp.dot(turned[b, r - a], wt[ab], preferred_element_type=F32)
        terms[r] = total.reshape(ny, nz, width)
    for j in range(parts_n):
        spot = lax.bitwise_xor(mine, j) * py
        value = terms[:, pl.ds(spot, py)]
        sends[j][...] = value.reshape(nx + 2, py * nz, width).astype(sends[j].dtype)


def deep_grad_body(windows, grad, theirs, mine, held):
    nx, rows, filters = grad.shape
    width = windows.shape[3] // 3
    turned = grad[...].reshape(nx * rows, filters).astype(F32).T.astype(BF16)
    chips, step, _ = mine.shape
    part = filters // 2
    total = 27 * part
    if chips * step > total:
        held[:, total:] = jnp.zeros((2, chips * step - total, width), F32)
    for ab in range(9):
        a, b = ab // 3, ab % 3
        value = jnp.dot(
            turned,
            windows[b, a : a + nx].reshape(nx * rows, 3 * width),
            preferred_element_type=F32,
        )
        for c in range(3):
            spot = (3 * ab + c) * part
            for side in range(2):
                held[side, spot : spot + part] = value[
                    side * part : (side + 1) * part, c * width : (c + 1) * width
                ]
    core = lax.rem(lax.axis_index("space"), 2)
    for q in range(chips):
        theirs[q] = held[1 - core, q * step : (q + 1) * step].astype(theirs.dtype)
        mine[q] = held[core, q * step : (q + 1) * step]


def early_grad_body(nz, *refs):
    parts, (sg, far_sg, turned, deep, out, grad, held, spread) = refs[:-8], refs[-8:]
    count, rows, wide = sg.shape
    total = parts[0][...]
    for part in parts[1:]:
        total = total + part[...].astype(F32)
    px, prow, _ = total.shape
    py = prow // nz
    total = jnp.concatenate([total, total], axis=2).reshape(px, py, 1, nz, wide)
    spread[...] = jnp.broadcast_to(total, (px, py, 2, nz, wide)).reshape(px, rows, wide)
    odd = lax.rem(lax.axis_index("space"), 2)
    for source, first in ((sg, count * (1 - odd)), (far_sg, count * odd)):
        for x in range(count):
            grad[first + x] = (spread[lax.div(first, 2) + x // 2] * source[x]).astype(BF16)
    early_grad_half(1 - odd, grad, turned, deep, out, held)


def early_grad_rest_body(grad, turned, deep, out, held):
    early_grad_half(lax.rem(lax.axis_index("space"), 2), grad, turned, deep, out, held)


def early_grad_half(side, grad, turned, deep, out, held):
    ext, rows, wide = grad.shape
    width = wide // 2
    part = turned.shape[2] // 4
    right = grad[...].reshape(ext * rows, wide)
    for ab in range(9):
        a, b = ab // 3, ab % 3
        value = jnp.dot(
            turned[b, side, :, a * rows : (a + ext) * rows], right, preferred_element_type=F32
        )
        for c in range(3):
            spot = (3 * ab + c) * part
            held[spot : spot + part] = (
                value[c * part : (c + 1) * part, :width]
                + value[(c + 1) * part : (c + 2) * part, width:]
            )
    step = held.shape[0] // out.shape[0]
    for q in range(out.shape[0]):
        out[q, :step] = held[q * step : (q + 1) * step].astype(out.dtype)
        out[q, step:] = deep[q].astype(out.dtype)


def core_sum_body(mine, other, *outs):
    chip = lax.div(lax.axis_index("space"), 2)
    for j, out in enumerate(outs):
        q = lax.bitwise_xor(chip, j)
        out[...] = (mine[q] + other[q].astype(F32)).astype(out.dtype)


def chip_sum_body(count, step, *refs):
    others, (deep, *outs, held) = refs[:count], refs[count:]
    total = others[0][...]
    for ref in others[1:]:
        total = total + ref[...].astype(F32)
    held[:step] = total[:step]
    if held.shape[0] > step:
        held[step:] = jnp.zeros((held.shape[0] - step, total.shape[1]), F32)
    deep[...] = total[step:].astype(BF16)
    size = outs[0].shape[0]
    for j, out in enumerate(outs):
        spot = pl.multiple_of(lax.bitwise_xor(lax.axis_index("filt"), j) * size, 8)
        out[...] = held[pl.ds(spot, size)].astype(out.dtype)


def sum_body(*refs):
    total = refs[0][...]
    for ref in refs[1:-1]:
        total = total + ref[...].astype(F32)
    refs[-1][...] = total.astype(BF16)


def line_up_body(*refs):
    shares, deep, out = refs[:-2], refs[-2], refs[-1]
    size = shares[0].shape[0]
    for j, share in enumerate(shares):
        spot = pl.multiple_of(lax.bitwise_xor(lax.axis_index("filt"), j) * size, 16)
        out[pl.ds(spot, size)] = share[...]
    out[size * len(shares) :] = deep[...]


def stack_body(*refs):
    out = refs[-1]
    chip = lax.div(lax.axis_index("space"), 2)
    for j, ref in enumerate(refs[:-1]):
        out[lax.bitwise_xor(chip, j)] = ref[...]


def finish_body(own, early_scale, deep_scale, early_rows, deep_rows, pieces, *refs):
    early, deep, early_held, deep_held, sem = refs[-5:]
    core = lax.rem(lax.axis_index("space"), 2)
    side = core if own else 1 - core
    copies = []
    for out, held, first, step, scale in (
        (early, early_held, 0, early_rows, early_scale),
        (deep, deep_held, pieces.shape[1] - deep_rows, deep_rows, deep_scale),
    ):
        part = held.shape[1]
        for tap in range(27):
            row = tap * part
            while row < (tap + 1) * part:
                q, inner = row // step, row % step
                size = min(step - inner, (tap + 1) * part - row)
                spot = row - tap * part
                held[tap, spot : spot + size] = (
                    pieces[q, first + inner : first + inner + size].astype(F32) * scale
                )
                row += size
            if tap % 9 == 8:
                taps = pl.ds(tap - 8, 9)
                copy = pltpu.make_async_copy(
                    held.at[taps], out.at[taps, pl.ds(side * part, part)], sem.at[len(copies)]
                )
                copy.start()
                copies.append(copy)
    for copy in copies:
        copy.wait()


def paired(values, axis, step=1):
    count = lax.axis_size(axis)
    got = {
        j: lax.ppermute(values[j], axis, [(i, i ^ (step * j)) for i in range(count)])
        for j in reversed(range(1, len(values)))
    }
    return [values[0]] + [got[j] for j in range(1, len(values))]


def backward(values):
    return [values[0]] + values[:0:-1]


def swap(value, axis, first):
    count = lax.axis_size(axis)
    pairs = [pair for i in range(first, count - 1, 2) for pair in ((i, i + 1), (i + 1, i))]
    return lax.ppermute(value, axis, pairs)


def shards(volume, w_early, w_deep, cotangent):
    nx, ny, nz, cin = volume.shape
    width = w_early.shape[2]
    filters = w_deep.shape[2]
    space = lax.axis_size("space")
    filt = lax.axis_size("filt")
    chips = space // 2
    half = nz // 2
    ext = nx + 6
    rows = ny * half
    edges, volume = call(
        edges_body, "edges", [struct((nx, 2, nz, cin)), struct(volume.shape)], (volume,)
    )
    yeven, yodd = swap(edges, "filt", 0), swap(edges, "filt", 1)
    rim = struct((3, ny + 2, nz, cin))
    sides, near, far = call(
        spread_body,
        "spread",
        [struct((nx, 2, nz, cin)), rim, rim],
        (volume, yeven, yodd),
        flops=1 << 32,
        moved=1 << 24,
    )
    far = swap(far, "space", 1)
    near = swap(near, "space", 0)
    windows, sg, near_pooled, wide = call(
        near_body,
        "early_near",
        (
            struct((3, nx + 3, rows, 4 * cin)),
            struct((nx, rows, 2 * width), F32),
            struct((nx // 2, rows // 2, width)),
            struct((9, 4 * cin, 2 * width)),
        ),
        (volume, sides, near, w_early),
        [pltpu.VMEM((nx + 3, ny + 2, nz + 16, cin), F32)],
        flops=2 * nx * rows * 36 * cin * 2 * width,
    )
    far_windows, far_sg, pooled = call(
        far_body,
        "early_far",
        (
            struct((3, 3, rows, 4 * cin)),
            struct((nx, rows, 2 * width), F32),
            struct((nx // 2 + 2, rows // 2, width)),
        ),
        (windows, far, wide, near_pooled),
        [
            pltpu.VMEM((3, ny + 2, nz + 16, cin), F32),
            pltpu.VMEM((3, 6, rows, 4 * cin), BF16),
        ],
        flops=2 * nx * rows * 36 * cin * 2 * width,
    )
    parts = paired([pooled] * filt, "filt")
    turned = call(
        transpose_body,
        "turn_windows",
        struct((3, 2, 2 * cin, ext * rows)),
        (windows, far_windows),
        flops=1 << 30,
    )
    *parts, turned = lax.optimization_barrier((*parts, turned))
    dx, dy, dz, _ = cotangent.shape
    px = dx + 2
    prow = rows // 2
    deep = call(
        functools.partial(deep_body, filt),
        "deep_conv",
        [
            struct(cotangent.shape),
            struct((dx, dy * dz, filters)),
            struct((3, px, dy * dz, 3 * width)),
            struct((px, prow, width), F32),
        ]
        + [struct((px, prow, width))] * (filt - 1),
        (*parts, jnp.swapaxes(w_deep, 1, 2).reshape(9, 3 * filters, width), cotangent),
        [
            pltpu.VMEM((px, dy + 2, dz, width), F32),
            pltpu.VMEM((9, filters, 3 * width), BF16),
            pltpu.VMEM((dx, dy + 2, dz, filters), F32),
            pltpu.VMEM((3, dx, dy * dz, 3 * filters), BF16),
            pltpu.VMEM((px, dy, dz, width), F32),
        ],
        flops=4 * dx * dy * dz * 27 * width * filters,
    )
    block_out, grad, deep_windows = deep[:3]
    terms = paired(deep[3:], "filt")

    early_rows = 27 * cin // space
    deep_rows = ceil_to(-(-27 * filters // space), 16)
    deep_first, deep_second = call(
        deep_grad_body,
        "deep_grad",
        [struct((chips, deep_rows, width)), struct((chips, deep_rows, width), F32)],
        (deep_windows, grad),
        [pltpu.VMEM((2, chips * deep_rows, width), F32)],
        flops=2 * dx * dy * dz * 27 * width * filters,
    )
    piece = (chips, early_rows + deep_rows, width)
    held = pltpu.VMEM((27 * cin // 2, width), F32)
    flops = (nx + 4) * rows * 36 * cin * 2 * width
    theirs, grad = call(
        functools.partial(early_grad_body, half),
        "early_grad",
        [struct(piece), struct((nx + 4, rows, 2 * width))],
        (*backward(terms), sg, far_sg, turned, deep_first),
        [held, pltpu.VMEM((px, rows, 2 * width), F32)],
        flops=flops,
    )
    theirs = lax.ppermute(theirs, "space", [(i, i ^ 1) for i in range(space)])
    mine = call(
        early_grad_rest_body,
        "early_grad_rest",
        struct(piece, F32),
        (grad, turned, deep_second),
        [held],
        flops=flops,
    )
    sums = call(
        core_sum_body,
        "core_sum",
        [struct(piece[1:], F32)] + [struct(piece[1:])] * (chips - 1),
        (mine, theirs),
    )
    sums = backward(paired(sums, "space", 2))
    small = ceil_to(-(-early_rows // filt), 16)
    deep_sum, *shares = call(
        functools.partial(chip_sum_body, chips, early_rows),
        "chip_sum",
        [struct((deep_rows, width)), struct((small, width), F32)]
        + [struct((small, width))] * (filt - 1),
        sums,
        [pltpu.VMEM((small * filt, width), F32)],
    )
    share = call(sum_body, "filt_sum", struct((small, width)), backward(paired(shares, "filt")))
    shares = paired([share] * filt, "filt")
    final_rows = small * filt + deep_rows
    final = call(line_up_body, "line_up", struct((final_rows, width)), (*shares, deep_sum))
    finals = paired([final] * chips, "space", 2)
    own = call(stack_body, "stack", struct((chips, final_rows, width)), finals)
    other = lax.ppermute(own, "space", [(i, i ^ 1) for i in range(space)])
    early_total = nx * ny * nz * space * filt
    deep_total = dx * dy * dz * space
    results = [struct((27, cin, width), F32), struct((27, filters, width), F32)]
    scales = (1.0 / math.sqrt(early_total), 1.0 / math.sqrt(deep_total), early_rows, deep_rows)
    scratch = [
        pltpu.VMEM((27, cin // 2, width), F32),
        pltpu.VMEM((27, filters // 2, width), F32),
        DMA((6,)),
    ]
    results = call(
        functools.partial(finish_body, True, *scales),
        "finish_own",
        results,
        (own,),
        scratch,
        outs=HBM,
    )
    grad_early, grad_deep = call(
        functools.partial(finish_body, False, *scales),
        "finish_other",
        [struct(value.shape, F32) for value in results],
        (other, *results),
        scratch,
        hbm=(1, 2),
        outs=HBM,
        alias=((1, 0), (2, 1)),
    )
    return (block_out, grad_early, jnp.swapaxes(grad_deep, 1, 2))


def solution(mesh):
    return jax.shard_map(
        shards,
        mesh=mesh,
        in_specs=(
            P("space", "filt", None, None),
            P(),
            P(None, None, "filt"),
            P("space", None, None, "filt"),
        ),
        out_specs=(P("space", None, None, "filt"), P(), P(None, None, "filt")),
        check_vma=False,
    )
```

```python
import functools
import math

import jax
import jax.numpy as jnp
from jax import lax
from jax.experimental import pallas as pl
from jax.experimental.pallas import tpu as pltpu
from jax.sharding import PartitionSpec as P

F32 = jnp.float32
BF16 = jnp.bfloat16
VMEM_LIMIT = 24 * 1024 * 1024
VMEM = pl.BlockSpec(memory_space=pltpu.VMEM)
HBM = pl.BlockSpec(memory_space=pltpu.HBM)
DMA = pltpu.SemaphoreType.DMA


def call(
    body, name, out_shape, operands, scratch=(), flops=0, moved=1 << 20, hbm=(), outs=VMEM, alias=()
):
    return pl.pallas_call(
        body,
        name=name,
        out_shape=out_shape,
        in_specs=[HBM if i in hbm else VMEM for i in range(len(operands))],
        out_specs=jax.tree.map(lambda _: outs, out_shape),
        scratch_shapes=list(scratch),
        input_output_aliases=dict(alias),
        compiler_params=pltpu.CompilerParams(vmem_limit_bytes=VMEM_LIMIT),
        cost_estimate=pl.CostEstimate(flops=flops, bytes_accessed=moved, transcendentals=0),
    )(*operands)


def struct(shape, dtype=BF16):
    return jax.ShapeDtypeStruct(shape, dtype)


def ceil_to(value, step):
    return -(-value // step) * step


def sigmoid(value):
    return 1.0 / (1.0 + jnp.exp(-value))


def is_even(axis):
    return lax.rem(lax.axis_index(axis), 2) == 0


def edges_body(center, edges, copied):
    ny = center.shape[1]
    edges[:, 0:1] = center[:, 0:1]
    edges[:, 1:2] = center[:, ny - 1 :]
    copied[...] = center[...]


def has_both(axis):
    here = lax.axis_index(axis)
    return (here > 0) & (here < lax.axis_size(axis) - 1)


def spread_body(center, yeven, yodd, sides, near, far):
    nx, ny, _, _ = center.shape
    even = is_even("filt")
    beyond = jnp.where(has_both("filt"), yodd[...], jnp.zeros(yodd.shape, BF16))
    sides[:, 0:1] = jnp.where(even, beyond[:, 1:2], yeven[:, 1:2])
    sides[:, 1:2] = jnp.where(even, yeven[:, 0:1], beyond[:, 0:1])
    odd = lax.rem(lax.axis_index("space"), 2)
    for out, start in ((near, (1 - odd) * (nx - 3)), (far, odd * (nx - 3))):
        rows = pl.ds(start, 3)
        out[:, 0:1] = sides[rows, 0:1]
        out[:, 1 : ny + 1] = center[rows]
        out[:, ny + 1 :] = sides[rows, 1:2]


def fill_windows(field, windows):
    count, wide_y, _, cin = field.shape
    ny = wide_y - 2
    half = windows.shape[2] // ny
    for x in range(count):
        for group in range(4):
            plane = field[x, :, pl.ds(7 + group, half, stride=2), :]
            for b in range(3):
                windows[b, x, :, group * cin : (group + 1) * cin] = (
                    plane[b : b + ny].reshape(ny * half, cin).astype(BF16)
                )


def clear_ends(field, nz):
    count, wide_y, _, cin = field.shape
    field[:, :, 0:8] = jnp.zeros((count, wide_y, 8, cin), F32)
    field[:, :, 8 + nz : 16 + nz] = jnp.zeros((count, wide_y, 8, cin), F32)


def early_rows_of(windows, start, wide, ny, keep):
    rows = windows.shape[2]
    cout = wide.shape[2] // 2
    acc = jnp.zeros((2 * rows, 2 * cout), F32)
    for ab in range(9):
        a, b = ab // 3, ab % 3
        left = windows[b, pl.ds(start + a, 2)].reshape(2 * rows, windows.shape[3])
        acc = acc + jnp.dot(left, wide[ab], preferred_element_type=F32)
    sig = sigmoid(acc)
    slope = (sig * (1.0 + acc * (1.0 - sig)) * keep).reshape(2, rows, 2 * cout)
    act = acc * sig
    act = act[:rows] + act[rows:]
    act = act[:, :cout] + act[:, cout:]
    act = act.reshape(ny // 2, 2, rows // ny, cout)
    act = (act[:, 0] + act[:, 1]) * keep
    return slope, act.reshape(rows // 2, cout).astype(BF16)


def near_body(center, sides, near, w, windows, sg, pooled, wide, field):
    nx, ny, nz, cin = center.shape
    cout = w.shape[2]
    for ab in range(9):
        for group in range(4):
            for side in range(2):
                tap = group - side
                value = w[3 * ab + tap] if 0 <= tap <= 2 else jnp.zeros((cin, cout), BF16)
                wide[
                    ab, group * cin : (group + 1) * cin, side * cout : (side + 1) * cout
                ] = value
    odd = lax.rem(lax.axis_index("space"), 2)
    clear_ends(field, nz)
    cells = slice(8, 8 + nz)
    own = pl.ds(3 * odd, nx)
    field[own, 1 : ny + 1, cells] = center[...].astype(F32)
    field[own, 0:1, cells] = sides[:, 0:1].astype(F32)
    field[own, ny + 1 :, cells] = sides[:, 1:2].astype(F32)
    field[pl.ds((1 - odd) * nx, 3), :, cells] = near[...].astype(F32)
    fill_windows(field, windows)
    for chunk in range(nx // 2):
        slope, pool = early_rows_of(windows, 1 - odd + 2 * chunk, wide, ny, 0.125)
        sg[2 * chunk : 2 * chunk + 2] = slope
        pooled[chunk] = pool


def far_body(windows, far, wide, near_pooled, far_windows, sg, pooled, field, held):
    _, wide_y, nz, _ = far.shape
    odd = lax.rem(lax.axis_index("space"), 2)
    clear_ends(field, nz)
    inside = jnp.where(has_both("space"), 1.0, 0.0).astype(F32)
    field[:, :, 8 : 8 + nz] = far[...].astype(F32) * inside
    fill_windows(field, far_windows)
    for b in range(3):
        held[b, pl.ds(3 * odd, 3)] = far_windows[b]
        held[b, pl.ds(3 - 3 * odd, 3)] = windows[b, pl.ds(4 * odd, 3)]
    first = jnp.where(odd == 0, inside, 1.0)
    second = jnp.where(odd == 1, inside, 1.0)
    count = near_pooled.shape[0]
    for chunk, flag in enumerate((first, second)):
        slope, pool = early_rows_of(held, 2 * chunk, wide, wide_y - 2, 0.125 * flag)
        sg[2 * chunk : 2 * chunk + 2] = slope
        pooled[count * odd + chunk] = pool
        pooled[count * (1 - odd) + chunk] = near_pooled[chunk]


def transpose_body(windows, far_windows, turned):
    rows = windows.shape[2]
    part = turned.shape[2] // 4
    odd = lax.rem(lax.axis_index("space"), 2)
    for source, first in ((windows, 3 * (1 - odd)), (far_windows, windows.shape[1] * odd)):
        for b in range(3):
            for x in range(source.shape[1]):
                value = source[b, x].T
                spot = pl.multiple_of((first + x) * rows, rows)
                for group in range(4):
                    for side in range(2):
                        row = (2 * group + side) * part
                        turned[
                            b, side, group * part : (group + 1) * part, pl.ds(spot, rows)
                        ] = value[row : row + part]


def roll_z(value, shift):
    size = value.shape[-2]
    rolled = pltpu.roll(value, shift % size, value.ndim - 2)
    spot = lax.broadcasted_iota(jnp.int32, value.shape, value.ndim - 2)
    edge = 0 if shift == 1 else size - 1
    return jnp.where(spot == edge, 0.0, rolled)


def deep_body(parts_n, *refs):
    parts = refs[:parts_n]
    wt, cot = refs[parts_n : parts_n + 2]
    block_out, grad, windows = refs[parts_n + 2 : parts_n + 5]
    sends = refs[parts_n + 5 : 2 * parts_n + 5]
    field, wide, slopes, turned, terms = refs[2 * parts_n + 5 :]
    nx, ny, nz, filters = cot.shape
    width = wt.shape[2]
    rows = ny * nz
    py = ny // parts_n
    mine = lax.axis_index("filt")
    for ab in range(9):
        for c in range(3):
            wide[ab, :, c * width : (c + 1) * width] = wt[
                ab, c * filters : (c + 1) * filters
            ]
    field[:, 0:1] = jnp.zeros((nx + 2, 1, nz, width), F32)
    field[:, ny + 1 : ny + 2] = jnp.zeros((nx + 2, 1, nz, width), F32)
    for j in range(parts_n):
        spot = lax.bitwise_xor(mine, j) * py + 1
        field[:, pl.ds(spot, py)] = parts[j][...].astype(F32).reshape(nx + 2, py, nz, width)
    for x in range(nx + 2):
        plane = field[x]
        for c in range(3):
            moved = plane if c == 1 else roll_z(plane, 1 - c)
            for b in range(3):
                windows[b, x, :, c * width : (c + 1) * width] = (
                    moved[b : b + ny].reshape(rows, width).astype(BF16)
                )
    slopes[:, 0:1] = jnp.zeros((nx, 1, nz, filters), F32)
    slopes[:, ny + 1 :] = jnp.zeros((nx, 1, nz, filters), F32)
    for x in range(nx):
        acc = jnp.zeros((rows, filters), F32)
        for ab in range(9):
            a, b = ab // 3, ab % 3
            acc = acc + lax.dot_general(
                windows[b, x + a], wide[ab], (((1,), (1,)), ((), ())), preferred_element_type=F32
            )
        sig = sigmoid(acc)
        block_out[x] = (acc * sig).reshape(ny, nz, filters).astype(BF16)
        slope = sig * (1.0 + acc * (1.0 - sig))
        value = (cot[x].astype(F32).reshape(rows, filters) * slope).astype(BF16)
        grad[x] = value
        slopes[x, 1 : ny + 1] = value.astype(F32).reshape(ny, nz, filters)
    for x in range(nx):
        plane = slopes[x]
        plane = jnp.concatenate([roll_z(plane, -1), plane, roll_z(plane, 1)], axis=2)
        for b in range(3):
            turned[b, x] = (
                plane[2 - b : 2 - b + ny].reshape(rows, 3 * filters).astype(BF16)
            )
    for r in range(nx + 2):
        total = jnp.zeros((rows, width), F32)
        for ab in range(9):
            a, b = ab // 3, ab % 3
            if 0 <= r - a < nx:
                total = total + jnp.dot(turned[b, r - a], wt[ab], preferred_element_type=F32)
        terms[r] = total.reshape(ny, nz, width)
    for j in range(parts_n):
        spot = lax.bitwise_xor(mine, j) * py
        value = terms[:, pl.ds(spot, py)]
        sends[j][...] = value.reshape(nx + 2, py * nz, width).astype(sends[j].dtype)


def deep_grad_body(windows, grad, theirs, mine, held):
    nx, rows, filters = grad.shape
    width = windows.shape[3] // 3
    turned = grad[...].reshape(nx * rows, filters).astype(F32).T.astype(BF16)
    chips, step, _ = mine.shape
    part = filters // 2
    total = 27 * part
    if chips * step > total:
        held[:, total:] = jnp.zeros((2, chips * step - total, width), F32)
    for ab in range(9):
        a, b = ab // 3, ab % 3
        value = jnp.dot(
            turned,
            windows[b, a : a + nx].reshape(nx * rows, 3 * width),
            preferred_element_type=F32,
        )
        for c in range(3):
            spot = (3 * ab + c) * part
            for side in range(2):
                held[side, spot : spot + part] = value[
                    side * part : (side + 1) * part, c * width : (c + 1) * width
                ]
    core = lax.rem(lax.axis_index("space"), 2)
    for q in range(chips):
        theirs[q] = held[1 - core, q * step : (q + 1) * step].astype(theirs.dtype)
        mine[q] = held[core, q * step : (q + 1) * step]


def early_grad_body(nz, *refs):
    parts, (sg, far_sg, turned, deep, out, grad, held, spread) = refs[:-8], refs[-8:]
    count, rows, wide = sg.shape
    total = parts[0][...]
    for part in parts[1:]:
        total = total + part[...].astype(F32)
    px, prow, _ = total.shape
    py = prow // nz
    total = jnp.concatenate([total, total], axis=2).reshape(px, py, 1, nz, wide)
    spread[...] = jnp.broadcast_to(total, (px, py, 2, nz, wide)).reshape(px, rows, wide)
    odd = lax.rem(lax.axis_index("space"), 2)
    for source, first in ((sg, count * (1 - odd)), (far_sg, count * odd)):
        for x in range(count):
            grad[first + x] = (spread[lax.div(first, 2) + x // 2] * source[x]).astype(BF16)
    early_grad_half(1 - odd, grad, turned, deep, out, held)


def early_grad_rest_body(grad, turned, deep, out, held):
    early_grad_half(lax.rem(lax.axis_index("space"), 2), grad, turned, deep, out, held)


def early_grad_half(side, grad, turned, deep, out, held):
    ext, rows, wide = grad.shape
    width = wide // 2
    part = turned.shape[2] // 4
    right = grad[...].reshape(ext * rows, wide)
    for ab in range(9):
        a, b = ab // 3, ab % 3
        value = jnp.dot(
            turned[b, side, :, a * rows : (a + ext) * rows], right, preferred_element_type=F32
        )
        for c in range(3):
            spot = (3 * ab + c) * part
            held[spot : spot + part] = (
                value[c * part : (c + 1) * part, :width]
                + value[(c + 1) * part : (c + 2) * part, width:]
            )
    step = held.shape[0] // out.shape[0]
    for q in range(out.shape[0]):
        out[q, :step] = held[q * step : (q + 1) * step].astype(out.dtype)
        out[q, step:] = deep[q].astype(out.dtype)


def core_sum_body(mine, other, *outs):
    chip = lax.div(lax.axis_index("space"), 2)
    for j, out in enumerate(outs):
        q = lax.bitwise_xor(chip, j)
        out[...] = (mine[q] + other[q].astype(F32)).astype(out.dtype)


def bit_of(axis, bit):
    return lax.rem(lax.div(lax.axis_index(axis), 1 << bit), 2)


def part_of(index, size):
    return pl.ds(pl.multiple_of(index * size, 16), size)


def chip_sum_body(count, step, bit, *refs):
    others, (deep, send, keep, held) = refs[:count], refs[count:]
    total = others[0][...]
    for ref in others[1:]:
        total = total + ref[...].astype(F32)
    held[:step] = total[:step]
    if held.shape[0] > step:
        held[step:] = jnp.zeros((held.shape[0] - step, total.shape[1]), F32)
    deep[...] = total[step:].astype(BF16)
    mine = bit_of("filt", bit)
    send[...] = held[part_of(1 - mine, send.shape[0])].astype(BF16)
    keep[...] = held[part_of(mine, keep.shape[0])]


def halve_body(bit, kept, got, send, keep, held):
    held[...] = kept[...] + got[...].astype(F32)
    mine = bit_of("filt", bit)
    send[...] = held[part_of(1 - mine, send.shape[0])].astype(BF16)
    keep[...] = held[part_of(mine, keep.shape[0])]


def sum_body(kept, got, out):
    out[...] = (kept[...] + got[...].astype(F32)).astype(BF16)


def join_body(bit, own, got, *refs):
    out = refs[-1]
    size = own.shape[0]
    mine = bit_of("filt", bit)
    out[part_of(mine, size)] = own[...]
    out[part_of(1 - mine, size)] = got[...]
    for ref in refs[:-1]:
        out[2 * size :] = ref[...]


def stack_body(*refs):
    out = refs[-1]
    chip = lax.div(lax.axis_index("space"), 2)
    for j, ref in enumerate(refs[:-1]):
        out[lax.bitwise_xor(chip, j)] = ref[...]


def finish_body(own, early_scale, deep_scale, early_rows, deep_rows, pieces, *refs):
    early, deep, early_held, deep_held, sem = refs[-5:]
    core = lax.rem(lax.axis_index("space"), 2)
    side = core if own else 1 - core
    copies = []
    for out, held, first, step, scale in (
        (early, early_held, 0, early_rows, early_scale),
        (deep, deep_held, pieces.shape[1] - deep_rows, deep_rows, deep_scale),
    ):
        part = held.shape[1]
        for tap in range(27):
            row = tap * part
            while row < (tap + 1) * part:
                q, inner = row // step, row % step
                size = min(step - inner, (tap + 1) * part - row)
                spot = row - tap * part
                held[tap, spot : spot + size] = (
                    pieces[q, first + inner : first + inner + size].astype(F32) * scale
                )
                row += size
            if tap % 9 == 8:
                taps = pl.ds(tap - 8, 9)
                copy = pltpu.make_async_copy(
                    held.at[taps], out.at[taps, pl.ds(side * part, part)], sem.at[len(copies)]
                )
                copy.start()
                copies.append(copy)
    for copy in copies:
        copy.wait()


def paired(values, axis, step=1):
    count = lax.axis_size(axis)
    got = {
        j: lax.ppermute(values[j], axis, [(i, i ^ (step * j)) for i in range(count)])
        for j in reversed(range(1, len(values)))
    }
    return [values[0]] + [got[j] for j in range(1, len(values))]


def exchange(value, axis, step):
    return lax.ppermute(value, axis, [(i, i ^ step) for i in range(lax.axis_size(axis))])


def backward(values):
    return [values[0]] + values[:0:-1]


def swap(value, axis, first):
    count = lax.axis_size(axis)
    other = {i: i for i in range(count)}
    for i in range(first, count - 1, 2):
        other[i], other[i + 1] = i + 1, i
    return lax.ppermute(value, axis, list(other.items()))


def shards(volume, w_early, w_deep, cotangent):
    nx, ny, nz, cin = volume.shape
    width = w_early.shape[2]
    filters = w_deep.shape[2]
    space = lax.axis_size("space")
    filt = lax.axis_size("filt")
    chips = space // 2
    half = nz // 2
    ext = nx + 6
    rows = ny * half
    edges, volume = call(
        edges_body, "edges", [struct((nx, 2, nz, cin)), struct(volume.shape)], (volume,)
    )
    yeven, yodd = swap(edges, "filt", 0), swap(edges, "filt", 1)
    rim = struct((3, ny + 2, nz, cin))
    sides, near, far = call(
        spread_body,
        "spread",
        [struct((nx, 2, nz, cin)), rim, rim],
        (volume, yeven, yodd),
        flops=1 << 32,
        moved=1 << 24,
    )
    far = swap(far, "space", 1)
    near = swap(near, "space", 0)
    windows, sg, near_pooled, wide = call(
        near_body,
        "early_near",
        (
            struct((3, nx + 3, rows, 4 * cin)),
            struct((nx, rows, 2 * width), F32),
            struct((nx // 2, rows // 2, width)),
            struct((9, 4 * cin, 2 * width)),
        ),
        (volume, sides, near, w_early),
        [pltpu.VMEM((nx + 3, ny + 2, nz + 16, cin), F32)],
        flops=2 * nx * rows * 36 * cin * 2 * width,
    )
    far_windows, far_sg, pooled = call(
        far_body,
        "early_far",
        (
            struct((3, 3, rows, 4 * cin)),
            struct((nx, rows, 2 * width), F32),
            struct((nx // 2 + 2, rows // 2, width)),
        ),
        (windows, far, wide, near_pooled),
        [
            pltpu.VMEM((3, ny + 2, nz + 16, cin), F32),
            pltpu.VMEM((3, 6, rows, 4 * cin), BF16),
        ],
        flops=2 * nx * rows * 36 * cin * 2 * width,
    )
    parts = paired([pooled] * filt, "filt")
    turned = call(
        transpose_body,
        "turn_windows",
        struct((3, 2, 2 * cin, ext * rows)),
        (windows, far_windows),
        flops=1 << 30,
    )
    *parts, turned = lax.optimization_barrier((*parts, turned))
    dx, dy, dz, _ = cotangent.shape
    px = dx + 2
    prow = rows // 2
    deep = call(
        functools.partial(deep_body, filt),
        "deep_conv",
        [
            struct(cotangent.shape),
            struct((dx, dy * dz, filters)),
            struct((3, px, dy * dz, 3 * width)),
            struct((px, prow, width), F32),
        ]
        + [struct((px, prow, width))] * (filt - 1),
        (*parts, jnp.swapaxes(w_deep, 1, 2).reshape(9, 3 * filters, width), cotangent),
        [
            pltpu.VMEM((px, dy + 2, dz, width), F32),
            pltpu.VMEM((9, filters, 3 * width), BF16),
            pltpu.VMEM((dx, dy + 2, dz, filters), F32),
            pltpu.VMEM((3, dx, dy * dz, 3 * filters), BF16),
            pltpu.VMEM((px, dy, dz, width), F32),
        ],
        flops=4 * dx * dy * dz * 27 * width * filters,
    )
    block_out, grad, deep_windows = deep[:3]
    terms = paired(deep[3:], "filt")

    early_rows = 27 * cin // space
    deep_rows = ceil_to(-(-27 * filters // space), 16)
    deep_first, deep_second = call(
        deep_grad_body,
        "deep_grad",
        [struct((chips, deep_rows, width)), struct((chips, deep_rows, width), F32)],
        (deep_windows, grad),
        [pltpu.VMEM((2, chips * deep_rows, width), F32)],
        flops=2 * dx * dy * dz * 27 * width * filters,
    )
    piece = (chips, early_rows + deep_rows, width)
    held = pltpu.VMEM((27 * cin // 2, width), F32)
    flops = (nx + 4) * rows * 36 * cin * 2 * width
    theirs, grad = call(
        functools.partial(early_grad_body, half),
        "early_grad",
        [struct(piece), struct((nx + 4, rows, 2 * width))],
        (*backward(terms), sg, far_sg, turned, deep_first),
        [held, pltpu.VMEM((px, rows, 2 * width), F32)],
        flops=flops,
    )
    theirs = exchange(theirs, "space", 1)
    mine = call(
        early_grad_rest_body,
        "early_grad_rest",
        struct(piece, F32),
        (grad, turned, deep_second),
        [held],
        flops=flops,
    )
    sums = call(
        core_sum_body,
        "core_sum",
        [struct(piece[1:], F32)] + [struct(piece[1:])] * (chips - 1),
        (mine, theirs),
    )
    sums = backward(paired(sums, "space", 2))
    small = ceil_to(-(-early_rows // filt), 16)
    bits = filt.bit_length() - 1
    size = small * filt // 2
    deep_sum, send, keep = call(
        functools.partial(chip_sum_body, chips, early_rows, bits - 1),
        "chip_sum",
        [struct((deep_rows, width)), struct((size, width)), struct((size, width), F32)],
        sums,
        [pltpu.VMEM((small * filt, width), F32)],
    )
    for bit in reversed(range(bits - 1)):
        got = exchange(send, "filt", 1 << (bit + 1))
        size //= 2
        send, keep = call(
            functools.partial(halve_body, bit),
            "filt_halve",
            [struct((size, width)), struct((size, width), F32)],
            (keep, got),
            [pltpu.VMEM((2 * size, width), F32)],
        )
    got = exchange(send, "filt", 1)
    final = call(sum_body, "filt_sum", struct((small, width)), (keep, got))
    for bit in range(bits):
        got = exchange(final, "filt", 1 << bit)
        size = 2 * final.shape[0]
        last = (deep_sum,) if bit == bits - 1 else ()
        final = call(
            functools.partial(join_body, bit),
            "filt_join",
            struct((size + deep_rows * len(last), width)),
            (final, got, *last),
        )
    final_rows = small * filt + deep_rows
    finals = paired([final] * chips, "space", 2)
    own = call(stack_body, "stack", struct((chips, final_rows, width)), finals)
    other = exchange(own, "space", 1)
    early_total = nx * ny * nz * space * filt
    deep_total = dx * dy * dz * space
    results = [struct((27, cin, width), F32), struct((27, filters, width), F32)]
    scales = (1.0 / math.sqrt(early_total), 1.0 / math.sqrt(deep_total), early_rows, deep_rows)
    scratch = [
        pltpu.VMEM((27, cin // 2, width), F32),
        pltpu.VMEM((27, filters // 2, width), F32),
        DMA((6,)),
    ]
    results = call(
        functools.partial(finish_body, True, *scales),
        "finish_own",
        results,
        (own,),
        scratch,
        outs=HBM,
    )
    grad_early, grad_deep = call(
        functools.partial(finish_body, False, *scales),
        "finish_other",
        [struct(value.shape, F32) for value in results],
        (other, *results),
        scratch,
        hbm=(1, 2),
        outs=HBM,
        alias=((1, 0), (2, 1)),
    )
    return (block_out, grad_early, jnp.swapaxes(grad_deep, 1, 2))


def solution(mesh):
    return jax.shard_map(
        shards,
        mesh=mesh,
        in_specs=(
            P("space", "filt", None, None),
            P(),
            P(None, None, "filt"),
            P("space", None, None, "filt"),
        ),
        out_specs=(P("space", None, None, "filt"), P(), P(None, None, "filt")),
        check_vma=False,
    )
```

```python
import functools
import math

import jax
import jax.numpy as jnp
from jax import lax
from jax.experimental import pallas as pl
from jax.experimental.pallas import tpu as pltpu
from jax.sharding import PartitionSpec as P

F32 = jnp.float32
BF16 = jnp.bfloat16
VMEM_LIMIT = 24 * 1024 * 1024
VMEM = pl.BlockSpec(memory_space=pltpu.VMEM)
HBM = pl.BlockSpec(memory_space=pltpu.HBM)
DMA = pltpu.SemaphoreType.DMA


def call(
    body, name, out_shape, operands, scratch=(), flops=0, moved=1 << 20, hbm=(), outs=VMEM, alias=()
):
    return pl.pallas_call(
        body,
        name=name,
        out_shape=out_shape,
        in_specs=[HBM if i in hbm else VMEM for i in range(len(operands))],
        out_specs=jax.tree.map(lambda _: outs, out_shape),
        scratch_shapes=list(scratch),
        input_output_aliases=dict(alias),
        compiler_params=pltpu.CompilerParams(vmem_limit_bytes=VMEM_LIMIT),
        cost_estimate=pl.CostEstimate(flops=flops, bytes_accessed=moved, transcendentals=0),
    )(*operands)


def struct(shape, dtype=BF16):
    return jax.ShapeDtypeStruct(shape, dtype)


def ceil_to(value, step):
    return -(-value // step) * step


def sigmoid(value):
    return 1.0 / (1.0 + jnp.exp(-value))


def is_even(axis):
    return lax.rem(lax.axis_index(axis), 2) == 0


def edges_body(center, edges, copied):
    ny = center.shape[1]
    edges[:, 0:1] = center[:, 0:1]
    edges[:, 1:2] = center[:, ny - 1 :]
    copied[...] = center[...]


def has_both(axis):
    here = lax.axis_index(axis)
    return (here > 0) & (here < lax.axis_size(axis) - 1)


def spread_body(center, yeven, yodd, sides, near, far):
    nx, ny, _, _ = center.shape
    even = is_even("filt")
    beyond = jnp.where(has_both("filt"), yodd[...], jnp.zeros(yodd.shape, BF16))
    sides[:, 0:1] = jnp.where(even, beyond[:, 1:2], yeven[:, 1:2])
    sides[:, 1:2] = jnp.where(even, yeven[:, 0:1], beyond[:, 0:1])
    odd = lax.rem(lax.axis_index("space"), 2)
    for out, start in ((near, (1 - odd) * (nx - 3)), (far, odd * (nx - 3))):
        rows = pl.ds(start, 3)
        out[:, 0:1] = sides[rows, 0:1]
        out[:, 1 : ny + 1] = center[rows]
        out[:, ny + 1 :] = sides[rows, 1:2]


def fill_windows(field, windows):
    count, wide_y, _, cin = field.shape
    ny = wide_y - 2
    half = windows.shape[2] // ny
    for x in range(count):
        for group in range(4):
            plane = field[x, :, pl.ds(7 + group, half, stride=2), :]
            for b in range(3):
                windows[b, x, :, group * cin : (group + 1) * cin] = (
                    plane[b : b + ny].reshape(ny * half, cin).astype(BF16)
                )


def clear_ends(field, nz):
    count, wide_y, _, cin = field.shape
    field[:, :, 0:8] = jnp.zeros((count, wide_y, 8, cin), F32)
    field[:, :, 8 + nz : 16 + nz] = jnp.zeros((count, wide_y, 8, cin), F32)


def early_rows_of(windows, start, wide, ny, keep):
    rows = windows.shape[2]
    cout = wide.shape[2] // 2
    acc = jnp.zeros((2 * rows, 2 * cout), F32)
    for ab in range(9):
        a, b = ab // 3, ab % 3
        left = windows[b, pl.ds(start + a, 2)].reshape(2 * rows, windows.shape[3])
        acc = acc + jnp.dot(left, wide[ab], preferred_element_type=F32)
    sig = sigmoid(acc)
    slope = (sig * (1.0 + acc * (1.0 - sig)) * keep).reshape(2, rows, 2 * cout)
    act = acc * sig
    act = act[:rows] + act[rows:]
    act = act[:, :cout] + act[:, cout:]
    act = act.reshape(ny // 2, 2, rows // ny, cout)
    act = (act[:, 0] + act[:, 1]) * keep
    return slope, act.reshape(rows // 2, cout).astype(BF16)


def near_body(center, sides, near, w, windows, sg, pooled, wide, field):
    nx, ny, nz, cin = center.shape
    cout = w.shape[2]
    for ab in range(9):
        for group in range(4):
            for side in range(2):
                tap = group - side
                value = w[3 * ab + tap] if 0 <= tap <= 2 else jnp.zeros((cin, cout), BF16)
                wide[
                    ab, group * cin : (group + 1) * cin, side * cout : (side + 1) * cout
                ] = value
    odd = lax.rem(lax.axis_index("space"), 2)
    clear_ends(field, nz)
    cells = slice(8, 8 + nz)
    own = pl.ds(3 * odd, nx)
    field[own, 1 : ny + 1, cells] = center[...].astype(F32)
    field[own, 0:1, cells] = sides[:, 0:1].astype(F32)
    field[own, ny + 1 :, cells] = sides[:, 1:2].astype(F32)
    field[pl.ds((1 - odd) * nx, 3), :, cells] = near[...].astype(F32)
    fill_windows(field, windows)
    for chunk in range(nx // 2):
        slope, pool = early_rows_of(windows, 1 - odd + 2 * chunk, wide, ny, 0.125)
        sg[2 * chunk : 2 * chunk + 2] = slope
        pooled[chunk] = pool


def far_body(windows, far, wide, far_windows, sg, pooled, field, held):
    _, wide_y, nz, _ = far.shape
    odd = lax.rem(lax.axis_index("space"), 2)
    clear_ends(field, nz)
    inside = jnp.where(has_both("space"), 1.0, 0.0).astype(F32)
    field[:, :, 8 : 8 + nz] = far[...].astype(F32) * inside
    fill_windows(field, far_windows)
    for b in range(3):
        held[b, pl.ds(3 * odd, 3)] = far_windows[b]
        held[b, pl.ds(3 - 3 * odd, 3)] = windows[b, pl.ds(4 * odd, 3)]
    first = jnp.where(odd == 0, inside, 1.0)
    second = jnp.where(odd == 1, inside, 1.0)
    for chunk, flag in enumerate((first, second)):
        slope, pool = early_rows_of(held, 2 * chunk, wide, wide_y - 2, 0.125 * flag)
        sg[2 * chunk : 2 * chunk + 2] = slope
        pooled[chunk] = pool


def transpose_body(windows, far_windows, turned):
    rows = windows.shape[2]
    part = turned.shape[2] // 4
    odd = lax.rem(lax.axis_index("space"), 2)
    for source, first in ((windows, 3 * (1 - odd)), (far_windows, windows.shape[1] * odd)):
        for b in range(3):
            for x in range(source.shape[1]):
                value = source[b, x].T
                spot = pl.multiple_of((first + x) * rows, rows)
                for group in range(4):
                    for side in range(2):
                        row = (2 * group + side) * part
                        turned[
                            b, side, group * part : (group + 1) * part, pl.ds(spot, rows)
                        ] = value[row : row + part]


def roll_z(value, shift):
    size = value.shape[-2]
    rolled = pltpu.roll(value, shift % size, value.ndim - 2)
    spot = lax.broadcasted_iota(jnp.int32, value.shape, value.ndim - 2)
    edge = 0 if shift == 1 else size - 1
    return jnp.where(spot == edge, 0.0, rolled)


def deep_body(parts_n, *refs):
    near, far, refs = refs[:parts_n], refs[parts_n : 2 * parts_n], refs[2 * parts_n :]
    wt, cot, block_out, grad, windows = refs[:5]
    sends = refs[5 : parts_n + 5]
    field, wide, slopes, turned, terms = refs[parts_n + 5 :]
    nx, ny, nz, filters = cot.shape
    width = wt.shape[2]
    rows = ny * nz
    py = ny // parts_n
    mine = lax.axis_index("filt")
    for ab in range(9):
        for c in range(3):
            wide[ab, :, c * width : (c + 1) * width] = wt[
                ab, c * filters : (c + 1) * filters
            ]
    field[:, 0:1] = jnp.zeros((nx + 2, 1, nz, width), F32)
    field[:, ny + 1 : ny + 2] = jnp.zeros((nx + 2, 1, nz, width), F32)
    odd = lax.rem(lax.axis_index("space"), 2)
    for parts, first in ((near, 2 * (1 - odd)), (far, 2 * odd)):
        for j in range(parts_n):
            spot = lax.bitwise_xor(mine, j) * py + 1
            field[pl.ds(first, 2), pl.ds(spot, py)] = (
                parts[j][...].astype(F32).reshape(2, py, nz, width)
            )
    for x in range(nx + 2):
        plane = field[x]
        for c in range(3):
            moved = plane if c == 1 else roll_z(plane, 1 - c)
            for b in range(3):
                windows[b, x, :, c * width : (c + 1) * width] = (
                    moved[b : b + ny].reshape(rows, width).astype(BF16)
                )
    slopes[:, 0:1] = jnp.zeros((nx, 1, nz, filters), F32)
    slopes[:, ny + 1 :] = jnp.zeros((nx, 1, nz, filters), F32)
    for x in range(nx):
        acc = jnp.zeros((rows, filters), F32)
        for ab in range(9):
            a, b = ab // 3, ab % 3
            acc = acc + lax.dot_general(
                windows[b, x + a], wide[ab], (((1,), (1,)), ((), ())), preferred_element_type=F32
            )
        sig = sigmoid(acc)
        block_out[x] = (acc * sig).reshape(ny, nz, filters).astype(BF16)
        slope = sig * (1.0 + acc * (1.0 - sig))
        value = (cot[x].astype(F32).reshape(rows, filters) * slope).astype(BF16)
        grad[x] = value
        slopes[x, 1 : ny + 1] = value.astype(F32).reshape(ny, nz, filters)
    for x in range(nx):
        plane = slopes[x]
        plane = jnp.concatenate([roll_z(plane, -1), plane, roll_z(plane, 1)], axis=2)
        for b in range(3):
            turned[b, x] = (
                plane[2 - b : 2 - b + ny].reshape(rows, 3 * filters).astype(BF16)
            )
    for r in range(nx + 2):
        total = jnp.zeros((rows, width), F32)
        for ab in range(9):
            a, b = ab // 3, ab % 3
            if 0 <= r - a < nx:
                total = total + jnp.dot(turned[b, r - a], wt[ab], preferred_element_type=F32)
        terms[r] = total.reshape(ny, nz, width)
    for j in range(parts_n):
        spot = lax.bitwise_xor(mine, j) * py
        value = terms[:, pl.ds(spot, py)]
        sends[j][...] = value.reshape(nx + 2, py * nz, width).astype(sends[j].dtype)


def deep_grad_body(windows, grad, theirs, mine, held):
    nx, rows, filters = grad.shape
    width = windows.shape[3] // 3
    turned = grad[...].reshape(nx * rows, filters).astype(F32).T.astype(BF16)
    chips, step, _ = mine.shape
    part = filters // 2
    total = 27 * part
    if chips * step > total:
        held[:, total:] = jnp.zeros((2, chips * step - total, width), F32)
    for ab in range(9):
        a, b = ab // 3, ab % 3
        value = jnp.dot(
            turned,
            windows[b, a : a + nx].reshape(nx * rows, 3 * width),
            preferred_element_type=F32,
        )
        for c in range(3):
            spot = (3 * ab + c) * part
            for side in range(2):
                held[side, spot : spot + part] = value[
                    side * part : (side + 1) * part, c * width : (c + 1) * width
                ]
    core = lax.rem(lax.axis_index("space"), 2)
    for q in range(chips):
        theirs[q] = held[1 - core, q * step : (q + 1) * step].astype(theirs.dtype)
        mine[q] = held[core, q * step : (q + 1) * step]


def early_grad_body(nz, *refs):
    parts, (sg, far_sg, turned, deep, out, grad, held, spread) = refs[:-8], refs[-8:]
    count, rows, wide = sg.shape
    total = parts[0][...]
    for part in parts[1:]:
        total = total + part[...].astype(F32)
    px, prow, _ = total.shape
    py = prow // nz
    total = jnp.concatenate([total, total], axis=2).reshape(px, py, 1, nz, wide)
    spread[...] = jnp.broadcast_to(total, (px, py, 2, nz, wide)).reshape(px, rows, wide)
    odd = lax.rem(lax.axis_index("space"), 2)
    for source, first in ((sg, count * (1 - odd)), (far_sg, count * odd)):
        for x in range(count):
            grad[first + x] = (spread[lax.div(first, 2) + x // 2] * source[x]).astype(BF16)
    early_grad_half(1 - odd, grad, turned, deep, out, held)


def early_grad_rest_body(grad, turned, deep, out, held):
    early_grad_half(lax.rem(lax.axis_index("space"), 2), grad, turned, deep, out, held)


def early_grad_half(side, grad, turned, deep, out, held):
    ext, rows, wide = grad.shape
    width = wide // 2
    part = turned.shape[2] // 4
    right = grad[...].reshape(ext * rows, wide)
    for ab in range(9):
        a, b = ab // 3, ab % 3
        value = jnp.dot(
            turned[b, side, :, a * rows : (a + ext) * rows], right, preferred_element_type=F32
        )
        for c in range(3):
            spot = (3 * ab + c) * part
            held[spot : spot + part] = (
                value[c * part : (c + 1) * part, :width]
                + value[(c + 1) * part : (c + 2) * part, width:]
            )
    step = held.shape[0] // out.shape[0]
    for q in range(out.shape[0]):
        out[q, :step] = held[q * step : (q + 1) * step].astype(out.dtype)
        out[q, step:] = deep[q].astype(out.dtype)


def core_sum_body(mine, other, *outs):
    chip = lax.div(lax.axis_index("space"), 2)
    for j, out in enumerate(outs):
        q = lax.bitwise_xor(chip, j)
        out[...] = (mine[q] + other[q].astype(F32)).astype(out.dtype)


def chip_sum_body(count, step, *refs):
    others, (deep, *outs, held) = refs[:count], refs[count:]
    total = others[0][...]
    for ref in others[1:]:
        total = total + ref[...].astype(F32)
    held[:step] = total[:step]
    if held.shape[0] > step:
        held[step:] = jnp.zeros((held.shape[0] - step, total.shape[1]), F32)
    deep[...] = total[step:].astype(BF16)
    size = outs[0].shape[0]
    for j, out in enumerate(outs):
        spot = pl.multiple_of(lax.bitwise_xor(lax.axis_index("filt"), j) * size, 8)
        out[...] = held[pl.ds(spot, size)].astype(out.dtype)


def sum_body(*refs):
    total = refs[0][...]
    for ref in refs[1:-1]:
        total = total + ref[...].astype(F32)
    refs[-1][...] = total.astype(BF16)


def line_up_body(*refs):
    shares, deep, out = refs[:-2], refs[-2], refs[-1]
    size = shares[0].shape[0]
    for j, share in enumerate(shares):
        spot = pl.multiple_of(lax.bitwise_xor(lax.axis_index("filt"), j) * size, 16)
        out[pl.ds(spot, size)] = share[...]
    out[size * len(shares) :] = deep[...]


def stack_body(*refs):
    out = refs[-1]
    chip = lax.div(lax.axis_index("space"), 2)
    for j, ref in enumerate(refs[:-1]):
        out[lax.bitwise_xor(chip, j)] = ref[...]


def finish_body(own, early_scale, deep_scale, early_rows, deep_rows, pieces, *refs):
    early, deep, early_held, deep_held, sem = refs[-5:]
    core = lax.rem(lax.axis_index("space"), 2)
    side = core if own else 1 - core
    copies = []
    for out, held, first, step, scale in (
        (early, early_held, 0, early_rows, early_scale),
        (deep, deep_held, pieces.shape[1] - deep_rows, deep_rows, deep_scale),
    ):
        part = held.shape[1]
        for tap in range(27):
            row = tap * part
            while row < (tap + 1) * part:
                q, inner = row // step, row % step
                size = min(step - inner, (tap + 1) * part - row)
                spot = row - tap * part
                held[tap, spot : spot + size] = (
                    pieces[q, first + inner : first + inner + size].astype(F32) * scale
                )
                row += size
            if tap % 9 == 8:
                taps = pl.ds(tap - 8, 9)
                copy = pltpu.make_async_copy(
                    held.at[taps], out.at[taps, pl.ds(side * part, part)], sem.at[len(copies)]
                )
                copy.start()
                copies.append(copy)
    for copy in copies:
        copy.wait()


def paired(values, axis, step=1):
    count = lax.axis_size(axis)
    got = {
        j: lax.ppermute(values[j], axis, [(i, i ^ (step * j)) for i in range(count)])
        for j in reversed(range(1, len(values)))
    }
    return [values[0]] + [got[j] for j in range(1, len(values))]


def backward(values):
    return [values[0]] + values[:0:-1]


def swap(value, axis, first):
    count = lax.axis_size(axis)
    pairs = [(i, (i + 1) % count) for i in range(first, count, 2)]
    return lax.ppermute(value, axis, pairs + [(b, a) for a, b in pairs])


def shards(volume, w_early, w_deep, cotangent):
    nx, ny, nz, cin = volume.shape
    width = w_early.shape[2]
    filters = w_deep.shape[2]
    space = lax.axis_size("space")
    filt = lax.axis_size("filt")
    chips = space // 2
    half = nz // 2
    ext = nx + 6
    rows = ny * half
    edges, volume = call(
        edges_body, "edges", [struct((nx, 2, nz, cin)), struct(volume.shape)], (volume,)
    )
    yeven, yodd = swap(edges, "filt", 0), swap(edges, "filt", 1)
    rim = struct((3, ny + 2, nz, cin))
    sides, near, far = call(
        spread_body,
        "spread",
        [struct((nx, 2, nz, cin)), rim, rim],
        (volume, yeven, yodd),
        flops=1 << 32,
        moved=1 << 24,
    )
    far = swap(far, "space", 1)
    near = swap(near, "space", 0)
    windows, sg, near_pooled, wide = call(
        near_body,
        "early_near",
        (
            struct((3, nx + 3, rows, 4 * cin)),
            struct((nx, rows, 2 * width), F32),
            struct((nx // 2, rows // 2, width)),
            struct((9, 4 * cin, 2 * width)),
        ),
        (volume, sides, near, w_early),
        [pltpu.VMEM((nx + 3, ny + 2, nz + 16, cin), F32)],
        flops=2 * nx * rows * 36 * cin * 2 * width,
    )
    near_parts = paired([near_pooled] * filt, "filt")
    far, *near_parts[2:] = lax.optimization_barrier((far, *near_parts[2:]))
    far_windows, far_sg, pooled = call(
        far_body,
        "early_far",
        (
            struct((3, 3, rows, 4 * cin)),
            struct((nx, rows, 2 * width), F32),
            struct((nx // 2, rows // 2, width)),
        ),
        (windows, far, wide),
        [
            pltpu.VMEM((3, ny + 2, nz + 16, cin), F32),
            pltpu.VMEM((3, 6, rows, 4 * cin), BF16),
        ],
        moved=0,
    )
    parts = paired([pooled] * filt, "filt")
    turned = call(
        transpose_body,
        "turn_windows",
        struct((3, 2, 2 * cin, ext * rows)),
        (windows, far_windows),
        flops=1 << 30,
    )
    *parts, turned = lax.optimization_barrier((*parts, turned))
    dx, dy, dz, _ = cotangent.shape
    px = dx + 2
    prow = rows // 2
    deep = call(
        functools.partial(deep_body, filt),
        "deep_conv",
        [
            struct(cotangent.shape),
            struct((dx, dy * dz, filters)),
            struct((3, px, dy * dz, 3 * width)),
            struct((px, prow, width), F32),
        ]
        + [struct((px, prow, width))] * (filt - 1),
        (*near_parts, *parts, jnp.swapaxes(w_deep, 1, 2).reshape(9, 3 * filters, width), cotangent),
        [
            pltpu.VMEM((px, dy + 2, dz, width), F32),
            pltpu.VMEM((9, filters, 3 * width), BF16),
            pltpu.VMEM((dx, dy + 2, dz, filters), F32),
            pltpu.VMEM((3, dx, dy * dz, 3 * filters), BF16),
            pltpu.VMEM((px, dy, dz, width), F32),
        ],
        flops=4 * dx * dy * dz * 27 * width * filters,
    )
    block_out, grad, deep_windows = deep[:3]
    terms = paired(deep[3:], "filt")

    early_rows = 27 * cin // space
    deep_rows = ceil_to(-(-27 * filters // space), 16)
    deep_first, deep_second = call(
        deep_grad_body,
        "deep_grad",
        [struct((chips, deep_rows, width)), struct((chips, deep_rows, width), F32)],
        (deep_windows, grad),
        [pltpu.VMEM((2, chips * deep_rows, width), F32)],
        flops=2 * dx * dy * dz * 27 * width * filters,
    )
    piece = (chips, early_rows + deep_rows, width)
    held = pltpu.VMEM((27 * cin // 2, width), F32)
    flops = (nx + 4) * rows * 36 * cin * 2 * width
    theirs, grad = call(
        functools.partial(early_grad_body, half),
        "early_grad",
        [struct(piece), struct((nx + 4, rows, 2 * width))],
        (*backward(terms), sg, far_sg, turned, deep_first),
        [held, pltpu.VMEM((px, rows, 2 * width), F32)],
        flops=flops,
    )
    theirs = lax.ppermute(theirs, "space", [(i, i ^ 1) for i in range(space)])
    mine = call(
        early_grad_rest_body,
        "early_grad_rest",
        struct(piece, F32),
        (grad, turned, deep_second),
        [held],
        flops=flops,
    )
    sums = call(
        core_sum_body,
        "core_sum",
        [struct(piece[1:], F32)] + [struct(piece[1:])] * (chips - 1),
        (mine, theirs),
    )
    sums = backward(paired(sums, "space", 2))
    small = ceil_to(-(-early_rows // filt), 16)
    deep_sum, *shares = call(
        functools.partial(chip_sum_body, chips, early_rows),
        "chip_sum",
        [struct((deep_rows, width)), struct((small, width), F32)]
        + [struct((small, width))] * (filt - 1),
        sums,
        [pltpu.VMEM((small * filt, width), F32)],
    )
    share = call(sum_body, "filt_sum", struct((small, width)), backward(paired(shares, "filt")))
    shares = paired([share] * filt, "filt")
    final_rows = small * filt + deep_rows
    final = call(line_up_body, "line_up", struct((final_rows, width)), (*shares, deep_sum))
    finals = paired([final] * chips, "space", 2)
    own = call(stack_body, "stack", struct((chips, final_rows, width)), finals)
    other = lax.ppermute(own, "space", [(i, i ^ 1) for i in range(space)])
    early_total = nx * ny * nz * space * filt
    deep_total = dx * dy * dz * space
    results = [struct((27, cin, width), F32), struct((27, filters, width), F32)]
    scales = (1.0 / math.sqrt(early_total), 1.0 / math.sqrt(deep_total), early_rows, deep_rows)
    scratch = [
        pltpu.VMEM((27, cin // 2, width), F32),
        pltpu.VMEM((27, filters // 2, width), F32),
        DMA((6,)),
    ]
    results = call(
        functools.partial(finish_body, True, *scales),
        "finish_own",
        results,
        (own,),
        scratch,
        outs=HBM,
    )
    grad_early, grad_deep = call(
        functools.partial(finish_body, False, *scales),
        "finish_other",
        [struct(value.shape, F32) for value in results],
        (other, *results),
        scratch,
        hbm=(1, 2),
        outs=HBM,
        alias=((1, 0), (2, 1)),
    )
    return (block_out, grad_early, jnp.swapaxes(grad_deep, 1, 2))


def solution(mesh):
    return jax.shard_map(
        shards,
        mesh=mesh,
        in_specs=(
            P("space", "filt", None, None),
            P(),
            P(None, None, "filt"),
            P("space", None, None, "filt"),
        ),
        out_specs=(P("space", None, None, "filt"), P(), P(None, None, "filt")),
        check_vma=False,
    )
```

```python
import functools
import math

import jax
import jax.numpy as jnp
from jax import lax
from jax.experimental import pallas as pl
from jax.experimental.pallas import tpu as pltpu
from jax.sharding import PartitionSpec as P

F32 = jnp.float32
BF16 = jnp.bfloat16
VMEM_LIMIT = 24 * 1024 * 1024
VMEM = pl.BlockSpec(memory_space=pltpu.VMEM)
HBM = pl.BlockSpec(memory_space=pltpu.HBM)
DMA = pltpu.SemaphoreType.DMA


def call(
    body, name, out_shape, operands, scratch=(), flops=0, moved=1 << 20, hbm=(), outs=VMEM, alias=()
):
    return pl.pallas_call(
        body,
        name=name,
        out_shape=out_shape,
        in_specs=[HBM if i in hbm else VMEM for i in range(len(operands))],
        out_specs=jax.tree.map(lambda _: outs, out_shape),
        scratch_shapes=list(scratch),
        input_output_aliases=dict(alias),
        compiler_params=pltpu.CompilerParams(vmem_limit_bytes=VMEM_LIMIT),
        cost_estimate=pl.CostEstimate(flops=flops, bytes_accessed=moved, transcendentals=0),
    )(*operands)


def struct(shape, dtype=BF16):
    return jax.ShapeDtypeStruct(shape, dtype)


def ceil_to(value, step):
    return -(-value // step) * step


def sigmoid(value):
    return 1.0 / (1.0 + jnp.exp(-value))


def is_even(axis):
    return lax.rem(lax.axis_index(axis), 2) == 0


def edges_body(edges, copied):
    copied[...] = edges[...]


def has_both(axis):
    here = lax.axis_index(axis)
    return (here > 0) & (here < lax.axis_size(axis) - 1)


def spread_body(center, yeven, yodd, copied, sides, near, far):
    copied[...] = center[...]
    nx, ny, _, _ = center.shape
    even = is_even("filt")
    beyond = jnp.where(has_both("filt"), yodd[...], jnp.zeros(yodd.shape, BF16))
    sides[:, 0:1] = jnp.where(even, beyond[:, 1:2], yeven[:, 1:2])
    sides[:, 1:2] = jnp.where(even, yeven[:, 0:1], beyond[:, 0:1])
    odd = lax.rem(lax.axis_index("space"), 2)
    for out, start in ((near, (1 - odd) * (nx - 3)), (far, odd * (nx - 3))):
        rows = pl.ds(start, 3)
        out[:, 0:1] = sides[rows, 0:1]
        out[:, 1 : ny + 1] = center[rows]
        out[:, ny + 1 :] = sides[rows, 1:2]


def fill_windows(field, windows):
    count, wide_y, _, cin = field.shape
    ny = wide_y - 2
    half = windows.shape[2] // ny
    for x in range(count):
        for group in range(4):
            plane = field[x, :, pl.ds(7 + group, half, stride=2), :]
            for b in range(3):
                windows[b, x, :, group * cin : (group + 1) * cin] = (
                    plane[b : b + ny].reshape(ny * half, cin).astype(BF16)
                )


def clear_ends(field, nz):
    count, wide_y, _, cin = field.shape
    field[:, :, 0:8] = jnp.zeros((count, wide_y, 8, cin), F32)
    field[:, :, 8 + nz : 16 + nz] = jnp.zeros((count, wide_y, 8, cin), F32)


def early_rows_of(windows, start, wide, ny, keep):
    rows = windows.shape[2]
    cout = wide.shape[2] // 2
    acc = jnp.zeros((2 * rows, 2 * cout), F32)
    for ab in range(9):
        a, b = ab // 3, ab % 3
        left = windows[b, pl.ds(start + a, 2)].reshape(2 * rows, windows.shape[3])
        acc = acc + jnp.dot(left, wide[ab], preferred_element_type=F32)
    sig = sigmoid(acc)
    slope = (sig * (1.0 + acc * (1.0 - sig)) * keep).reshape(2, rows, 2 * cout)
    act = acc * sig
    act = act[:rows] + act[rows:]
    act = act[:, :cout] + act[:, cout:]
    act = act.reshape(ny // 2, 2, rows // ny, cout)
    act = (act[:, 0] + act[:, 1]) * keep
    return slope, act.reshape(rows // 2, cout).astype(BF16)


def near_body(center, sides, near, w, windows, sg, pooled, wide, field):
    nx, ny, nz, cin = center.shape
    cout = w.shape[2]
    for ab in range(9):
        for group in range(4):
            for side in range(2):
                tap = group - side
                value = w[3 * ab + tap] if 0 <= tap <= 2 else jnp.zeros((cin, cout), BF16)
                wide[
                    ab, group * cin : (group + 1) * cin, side * cout : (side + 1) * cout
                ] = value
    odd = lax.rem(lax.axis_index("space"), 2)
    clear_ends(field, nz)
    cells = slice(8, 8 + nz)
    own = pl.ds(3 * odd, nx)
    field[own, 1 : ny + 1, cells] = center[...].astype(F32)
    field[own, 0:1, cells] = sides[:, 0:1].astype(F32)
    field[own, ny + 1 :, cells] = sides[:, 1:2].astype(F32)
    field[pl.ds((1 - odd) * nx, 3), :, cells] = near[...].astype(F32)
    fill_windows(field, windows)
    for chunk in range(nx // 2):
        slope, pool = early_rows_of(windows, 1 - odd + 2 * chunk, wide, ny, 0.125)
        sg[2 * chunk : 2 * chunk + 2] = slope
        pooled[chunk] = pool


def far_body(windows, far, wide, near_pooled, far_windows, sg, pooled, field, held):
    _, wide_y, nz, _ = far.shape
    odd = lax.rem(lax.axis_index("space"), 2)
    clear_ends(field, nz)
    inside = jnp.where(has_both("space"), 1.0, 0.0).astype(F32)
    field[:, :, 8 : 8 + nz] = far[...].astype(F32) * inside
    fill_windows(field, far_windows)
    for b in range(3):
        held[b, pl.ds(3 * odd, 3)] = far_windows[b]
        held[b, pl.ds(3 - 3 * odd, 3)] = windows[b, pl.ds(4 * odd, 3)]
    first = jnp.where(odd == 0, inside, 1.0)
    second = jnp.where(odd == 1, inside, 1.0)
    count = near_pooled.shape[0]
    for chunk, flag in enumerate((first, second)):
        slope, pool = early_rows_of(held, 2 * chunk, wide, wide_y - 2, 0.125 * flag)
        sg[2 * chunk : 2 * chunk + 2] = slope
        pooled[count * odd + chunk] = pool
        pooled[count * (1 - odd) + chunk] = near_pooled[chunk]


def transpose_body(windows, far_windows, turned):
    rows = windows.shape[2]
    part = turned.shape[2] // 4
    odd = lax.rem(lax.axis_index("space"), 2)
    for source, first in ((windows, 3 * (1 - odd)), (far_windows, windows.shape[1] * odd)):
        for b in range(3):
            for x in range(source.shape[1]):
                value = source[b, x].T
                spot = pl.multiple_of((first + x) * rows, rows)
                for group in range(4):
                    for side in range(2):
                        row = (2 * group + side) * part
                        turned[
                            b, side, group * part : (group + 1) * part, pl.ds(spot, rows)
                        ] = value[row : row + part]


def roll_z(value, shift):
    size = value.shape[-2]
    rolled = pltpu.roll(value, shift % size, value.ndim - 2)
    spot = lax.broadcasted_iota(jnp.int32, value.shape, value.ndim - 2)
    edge = 0 if shift == 1 else size - 1
    return jnp.where(spot == edge, 0.0, rolled)


def deep_body(parts_n, *refs):
    parts, refs = refs[:parts_n], refs[parts_n:]
    wt, cot, block_out, grad, windows = refs[:5]
    sends = refs[5 : parts_n + 5]
    field, wide, slopes, turned, terms = refs[parts_n + 5 :]
    nx, ny, nz, filters = cot.shape
    width = wt.shape[2]
    rows = ny * nz
    py = ny // parts_n
    mine = lax.axis_index("filt")
    for ab in range(9):
        for c in range(3):
            wide[ab, :, c * width : (c + 1) * width] = wt[
                ab, c * filters : (c + 1) * filters
            ]
    field[:, 0:1] = jnp.zeros((nx + 2, 1, nz, width), F32)
    field[:, ny + 1 : ny + 2] = jnp.zeros((nx + 2, 1, nz, width), F32)
    for j in range(parts_n):
        spot = lax.bitwise_xor(mine, j) * py + 1
        field[:, pl.ds(spot, py)] = parts[j][...].astype(F32).reshape(nx + 2, py, nz, width)
    for x in range(nx + 2):
        plane = field[x]
        for c in range(3):
            moved = plane if c == 1 else roll_z(plane, 1 - c)
            for b in range(3):
                windows[b, x, :, c * width : (c + 1) * width] = (
                    moved[b : b + ny].reshape(rows, width).astype(BF16)
                )
    slopes[:, 0:1] = jnp.zeros((nx, 1, nz, filters), F32)
    slopes[:, ny + 1 :] = jnp.zeros((nx, 1, nz, filters), F32)
    for x in range(nx):
        acc = jnp.zeros((rows, filters), F32)
        for ab in range(9):
            a, b = ab // 3, ab % 3
            acc = acc + lax.dot_general(
                windows[b, x + a], wide[ab], (((1,), (1,)), ((), ())), preferred_element_type=F32
            )
        sig = sigmoid(acc)
        block_out[x] = (acc * sig).reshape(ny, nz, filters).astype(BF16)
        slope = sig * (1.0 + acc * (1.0 - sig))
        value = (cot[x].astype(F32).reshape(rows, filters) * slope).astype(BF16)
        grad[x] = value
        slopes[x, 1 : ny + 1] = value.astype(F32).reshape(ny, nz, filters)
    for x in range(nx):
        plane = slopes[x]
        plane = jnp.concatenate([roll_z(plane, -1), plane, roll_z(plane, 1)], axis=2)
        for b in range(3):
            turned[b, x] = (
                plane[2 - b : 2 - b + ny].reshape(rows, 3 * filters).astype(BF16)
            )
    for r in range(nx + 2):
        total = jnp.zeros((rows, width), F32)
        for ab in range(9):
            a, b = ab // 3, ab % 3
            if 0 <= r - a < nx:
                total = total + jnp.dot(turned[b, r - a], wt[ab], preferred_element_type=F32)
        terms[r] = total.reshape(ny, nz, width)
    for j in range(parts_n):
        spot = lax.bitwise_xor(mine, j) * py
        value = terms[:, pl.ds(spot, py)]
        sends[j][...] = value.reshape(nx + 2, py * nz, width).astype(sends[j].dtype)


def deep_grad_body(windows, grad, theirs, mine, held):
    nx, rows, filters = grad.shape
    width = windows.shape[3] // 3
    turned = grad[...].reshape(nx * rows, filters).astype(F32).T.astype(BF16)
    chips, step, _ = mine.shape
    part = filters // 2
    total = 27 * part
    if chips * step > total:
        held[:, total:] = jnp.zeros((2, chips * step - total, width), F32)
    for ab in range(9):
        a, b = ab // 3, ab % 3
        value = jnp.dot(
            turned,
            windows[b, a : a + nx].reshape(nx * rows, 3 * width),
            preferred_element_type=F32,
        )
        for c in range(3):
            spot = (3 * ab + c) * part
            for side in range(2):
                held[side, spot : spot + part] = value[
                    side * part : (side + 1) * part, c * width : (c + 1) * width
                ]
    core = lax.rem(lax.axis_index("space"), 2)
    for q in range(chips):
        theirs[q] = held[1 - core, q * step : (q + 1) * step].astype(theirs.dtype)
        mine[q] = held[core, q * step : (q + 1) * step]


def early_grad_body(nz, *refs):
    parts, (sg, far_sg, turned, deep, out, grad, held, spread) = refs[:-8], refs[-8:]
    count, rows, wide = sg.shape
    total = parts[0][...]
    for part in parts[1:]:
        total = total + part[...].astype(F32)
    px, prow, _ = total.shape
    py = prow // nz
    total = jnp.concatenate([total, total], axis=2).reshape(px, py, 1, nz, wide)
    spread[...] = jnp.broadcast_to(total, (px, py, 2, nz, wide)).reshape(px, rows, wide)
    odd = lax.rem(lax.axis_index("space"), 2)
    for source, first in ((sg, count * (1 - odd)), (far_sg, count * odd)):
        for x in range(count):
            grad[first + x] = (spread[lax.div(first, 2) + x // 2] * source[x]).astype(BF16)
    early_grad_half(1 - odd, grad, turned, deep, out, held)


def early_grad_rest_body(grad, turned, deep, out, held):
    early_grad_half(lax.rem(lax.axis_index("space"), 2), grad, turned, deep, out, held)


def early_grad_half(side, grad, turned, deep, out, held):
    ext, rows, wide = grad.shape
    width = wide // 2
    part = turned.shape[2] // 4
    right = grad[...].reshape(ext * rows, wide)
    for ab in range(9):
        a, b = ab // 3, ab % 3
        value = jnp.dot(
            turned[b, side, :, a * rows : (a + ext) * rows], right, preferred_element_type=F32
        )
        for c in range(3):
            spot = (3 * ab + c) * part
            held[spot : spot + part] = (
                value[c * part : (c + 1) * part, :width]
                + value[(c + 1) * part : (c + 2) * part, width:]
            )
    step = held.shape[0] // out.shape[0]
    for q in range(out.shape[0]):
        out[q, :step] = held[q * step : (q + 1) * step].astype(out.dtype)
        out[q, step:] = deep[q].astype(out.dtype)


def core_sum_body(mine, other, *outs):
    chip = lax.div(lax.axis_index("space"), 2)
    for j, out in enumerate(outs):
        q = lax.bitwise_xor(chip, j)
        out[...] = (mine[q] + other[q].astype(F32)).astype(out.dtype)


def chip_sum_body(step, *refs):
    *others, early, deep = refs
    total = others[0][...]
    for ref in others[1:]:
        total = total + ref[...].astype(F32)
    early[...] = total[:step].astype(BF16)
    deep[...] = total[step:].astype(BF16)


def filt_sum_body(*refs):
    *parts, out = refs
    values = [part[...].astype(F32) for part in parts]
    while len(values) > 1:
        values = [low + high for low, high in zip(values[::2], values[1::2])]
    out[...] = values[0].astype(BF16)


def stack_body(*refs):
    out = refs[-1]
    chips, rows, _ = out.shape
    chip = lax.div(lax.axis_index("space"), 2)
    for j in range(chips):
        step = refs[j].shape[0]
        q = lax.bitwise_xor(chip, j)
        out[q, :step] = refs[j][...]
        out[q, step:] = refs[chips + j][...]


def finish_body(own, early_scale, deep_scale, early_rows, deep_rows, pieces, *refs):
    early, deep, early_held, deep_held, sem = refs[-5:]
    core = lax.rem(lax.axis_index("space"), 2)
    side = core if own else 1 - core
    copies = []
    for out, held, first, step, scale in (
        (early, early_held, 0, early_rows, early_scale),
        (deep, deep_held, pieces.shape[1] - deep_rows, deep_rows, deep_scale),
    ):
        part = held.shape[1]
        for tap in range(27):
            row = tap * part
            while row < (tap + 1) * part:
                q, inner = row // step, row % step
                size = min(step - inner, (tap + 1) * part - row)
                spot = row - tap * part
                held[tap, spot : spot + size] = (
                    pieces[q, first + inner : first + inner + size].astype(F32) * scale
                )
                row += size
            if tap % 9 == 8:
                taps = pl.ds(tap - 8, 9)
                copy = pltpu.make_async_copy(
                    held.at[taps], out.at[taps, pl.ds(side * part, part)], sem.at[len(copies)]
                )
                copy.start()
                copies.append(copy)
    for copy in copies:
        copy.wait()


def paired(values, axis, step=1):
    count = lax.axis_size(axis)
    got = {
        j: lax.ppermute(values[j], axis, [(i, i ^ (step * j)) for i in range(count)])
        for j in reversed(range(1, len(values)))
    }
    return [values[0]] + [got[j] for j in range(1, len(values))]


def backward(values):
    return [values[0]] + values[:0:-1]


def swap(value, axis, first):
    count = lax.axis_size(axis)
    pairs = [(i, (i + 1) % count) for i in range(first, count, 2)]
    return lax.ppermute(value, axis, pairs + [(b, a) for a, b in pairs])


def shards(volume, w_early, w_deep, cotangent):
    nx, ny, nz, cin = volume.shape
    width = w_early.shape[2]
    filters = w_deep.shape[2]
    space = lax.axis_size("space")
    filt = lax.axis_size("filt")
    chips = space // 2
    half = nz // 2
    ext = nx + 6
    rows = ny * half
    edges = jnp.concatenate([volume[:, :1], volume[:, ny - 1 :]], axis=1)
    edges = call(edges_body, "edges", struct(edges.shape), (edges,), flops=1 << 32)
    yeven, yodd = swap(edges, "filt", 0), swap(edges, "filt", 1)
    rim = struct((3, ny + 2, nz, cin))
    volume, sides, near, far = call(
        spread_body,
        "spread",
        [struct(volume.shape), struct((nx, 2, nz, cin)), rim, rim],
        (volume, yeven, yodd),
        flops=1 << 32,
        moved=1 << 24,
    )
    far = swap(far, "space", 1)
    near = swap(near, "space", 0)
    windows, sg, near_pooled, wide = call(
        near_body,
        "early_near",
        (
            struct((3, nx + 3, rows, 4 * cin)),
            struct((nx, rows, 2 * width), F32),
            struct((nx // 2, rows // 2, width)),
            struct((9, 4 * cin, 2 * width)),
        ),
        (volume, sides, near, w_early),
        [pltpu.VMEM((nx + 3, ny + 2, nz + 16, cin), F32)],
        flops=2 * nx * rows * 36 * cin * 2 * width,
    )
    far_windows, far_sg, pooled = call(
        far_body,
        "early_far",
        (
            struct((3, 3, rows, 4 * cin)),
            struct((nx, rows, 2 * width), F32),
            struct((nx // 2 + 2, rows // 2, width)),
        ),
        (windows, far, wide, near_pooled),
        [
            pltpu.VMEM((3, ny + 2, nz + 16, cin), F32),
            pltpu.VMEM((3, 6, rows, 4 * cin), BF16),
        ],
        flops=2 * nx * rows * 36 * cin * 2 * width,
    )
    parts = paired([pooled] * filt, "filt")
    turned = call(
        transpose_body,
        "turn_windows",
        struct((3, 2, 2 * cin, ext * rows)),
        (windows, far_windows),
        flops=1 << 30,
    )
    *parts, turned = lax.optimization_barrier((*parts, turned))
    dx, dy, dz, _ = cotangent.shape
    px = dx + 2
    prow = rows // 2
    deep = call(
        functools.partial(deep_body, filt),
        "deep_conv",
        [
            struct(cotangent.shape),
            struct((dx, dy * dz, filters)),
            struct((3, px, dy * dz, 3 * width)),
            struct((px, prow, width), F32),
        ]
        + [struct((px, prow, width))] * (filt - 1),
        (*parts, jnp.swapaxes(w_deep, 1, 2).reshape(9, 3 * filters, width), cotangent),
        [
            pltpu.VMEM((px, dy + 2, dz, width), F32),
            pltpu.VMEM((9, filters, 3 * width), BF16),
            pltpu.VMEM((dx, dy + 2, dz, filters), F32),
            pltpu.VMEM((3, dx, dy * dz, 3 * filters), BF16),
            pltpu.VMEM((px, dy, dz, width), F32),
        ],
        flops=4 * dx * dy * dz * 27 * width * filters,
    )
    block_out, grad, deep_windows = deep[:3]
    terms = paired(deep[3:], "filt")

    early_rows = 27 * cin // space
    deep_rows = ceil_to(-(-27 * filters // space), 16)
    deep_first, deep_second = call(
        deep_grad_body,
        "deep_grad",
        [struct((chips, deep_rows, width)), struct((chips, deep_rows, width), F32)],
        (deep_windows, grad),
        [pltpu.VMEM((2, chips * deep_rows, width), F32)],
        flops=2 * dx * dy * dz * 27 * width * filters,
    )
    piece = (chips, early_rows + deep_rows, width)
    held = pltpu.VMEM((27 * cin // 2, width), F32)
    flops = (nx + 4) * rows * 36 * cin * 2 * width
    theirs, grad = call(
        functools.partial(early_grad_body, half),
        "early_grad",
        [struct(piece), struct((nx + 4, rows, 2 * width))],
        (*backward(terms), sg, far_sg, turned, deep_first),
        [held, pltpu.VMEM((px, rows, 2 * width), F32)],
        flops=flops,
    )
    theirs = lax.ppermute(theirs, "space", [(i, i ^ 1) for i in range(space)])
    mine = call(
        early_grad_rest_body,
        "early_grad_rest",
        struct(piece, F32),
        (grad, turned, deep_second),
        [held],
        flops=flops,
    )
    sums = call(
        core_sum_body,
        "core_sum",
        [struct(piece[1:], F32)] + [struct(piece[1:])] * (chips - 1),
        (mine, theirs),
    )
    sums = backward(paired(sums, "space", 2))
    early, deep = call(
        functools.partial(chip_sum_body, early_rows),
        "chip_sum",
        [struct((early_rows, width)), struct((deep_rows, width))],
        sums,
    )
    shares = paired([early] * filt, "filt")
    deeps = paired([deep] * chips, "space", 2)
    *shares, deeps[1:] = lax.optimization_barrier((*shares, deeps[1:]))
    share = call(filt_sum_body, "filt_sum", struct((early_rows, width)), shares)
    finals = paired([share] * chips, "space", 2)
    own = call(stack_body, "stack", struct(piece), (*finals, *deeps))
    other = lax.ppermute(own, "space", [(i, i ^ 1) for i in range(space)])
    early_total = nx * ny * nz * space * filt
    deep_total = dx * dy * dz * space
    results = [struct((27, cin, width), F32), struct((27, filters, width), F32)]
    scales = (1.0 / math.sqrt(early_total), 1.0 / math.sqrt(deep_total), early_rows, deep_rows)
    scratch = [
        pltpu.VMEM((27, cin // 2, width), F32),
        pltpu.VMEM((27, filters // 2, width), F32),
        DMA((6,)),
    ]
    results = call(
        functools.partial(finish_body, True, *scales),
        "finish_own",
        results,
        (own,),
        scratch,
        outs=HBM,
    )
    grad_early, grad_deep = call(
        functools.partial(finish_body, False, *scales),
        "finish_other",
        [struct(value.shape, F32) for value in results],
        (other, *results),
        scratch,
        hbm=(1, 2),
        outs=HBM,
        alias=((1, 0), (2, 1)),
    )
    return (block_out, grad_early, jnp.swapaxes(grad_deep, 1, 2))


def solution(mesh):
    return jax.shard_map(
        shards,
        mesh=mesh,
        in_specs=(
            P("space", "filt", None, None),
            P(),
            P(None, None, "filt"),
            P("space", None, None, "filt"),
        ),
        out_specs=(P("space", None, None, "filt"), P(), P(None, None, "filt")),
        check_vma=False,
    )
```

```python
import functools
import math

import jax
import jax.numpy as jnp
from jax import lax
from jax.experimental import pallas as pl
from jax.experimental.pallas import tpu as pltpu
from jax.sharding import PartitionSpec as P

F32 = jnp.float32
BF16 = jnp.bfloat16
VMEM_LIMIT = 24 * 1024 * 1024
VMEM = pl.BlockSpec(memory_space=pltpu.VMEM)
HBM = pl.BlockSpec(memory_space=pltpu.HBM)
DMA = pltpu.SemaphoreType.DMA


def call(
    body, name, out_shape, operands, scratch=(), flops=0, moved=1 << 20, hbm=(), outs=VMEM, alias=()
):
    return pl.pallas_call(
        body,
        name=name,
        out_shape=out_shape,
        in_specs=[HBM if i in hbm else VMEM for i in range(len(operands))],
        out_specs=jax.tree.map(lambda _: outs, out_shape),
        scratch_shapes=list(scratch),
        input_output_aliases=dict(alias),
        compiler_params=pltpu.CompilerParams(vmem_limit_bytes=VMEM_LIMIT),
        cost_estimate=pl.CostEstimate(flops=flops, bytes_accessed=moved, transcendentals=0),
    )(*operands)


def struct(shape, dtype=BF16):
    return jax.ShapeDtypeStruct(shape, dtype)


def ceil_to(value, step):
    return -(-value // step) * step


def sigmoid(value):
    return 1.0 / (1.0 + jnp.exp(-value))


def is_even(axis):
    return lax.rem(lax.axis_index(axis), 2) == 0


def edges_body(edges, copied):
    copied[...] = edges[...]


def has_both(axis):
    here = lax.axis_index(axis)
    return (here > 0) & (here < lax.axis_size(axis) - 1)


def spread_body(center, yeven, yodd, copied, sides, near, far):
    copied[...] = center[...]
    nx, ny, _, _ = center.shape
    even = is_even("filt")
    beyond = jnp.where(has_both("filt"), yodd[...], jnp.zeros(yodd.shape, BF16))
    sides[:, 0:1] = jnp.where(even, beyond[:, 1:2], yeven[:, 1:2])
    sides[:, 1:2] = jnp.where(even, yeven[:, 0:1], beyond[:, 0:1])
    odd = lax.rem(lax.axis_index("space"), 2)
    for out, start in ((near, (1 - odd) * (nx - 3)), (far, odd * (nx - 3))):
        rows = pl.ds(start, 3)
        out[:, 0:1] = sides[rows, 0:1]
        out[:, 1 : ny + 1] = center[rows]
        out[:, ny + 1 :] = sides[rows, 1:2]


def fill_windows(field, windows):
    count, wide_y, _, cin = field.shape
    ny = wide_y - 2
    half = windows.shape[2] // ny
    for x in range(count):
        for group in range(4):
            plane = field[x, :, pl.ds(7 + group, half, stride=2), :]
            for b in range(3):
                windows[b, x, :, group * cin : (group + 1) * cin] = (
                    plane[b : b + ny].reshape(ny * half, cin).astype(BF16)
                )


def clear_ends(field, nz):
    count, wide_y, _, cin = field.shape
    field[:, :, 0:8] = jnp.zeros((count, wide_y, 8, cin), F32)
    field[:, :, 8 + nz : 16 + nz] = jnp.zeros((count, wide_y, 8, cin), F32)


def early_rows_of(windows, start, wide, ny, keep):
    rows = windows.shape[2]
    cout = wide.shape[2] // 2
    acc = jnp.zeros((2 * rows, 2 * cout), F32)
    for ab in range(9):
        a, b = ab // 3, ab % 3
        left = windows[b, pl.ds(start + a, 2)].reshape(2 * rows, windows.shape[3])
        acc = acc + jnp.dot(left, wide[ab], preferred_element_type=F32)
    sig = sigmoid(acc)
    slope = (sig * (1.0 + acc * (1.0 - sig)) * keep).reshape(2, rows, 2 * cout)
    act = acc * sig
    act = act[:rows] + act[rows:]
    act = act[:, :cout] + act[:, cout:]
    act = act.reshape(ny // 2, 2, rows // ny, cout)
    act = (act[:, 0] + act[:, 1]) * keep
    return slope, act.reshape(rows // 2, cout).astype(BF16)


def near_body(center, sides, near, w, windows, sg, pooled, wide, field):
    nx, ny, nz, cin = center.shape
    cout = w.shape[2]
    for ab in range(9):
        for group in range(4):
            for side in range(2):
                tap = group - side
                value = w[3 * ab + tap] if 0 <= tap <= 2 else jnp.zeros((cin, cout), BF16)
                wide[
                    ab, group * cin : (group + 1) * cin, side * cout : (side + 1) * cout
                ] = value
    odd = lax.rem(lax.axis_index("space"), 2)
    clear_ends(field, nz)
    cells = slice(8, 8 + nz)
    own = pl.ds(3 * odd, nx)
    field[own, 1 : ny + 1, cells] = center[...].astype(F32)
    field[own, 0:1, cells] = sides[:, 0:1].astype(F32)
    field[own, ny + 1 :, cells] = sides[:, 1:2].astype(F32)
    field[pl.ds((1 - odd) * nx, 3), :, cells] = near[...].astype(F32)
    fill_windows(field, windows)
    for chunk in range(nx // 2):
        slope, pool = early_rows_of(windows, 1 - odd + 2 * chunk, wide, ny, 0.125)
        sg[2 * chunk : 2 * chunk + 2] = slope
        pooled[chunk] = pool


def far_body(windows, far, wide, far_windows, sg, pooled, field, held):
    _, wide_y, nz, _ = far.shape
    odd = lax.rem(lax.axis_index("space"), 2)
    clear_ends(field, nz)
    inside = jnp.where(has_both("space"), 1.0, 0.0).astype(F32)
    field[:, :, 8 : 8 + nz] = far[...].astype(F32) * inside
    fill_windows(field, far_windows)
    for b in range(3):
        held[b, pl.ds(3 * odd, 3)] = far_windows[b]
        held[b, pl.ds(3 - 3 * odd, 3)] = windows[b, pl.ds(4 * odd, 3)]
    first = jnp.where(odd == 0, inside, 1.0)
    second = jnp.where(odd == 1, inside, 1.0)
    for chunk, flag in enumerate((first, second)):
        slope, pool = early_rows_of(held, 2 * chunk, wide, wide_y - 2, 0.125 * flag)
        sg[2 * chunk : 2 * chunk + 2] = slope
        pooled[chunk] = pool


def transpose_body(windows, far_windows, turned):
    rows = windows.shape[2]
    part = turned.shape[2] // 4
    odd = lax.rem(lax.axis_index("space"), 2)
    for source, first in ((windows, 3 * (1 - odd)), (far_windows, windows.shape[1] * odd)):
        for b in range(3):
            for x in range(source.shape[1]):
                value = source[b, x].T
                spot = pl.multiple_of((first + x) * rows, rows)
                for group in range(4):
                    for side in range(2):
                        row = (2 * group + side) * part
                        turned[
                            b, side, group * part : (group + 1) * part, pl.ds(spot, rows)
                        ] = value[row : row + part]


def roll_z(value, shift):
    size = value.shape[-2]
    rolled = pltpu.roll(value, shift % size, value.ndim - 2)
    spot = lax.broadcasted_iota(jnp.int32, value.shape, value.ndim - 2)
    edge = 0 if shift == 1 else size - 1
    return jnp.where(spot == edge, 0.0, rolled)


def deep_body(parts_n, *refs):
    far, near, refs = refs[:parts_n], refs[parts_n : 2 * parts_n], refs[2 * parts_n :]
    wt, cot, block_out, grad, windows = refs[:5]
    sends = refs[5 : parts_n + 5]
    field, wide, slopes, turned, terms = refs[parts_n + 5 :]
    nx, ny, nz, filters = cot.shape
    width = wt.shape[2]
    rows = ny * nz
    py = ny // parts_n
    mine = lax.axis_index("filt")
    for ab in range(9):
        for c in range(3):
            wide[ab, :, c * width : (c + 1) * width] = wt[
                ab, c * filters : (c + 1) * filters
            ]
    field[:, 0:1] = jnp.zeros((nx + 2, 1, nz, width), F32)
    field[:, ny + 1 : ny + 2] = jnp.zeros((nx + 2, 1, nz, width), F32)
    odd = lax.rem(lax.axis_index("space"), 2)
    for parts, first in ((near, 2 * (1 - odd)), (far, 2 * odd)):
        for j in range(parts_n):
            spot = lax.bitwise_xor(mine, j) * py + 1
            field[pl.ds(first, 2), pl.ds(spot, py)] = (
                parts[-j][...].astype(F32).reshape(2, py, nz, width)
            )
    for x in range(nx + 2):
        plane = field[x]
        for c in range(3):
            moved = plane if c == 1 else roll_z(plane, 1 - c)
            for b in range(3):
                windows[b, x, :, c * width : (c + 1) * width] = (
                    moved[b : b + ny].reshape(rows, width).astype(BF16)
                )
    slopes[:, 0:1] = jnp.zeros((nx, 1, nz, filters), F32)
    slopes[:, ny + 1 :] = jnp.zeros((nx, 1, nz, filters), F32)
    for x in range(nx):
        acc = jnp.zeros((rows, filters), F32)
        for ab in range(9):
            a, b = ab // 3, ab % 3
            acc = acc + lax.dot_general(
                windows[b, x + a], wide[ab], (((1,), (1,)), ((), ())), preferred_element_type=F32
            )
        sig = sigmoid(acc)
        block_out[x] = (acc * sig).reshape(ny, nz, filters).astype(BF16)
        slope = sig * (1.0 + acc * (1.0 - sig))
        value = (cot[x].astype(F32).reshape(rows, filters) * slope).astype(BF16)
        grad[x] = value
        slopes[x, 1 : ny + 1] = value.astype(F32).reshape(ny, nz, filters)
    for x in range(nx):
        plane = slopes[x]
        plane = jnp.concatenate([roll_z(plane, -1), plane, roll_z(plane, 1)], axis=2)
        for b in range(3):
            turned[b, x] = (
                plane[2 - b : 2 - b + ny].reshape(rows, 3 * filters).astype(BF16)
            )
    for r in range(nx + 2):
        total = jnp.zeros((rows, width), F32)
        for ab in range(9):
            a, b = ab // 3, ab % 3
            if 0 <= r - a < nx:
                total = total + jnp.dot(turned[b, r - a], wt[ab], preferred_element_type=F32)
        terms[r] = total.reshape(ny, nz, width)
    for j in range(parts_n):
        spot = lax.bitwise_xor(mine, j) * py
        value = terms[:, pl.ds(spot, py)]
        sends[j][...] = value.reshape(nx + 2, py * nz, width).astype(sends[j].dtype)


def deep_grad_body(windows, grad, theirs, mine, held):
    nx, rows, filters = grad.shape
    width = windows.shape[3] // 3
    turned = grad[...].reshape(nx * rows, filters).astype(F32).T.astype(BF16)
    chips, step, _ = mine.shape
    part = filters // 2
    total = 27 * part
    if chips * step > total:
        held[:, total:] = jnp.zeros((2, chips * step - total, width), F32)
    for ab in range(9):
        a, b = ab // 3, ab % 3
        value = jnp.dot(
            turned,
            windows[b, a : a + nx].reshape(nx * rows, 3 * width),
            preferred_element_type=F32,
        )
        for c in range(3):
            spot = (3 * ab + c) * part
            for side in range(2):
                held[side, spot : spot + part] = value[
                    side * part : (side + 1) * part, c * width : (c + 1) * width
                ]
    core = lax.rem(lax.axis_index("space"), 2)
    for q in range(chips):
        theirs[q] = held[1 - core, q * step : (q + 1) * step].astype(theirs.dtype)
        mine[q] = held[core, q * step : (q + 1) * step]


def early_grad_body(nz, *refs):
    parts, (sg, far_sg, turned, deep, out, grad, held, spread) = refs[:-8], refs[-8:]
    count, rows, wide = sg.shape
    total = parts[0][...]
    for part in parts[1:]:
        total = total + part[...].astype(F32)
    px, prow, _ = total.shape
    py = prow // nz
    total = jnp.concatenate([total, total], axis=2).reshape(px, py, 1, nz, wide)
    spread[...] = jnp.broadcast_to(total, (px, py, 2, nz, wide)).reshape(px, rows, wide)
    odd = lax.rem(lax.axis_index("space"), 2)
    for source, first in ((sg, count * (1 - odd)), (far_sg, count * odd)):
        for x in range(count):
            grad[first + x] = (spread[lax.div(first, 2) + x // 2] * source[x]).astype(BF16)
    early_grad_half(1 - odd, grad, turned, deep, out, held)


def early_grad_rest_body(grad, turned, deep, out, held):
    early_grad_half(lax.rem(lax.axis_index("space"), 2), grad, turned, deep, out, held)


def early_grad_half(side, grad, turned, deep, out, held):
    ext, rows, wide = grad.shape
    width = wide // 2
    part = turned.shape[2] // 4
    right = grad[...].reshape(ext * rows, wide)
    for ab in range(9):
        a, b = ab // 3, ab % 3
        value = jnp.dot(
            turned[b, side, :, a * rows : (a + ext) * rows], right, preferred_element_type=F32
        )
        for c in range(3):
            spot = (3 * ab + c) * part
            held[spot : spot + part] = (
                value[c * part : (c + 1) * part, :width]
                + value[(c + 1) * part : (c + 2) * part, width:]
            )
    step = held.shape[0] // out.shape[0]
    for q in range(out.shape[0]):
        out[q, :step] = held[q * step : (q + 1) * step].astype(out.dtype)
        out[q, step:] = deep[q].astype(out.dtype)


def core_sum_body(mine, other, *outs):
    chip = lax.div(lax.axis_index("space"), 2)
    for j, out in enumerate(outs):
        q = lax.bitwise_xor(chip, j)
        out[...] = (mine[q] + other[q].astype(F32)).astype(out.dtype)


def chip_sum_body(step, *refs):
    *others, early, deep = refs
    total = others[0][...]
    for ref in others[1:]:
        total = total + ref[...].astype(F32)
    early[...] = total[:step].astype(BF16)
    deep[...] = total[step:].astype(BF16)


def filt_sum_body(*refs):
    *parts, out = refs
    values = [part[...].astype(F32) for part in parts]
    while len(values) > 1:
        values = [low + high for low, high in zip(values[::2], values[1::2])]
    out[...] = values[0].astype(BF16)


def stack_body(*refs):
    out = refs[-1]
    chip = lax.div(lax.axis_index("space"), 2)
    for j, ref in enumerate(refs[:-1]):
        out[lax.bitwise_xor(chip, j)] = ref[...]


def spread_pieces(pieces, held, scale, taps, done):
    chips, step, _ = pieces.shape
    part = held.shape[1]
    for tap in range(27):
        row = tap * part
        while row < (tap + 1) * part:
            q, inner = row // step, row % step
            size = min(step - inner, (tap + 1) * part - row)
            spot = row - tap * part
            held[tap, spot : spot + size] = (
                pieces[q, inner : inner + size].astype(F32) * scale
            )
            row += size
        if (tap + 1) % taps == 0:
            done(tap + 1 - taps)


def finish_body(own, scale, pieces, *refs):
    out, held, sem = refs[-3:]
    core = lax.rem(lax.axis_index("space"), 2)
    side = core if own else 1 - core
    part = held.shape[1]
    copies = []

    def write(first):
        taps = pl.ds(first, 3)
        copy = pltpu.make_async_copy(
            held.at[taps], out.at[taps, pl.ds(side * part, part)], sem.at[first // 3]
        )
        copy.start()
        copies.append(copy)

    spread_pieces(pieces, held, scale, 3, write)
    for copy in copies:
        copy.wait()


def finish_deep_body(scale, mine, other, out, held):
    core = lax.rem(lax.axis_index("space"), 2)
    part = held.shape[1]
    for pieces, side in ((mine, core), (other, 1 - core)):
        spread_pieces(pieces, held, scale, 27, lambda first: None)
        out[:, pl.ds(pl.multiple_of(side * part, 8), part)] = held[...]


def paired(values, axis, step=1):
    count = lax.axis_size(axis)
    got = {
        j: lax.ppermute(values[j], axis, [(i, i ^ (step * j)) for i in range(count)])
        for j in reversed(range(1, len(values)))
    }
    return [values[0]] + [got[j] for j in range(1, len(values))]


def exchange(value, axis, step):
    return lax.ppermute(value, axis, [(i, i ^ step) for i in range(lax.axis_size(axis))])


def backward(values):
    return [values[0]] + values[:0:-1]


def swap(value, axis, first):
    count = lax.axis_size(axis)
    pairs = [(i, (i + 1) % count) for i in range(first, count, 2)]
    return lax.ppermute(value, axis, pairs + [(b, a) for a, b in pairs])


def shards(volume, w_early, w_deep, cotangent):
    nx, ny, nz, cin = volume.shape
    width = w_early.shape[2]
    filters = w_deep.shape[2]
    space = lax.axis_size("space")
    filt = lax.axis_size("filt")
    chips = space // 2
    half = nz // 2
    ext = nx + 6
    rows = ny * half
    edges = jnp.concatenate([volume[:, :1], volume[:, ny - 1 :]], axis=1)
    edges = call(edges_body, "edges", struct(edges.shape), (edges,), flops=1 << 32)
    yeven, yodd = swap(edges, "filt", 0), swap(edges, "filt", 1)
    rim = struct((3, ny + 2, nz, cin))
    volume, sides, near, far = call(
        spread_body,
        "spread",
        [struct(volume.shape), struct((nx, 2, nz, cin)), rim, rim],
        (volume, yeven, yodd),
        flops=1 << 32,
        moved=1 << 24,
    )
    far = swap(far, "space", 1)
    near = swap(near, "space", 0)
    windows, sg, near_pooled, wide = call(
        near_body,
        "early_near",
        (
            struct((3, nx + 3, rows, 4 * cin)),
            struct((nx, rows, 2 * width), F32),
            struct((nx // 2, rows // 2, width)),
            struct((9, 4 * cin, 2 * width)),
        ),
        (volume, sides, near, w_early),
        [pltpu.VMEM((nx + 3, ny + 2, nz + 16, cin), F32)],
        flops=2 * nx * rows * 36 * cin * 2 * width,
    )
    near_parts = paired([near_pooled] * filt, "filt")
    far_windows, far_sg, pooled = call(
        far_body,
        "early_far",
        (
            struct((3, 3, rows, 4 * cin)),
            struct((nx, rows, 2 * width), F32),
            struct((nx // 2, rows // 2, width)),
        ),
        (windows, far, wide),
        [
            pltpu.VMEM((3, ny + 2, nz + 16, cin), F32),
            pltpu.VMEM((3, 6, rows, 4 * cin), BF16),
        ],
        flops=2 * nx * rows * 36 * cin * 2 * width,
    )
    parts = backward(paired([pooled] * filt, "filt"))
    near_parts = backward(near_parts)
    windows, *near_parts = lax.optimization_barrier((windows, *near_parts))
    turned = call(
        transpose_body,
        "turn_windows",
        struct((3, 2, 2 * cin, ext * rows)),
        (windows, far_windows),
        flops=1 << 30,
    )
    *parts, turned = lax.optimization_barrier((*parts, turned))
    dx, dy, dz, _ = cotangent.shape
    px = dx + 2
    prow = rows // 2
    deep = call(
        functools.partial(deep_body, filt),
        "deep_conv",
        [
            struct(cotangent.shape),
            struct((dx, dy * dz, filters)),
            struct((3, px, dy * dz, 3 * width)),
            struct((px, prow, width), F32),
        ]
        + [struct((px, prow, width))] * (filt - 1),
        (*parts, *near_parts, jnp.swapaxes(w_deep, 1, 2).reshape(9, 3 * filters, width), cotangent),
        [
            pltpu.VMEM((px, dy + 2, dz, width), F32),
            pltpu.VMEM((9, filters, 3 * width), BF16),
            pltpu.VMEM((dx, dy + 2, dz, filters), F32),
            pltpu.VMEM((3, dx, dy * dz, 3 * filters), BF16),
            pltpu.VMEM((px, dy, dz, width), F32),
        ],
        flops=4 * dx * dy * dz * 27 * width * filters,
    )
    block_out, grad, deep_windows = deep[:3]
    terms = paired(deep[3:], "filt")

    early_rows = 27 * cin // space
    deep_rows = ceil_to(-(-27 * filters // space), 16)
    deep_first, deep_second = call(
        deep_grad_body,
        "deep_grad",
        [struct((chips, deep_rows, width)), struct((chips, deep_rows, width), F32)],
        (deep_windows, grad),
        [pltpu.VMEM((2, chips * deep_rows, width), F32)],
        flops=2 * dx * dy * dz * 27 * width * filters,
    )
    piece = (chips, early_rows + deep_rows, width)
    held = pltpu.VMEM((27 * cin // 2, width), F32)
    flops = (nx + 4) * rows * 36 * cin * 2 * width
    theirs, grad = call(
        functools.partial(early_grad_body, half),
        "early_grad",
        [struct(piece), struct((nx + 4, rows, 2 * width))],
        (*backward(terms), sg, far_sg, turned, deep_first),
        [held, pltpu.VMEM((px, rows, 2 * width), F32)],
        flops=flops,
    )
    theirs = lax.ppermute(theirs, "space", [(i, i ^ 1) for i in range(space)])
    mine = call(
        early_grad_rest_body,
        "early_grad_rest",
        struct(piece, F32),
        (grad, turned, deep_second),
        [held],
        flops=flops,
    )
    sums = call(
        core_sum_body,
        "core_sum",
        [struct(piece[1:], F32)] + [struct(piece[1:])] * (chips - 1),
        (mine, theirs),
    )
    sums = backward(paired(sums, "space", 2))
    early, deep = call(
        functools.partial(chip_sum_body, early_rows),
        "chip_sum",
        [struct((early_rows, width)), struct((deep_rows, width))],
        sums,
    )
    shares = paired([early] * filt, "filt")
    deeps = paired([deep] * chips, "space", 2)
    *shares, deeps[1:] = lax.optimization_barrier((*shares, deeps[1:]))
    share = call(filt_sum_body, "filt_sum", struct((early_rows, width)), shares)
    finals = paired([share] * chips, "space", 2)
    deep_pieces = call(stack_body, "stack_deep", struct((chips, deep_rows, width)), deeps)
    deep_total = dx * dy * dz * space
    grad_deep = call(
        functools.partial(finish_deep_body, 1.0 / math.sqrt(deep_total)),
        "finish_deep",
        struct((27, filters, width), F32),
        (deep_pieces, exchange(deep_pieces, "space", 1)),
        [pltpu.VMEM((27, filters // 2, width), F32)],
        flops=1 << 30,
    )
    finals[0], grad_deep = lax.optimization_barrier((finals[0], grad_deep))
    own = call(stack_body, "stack", struct((chips, early_rows, width)), finals)
    other = exchange(own, "space", 1)
    early_total = nx * ny * nz * space * filt
    scale = 1.0 / math.sqrt(early_total)
    result = struct((27, cin, width), F32)
    scratch = [pltpu.VMEM((27, cin // 2, width), F32), DMA((9,))]
    grad_early = call(
        functools.partial(finish_body, True, scale),
        "finish_own",
        result,
        (own,),
        scratch,
        outs=HBM,
    )
    grad_early = call(
        functools.partial(finish_body, False, scale),
        "finish_other",
        result,
        (other, grad_early),
        scratch,
        hbm=(1,),
        outs=HBM,
        alias=((1, 0),),
    )
    return (block_out, grad_early, jnp.swapaxes(grad_deep, 1, 2))


def solution(mesh):
    return jax.shard_map(
        shards,
        mesh=mesh,
        in_specs=(
            P("space", "filt", None, None),
            P(),
            P(None, None, "filt"),
            P("space", None, None, "filt"),
        ),
        out_specs=(P("space", None, None, "filt"), P(), P(None, None, "filt")),
        check_vma=False,
    )
```

```python
import functools
import math

import jax
import jax.numpy as jnp
from jax import lax
from jax.experimental import pallas as pl
from jax.experimental.pallas import tpu as pltpu
from jax.sharding import PartitionSpec as P

F32 = jnp.float32
BF16 = jnp.bfloat16
HOLD = 1 << 32
VMEM_LIMIT = 24 * 1024 * 1024
VMEM = pl.BlockSpec(memory_space=pltpu.VMEM)
HBM = pl.BlockSpec(memory_space=pltpu.HBM)
DMA = pltpu.SemaphoreType.DMA


def call(
    body, name, out_shape, operands, scratch=(), flops=0, moved=1 << 20, hbm=(), outs=VMEM, alias=()
):
    return pl.pallas_call(
        body,
        name=name,
        out_shape=out_shape,
        in_specs=[HBM if i in hbm else VMEM for i in range(len(operands))],
        out_specs=jax.tree.map(lambda _: outs, out_shape),
        scratch_shapes=list(scratch),
        input_output_aliases=dict(alias),
        compiler_params=pltpu.CompilerParams(vmem_limit_bytes=VMEM_LIMIT),
        cost_estimate=pl.CostEstimate(flops=flops, bytes_accessed=moved, transcendentals=0),
    )(*operands)


def struct(shape, dtype=BF16):
    return jax.ShapeDtypeStruct(shape, dtype)


def ceil_to(value, step):
    return -(-value // step) * step


def sigmoid(value):
    return 1.0 / (1.0 + jnp.exp(-value))


def is_even(axis):
    return lax.rem(lax.axis_index(axis), 2) == 0


def edges_body(edges, copied):
    copied[...] = edges[...]


def has_both(axis):
    here = lax.axis_index(axis)
    return (here > 0) & (here < lax.axis_size(axis) - 1)


def spread_body(center, yeven, yodd, copied, sides, near, far):
    copied[...] = center[...]
    nx, ny, _, _ = center.shape
    even = is_even("filt")
    beyond = jnp.where(has_both("filt"), yodd[...], jnp.zeros(yodd.shape, BF16))
    sides[:, 0:1] = jnp.where(even, beyond[:, 1:2], yeven[:, 1:2])
    sides[:, 1:2] = jnp.where(even, yeven[:, 0:1], beyond[:, 0:1])
    odd = lax.rem(lax.axis_index("space"), 2)
    for out, start in ((near, (1 - odd) * (nx - 3)), (far, odd * (nx - 3))):
        rows = pl.ds(start, 3)
        out[:, 0:1] = sides[rows, 0:1]
        out[:, 1 : ny + 1] = center[rows]
        out[:, ny + 1 :] = sides[rows, 1:2]


def fill_windows(field, windows):
    count, wide_y, _, cin = field.shape
    ny = wide_y - 2
    half = windows.shape[2] // ny
    for x in range(count):
        for group in range(4):
            plane = field[x, :, pl.ds(7 + group, half, stride=2), :]
            for b in range(3):
                windows[b, x, :, group * cin : (group + 1) * cin] = (
                    plane[b : b + ny].reshape(ny * half, cin).astype(BF16)
                )


def clear_ends(field, nz):
    count, wide_y, _, cin = field.shape
    field[:, :, 0:8] = jnp.zeros((count, wide_y, 8, cin), F32)
    field[:, :, 8 + nz : 16 + nz] = jnp.zeros((count, wide_y, 8, cin), F32)


def early_rows_of(windows, start, wide, ny, keep):
    rows = windows.shape[2]
    cout = wide.shape[2] // 2
    acc = jnp.zeros((2 * rows, 2 * cout), F32)
    for ab in range(9):
        a, b = ab // 3, ab % 3
        left = windows[b, pl.ds(start + a, 2)].reshape(2 * rows, windows.shape[3])
        acc = acc + jnp.dot(left, wide[ab], preferred_element_type=F32)
    sig = sigmoid(acc)
    slope = (sig * (1.0 + acc * (1.0 - sig)) * keep).reshape(2, rows, 2 * cout)
    act = acc * sig
    act = act[:rows] + act[rows:]
    act = act[:, :cout] + act[:, cout:]
    act = act.reshape(ny // 2, 2, rows // ny, cout)
    act = (act[:, 0] + act[:, 1]) * keep
    return slope, act.reshape(rows // 2, cout).astype(BF16)


def near_body(center, sides, near, w, windows, sg, pooled, wide, field):
    nx, ny, nz, cin = center.shape
    cout = w.shape[2]
    for ab in range(9):
        for group in range(4):
            for side in range(2):
                tap = group - side
                value = w[3 * ab + tap] if 0 <= tap <= 2 else jnp.zeros((cin, cout), BF16)
                wide[
                    ab, group * cin : (group + 1) * cin, side * cout : (side + 1) * cout
                ] = value
    odd = lax.rem(lax.axis_index("space"), 2)
    clear_ends(field, nz)
    cells = slice(8, 8 + nz)
    own = pl.ds(3 * odd, nx)
    field[own, 1 : ny + 1, cells] = center[...].astype(F32)
    field[own, 0:1, cells] = sides[:, 0:1].astype(F32)
    field[own, ny + 1 :, cells] = sides[:, 1:2].astype(F32)
    field[pl.ds((1 - odd) * nx, 3), :, cells] = near[...].astype(F32)
    fill_windows(field, windows)
    for chunk in range(nx // 2):
        slope, pool = early_rows_of(windows, 1 - odd + 2 * chunk, wide, ny, 0.125)
        sg[2 * chunk : 2 * chunk + 2] = slope
        pooled[chunk] = pool


def far_body(windows, far, wide, far_windows, sg, pooled, field, held):
    _, wide_y, nz, _ = far.shape
    odd = lax.rem(lax.axis_index("space"), 2)
    clear_ends(field, nz)
    inside = jnp.where(has_both("space"), 1.0, 0.0).astype(F32)
    field[:, :, 8 : 8 + nz] = far[...].astype(F32) * inside
    fill_windows(field, far_windows)
    for b in range(3):
        held[b, pl.ds(3 * odd, 3)] = far_windows[b]
        held[b, pl.ds(3 - 3 * odd, 3)] = windows[b, pl.ds(4 * odd, 3)]
    first = jnp.where(odd == 0, inside, 1.0)
    second = jnp.where(odd == 1, inside, 1.0)
    for chunk, flag in enumerate((first, second)):
        slope, pool = early_rows_of(held, 2 * chunk, wide, wide_y - 2, 0.125 * flag)
        sg[2 * chunk : 2 * chunk + 2] = slope
        pooled[chunk] = pool


def transpose_body(windows, far_windows, turned):
    rows = windows.shape[2]
    part = turned.shape[2] // 4
    odd = lax.rem(lax.axis_index("space"), 2)
    for source, first in ((windows, 3 * (1 - odd)), (far_windows, windows.shape[1] * odd)):
        for b in range(3):
            for x in range(source.shape[1]):
                value = source[b, x].T
                spot = pl.multiple_of((first + x) * rows, rows)
                for group in range(4):
                    for side in range(2):
                        row = (2 * group + side) * part
                        turned[
                            b, side, group * part : (group + 1) * part, pl.ds(spot, rows)
                        ] = value[row : row + part]


def roll_z(value, shift):
    size = value.shape[-2]
    rolled = pltpu.roll(value, shift % size, value.ndim - 2)
    spot = lax.broadcasted_iota(jnp.int32, value.shape, value.ndim - 2)
    edge = 0 if shift == 1 else size - 1
    return jnp.where(spot == edge, 0.0, rolled)


def deep_body(parts_n, *refs):
    far, near, refs = refs[:parts_n], refs[parts_n : 2 * parts_n], refs[2 * parts_n :]
    wt, cot, block_out, grad, windows = refs[:5]
    sends = refs[5 : parts_n + 5]
    field, wide, slopes, turned, terms = refs[parts_n + 5 :]
    nx, ny, nz, filters = cot.shape
    width = wt.shape[2]
    rows = ny * nz
    py = ny // parts_n
    mine = lax.axis_index("filt")
    for ab in range(9):
        for c in range(3):
            wide[ab, :, c * width : (c + 1) * width] = wt[
                ab, c * filters : (c + 1) * filters
            ]
    field[:, 0:1] = jnp.zeros((nx + 2, 1, nz, width), F32)
    field[:, ny + 1 : ny + 2] = jnp.zeros((nx + 2, 1, nz, width), F32)
    odd = lax.rem(lax.axis_index("space"), 2)
    for parts, first in ((near, 2 * (1 - odd)), (far, 2 * odd)):
        for j in range(parts_n):
            spot = lax.bitwise_xor(mine, j) * py + 1
            field[pl.ds(first, 2), pl.ds(spot, py)] = (
                parts[-j][...].astype(F32).reshape(2, py, nz, width)
            )
    for x in range(nx + 2):
        plane = field[x]
        for c in range(3):
            moved = plane if c == 1 else roll_z(plane, 1 - c)
            for b in range(3):
                windows[b, x, :, c * width : (c + 1) * width] = (
                    moved[b : b + ny].reshape(rows, width).astype(BF16)
                )
    slopes[:, 0:1] = jnp.zeros((nx, 1, nz, filters), F32)
    slopes[:, ny + 1 :] = jnp.zeros((nx, 1, nz, filters), F32)
    for x in range(nx):
        acc = jnp.zeros((rows, filters), F32)
        for ab in range(9):
            a, b = ab // 3, ab % 3
            acc = acc + lax.dot_general(
                windows[b, x + a], wide[ab], (((1,), (1,)), ((), ())), preferred_element_type=F32
            )
        sig = sigmoid(acc)
        block_out[x] = (acc * sig).reshape(ny, nz, filters).astype(BF16)
        slope = sig * (1.0 + acc * (1.0 - sig))
        value = (cot[x].astype(F32).reshape(rows, filters) * slope).astype(BF16)
        grad[x] = value
        slopes[x, 1 : ny + 1] = value.astype(F32).reshape(ny, nz, filters)
    for x in range(nx):
        plane = slopes[x]
        plane = jnp.concatenate([roll_z(plane, -1), plane, roll_z(plane, 1)], axis=2)
        for b in range(3):
            turned[b, x] = (
                plane[2 - b : 2 - b + ny].reshape(rows, 3 * filters).astype(BF16)
            )
    for r in range(nx + 2):
        total = jnp.zeros((rows, width), F32)
        for ab in range(9):
            a, b = ab // 3, ab % 3
            if 0 <= r - a < nx:
                total = total + jnp.dot(turned[b, r - a], wt[ab], preferred_element_type=F32)
        terms[r] = total.reshape(ny, nz, width)
    for j in range(parts_n):
        spot = lax.bitwise_xor(mine, j) * py
        value = terms[:, pl.ds(spot, py)]
        sends[j][...] = value.reshape(nx + 2, py * nz, width).astype(sends[j].dtype)


def deep_grad_body(windows, grad, theirs, mine, held):
    nx, rows, filters = grad.shape
    width = windows.shape[3] // 3
    turned = grad[...].reshape(nx * rows, filters).astype(F32).T.astype(BF16)
    chips, step, _ = mine.shape
    part = filters // 2
    total = 27 * part
    if chips * step > total:
        held[:, total:] = jnp.zeros((2, chips * step - total, width), F32)
    for ab in range(9):
        a, b = ab // 3, ab % 3
        value = jnp.dot(
            turned,
            windows[b, a : a + nx].reshape(nx * rows, 3 * width),
            preferred_element_type=F32,
        )
        for c in range(3):
            spot = (3 * ab + c) * part
            for side in range(2):
                held[side, spot : spot + part] = value[
                    side * part : (side + 1) * part, c * width : (c + 1) * width
                ]
    core = lax.rem(lax.axis_index("space"), 2)
    for q in range(chips):
        theirs[q] = held[1 - core, q * step : (q + 1) * step].astype(theirs.dtype)
        mine[q] = held[core, q * step : (q + 1) * step]


def early_grad_body(nz, *refs):
    parts, (sg, far_sg, turned, deep, out, grad, held, spread) = refs[:-8], refs[-8:]
    count, rows, wide = sg.shape
    total = parts[0][...]
    for part in parts[1:]:
        total = total + part[...].astype(F32)
    px, prow, _ = total.shape
    py = prow // nz
    total = jnp.concatenate([total, total], axis=2).reshape(px, py, 1, nz, wide)
    spread[...] = jnp.broadcast_to(total, (px, py, 2, nz, wide)).reshape(px, rows, wide)
    odd = lax.rem(lax.axis_index("space"), 2)
    for source, first in ((sg, count * (1 - odd)), (far_sg, count * odd)):
        for x in range(count):
            grad[first + x] = (spread[lax.div(first, 2) + x // 2] * source[x]).astype(BF16)
    early_grad_half(1 - odd, grad, turned, deep, out, held)


def early_grad_rest_body(grad, turned, deep, out, held):
    early_grad_half(lax.rem(lax.axis_index("space"), 2), grad, turned, deep, out, held)


def early_grad_half(side, grad, turned, deep, out, held):
    ext, rows, wide = grad.shape
    width = wide // 2
    part = turned.shape[2] // 4
    right = grad[...].reshape(ext * rows, wide)
    for ab in range(9):
        a, b = ab // 3, ab % 3
        value = jnp.dot(
            turned[b, side, :, a * rows : (a + ext) * rows], right, preferred_element_type=F32
        )
        for c in range(3):
            spot = (3 * ab + c) * part
            held[spot : spot + part] = (
                value[c * part : (c + 1) * part, :width]
                + value[(c + 1) * part : (c + 2) * part, width:]
            )
    step = held.shape[0] // out.shape[0]
    for q in range(out.shape[0]):
        out[q, :step] = held[q * step : (q + 1) * step].astype(out.dtype)
        out[q, step:] = deep[q].astype(out.dtype)


def core_sum_body(first, mine, other, *outs):
    chip = lax.div(lax.axis_index("space"), 2)
    rows = slice(first, first + outs[0].shape[0])
    for j, out in enumerate(outs):
        q = lax.bitwise_xor(chip, j)
        out[...] = (mine[q, rows] + other[q, rows].astype(F32)).astype(out.dtype)


def chip_sum_body(count, *refs):
    others, outs = refs[:count], refs[count:]
    total = others[0][...]
    for ref in others[1:]:
        total = total + ref[...].astype(F32)
    row = 0
    for out in outs:
        size = out.shape[0]
        out[...] = total[row : row + size].astype(BF16)
        row += size


def filt_sum_body(*refs):
    *parts, out = refs
    values = [part[...].astype(F32) for part in parts]
    while len(values) > 1:
        values = [low + high for low, high in zip(values[::2], values[1::2])]
    out[...] = values[0].astype(BF16)


def stack_body(*refs):
    *parts, out = refs
    chips = out.shape[0]
    chip = lax.div(lax.axis_index("space"), 2)
    for j in range(chips):
        row = 0
        for ref in parts[j::chips]:
            size = ref.shape[0]
            out[lax.bitwise_xor(chip, j), row : row + size] = ref[...]
            row += size


def spread_pieces(pieces, held, scale, taps, done):
    chips, step, _ = pieces.shape
    part = held.shape[1]
    for tap in range(27):
        row = tap * part
        while row < (tap + 1) * part:
            q, inner = row // step, row % step
            size = min(step - inner, (tap + 1) * part - row)
            spot = row - tap * part
            held[tap, spot : spot + size] = (
                pieces[q, inner : inner + size].astype(F32) * scale
            )
            row += size
        if (tap + 1) % taps == 0:
            done(tap + 1 - taps)


def finish_body(own, scale, pieces, *refs):
    out, held, sem = refs[-3:]
    core = lax.rem(lax.axis_index("space"), 2)
    side = core if own else 1 - core
    part = held.shape[1]
    copies = []

    def write(first):
        taps = pl.ds(first, 3)
        copy = pltpu.make_async_copy(
            held.at[taps], out.at[taps, pl.ds(side * part, part)], sem.at[first // 3]
        )
        copy.start()
        copies.append(copy)

    spread_pieces(pieces, held, scale, 3, write)
    for copy in copies:
        copy.wait()


def finish_deep_body(scale, mine, other, out, held):
    core = lax.rem(lax.axis_index("space"), 2)
    part = held.shape[1]
    for pieces, side in ((mine, core), (other, 1 - core)):
        spread_pieces(pieces, held, scale, 27, lambda first: None)
        out[:, pl.ds(pl.multiple_of(side * part, 8), part)] = held[...]


def paired(values, axis, step=1):
    count = lax.axis_size(axis)
    got = {
        j: lax.ppermute(values[j], axis, [(i, i ^ (step * j)) for i in range(count)])
        for j in reversed(range(1, len(values)))
    }
    return [values[0]] + [got[j] for j in range(1, len(values))]


def exchange(value, axis, step):
    return lax.ppermute(value, axis, [(i, i ^ step) for i in range(lax.axis_size(axis))])


def backward(values):
    return [values[0]] + values[:0:-1]


def swap(value, axis, first):
    count = lax.axis_size(axis)
    pairs = [(i, (i + 1) % count) for i in range(first, count, 2)]
    return lax.ppermute(value, axis, pairs + [(b, a) for a, b in pairs])


def shards(volume, w_early, w_deep, cotangent):
    nx, ny, nz, cin = volume.shape
    width = w_early.shape[2]
    filters = w_deep.shape[2]
    space = lax.axis_size("space")
    filt = lax.axis_size("filt")
    chips = space // 2
    half = nz // 2
    ext = nx + 6
    rows = ny * half
    edges = jnp.concatenate([volume[:, :1], volume[:, ny - 1 :]], axis=1)
    edges = call(edges_body, "edges", struct(edges.shape), (edges,), flops=1 << 32)
    yeven, yodd = swap(edges, "filt", 0), swap(edges, "filt", 1)
    rim = struct((3, ny + 2, nz, cin))
    volume, sides, near, far = call(
        spread_body,
        "spread",
        [struct(volume.shape), struct((nx, 2, nz, cin)), rim, rim],
        (volume, yeven, yodd),
        flops=HOLD,
        moved=1 << 24,
    )
    far = swap(far, "space", 1)
    near = swap(near, "space", 0)
    windows, sg, near_pooled, wide = call(
        near_body,
        "early_near",
        (
            struct((3, nx + 3, rows, 4 * cin)),
            struct((nx, rows, 2 * width), F32),
            struct((nx // 2, rows // 2, width)),
            struct((9, 4 * cin, 2 * width)),
        ),
        (volume, sides, near, w_early),
        [pltpu.VMEM((nx + 3, ny + 2, nz + 16, cin), F32)],
        flops=2 * nx * rows * 36 * cin * 2 * width,
    )
    near_parts = paired([near_pooled] * filt, "filt")
    far_windows, far_sg, pooled = call(
        far_body,
        "early_far",
        (
            struct((3, 3, rows, 4 * cin)),
            struct((nx, rows, 2 * width), F32),
            struct((nx // 2, rows // 2, width)),
        ),
        (windows, far, wide),
        [
            pltpu.VMEM((3, ny + 2, nz + 16, cin), F32),
            pltpu.VMEM((3, 6, rows, 4 * cin), BF16),
        ],
        flops=2 * nx * rows * 36 * cin * 2 * width,
    )
    parts = backward(paired([pooled] * filt, "filt"))
    near_parts = backward(near_parts)
    windows, *near_parts = lax.optimization_barrier((windows, *near_parts))
    turned = call(
        transpose_body,
        "turn_windows",
        struct((3, 2, 2 * cin, ext * rows)),
        (windows, far_windows),
        flops=1 << 30,
    )
    *parts, turned = lax.optimization_barrier((*parts, turned))
    dx, dy, dz, _ = cotangent.shape
    px = dx + 2
    prow = rows // 2
    deep = call(
        functools.partial(deep_body, filt),
        "deep_conv",
        [
            struct(cotangent.shape),
            struct((dx, dy * dz, filters)),
            struct((3, px, dy * dz, 3 * width)),
            struct((px, prow, width), F32),
        ]
        + [struct((px, prow, width))] * (filt - 1),
        (*parts, *near_parts, jnp.swapaxes(w_deep, 1, 2).reshape(9, 3 * filters, width), cotangent),
        [
            pltpu.VMEM((px, dy + 2, dz, width), F32),
            pltpu.VMEM((9, filters, 3 * width), BF16),
            pltpu.VMEM((dx, dy + 2, dz, filters), F32),
            pltpu.VMEM((3, dx, dy * dz, 3 * filters), BF16),
            pltpu.VMEM((px, dy, dz, width), F32),
        ],
        flops=4 * dx * dy * dz * 27 * width * filters,
    )
    block_out, grad, deep_windows = deep[:3]
    terms = paired(deep[3:], "filt")

    early_rows = 27 * cin // space
    deep_rows = ceil_to(-(-27 * filters // space), 16)
    deep_first, deep_second = call(
        deep_grad_body,
        "deep_grad",
        [struct((chips, deep_rows, width)), struct((chips, deep_rows, width), F32)],
        (deep_windows, grad),
        [pltpu.VMEM((2, chips * deep_rows, width), F32)],
        flops=2 * dx * dy * dz * 27 * width * filters,
    )
    piece = (chips, early_rows + deep_rows, width)
    held = pltpu.VMEM((27 * cin // 2, width), F32)
    flops = (nx + 4) * rows * 36 * cin * 2 * width
    theirs, grad = call(
        functools.partial(early_grad_body, half),
        "early_grad",
        [struct(piece), struct((nx + 4, rows, 2 * width))],
        (*backward(terms), sg, far_sg, turned, deep_first),
        [held, pltpu.VMEM((px, rows, 2 * width), F32)],
        flops=flops,
    )
    theirs = lax.ppermute(theirs, "space", [(i, i ^ 1) for i in range(space)])
    mine = call(
        early_grad_rest_body,
        "early_grad_rest",
        struct(piece, F32),
        (grad, turned, deep_second),
        [held],
        flops=flops,
    )
    cut = ceil_to(early_rows // 2, 16)
    sums = [
        call(
            functools.partial(core_sum_body, start),
            name,
            [struct((size, width), F32 if j == 0 else BF16) for j in range(chips)],
            (mine, theirs),
            flops=flops,
        )
        for name, start, size, flops in (
            ("core_sum", 0, cut, 0),
            ("core_sum_rest", cut, early_rows - cut + deep_rows, HOLD),
        )
    ]
    first = backward(paired(sums[0], "space", 2))
    second = backward(paired(sums[1], "space", 2))
    (early,) = call(
        functools.partial(chip_sum_body, chips), "chip_sum", [struct((cut, width))], first
    )
    first = paired([early] * filt, "filt")
    *second, first[0] = lax.optimization_barrier((*second, first[0]))
    early, deep = call(
        functools.partial(chip_sum_body, chips),
        "chip_sum_rest",
        [struct((early_rows - cut, width)), struct((deep_rows, width))],
        second,
        flops=HOLD,
    )
    second = paired([early] * filt, "filt")
    deeps = paired([deep] * chips, "space", 2)
    *first, second[0] = lax.optimization_barrier((*first, second[0]))
    first = call(filt_sum_body, "filt_sum", struct((cut, width)), first, flops=HOLD)
    first = paired([first] * chips, "space", 2)
    *second, first[0] = lax.optimization_barrier((*second, first[0]))
    second = call(
        filt_sum_body,
        "filt_sum_rest",
        struct((early_rows - cut, width)),
        second,
        flops=HOLD,
    )
    second = paired([second] * chips, "space", 2)
    finals = [*first, *second]
    deep_pieces = call(stack_body, "stack_deep", struct((chips, deep_rows, width)), deeps)
    deep_total = dx * dy * dz * space
    grad_deep = call(
        functools.partial(finish_deep_body, 1.0 / math.sqrt(deep_total)),
        "finish_deep",
        struct((27, filters, width), F32),
        (deep_pieces, exchange(deep_pieces, "space", 1)),
        [pltpu.VMEM((27, filters // 2, width), F32)],
        flops=1 << 30,
    )
    finals[0], grad_deep = lax.optimization_barrier((finals[0], grad_deep))
    own = call(stack_body, "stack", struct((chips, early_rows, width)), finals)
    other = exchange(own, "space", 1)
    early_total = nx * ny * nz * space * filt
    scale = 1.0 / math.sqrt(early_total)
    result = struct((27, cin, width), F32)
    scratch = [pltpu.VMEM((27, cin // 2, width), F32), DMA((9,))]
    grad_early = call(
        functools.partial(finish_body, True, scale),
        "finish_own",
        result,
        (own,),
        scratch,
        outs=HBM,
    )
    grad_early = call(
        functools.partial(finish_body, False, scale),
        "finish_other",
        result,
        (other, grad_early),
        scratch,
        hbm=(1,),
        outs=HBM,
        alias=((1, 0),),
    )
    return (block_out, grad_early, jnp.swapaxes(grad_deep, 1, 2))


def solution(mesh):
    return jax.shard_map(
        shards,
        mesh=mesh,
        in_specs=(
            P("space", "filt", None, None),
            P(),
            P(None, None, "filt"),
            P("space", None, None, "filt"),
        ),
        out_specs=(P("space", None, None, "filt"), P(), P(None, None, "filt")),
        check_vma=False,
    )
```

```python
import functools
import math

import jax
import jax.numpy as jnp
from jax import lax
from jax.experimental import pallas as pl
from jax.experimental.pallas import tpu as pltpu
from jax.sharding import PartitionSpec as P

F32 = jnp.float32
BF16 = jnp.bfloat16
HOLD = 1 << 32
VMEM_LIMIT = 24 * 1024 * 1024
VMEM = pl.BlockSpec(memory_space=pltpu.VMEM)
HBM = pl.BlockSpec(memory_space=pltpu.HBM)
DMA = pltpu.SemaphoreType.DMA


def call(
    body, name, out_shape, operands, scratch=(), flops=0, moved=1 << 20, hbm=(), outs=VMEM, alias=()
):
    return pl.pallas_call(
        body,
        name=name,
        out_shape=out_shape,
        in_specs=[HBM if i in hbm else VMEM for i in range(len(operands))],
        out_specs=outs if isinstance(outs, list) else jax.tree.map(lambda _: outs, out_shape),
        scratch_shapes=list(scratch),
        input_output_aliases=dict(alias),
        compiler_params=pltpu.CompilerParams(vmem_limit_bytes=VMEM_LIMIT),
        cost_estimate=pl.CostEstimate(flops=flops, bytes_accessed=moved, transcendentals=0),
    )(*operands)


def struct(shape, dtype=BF16):
    return jax.ShapeDtypeStruct(shape, dtype)


def ceil_to(value, step):
    return -(-value // step) * step


def sigmoid(value):
    return 1.0 / (1.0 + jnp.exp(-value))


def is_even(axis):
    return lax.rem(lax.axis_index(axis), 2) == 0


def edges_body(edges, copied):
    copied[...] = edges[...]


def has_both(axis):
    here = lax.axis_index(axis)
    return (here > 0) & (here < lax.axis_size(axis) - 1)


def spread_body(center, yeven, yodd, copied, sides, near, far):
    copied[...] = center[...]
    nx, ny, _, _ = center.shape
    even = is_even("filt")
    beyond = jnp.where(has_both("filt"), yodd[...], jnp.zeros(yodd.shape, BF16))
    sides[:, 0:1] = jnp.where(even, beyond[:, 1:2], yeven[:, 1:2])
    sides[:, 1:2] = jnp.where(even, yeven[:, 0:1], beyond[:, 0:1])
    odd = lax.rem(lax.axis_index("space"), 2)
    for out, start in ((near, (1 - odd) * (nx - 3)), (far, odd * (nx - 3))):
        rows = pl.ds(start, 3)
        out[:, 0:1] = sides[rows, 0:1]
        out[:, 1 : ny + 1] = center[rows]
        out[:, ny + 1 :] = sides[rows, 1:2]


def fill_windows(field, windows):
    count, wide_y, _, cin = field.shape
    ny = wide_y - 2
    half = windows.shape[2] // ny
    for x in range(count):
        for group in range(4):
            plane = field[x, :, pl.ds(7 + group, half, stride=2), :]
            for b in range(3):
                windows[b, x, :, group * cin : (group + 1) * cin] = (
                    plane[b : b + ny].reshape(ny * half, cin).astype(BF16)
                )


def clear_ends(field, nz):
    count, wide_y, _, cin = field.shape
    field[:, :, 0:8] = jnp.zeros((count, wide_y, 8, cin), F32)
    field[:, :, 8 + nz : 16 + nz] = jnp.zeros((count, wide_y, 8, cin), F32)


def early_rows_of(windows, start, wide, ny, keep):
    rows = windows.shape[2]
    cout = wide.shape[2] // 2
    acc = jnp.zeros((2 * rows, 2 * cout), F32)
    for ab in range(9):
        a, b = ab // 3, ab % 3
        left = windows[b, pl.ds(start + a, 2)].reshape(2 * rows, windows.shape[3])
        acc = acc + jnp.dot(left, wide[ab], preferred_element_type=F32)
    sig = sigmoid(acc)
    slope = (sig * (1.0 + acc * (1.0 - sig)) * keep).reshape(2, rows, 2 * cout)
    act = acc * sig
    act = act[:rows] + act[rows:]
    act = act[:, :cout] + act[:, cout:]
    act = act.reshape(ny // 2, 2, rows // ny, cout)
    act = (act[:, 0] + act[:, 1]) * keep
    return slope, act.reshape(rows // 2, cout).astype(BF16)


def near_body(center, sides, near, w, windows, sg, pooled, wide, field):
    nx, ny, nz, cin = center.shape
    cout = w.shape[2]
    for ab in range(9):
        for group in range(4):
            for side in range(2):
                tap = group - side
                value = w[3 * ab + tap] if 0 <= tap <= 2 else jnp.zeros((cin, cout), BF16)
                wide[
                    ab, group * cin : (group + 1) * cin, side * cout : (side + 1) * cout
                ] = value
    odd = lax.rem(lax.axis_index("space"), 2)
    clear_ends(field, nz)
    cells = slice(8, 8 + nz)
    own = pl.ds(3 * odd, nx)
    field[own, 1 : ny + 1, cells] = center[...].astype(F32)
    field[own, 0:1, cells] = sides[:, 0:1].astype(F32)
    field[own, ny + 1 :, cells] = sides[:, 1:2].astype(F32)
    field[pl.ds((1 - odd) * nx, 3), :, cells] = near[...].astype(F32)
    fill_windows(field, windows)
    for chunk in range(nx // 2):
        slope, pool = early_rows_of(windows, 1 - odd + 2 * chunk, wide, ny, 0.125)
        sg[2 * chunk : 2 * chunk + 2] = slope
        pooled[chunk] = pool


def far_body(windows, far, wide, far_windows, sg, pooled, field, held):
    _, wide_y, nz, _ = far.shape
    odd = lax.rem(lax.axis_index("space"), 2)
    clear_ends(field, nz)
    inside = jnp.where(has_both("space"), 1.0, 0.0).astype(F32)
    field[:, :, 8 : 8 + nz] = far[...].astype(F32) * inside
    fill_windows(field, far_windows)
    for b in range(3):
        held[b, pl.ds(3 * odd, 3)] = far_windows[b]
        held[b, pl.ds(3 - 3 * odd, 3)] = windows[b, pl.ds(4 * odd, 3)]
    first = jnp.where(odd == 0, inside, 1.0)
    second = jnp.where(odd == 1, inside, 1.0)
    for chunk, flag in enumerate((first, second)):
        slope, pool = early_rows_of(held, 2 * chunk, wide, wide_y - 2, 0.125 * flag)
        sg[2 * chunk : 2 * chunk + 2] = slope
        pooled[chunk] = pool


def transpose_body(windows, far_windows, turned):
    rows = windows.shape[2]
    part = turned.shape[2] // 4
    odd = lax.rem(lax.axis_index("space"), 2)
    for source, first in ((windows, 3 * (1 - odd)), (far_windows, windows.shape[1] * odd)):
        for b in range(3):
            for x in range(source.shape[1]):
                value = source[b, x].T
                spot = pl.multiple_of((first + x) * rows, rows)
                for group in range(4):
                    for side in range(2):
                        row = (2 * group + side) * part
                        turned[
                            b, side, group * part : (group + 1) * part, pl.ds(spot, rows)
                        ] = value[row : row + part]


def roll_z(value, shift):
    size = value.shape[-2]
    rolled = pltpu.roll(value, shift % size, value.ndim - 2)
    spot = lax.broadcasted_iota(jnp.int32, value.shape, value.ndim - 2)
    edge = 0 if shift == 1 else size - 1
    return jnp.where(spot == edge, 0.0, rolled)


def deep_body(parts_n, *refs):
    far, near, refs = refs[:parts_n], refs[parts_n : 2 * parts_n], refs[2 * parts_n :]
    wt, cot, block_out, grad, windows = refs[:5]
    sends = refs[5 : parts_n + 5]
    field, wide, slopes, turned, terms = refs[parts_n + 5 :]
    nx, ny, nz, filters = cot.shape
    width = wt.shape[2]
    rows = ny * nz
    py = ny // parts_n
    mine = lax.axis_index("filt")
    for ab in range(9):
        for c in range(3):
            wide[ab, :, c * width : (c + 1) * width] = wt[
                ab, c * filters : (c + 1) * filters
            ]
    field[:, 0:1] = jnp.zeros((nx + 2, 1, nz, width), F32)
    field[:, ny + 1 : ny + 2] = jnp.zeros((nx + 2, 1, nz, width), F32)
    odd = lax.rem(lax.axis_index("space"), 2)
    for parts, first in ((near, 2 * (1 - odd)), (far, 2 * odd)):
        for j in range(parts_n):
            spot = lax.bitwise_xor(mine, j) * py + 1
            field[pl.ds(first, 2), pl.ds(spot, py)] = (
                parts[-j][...].astype(F32).reshape(2, py, nz, width)
            )
    for x in range(nx + 2):
        plane = field[x]
        for c in range(3):
            moved = plane if c == 1 else roll_z(plane, 1 - c)
            for b in range(3):
                windows[b, x, :, c * width : (c + 1) * width] = (
                    moved[b : b + ny].reshape(rows, width).astype(BF16)
                )
    slopes[:, 0:1] = jnp.zeros((nx, 1, nz, filters), F32)
    slopes[:, ny + 1 :] = jnp.zeros((nx, 1, nz, filters), F32)
    for x in range(nx):
        acc = jnp.zeros((rows, filters), F32)
        for ab in range(9):
            a, b = ab // 3, ab % 3
            acc = acc + lax.dot_general(
                windows[b, x + a], wide[ab], (((1,), (1,)), ((), ())), preferred_element_type=F32
            )
        sig = sigmoid(acc)
        block_out[x] = (acc * sig).reshape(ny, nz, filters).astype(BF16)
        slope = sig * (1.0 + acc * (1.0 - sig))
        value = (cot[x].astype(F32).reshape(rows, filters) * slope).astype(BF16)
        grad[x] = value
        slopes[x, 1 : ny + 1] = value.astype(F32).reshape(ny, nz, filters)
    for x in range(nx):
        plane = slopes[x]
        plane = jnp.concatenate([roll_z(plane, -1), plane, roll_z(plane, 1)], axis=2)
        for b in range(3):
            turned[b, x] = (
                plane[2 - b : 2 - b + ny].reshape(rows, 3 * filters).astype(BF16)
            )
    for r in range(nx + 2):
        total = jnp.zeros((rows, width), F32)
        for ab in range(9):
            a, b = ab // 3, ab % 3
            if 0 <= r - a < nx:
                total = total + jnp.dot(turned[b, r - a], wt[ab], preferred_element_type=F32)
        terms[r] = total.reshape(ny, nz, width)
    for j in range(parts_n):
        spot = lax.bitwise_xor(mine, j) * py
        value = terms[:, pl.ds(spot, py)]
        sends[j][...] = value.reshape(nx + 2, py * nz, width).astype(sends[j].dtype)


def deep_grad_body(windows, grad, theirs, mine, held):
    nx, rows, filters = grad.shape
    width = windows.shape[3] // 3
    turned = grad[...].reshape(nx * rows, filters).astype(F32).T.astype(BF16)
    chips, step, _ = mine.shape
    part = filters // 2
    total = 27 * part
    if chips * step > total:
        held[:, total:] = jnp.zeros((2, chips * step - total, width), F32)
    for ab in range(9):
        a, b = ab // 3, ab % 3
        value = jnp.dot(
            turned,
            windows[b, a : a + nx].reshape(nx * rows, 3 * width),
            preferred_element_type=F32,
        )
        for c in range(3):
            spot = (3 * ab + c) * part
            for side in range(2):
                held[side, spot : spot + part] = value[
                    side * part : (side + 1) * part, c * width : (c + 1) * width
                ]
    core = lax.rem(lax.axis_index("space"), 2)
    for q in range(chips):
        theirs[q] = held[1 - core, q * step : (q + 1) * step].astype(theirs.dtype)
        mine[q] = held[core, q * step : (q + 1) * step]


def early_grad_body(nz, *refs):
    parts, (sg, far_sg, turned, deep, out, grad, held, spread) = refs[:-8], refs[-8:]
    count, rows, wide = sg.shape
    total = parts[0][...]
    for part in parts[1:]:
        total = total + part[...].astype(F32)
    px, prow, _ = total.shape
    py = prow // nz
    total = jnp.concatenate([total, total], axis=2).reshape(px, py, 1, nz, wide)
    spread[...] = jnp.broadcast_to(total, (px, py, 2, nz, wide)).reshape(px, rows, wide)
    odd = lax.rem(lax.axis_index("space"), 2)
    for source, first in ((sg, count * (1 - odd)), (far_sg, count * odd)):
        for x in range(count):
            grad[first + x] = (spread[lax.div(first, 2) + x // 2] * source[x]).astype(BF16)
    early_grad_half(1 - odd, grad, turned, deep, out, held)


def early_grad_rest_body(grad, turned, deep, out, held):
    early_grad_half(lax.rem(lax.axis_index("space"), 2), grad, turned, deep, out, held)


def early_grad_half(side, grad, turned, deep, out, held):
    ext, rows, wide = grad.shape
    width = wide // 2
    part = turned.shape[2] // 4
    right = grad[...].reshape(ext * rows, wide)
    for ab in range(9):
        a, b = ab // 3, ab % 3
        value = jnp.dot(
            turned[b, side, :, a * rows : (a + ext) * rows], right, preferred_element_type=F32
        )
        for c in range(3):
            spot = (3 * ab + c) * part
            held[spot : spot + part] = (
                value[c * part : (c + 1) * part, :width]
                + value[(c + 1) * part : (c + 2) * part, width:]
            )
    step = held.shape[0] // out.shape[0]
    for q in range(out.shape[0]):
        out[q, :step] = held[q * step : (q + 1) * step].astype(out.dtype)
        out[q, step:] = deep[q].astype(out.dtype)


def core_sum_body(first, mine, other, *outs):
    chip = lax.div(lax.axis_index("space"), 2)
    rows = slice(first, first + outs[0].shape[0])
    for j, out in enumerate(outs):
        q = lax.bitwise_xor(chip, j)
        out[...] = (mine[q, rows] + other[q, rows].astype(F32)).astype(out.dtype)


def chip_sum_body(count, *refs):
    others, outs = refs[:count], refs[count:]
    total = others[0][...]
    for ref in others[1:]:
        total = total + ref[...].astype(F32)
    row = 0
    for out in outs:
        size = out.shape[0]
        out[...] = total[row : row + size].astype(BF16)
        row += size


def filt_sum_body(count, *refs):
    parts, rest, out = refs[:count], refs[count:-1], refs[-1]
    values = [part[...].astype(F32) for part in parts]
    while len(values) > 1:
        values = [low + high for low, high in zip(values[::2], values[1::2])]
    size = values[0].shape[0]
    out[:size] = values[0].astype(BF16)
    for ref in rest:
        out[size:] = ref[...]


def stack_body(*refs):
    out = refs[-1]
    chip = lax.div(lax.axis_index("space"), 2)
    for j, ref in enumerate(refs[:-1]):
        out[lax.bitwise_xor(chip, j)] = ref[...]


def write_early(pieces, first, step, scale, side, out, held, sem):
    chips, rows, _ = held.shape
    part = out.shape[1] // 2
    copies = []
    for q in range(chips):
        held[q] = pieces[q, :rows].astype(F32) * scale
        done = 0
        while done < rows:
            tap, inner = (q * step + first + done) // part, (q * step + first + done) % part
            size = min(part - inner, rows - done)
            spot = pl.multiple_of(side * part + inner, 8)
            copy = pltpu.make_async_copy(
                held.at[q, pl.ds(done, size)], out.at[tap, pl.ds(spot, size)], sem.at[len(copies)]
            )
            copy.start()
            copies.append(copy)
            done += size
    return copies


def finish_first_body(
    scale, deep_scale, step, cut, mine, other, early, deep, held, other_held, deep_held, sem
):
    core = lax.rem(lax.axis_index("space"), 2)
    copies = write_early(mine, 0, step, scale, core, early, held, sem.at[0])
    copies += write_early(other, 0, step, scale, 1 - core, early, other_held, sem.at[1])
    part = deep_held.shape[1]
    chips, rows, _ = mine.shape
    for pieces, side in ((mine, core), (other, 1 - core)):
        for tap in range(27):
            row = tap * part
            while row < (tap + 1) * part:
                q, inner = row // (rows - cut), row % (rows - cut)
                size = min(rows - cut - inner, (tap + 1) * part - row)
                spot = row - tap * part
                deep_held[tap, spot : spot + size] = (
                    pieces[q, cut + inner : cut + inner + size].astype(F32) * deep_scale
                )
                row += size
        deep[:, pl.ds(pl.multiple_of(side * part, 8), part)] = deep_held[...]
    for copy in copies:
        copy.wait()


def finish_rest_body(own, scale, step, cut, pieces, _, early, held, sem):
    core = lax.rem(lax.axis_index("space"), 2)
    side = core if own else 1 - core
    for copy in write_early(pieces, cut, step, scale, side, early, held, sem):
        copy.wait()


def paired(values, axis, step=1):
    count = lax.axis_size(axis)
    got = {
        j: lax.ppermute(values[j], axis, [(i, i ^ (step * j)) for i in range(count)])
        for j in reversed(range(1, len(values)))
    }
    return [values[0]] + [got[j] for j in range(1, len(values))]


def exchange(value, axis, step):
    return lax.ppermute(value, axis, [(i, i ^ step) for i in range(lax.axis_size(axis))])


def backward(values):
    return [values[0]] + values[:0:-1]


def swap(value, axis, first):
    count = lax.axis_size(axis)
    pairs = [(i, (i + 1) % count) for i in range(first, count, 2)]
    return lax.ppermute(value, axis, pairs + [(b, a) for a, b in pairs])


def shards(volume, w_early, w_deep, cotangent):
    nx, ny, nz, cin = volume.shape
    width = w_early.shape[2]
    filters = w_deep.shape[2]
    space = lax.axis_size("space")
    filt = lax.axis_size("filt")
    chips = space // 2
    half = nz // 2
    ext = nx + 6
    rows = ny * half
    edges = jnp.concatenate([volume[:, :1], volume[:, ny - 1 :]], axis=1)
    edges = call(edges_body, "edges", struct(edges.shape), (edges,), flops=1 << 32)
    yeven, yodd = swap(edges, "filt", 0), swap(edges, "filt", 1)
    rim = struct((3, ny + 2, nz, cin))
    volume, sides, near, far = call(
        spread_body,
        "spread",
        [struct(volume.shape), struct((nx, 2, nz, cin)), rim, rim],
        (volume, yeven, yodd),
        flops=HOLD,
        moved=1 << 24,
    )
    far = swap(far, "space", 1)
    near = swap(near, "space", 0)
    windows, sg, near_pooled, wide = call(
        near_body,
        "early_near",
        (
            struct((3, nx + 3, rows, 4 * cin)),
            struct((nx, rows, 2 * width), F32),
            struct((nx // 2, rows // 2, width)),
            struct((9, 4 * cin, 2 * width)),
        ),
        (volume, sides, near, w_early),
        [pltpu.VMEM((nx + 3, ny + 2, nz + 16, cin), F32)],
        flops=2 * nx * rows * 36 * cin * 2 * width,
    )
    near_parts = paired([near_pooled] * filt, "filt")
    far_windows, far_sg, pooled = call(
        far_body,
        "early_far",
        (
            struct((3, 3, rows, 4 * cin)),
            struct((nx, rows, 2 * width), F32),
            struct((nx // 2, rows // 2, width)),
        ),
        (windows, far, wide),
        [
            pltpu.VMEM((3, ny + 2, nz + 16, cin), F32),
            pltpu.VMEM((3, 6, rows, 4 * cin), BF16),
        ],
        flops=2 * nx * rows * 36 * cin * 2 * width,
    )
    parts = backward(paired([pooled] * filt, "filt"))
    near_parts = backward(near_parts)
    windows, *near_parts = lax.optimization_barrier((windows, *near_parts))
    turned = call(
        transpose_body,
        "turn_windows",
        struct((3, 2, 2 * cin, ext * rows)),
        (windows, far_windows),
        flops=1 << 30,
    )
    *parts, turned = lax.optimization_barrier((*parts, turned))
    dx, dy, dz, _ = cotangent.shape
    px = dx + 2
    prow = rows // 2
    deep = call(
        functools.partial(deep_body, filt),
        "deep_conv",
        [
            struct(cotangent.shape),
            struct((dx, dy * dz, filters)),
            struct((3, px, dy * dz, 3 * width)),
            struct((px, prow, width), F32),
        ]
        + [struct((px, prow, width))] * (filt - 1),
        (*parts, *near_parts, jnp.swapaxes(w_deep, 1, 2).reshape(9, 3 * filters, width), cotangent),
        [
            pltpu.VMEM((px, dy + 2, dz, width), F32),
            pltpu.VMEM((9, filters, 3 * width), BF16),
            pltpu.VMEM((dx, dy + 2, dz, filters), F32),
            pltpu.VMEM((3, dx, dy * dz, 3 * filters), BF16),
            pltpu.VMEM((px, dy, dz, width), F32),
        ],
        flops=4 * dx * dy * dz * 27 * width * filters,
    )
    block_out, grad, deep_windows = deep[:3]
    terms = paired(deep[3:], "filt")

    early_rows = 27 * cin // space
    deep_rows = ceil_to(-(-27 * filters // space), 16)
    deep_first, deep_second = call(
        deep_grad_body,
        "deep_grad",
        [struct((chips, deep_rows, width)), struct((chips, deep_rows, width), F32)],
        (deep_windows, grad),
        [pltpu.VMEM((2, chips * deep_rows, width), F32)],
        flops=2 * dx * dy * dz * 27 * width * filters,
    )
    piece = (chips, early_rows + deep_rows, width)
    held = pltpu.VMEM((27 * cin // 2, width), F32)
    flops = (nx + 4) * rows * 36 * cin * 2 * width
    theirs, grad = call(
        functools.partial(early_grad_body, half),
        "early_grad",
        [struct(piece), struct((nx + 4, rows, 2 * width))],
        (*backward(terms), sg, far_sg, turned, deep_first),
        [held, pltpu.VMEM((px, rows, 2 * width), F32)],
        flops=flops,
    )
    theirs = lax.ppermute(theirs, "space", [(i, i ^ 1) for i in range(space)])
    mine = call(
        early_grad_rest_body,
        "early_grad_rest",
        struct(piece, F32),
        (grad, turned, deep_second),
        [held],
        flops=flops,
    )
    cut = ceil_to(early_rows // 2, 16)
    sums = [
        call(
            functools.partial(core_sum_body, start),
            name,
            [struct((size, width), F32 if j == 0 else BF16) for j in range(chips)],
            (mine, theirs),
            flops=flops,
        )
        for name, start, size, flops in (
            ("core_sum", 0, cut, 0),
            ("core_sum_rest", cut, early_rows - cut + deep_rows, HOLD),
        )
    ]
    first = backward(paired(sums[0], "space", 2))
    *sums[1], first = lax.optimization_barrier((*sums[1], first))
    second = backward(paired(sums[1], "space", 2))
    (early,) = call(
        functools.partial(chip_sum_body, chips), "chip_sum", [struct((cut, width))], first
    )
    first = paired([early] * filt, "filt")
    *second, first[0] = lax.optimization_barrier((*second, first[0]))
    early, deep = call(
        functools.partial(chip_sum_body, chips),
        "chip_sum_rest",
        [struct((early_rows - cut, width)), struct((deep_rows, width))],
        second,
        flops=HOLD,
    )
    second = paired([early] * filt, "filt")
    *first, second[0] = lax.optimization_barrier((*first, second[0]))
    sum_body = functools.partial(filt_sum_body, filt)
    first = call(
        sum_body, "filt_sum", struct((cut + deep_rows, width)), (*first, deep), flops=HOLD
    )
    first = paired([first] * chips, "space", 2)
    *second, first[0] = lax.optimization_barrier((*second, first[0]))
    second = call(
        sum_body, "filt_sum_rest", struct((early_rows - cut, width)), second, flops=HOLD
    )
    *first, _ = lax.optimization_barrier((*first, second))
    second = paired([second] * chips, "space", 2)

    early_total = nx * ny * nz * space * filt
    deep_total = dx * dy * dz * space
    scale = 1.0 / math.sqrt(early_total)
    result = struct((27, cin, width), F32)
    own = call(stack_body, "stack", struct((chips, cut + deep_rows, width)), first)
    pieces_most = chips * (cut // (cin // 2) + 2)
    held = pltpu.VMEM((chips, cut, width), F32)
    grad_early, grad_deep = call(
        functools.partial(
            finish_first_body, scale, 1.0 / math.sqrt(deep_total), early_rows, cut
        ),
        "finish_first",
        [result, struct((27, filters, width), F32)],
        (own, exchange(own, "space", 1)),
        [held, held, pltpu.VMEM((27, filters // 2, width), F32), DMA((2, pieces_most))],
        flops=HOLD,
        outs=[HBM, VMEM],
    )
    own = call(stack_body, "stack_rest", struct((chips, early_rows - cut, width)), second)
    for mine, pieces in ((True, own), (False, exchange(own, "space", 1))):
        grad_early = call(
            functools.partial(finish_rest_body, mine, scale, early_rows, cut),
            "finish_own" if mine else "finish_other",
            result,
            (pieces, grad_early),
            [pltpu.VMEM((chips, early_rows - cut, width), F32), DMA((pieces_most,))],
            hbm=(1,),
            outs=HBM,
            alias=((1, 0),),
        )
    return (block_out, grad_early, jnp.swapaxes(grad_deep, 1, 2))


def solution(mesh):
    return jax.shard_map(
        shards,
        mesh=mesh,
        in_specs=(
            P("space", "filt", None, None),
            P(),
            P(None, None, "filt"),
            P("space", None, None, "filt"),
        ),
        out_specs=(P("space", None, None, "filt"), P(), P(None, None, "filt")),
        check_vma=False,
    )
```

```python
import functools
import math

import jax
import jax.numpy as jnp
from jax import lax
from jax.experimental import pallas as pl
from jax.experimental.pallas import tpu as pltpu
from jax.sharding import PartitionSpec as P

F32 = jnp.float32
BF16 = jnp.bfloat16
HOLD = 1 << 32
VMEM_LIMIT = 24 * 1024 * 1024
VMEM = pl.BlockSpec(memory_space=pltpu.VMEM)
HBM = pl.BlockSpec(memory_space=pltpu.HBM)
DMA = pltpu.SemaphoreType.DMA


def call(
    body, name, out_shape, operands, scratch=(), flops=0, moved=1 << 20, hbm=(), outs=VMEM, alias=()
):
    return pl.pallas_call(
        body,
        name=name,
        out_shape=out_shape,
        in_specs=[HBM if i in hbm else VMEM for i in range(len(operands))],
        out_specs=outs if isinstance(outs, list) else jax.tree.map(lambda _: outs, out_shape),
        scratch_shapes=list(scratch),
        input_output_aliases=dict(alias),
        compiler_params=pltpu.CompilerParams(vmem_limit_bytes=VMEM_LIMIT),
        cost_estimate=pl.CostEstimate(flops=flops, bytes_accessed=moved, transcendentals=0),
    )(*operands)


def struct(shape, dtype=BF16):
    return jax.ShapeDtypeStruct(shape, dtype)


def ceil_to(value, step):
    return -(-value // step) * step


def sigmoid(value):
    return 1.0 / (1.0 + jnp.exp(-value))


def is_even(axis):
    return lax.rem(lax.axis_index(axis), 2) == 0


def edges_body(edges, copied):
    copied[...] = edges[...]


def has_both(axis):
    here = lax.axis_index(axis)
    return (here > 0) & (here < lax.axis_size(axis) - 1)


def spread_body(center, yeven, yodd, copied, sides, near, far):
    copied[...] = center[...]
    nx, ny, _, _ = center.shape
    even = is_even("filt")
    beyond = jnp.where(has_both("filt"), yodd[...], jnp.zeros(yodd.shape, BF16))
    sides[:, 0:1] = jnp.where(even, beyond[:, 1:2], yeven[:, 1:2])
    sides[:, 1:2] = jnp.where(even, yeven[:, 0:1], beyond[:, 0:1])
    odd = lax.rem(lax.axis_index("space"), 2)
    for out, start in ((near, (1 - odd) * (nx - 3)), (far, odd * (nx - 3))):
        rows = pl.ds(start, 3)
        out[:, 0:1] = sides[rows, 0:1]
        out[:, 1 : ny + 1] = center[rows]
        out[:, ny + 1 :] = sides[rows, 1:2]


def fill_windows(field, windows):
    count, wide_y, _, cin = field.shape
    ny = wide_y - 2
    half = windows.shape[2] // ny
    for x in range(count):
        for group in range(4):
            plane = field[x, :, pl.ds(7 + group, half, stride=2), :]
            for b in range(3):
                windows[b, x, :, group * cin : (group + 1) * cin] = (
                    plane[b : b + ny].reshape(ny * half, cin).astype(BF16)
                )


def clear_ends(field, nz):
    count, wide_y, _, cin = field.shape
    field[:, :, 0:8] = jnp.zeros((count, wide_y, 8, cin), F32)
    field[:, :, 8 + nz : 16 + nz] = jnp.zeros((count, wide_y, 8, cin), F32)


def early_rows_of(windows, start, wide, ny, keep):
    rows = windows.shape[2]
    cout = wide.shape[2] // 2
    acc = jnp.zeros((2 * rows, 2 * cout), F32)
    for ab in range(9):
        a, b = ab // 3, ab % 3
        left = windows[b, pl.ds(start + a, 2)].reshape(2 * rows, windows.shape[3])
        acc = acc + jnp.dot(left, wide[ab], preferred_element_type=F32)
    sig = sigmoid(acc)
    slope = (sig * (1.0 + acc * (1.0 - sig)) * keep).reshape(2, rows, 2 * cout)
    act = acc * sig
    act = act[:rows] + act[rows:]
    act = act[:, :cout] + act[:, cout:]
    act = act.reshape(ny // 2, 2, rows // ny, cout)
    act = (act[:, 0] + act[:, 1]) * keep
    return slope, act.reshape(rows // 2, cout).astype(BF16)


def near_body(center, sides, near, w, windows, sg, pooled, wide, field):
    nx, ny, nz, cin = center.shape
    cout = w.shape[2]
    for ab in range(9):
        for group in range(4):
            for side in range(2):
                tap = group - side
                value = w[3 * ab + tap] if 0 <= tap <= 2 else jnp.zeros((cin, cout), BF16)
                wide[
                    ab, group * cin : (group + 1) * cin, side * cout : (side + 1) * cout
                ] = value
    odd = lax.rem(lax.axis_index("space"), 2)
    clear_ends(field, nz)
    cells = slice(8, 8 + nz)
    own = pl.ds(3 * odd, nx)
    field[own, 1 : ny + 1, cells] = center[...].astype(F32)
    field[own, 0:1, cells] = sides[:, 0:1].astype(F32)
    field[own, ny + 1 :, cells] = sides[:, 1:2].astype(F32)
    field[pl.ds((1 - odd) * nx, 3), :, cells] = near[...].astype(F32)
    fill_windows(field, windows)
    for chunk in range(nx // 2):
        slope, pool = early_rows_of(windows, 1 - odd + 2 * chunk, wide, ny, 0.125)
        sg[2 * chunk : 2 * chunk + 2] = slope
        pooled[chunk] = pool


def far_body(windows, far, wide, far_windows, sg, pooled, field, held):
    _, wide_y, nz, _ = far.shape
    odd = lax.rem(lax.axis_index("space"), 2)
    clear_ends(field, nz)
    inside = jnp.where(has_both("space"), 1.0, 0.0).astype(F32)
    field[:, :, 8 : 8 + nz] = far[...].astype(F32) * inside
    fill_windows(field, far_windows)
    for b in range(3):
        held[b, pl.ds(3 * odd, 3)] = far_windows[b]
        held[b, pl.ds(3 - 3 * odd, 3)] = windows[b, pl.ds(4 * odd, 3)]
    first = jnp.where(odd == 0, inside, 1.0)
    second = jnp.where(odd == 1, inside, 1.0)
    for chunk, flag in enumerate((first, second)):
        slope, pool = early_rows_of(held, 2 * chunk, wide, wide_y - 2, 0.125 * flag)
        sg[2 * chunk : 2 * chunk + 2] = slope
        pooled[chunk] = pool


def transpose_body(windows, far_windows, turned):
    rows = windows.shape[2]
    part = turned.shape[2] // 4
    odd = lax.rem(lax.axis_index("space"), 2)
    for source, first in ((windows, 3 * (1 - odd)), (far_windows, windows.shape[1] * odd)):
        for b in range(3):
            for x in range(source.shape[1]):
                value = source[b, x].T
                spot = pl.multiple_of((first + x) * rows, rows)
                for group in range(4):
                    for side in range(2):
                        row = (2 * group + side) * part
                        turned[
                            b, side, group * part : (group + 1) * part, pl.ds(spot, rows)
                        ] = value[row : row + part]


def roll_z(value, shift):
    size = value.shape[-2]
    rolled = pltpu.roll(value, shift % size, value.ndim - 2)
    spot = lax.broadcasted_iota(jnp.int32, value.shape, value.ndim - 2)
    edge = 0 if shift == 1 else size - 1
    return jnp.where(spot == edge, 0.0, rolled)


def deep_body(parts_n, *refs):
    far, near, refs = refs[:parts_n], refs[parts_n : 2 * parts_n], refs[2 * parts_n :]
    wt, cot, block_out, grad, windows = refs[:5]
    sends = refs[5 : parts_n + 5]
    field, wide, slopes, turned, terms = refs[parts_n + 5 :]
    nx, ny, nz, filters = cot.shape
    width = wt.shape[2]
    rows = ny * nz
    py = ny // parts_n
    mine = lax.axis_index("filt")
    for ab in range(9):
        for c in range(3):
            wide[ab, :, c * width : (c + 1) * width] = wt[
                ab, c * filters : (c + 1) * filters
            ]
    field[:, 0:1] = jnp.zeros((nx + 2, 1, nz, width), F32)
    field[:, ny + 1 : ny + 2] = jnp.zeros((nx + 2, 1, nz, width), F32)
    odd = lax.rem(lax.axis_index("space"), 2)
    for parts, first in ((near, 2 * (1 - odd)), (far, 2 * odd)):
        for j in range(parts_n):
            spot = lax.bitwise_xor(mine, j) * py + 1
            field[pl.ds(first, 2), pl.ds(spot, py)] = (
                parts[-j][...].astype(F32).reshape(2, py, nz, width)
            )
    for x in range(nx + 2):
        plane = field[x]
        for c in range(3):
            moved = plane if c == 1 else roll_z(plane, 1 - c)
            for b in range(3):
                windows[b, x, :, c * width : (c + 1) * width] = (
                    moved[b : b + ny].reshape(rows, width).astype(BF16)
                )
    slopes[:, 0:1] = jnp.zeros((nx, 1, nz, filters), F32)
    slopes[:, ny + 1 :] = jnp.zeros((nx, 1, nz, filters), F32)
    for x in range(nx):
        acc = jnp.zeros((rows, filters), F32)
        for ab in range(9):
            a, b = ab // 3, ab % 3
            acc = acc + lax.dot_general(
                windows[b, x + a], wide[ab], (((1,), (1,)), ((), ())), preferred_element_type=F32
            )
        sig = sigmoid(acc)
        block_out[x] = (acc * sig).reshape(ny, nz, filters).astype(BF16)
        slope = sig * (1.0 + acc * (1.0 - sig))
        value = (cot[x].astype(F32).reshape(rows, filters) * slope).astype(BF16)
        grad[x] = value
        slopes[x, 1 : ny + 1] = value.astype(F32).reshape(ny, nz, filters)
    for x in range(nx):
        plane = slopes[x]
        plane = jnp.concatenate([roll_z(plane, -1), plane, roll_z(plane, 1)], axis=2)
        for b in range(3):
            turned[b, x] = (
                plane[2 - b : 2 - b + ny].reshape(rows, 3 * filters).astype(BF16)
            )
    for r in range(nx + 2):
        total = jnp.zeros((rows, width), F32)
        for ab in range(9):
            a, b = ab // 3, ab % 3
            if 0 <= r - a < nx:
                total = total + jnp.dot(turned[b, r - a], wt[ab], preferred_element_type=F32)
        terms[r] = total.reshape(ny, nz, width)
    for j in range(parts_n):
        spot = lax.bitwise_xor(mine, j) * py
        value = terms[:, pl.ds(spot, py)]
        sends[j][...] = value.reshape(nx + 2, py * nz, width).astype(sends[j].dtype)


def deep_grad_body(windows, grad, theirs, mine, held):
    nx, rows, filters = grad.shape
    width = windows.shape[3] // 3
    turned = grad[...].reshape(nx * rows, filters).astype(F32).T.astype(BF16)
    chips, step, _ = mine.shape
    part = filters // 2
    total = 27 * part
    if chips * step > total:
        held[:, total:] = jnp.zeros((2, chips * step - total, width), F32)
    for ab in range(9):
        a, b = ab // 3, ab % 3
        value = jnp.dot(
            turned,
            windows[b, a : a + nx].reshape(nx * rows, 3 * width),
            preferred_element_type=F32,
        )
        for c in range(3):
            spot = (3 * ab + c) * part
            for side in range(2):
                held[side, spot : spot + part] = value[
                    side * part : (side + 1) * part, c * width : (c + 1) * width
                ]
    core = lax.rem(lax.axis_index("space"), 2)
    for q in range(chips):
        theirs[q] = held[1 - core, q * step : (q + 1) * step].astype(theirs.dtype)
        mine[q] = held[core, q * step : (q + 1) * step]


def early_grad_body(nz, *refs):
    parts, (sg, far_sg, turned, deep, out, grad, held, spread) = refs[:-8], refs[-8:]
    count, rows, wide = sg.shape
    total = parts[0][...]
    for part in parts[1:]:
        total = total + part[...].astype(F32)
    px, prow, _ = total.shape
    py = prow // nz
    total = jnp.concatenate([total, total], axis=2).reshape(px, py, 1, nz, wide)
    spread[...] = jnp.broadcast_to(total, (px, py, 2, nz, wide)).reshape(px, rows, wide)
    odd = lax.rem(lax.axis_index("space"), 2)
    for source, first in ((sg, count * (1 - odd)), (far_sg, count * odd)):
        for x in range(count):
            grad[first + x] = (spread[lax.div(first, 2) + x // 2] * source[x]).astype(BF16)
    early_grad_half(1 - odd, grad, turned, deep, out, held)


def early_grad_rest_body(grad, turned, deep, out, held):
    early_grad_half(lax.rem(lax.axis_index("space"), 2), grad, turned, deep, out, held)


def early_grad_half(side, grad, turned, deep, out, held):
    ext, rows, wide = grad.shape
    width = wide // 2
    part = turned.shape[2] // 4
    right = grad[...].reshape(ext * rows, wide)
    for ab in range(9):
        a, b = ab // 3, ab % 3
        value = jnp.dot(
            turned[b, side, :, a * rows : (a + ext) * rows], right, preferred_element_type=F32
        )
        for c in range(3):
            spot = (3 * ab + c) * part
            held[spot : spot + part] = (
                value[c * part : (c + 1) * part, :width]
                + value[(c + 1) * part : (c + 2) * part, width:]
            )
    step = held.shape[0] // out.shape[0]
    for q in range(out.shape[0]):
        out[q, :step] = held[q * step : (q + 1) * step].astype(out.dtype)
        out[q, step:] = deep[q].astype(out.dtype)


def core_sum_body(first, mine, other, *outs):
    chip = lax.div(lax.axis_index("space"), 2)
    rows = slice(first, first + outs[0].shape[0])
    for j, out in enumerate(outs):
        q = lax.bitwise_xor(chip, j)
        out[...] = (mine[q, rows] + other[q, rows].astype(F32)).astype(out.dtype)


def chip_sum_body(count, *refs):
    others, outs = refs[:count], refs[count:]
    total = others[0][...]
    for ref in others[1:]:
        total = total + ref[...].astype(F32)
    row = 0
    for out in outs:
        size = out.shape[0]
        out[...] = total[row : row + size].astype(BF16)
        row += size


def filt_sum_body(count, *refs):
    parts, rest, out = refs[:count], refs[count:-1], refs[-1]
    values = [part[...].astype(F32) for part in parts]
    while len(values) > 1:
        values = [low + high for low, high in zip(values[::2], values[1::2])]
    size = values[0].shape[0]
    out[:size] = values[0].astype(BF16)
    for ref in rest:
        out[size:] = ref[...]


def stack_body(step, *refs):
    *parts, out = refs
    chips = out.shape[0]
    chip = lax.div(lax.axis_index("space"), 2)
    for j in range(chips):
        first, second = parts[j], parts[chips + j]
        q = lax.bitwise_xor(chip, j)
        cut = step - second.shape[0]
        out[q, :cut] = first[:cut]
        out[q, cut:step] = second[...]
        out[q, step:] = first[cut:]


def finish_body(own, early_scale, deep_scale, early_rows, deep_rows, pieces, *refs):
    early, deep, early_held, deep_held, sem = refs[-5:]
    core = lax.rem(lax.axis_index("space"), 2)
    side = core if own else 1 - core
    copies = []
    for out, held, first, step, scale in (
        (early, early_held, 0, early_rows, early_scale),
        (deep, deep_held, pieces.shape[1] - deep_rows, deep_rows, deep_scale),
    ):
        part = held.shape[1]
        for tap in range(27):
            row = tap * part
            while row < (tap + 1) * part:
                q, inner = row // step, row % step
                size = min(step - inner, (tap + 1) * part - row)
                spot = row - tap * part
                held[tap, spot : spot + size] = (
                    pieces[q, first + inner : first + inner + size].astype(F32) * scale
                )
                row += size
            if tap % 9 == 8:
                taps = pl.ds(tap - 8, 9)
                copy = pltpu.make_async_copy(
                    held.at[taps], out.at[taps, pl.ds(side * part, part)], sem.at[len(copies)]
                )
                copy.start()
                copies.append(copy)
    for copy in copies:
        copy.wait()


def paired(values, axis, step=1):
    count = lax.axis_size(axis)
    got = {
        j: lax.ppermute(values[j], axis, [(i, i ^ (step * j)) for i in range(count)])
        for j in reversed(range(1, len(values)))
    }
    return [values[0]] + [got[j] for j in range(1, len(values))]


def exchange(value, axis, step):
    return lax.ppermute(value, axis, [(i, i ^ step) for i in range(lax.axis_size(axis))])


def backward(values):
    return [values[0]] + values[:0:-1]


def swap(value, axis, first):
    count = lax.axis_size(axis)
    pairs = [(i, (i + 1) % count) for i in range(first, count, 2)]
    return lax.ppermute(value, axis, pairs + [(b, a) for a, b in pairs])


def shards(volume, w_early, w_deep, cotangent):
    nx, ny, nz, cin = volume.shape
    width = w_early.shape[2]
    filters = w_deep.shape[2]
    space = lax.axis_size("space")
    filt = lax.axis_size("filt")
    chips = space // 2
    half = nz // 2
    ext = nx + 6
    rows = ny * half
    edges = jnp.concatenate([volume[:, :1], volume[:, ny - 1 :]], axis=1)
    edges = call(edges_body, "edges", struct(edges.shape), (edges,), flops=1 << 32)
    yeven, yodd = swap(edges, "filt", 0), swap(edges, "filt", 1)
    rim = struct((3, ny + 2, nz, cin))
    volume, sides, near, far = call(
        spread_body,
        "spread",
        [struct(volume.shape), struct((nx, 2, nz, cin)), rim, rim],
        (volume, yeven, yodd),
        flops=HOLD,
        moved=1 << 24,
    )
    far = swap(far, "space", 1)
    near = swap(near, "space", 0)
    windows, sg, near_pooled, wide = call(
        near_body,
        "early_near",
        (
            struct((3, nx + 3, rows, 4 * cin)),
            struct((nx, rows, 2 * width), F32),
            struct((nx // 2, rows // 2, width)),
            struct((9, 4 * cin, 2 * width)),
        ),
        (volume, sides, near, w_early),
        [pltpu.VMEM((nx + 3, ny + 2, nz + 16, cin), F32)],
        flops=2 * nx * rows * 36 * cin * 2 * width,
    )
    near_parts = paired([near_pooled] * filt, "filt")
    far_windows, far_sg, pooled = call(
        far_body,
        "early_far",
        (
            struct((3, 3, rows, 4 * cin)),
            struct((nx, rows, 2 * width), F32),
            struct((nx // 2, rows // 2, width)),
        ),
        (windows, far, wide),
        [
            pltpu.VMEM((3, ny + 2, nz + 16, cin), F32),
            pltpu.VMEM((3, 6, rows, 4 * cin), BF16),
        ],
        flops=2 * nx * rows * 36 * cin * 2 * width,
    )
    parts = backward(paired([pooled] * filt, "filt"))
    near_parts = backward(near_parts)
    windows, *near_parts = lax.optimization_barrier((windows, *near_parts))
    turned = call(
        transpose_body,
        "turn_windows",
        struct((3, 2, 2 * cin, ext * rows)),
        (windows, far_windows),
        flops=1 << 30,
    )
    *parts, turned = lax.optimization_barrier((*parts, turned))
    dx, dy, dz, _ = cotangent.shape
    px = dx + 2
    prow = rows // 2
    deep = call(
        functools.partial(deep_body, filt),
        "deep_conv",
        [
            struct(cotangent.shape),
            struct((dx, dy * dz, filters)),
            struct((3, px, dy * dz, 3 * width)),
            struct((px, prow, width), F32),
        ]
        + [struct((px, prow, width))] * (filt - 1),
        (*parts, *near_parts, jnp.swapaxes(w_deep, 1, 2).reshape(9, 3 * filters, width), cotangent),
        [
            pltpu.VMEM((px, dy + 2, dz, width), F32),
            pltpu.VMEM((9, filters, 3 * width), BF16),
            pltpu.VMEM((dx, dy + 2, dz, filters), F32),
            pltpu.VMEM((3, dx, dy * dz, 3 * filters), BF16),
            pltpu.VMEM((px, dy, dz, width), F32),
        ],
        flops=4 * dx * dy * dz * 27 * width * filters,
    )
    block_out, grad, deep_windows = deep[:3]
    terms = paired(deep[3:], "filt")

    early_rows = 27 * cin // space
    deep_rows = ceil_to(-(-27 * filters // space), 16)
    deep_first, deep_second = call(
        deep_grad_body,
        "deep_grad",
        [struct((chips, deep_rows, width)), struct((chips, deep_rows, width), F32)],
        (deep_windows, grad),
        [pltpu.VMEM((2, chips * deep_rows, width), F32)],
        flops=2 * dx * dy * dz * 27 * width * filters,
    )
    piece = (chips, early_rows + deep_rows, width)
    held = pltpu.VMEM((27 * cin // 2, width), F32)
    flops = (nx + 4) * rows * 36 * cin * 2 * width
    theirs, grad = call(
        functools.partial(early_grad_body, half),
        "early_grad",
        [struct(piece), struct((nx + 4, rows, 2 * width))],
        (*backward(terms), sg, far_sg, turned, deep_first),
        [held, pltpu.VMEM((px, rows, 2 * width), F32)],
        flops=flops,
    )
    theirs = lax.ppermute(theirs, "space", [(i, i ^ 1) for i in range(space)])
    mine = call(
        early_grad_rest_body,
        "early_grad_rest",
        struct(piece, F32),
        (grad, turned, deep_second),
        [held],
        flops=flops,
    )
    cut = ceil_to(early_rows // 2, 16)
    sums = [
        call(
            functools.partial(core_sum_body, start),
            name,
            [struct((size, width), F32 if j == 0 else BF16) for j in range(chips)],
            (mine, theirs),
            flops=flops,
        )
        for name, start, size, flops in (
            ("core_sum", 0, cut, 0),
            ("core_sum_rest", cut, early_rows - cut + deep_rows, HOLD),
        )
    ]
    first = backward(paired(sums[0], "space", 2))
    *sums[1], first = lax.optimization_barrier((*sums[1], first))
    second = backward(paired(sums[1], "space", 2))
    (early,) = call(
        functools.partial(chip_sum_body, chips), "chip_sum", [struct((cut, width))], first
    )
    first = paired([early] * filt, "filt")
    *second, first[0] = lax.optimization_barrier((*second, first[0]))
    early, deep = call(
        functools.partial(chip_sum_body, chips),
        "chip_sum_rest",
        [struct((early_rows - cut, width)), struct((deep_rows, width))],
        second,
        flops=HOLD,
    )
    second = paired([early] * filt, "filt")
    *first, second[0] = lax.optimization_barrier((*first, second[0]))
    sum_body = functools.partial(filt_sum_body, filt)
    first = call(
        sum_body, "filt_sum", struct((cut + deep_rows, width)), (*first, deep), flops=HOLD
    )
    first = paired([first] * chips, "space", 2)
    *second, first[0] = lax.optimization_barrier((*second, first[0]))
    second = call(
        sum_body, "filt_sum_rest", struct((early_rows - cut, width)), second, flops=HOLD
    )
    late, first[1] = lax.optimization_barrier((second, first[1]))
    second = paired([second, late] + [second] * (chips - 2), "space", 2)

    own = call(functools.partial(stack_body, early_rows), "stack", struct(piece), (*first, *second))
    other = exchange(own, "space", 1)
    early_total = nx * ny * nz * space * filt
    deep_total = dx * dy * dz * space
    results = [struct((27, cin, width), F32), struct((27, filters, width), F32)]
    scales = (1.0 / math.sqrt(early_total), 1.0 / math.sqrt(deep_total), early_rows, deep_rows)
    scratch = [
        pltpu.VMEM((27, cin // 2, width), F32),
        pltpu.VMEM((27, filters // 2, width), F32),
        DMA((6,)),
    ]
    results = call(
        functools.partial(finish_body, True, *scales),
        "finish_own",
        results,
        (own,),
        scratch,
        outs=HBM,
    )
    grad_early, grad_deep = call(
        functools.partial(finish_body, False, *scales),
        "finish_other",
        [struct(value.shape, F32) for value in results],
        (other, *results),
        scratch,
        hbm=(1, 2),
        outs=HBM,
        alias=((1, 0), (2, 1)),
    )
    return (block_out, grad_early, jnp.swapaxes(grad_deep, 1, 2))


def solution(mesh):
    return jax.shard_map(
        shards,
        mesh=mesh,
        in_specs=(
            P("space", "filt", None, None),
            P(),
            P(None, None, "filt"),
            P("space", None, None, "filt"),
        ),
        out_specs=(P("space", None, None, "filt"), P(), P(None, None, "filt")),
        check_vma=False,
    )
```

```python
import functools
import math

import jax
import jax.numpy as jnp
from jax import lax
from jax.experimental import pallas as pl
from jax.experimental.pallas import tpu as pltpu
from jax.sharding import PartitionSpec as P

F32 = jnp.float32
BF16 = jnp.bfloat16
HOLD = 1 << 32
VMEM_LIMIT = 24 * 1024 * 1024
VMEM = pl.BlockSpec(memory_space=pltpu.VMEM)
HBM = pl.BlockSpec(memory_space=pltpu.HBM)
DMA = pltpu.SemaphoreType.DMA


def call(
    body, name, out_shape, operands, scratch=(), flops=0, moved=1 << 20, hbm=(), outs=VMEM, alias=()
):
    return pl.pallas_call(
        body,
        name=name,
        out_shape=out_shape,
        in_specs=[HBM if i in hbm else VMEM for i in range(len(operands))],
        out_specs=outs if isinstance(outs, list) else jax.tree.map(lambda _: outs, out_shape),
        scratch_shapes=list(scratch),
        input_output_aliases=dict(alias),
        compiler_params=pltpu.CompilerParams(vmem_limit_bytes=VMEM_LIMIT),
        cost_estimate=pl.CostEstimate(flops=flops, bytes_accessed=moved, transcendentals=0),
    )(*operands)


def struct(shape, dtype=BF16):
    return jax.ShapeDtypeStruct(shape, dtype)


def ceil_to(value, step):
    return -(-value // step) * step


def sigmoid(value):
    return 1.0 / (1.0 + jnp.exp(-value))


def is_even(axis):
    return lax.rem(lax.axis_index(axis), 2) == 0


def edges_body(edges, copied):
    copied[...] = edges[...]


def has_both(axis):
    here = lax.axis_index(axis)
    return (here > 0) & (here < lax.axis_size(axis) - 1)


def spread_body(center, yeven, yodd, copied, sides, near, far):
    copied[...] = center[...]
    nx, ny, _, _ = center.shape
    even = is_even("filt")
    beyond = jnp.where(has_both("filt"), yodd[...], jnp.zeros(yodd.shape, BF16))
    sides[:, 0:1] = jnp.where(even, beyond[:, 1:2], yeven[:, 1:2])
    sides[:, 1:2] = jnp.where(even, yeven[:, 0:1], beyond[:, 0:1])
    odd = lax.rem(lax.axis_index("space"), 2)
    for out, start in ((near, (1 - odd) * (nx - 3)), (far, odd * (nx - 3))):
        rows = pl.ds(start, 3)
        out[:, 0:1] = sides[rows, 0:1]
        out[:, 1 : ny + 1] = center[rows]
        out[:, ny + 1 :] = sides[rows, 1:2]


def fill_windows(field, windows):
    count, wide_y, _, cin = field.shape
    ny = wide_y - 2
    half = windows.shape[2] // ny
    for x in range(count):
        for group in range(4):
            plane = field[x, :, pl.ds(7 + group, half, stride=2), :]
            for b in range(3):
                windows[b, x, :, group * cin : (group + 1) * cin] = (
                    plane[b : b + ny].reshape(ny * half, cin).astype(BF16)
                )


def clear_ends(field, nz):
    count, wide_y, _, cin = field.shape
    field[:, :, 0:8] = jnp.zeros((count, wide_y, 8, cin), F32)
    field[:, :, 8 + nz : 16 + nz] = jnp.zeros((count, wide_y, 8, cin), F32)


def early_rows_of(windows, start, wide, ny, keep):
    rows = windows.shape[2]
    cout = wide.shape[2] // 2
    acc = jnp.zeros((2 * rows, 2 * cout), F32)
    for ab in range(9):
        a, b = ab // 3, ab % 3
        left = windows[b, pl.ds(start + a, 2)].reshape(2 * rows, windows.shape[3])
        acc = acc + jnp.dot(left, wide[ab], preferred_element_type=F32)
    sig = sigmoid(acc)
    slope = (sig * (1.0 + acc * (1.0 - sig)) * keep).reshape(2, rows, 2 * cout)
    act = acc * sig
    act = act[:rows] + act[rows:]
    act = act[:, :cout] + act[:, cout:]
    act = act.reshape(ny // 2, 2, rows // ny, cout)
    act = (act[:, 0] + act[:, 1]) * keep
    return slope, act.reshape(rows // 2, cout).astype(BF16)


def near_body(center, sides, near, w, windows, sg, pooled, wide, field):
    nx, ny, nz, cin = center.shape
    cout = w.shape[2]
    for ab in range(9):
        for group in range(4):
            for side in range(2):
                tap = group - side
                value = w[3 * ab + tap] if 0 <= tap <= 2 else jnp.zeros((cin, cout), BF16)
                wide[
                    ab, group * cin : (group + 1) * cin, side * cout : (side + 1) * cout
                ] = value
    odd = lax.rem(lax.axis_index("space"), 2)
    clear_ends(field, nz)
    cells = slice(8, 8 + nz)
    own = pl.ds(3 * odd, nx)
    field[own, 1 : ny + 1, cells] = center[...].astype(F32)
    field[own, 0:1, cells] = sides[:, 0:1].astype(F32)
    field[own, ny + 1 :, cells] = sides[:, 1:2].astype(F32)
    field[pl.ds((1 - odd) * nx, 3), :, cells] = near[...].astype(F32)
    fill_windows(field, windows)
    for chunk in range(nx // 2):
        slope, pool = early_rows_of(windows, 1 - odd + 2 * chunk, wide, ny, 0.125)
        sg[2 * chunk : 2 * chunk + 2] = slope
        pooled[chunk] = pool


def far_body(windows, far, wide, far_windows, sg, pooled, field, held):
    _, wide_y, nz, _ = far.shape
    odd = lax.rem(lax.axis_index("space"), 2)
    clear_ends(field, nz)
    inside = jnp.where(has_both("space"), 1.0, 0.0).astype(F32)
    field[:, :, 8 : 8 + nz] = far[...].astype(F32) * inside
    fill_windows(field, far_windows)
    for b in range(3):
        held[b, pl.ds(3 * odd, 3)] = far_windows[b]
        held[b, pl.ds(3 - 3 * odd, 3)] = windows[b, pl.ds(4 * odd, 3)]
    first = jnp.where(odd == 0, inside, 1.0)
    second = jnp.where(odd == 1, inside, 1.0)
    for chunk, flag in enumerate((first, second)):
        slope, pool = early_rows_of(held, 2 * chunk, wide, wide_y - 2, 0.125 * flag)
        sg[2 * chunk : 2 * chunk + 2] = slope
        pooled[chunk] = pool


def transpose_body(windows, far_windows, turned):
    rows = windows.shape[2]
    part = turned.shape[2] // 4
    odd = lax.rem(lax.axis_index("space"), 2)
    for source, first in ((windows, 3 * (1 - odd)), (far_windows, windows.shape[1] * odd)):
        for b in range(3):
            for x in range(source.shape[1]):
                value = source[b, x].T
                spot = pl.multiple_of((first + x) * rows, rows)
                for group in range(4):
                    for side in range(2):
                        row = (2 * group + side) * part
                        turned[
                            b, side, group * part : (group + 1) * part, pl.ds(spot, rows)
                        ] = value[row : row + part]


def roll_z(value, shift):
    size = value.shape[-2]
    rolled = pltpu.roll(value, shift % size, value.ndim - 2)
    spot = lax.broadcasted_iota(jnp.int32, value.shape, value.ndim - 2)
    edge = 0 if shift == 1 else size - 1
    return jnp.where(spot == edge, 0.0, rolled)


def deep_body(parts_n, *refs):
    far, near, refs = refs[:parts_n], refs[parts_n : 2 * parts_n], refs[2 * parts_n :]
    wt, cot, block_out, grad, windows = refs[:5]
    sends = refs[5 : parts_n + 5]
    field, wide, slopes, turned, terms = refs[parts_n + 5 :]
    nx, ny, nz, filters = cot.shape
    width = wt.shape[2]
    rows = ny * nz
    py = ny // parts_n
    mine = lax.axis_index("filt")
    for ab in range(9):
        for c in range(3):
            wide[ab, :, c * width : (c + 1) * width] = wt[
                ab, c * filters : (c + 1) * filters
            ]
    field[:, 0:1] = jnp.zeros((nx + 2, 1, nz, width), F32)
    field[:, ny + 1 : ny + 2] = jnp.zeros((nx + 2, 1, nz, width), F32)
    odd = lax.rem(lax.axis_index("space"), 2)
    for parts, first in ((near, 2 * (1 - odd)), (far, 2 * odd)):
        for j in range(parts_n):
            spot = lax.bitwise_xor(mine, j) * py + 1
            field[pl.ds(first, 2), pl.ds(spot, py)] = (
                parts[-j][...].astype(F32).reshape(2, py, nz, width)
            )
    for x in range(nx + 2):
        plane = field[x]
        for c in range(3):
            moved = plane if c == 1 else roll_z(plane, 1 - c)
            for b in range(3):
                windows[b, x, :, c * width : (c + 1) * width] = (
                    moved[b : b + ny].reshape(rows, width).astype(BF16)
                )
    slopes[:, 0:1] = jnp.zeros((nx, 1, nz, filters), F32)
    slopes[:, ny + 1 :] = jnp.zeros((nx, 1, nz, filters), F32)
    for x in range(nx):
        acc = jnp.zeros((rows, filters), F32)
        for ab in range(9):
            a, b = ab // 3, ab % 3
            acc = acc + lax.dot_general(
                windows[b, x + a], wide[ab], (((1,), (1,)), ((), ())), preferred_element_type=F32
            )
        sig = sigmoid(acc)
        block_out[x] = (acc * sig).reshape(ny, nz, filters).astype(BF16)
        slope = sig * (1.0 + acc * (1.0 - sig))
        value = (cot[x].astype(F32).reshape(rows, filters) * slope).astype(BF16)
        grad[x] = value
        slopes[x, 1 : ny + 1] = value.astype(F32).reshape(ny, nz, filters)
    for x in range(nx):
        plane = slopes[x]
        plane = jnp.concatenate([roll_z(plane, -1), plane, roll_z(plane, 1)], axis=2)
        for b in range(3):
            turned[b, x] = (
                plane[2 - b : 2 - b + ny].reshape(rows, 3 * filters).astype(BF16)
            )
    for r in range(nx + 2):
        total = jnp.zeros((rows, width), F32)
        for ab in range(9):
            a, b = ab // 3, ab % 3
            if 0 <= r - a < nx:
                total = total + jnp.dot(turned[b, r - a], wt[ab], preferred_element_type=F32)
        terms[r] = total.reshape(ny, nz, width)
    for j in range(parts_n):
        spot = lax.bitwise_xor(mine, j) * py
        value = terms[:, pl.ds(spot, py)]
        sends[j][...] = value.reshape(nx + 2, py * nz, width).astype(sends[j].dtype)


def deep_grad_body(windows, grad, theirs, mine, held):
    nx, rows, filters = grad.shape
    width = windows.shape[3] // 3
    turned = grad[...].reshape(nx * rows, filters).astype(F32).T.astype(BF16)
    chips, step, _ = mine.shape
    part = filters // 2
    total = 27 * part
    if chips * step > total:
        held[:, total:] = jnp.zeros((2, chips * step - total, width), F32)
    for ab in range(9):
        a, b = ab // 3, ab % 3
        value = jnp.dot(
            turned,
            windows[b, a : a + nx].reshape(nx * rows, 3 * width),
            preferred_element_type=F32,
        )
        for c in range(3):
            spot = (3 * ab + c) * part
            for side in range(2):
                held[side, spot : spot + part] = value[
                    side * part : (side + 1) * part, c * width : (c + 1) * width
                ]
    core = lax.rem(lax.axis_index("space"), 2)
    for q in range(chips):
        theirs[q] = held[1 - core, q * step : (q + 1) * step].astype(theirs.dtype)
        mine[q] = held[core, q * step : (q + 1) * step]


def early_grad_body(nz, taps, *refs):
    parts, (sg, far_sg, turned, out, grad, held, spread) = refs[:-7], refs[-7:]
    count, rows, wide = sg.shape
    total = parts[0][...]
    for part in parts[1:]:
        total = total + part[...].astype(F32)
    px, prow, _ = total.shape
    py = prow // nz
    total = jnp.concatenate([total, total], axis=2).reshape(px, py, 1, nz, wide)
    spread[...] = jnp.broadcast_to(total, (px, py, 2, nz, wide)).reshape(px, rows, wide)
    odd = lax.rem(lax.axis_index("space"), 2)
    for source, first in ((sg, count * (1 - odd)), (far_sg, count * odd)):
        for x in range(count):
            grad[first + x] = (spread[lax.div(first, 2) + x // 2] * source[x]).astype(BF16)
    early_grad_half(1 - odd, taps, grad, turned, out, held)


def early_grad_rest_body(own, taps, *refs):
    grad, turned, *deep, out, held = refs
    core = lax.rem(lax.axis_index("space"), 2)
    early_grad_half(core if own else 1 - core, taps, grad, turned, out, held)
    step = out.shape[1] - (deep[0].shape[1] if deep else 0)
    for ref in deep:
        out[:, step:] = ref[...].astype(out.dtype)


def early_grad_half(side, taps, grad, turned, out, held):
    ext, rows, wide = grad.shape
    width = wide // 2
    part = turned.shape[2] // 4
    right = grad[...].reshape(ext * rows, wide)
    for ab in range(*taps):
        a, b = ab // 3, ab % 3
        value = jnp.dot(
            turned[b, side, :, a * rows : (a + ext) * rows], right, preferred_element_type=F32
        )
        for c in range(3):
            spot = (3 * (ab - taps[0]) + c) * part
            held[spot : spot + part] = (
                value[c * part : (c + 1) * part, :width]
                + value[(c + 1) * part : (c + 2) * part, width:]
            )
    step = held.shape[0] // out.shape[0]
    for q in range(out.shape[0]):
        out[q, :step] = held[q * step : (q + 1) * step].astype(out.dtype)


def core_sum_body(mine, other, *outs):
    chip = lax.div(lax.axis_index("space"), 2)
    for j, out in enumerate(outs):
        q = lax.bitwise_xor(chip, j)
        out[...] = (mine[q] + other[q].astype(F32)).astype(out.dtype)


def chip_sum_body(count, *refs):
    others, outs = refs[:count], refs[count:]
    total = others[0][...]
    for ref in others[1:]:
        total = total + ref[...].astype(F32)
    row = 0
    for out in outs:
        size = out.shape[0]
        out[...] = total[row : row + size].astype(BF16)
        row += size


def filt_sum_body(count, *refs):
    parts, rest, out = refs[:count], refs[count:-1], refs[-1]
    values = [part[...].astype(F32) for part in backward(list(parts))]
    while len(values) > 1:
        values = [low + high for low, high in zip(values[::2], values[1::2])]
    size = values[0].shape[0]
    out[:size] = values[0].astype(BF16)
    for ref in rest:
        out[size:] = ref[...]


def stack_body(step, *refs):
    *parts, out = refs
    chips = out.shape[0]
    chip = lax.div(lax.axis_index("space"), 2)
    for j in range(chips):
        first, second = parts[j], parts[chips + j]
        q = lax.bitwise_xor(chip, j)
        cut = step - second.shape[0]
        out[q, :cut] = first[:cut]
        out[q, cut:step] = second[...]
        out[q, step:] = first[cut:]


def finish_body(own, early_scale, deep_scale, steps, cut, pieces, *refs):
    early, deep, early_held, deep_held, sem = refs[-5:]
    core = lax.rem(lax.axis_index("space"), 2)
    side = core if own else 1 - core
    copies = []
    first = 0
    for out, held, begin, end, step, scale in (
        (early, early_held, 0, cut, steps[0], early_scale),
        (early, early_held, cut, 27, steps[1], early_scale),
        (deep, deep_held, 0, 27, steps[2], deep_scale),
    ):
        part = held.shape[1]
        for tap in range(begin, end):
            row = (tap - begin) * part
            stop = row + part
            while row < stop:
                q, inner = row // step, row % step
                size = min(step - inner, stop - row)
                spot = part - (stop - row)
                held[tap, spot : spot + size] = (
                    pieces[q, first + inner : first + inner + size].astype(F32) * scale
                )
                row += size
            if tap % 3 == 2:
                taps = pl.ds(tap - 2, 3)
                copy = pltpu.make_async_copy(
                    held.at[taps], out.at[taps, pl.ds(side * part, part)], sem.at[len(copies)]
                )
                copy.start()
                copies.append(copy)
        first += step
    for copy in copies:
        copy.wait()


def paired(values, axis, step=1):
    count = lax.axis_size(axis)
    got = {
        j: lax.ppermute(values[j], axis, [(i, i ^ (step * j)) for i in range(count)])
        for j in reversed(range(1, len(values)))
    }
    return [values[0]] + [got[j] for j in range(1, len(values))]


def exchange(value, axis, step):
    return lax.ppermute(value, axis, [(i, i ^ step) for i in range(lax.axis_size(axis))])


def backward(values):
    return [values[0]] + values[:0:-1]


def swap(value, axis, first):
    count = lax.axis_size(axis)
    pairs = [(i, (i + 1) % count) for i in range(first, count, 2)]
    return lax.ppermute(value, axis, pairs + [(b, a) for a, b in pairs])


def shards(volume, w_early, w_deep, cotangent):
    nx, ny, nz, cin = volume.shape
    width = w_early.shape[2]
    filters = w_deep.shape[2]
    space = lax.axis_size("space")
    filt = lax.axis_size("filt")
    chips = space // 2
    half = nz // 2
    ext = nx + 6
    rows = ny * half
    edges = jnp.concatenate([volume[:, :1], volume[:, ny - 1 :]], axis=1)
    edges = call(edges_body, "edges", struct(edges.shape), (edges,), flops=1 << 32)
    yeven, yodd = swap(edges, "filt", 0), swap(edges, "filt", 1)
    rim = struct((3, ny + 2, nz, cin))
    volume, sides, near, far = call(
        spread_body,
        "spread",
        [struct(volume.shape), struct((nx, 2, nz, cin)), rim, rim],
        (volume, yeven, yodd),
        flops=HOLD,
        moved=1 << 24,
    )
    far = swap(far, "space", 1)
    near = swap(near, "space", 0)
    windows, sg, near_pooled, wide = call(
        near_body,
        "early_near",
        (
            struct((3, nx + 3, rows, 4 * cin)),
            struct((nx, rows, 2 * width), F32),
            struct((nx // 2, rows // 2, width)),
            struct((9, 4 * cin, 2 * width)),
        ),
        (volume, sides, near, w_early),
        [pltpu.VMEM((nx + 3, ny + 2, nz + 16, cin), F32)],
        flops=2 * nx * rows * 36 * cin * 2 * width,
    )
    near_parts = paired([near_pooled] * filt, "filt")
    far_windows, far_sg, pooled = call(
        far_body,
        "early_far",
        (
            struct((3, 3, rows, 4 * cin)),
            struct((nx, rows, 2 * width), F32),
            struct((nx // 2, rows // 2, width)),
        ),
        (windows, far, wide),
        [
            pltpu.VMEM((3, ny + 2, nz + 16, cin), F32),
            pltpu.VMEM((3, 6, rows, 4 * cin), BF16),
        ],
        flops=2 * nx * rows * 36 * cin * 2 * width,
    )
    parts = backward(paired([pooled] * filt, "filt"))
    near_parts = backward(near_parts)
    windows, *near_parts = lax.optimization_barrier((windows, *near_parts))
    turned = call(
        transpose_body,
        "turn_windows",
        struct((3, 2, 2 * cin, ext * rows)),
        (windows, far_windows),
        flops=1 << 30,
    )
    *parts, turned = lax.optimization_barrier((*parts, turned))
    dx, dy, dz, _ = cotangent.shape
    px = dx + 2
    prow = rows // 2
    deep = call(
        functools.partial(deep_body, filt),
        "deep_conv",
        [
            struct(cotangent.shape),
            struct((dx, dy * dz, filters)),
            struct((3, px, dy * dz, 3 * width)),
            struct((px, prow, width), F32),
        ]
        + [struct((px, prow, width))] * (filt - 1),
        (*parts, *near_parts, jnp.swapaxes(w_deep, 1, 2).reshape(9, 3 * filters, width), cotangent),
        [
            pltpu.VMEM((px, dy + 2, dz, width), F32),
            pltpu.VMEM((9, filters, 3 * width), BF16),
            pltpu.VMEM((dx, dy + 2, dz, filters), F32),
            pltpu.VMEM((3, dx, dy * dz, 3 * filters), BF16),
            pltpu.VMEM((px, dy, dz, width), F32),
        ],
        flops=4 * dx * dy * dz * 27 * width * filters,
    )
    block_out, grad, deep_windows = deep[:3]
    terms = paired(deep[3:], "filt")

    deep_rows = ceil_to(-(-27 * filters // space), 16)
    deep_first, deep_second = call(
        deep_grad_body,
        "deep_grad",
        [struct((chips, deep_rows, width)), struct((chips, deep_rows, width), F32)],
        (deep_windows, grad),
        [pltpu.VMEM((2, chips * deep_rows, width), F32)],
        flops=2 * dx * dy * dz * 27 * width * filters,
    )
    cuts = ((0, 5), (5, 9))
    steps = [3 * (end - begin) * (cin // 2) // chips for begin, end in cuts]
    flops = 2 * (nx + 4) * rows * 18 * cin * 2 * width
    helds = [pltpu.VMEM((step * chips, width), F32) for step in steps]

    def core_sums(name, mine, theirs):
        size = mine.shape[1:]
        shapes = [struct(size, F32)] + [struct(size)] * (chips - 1)
        return list(call(core_sum_body, name, shapes, (mine, theirs)))

    theirs, grad = call(
        functools.partial(early_grad_body, half, cuts[0]),
        "early_grad",
        [struct((chips, steps[0], width)), struct((nx + 4, rows, 2 * width))],
        (*backward(terms), sg, far_sg, turned),
        [helds[0], pltpu.VMEM((px, rows, 2 * width), F32)],
        flops=flops,
    )
    theirs = exchange(theirs, "space", 1)
    mine = call(
        functools.partial(early_grad_rest_body, True, cuts[0]),
        "early_grad_own",
        struct((chips, steps[0], width), F32),
        (grad, turned),
        [helds[0]],
        flops=flops,
    )
    sums = core_sums("core_sum", mine, theirs)
    grad, sums[0] = lax.optimization_barrier((grad, sums[0]))
    size = (chips, steps[1] + deep_rows, width)
    theirs = call(
        functools.partial(early_grad_rest_body, False, cuts[1]),
        "early_grad_rest",
        struct(size),
        (grad, turned, deep_first),
        [helds[1]],
        flops=flops,
    )
    theirs = exchange(theirs, "space", 1)
    mine = call(
        functools.partial(early_grad_rest_body, True, cuts[1]),
        "early_grad_rest_own",
        struct(size, F32),
        (grad, turned, deep_second),
        [helds[1]],
        flops=flops,
    )
    sums = [sums, core_sums("core_sum_rest", mine, theirs)]
    first = backward(paired(sums[0], "space", 2))
    *sums[1], first = lax.optimization_barrier((*sums[1], first))
    second = backward(paired(sums[1], "space", 2))
    (early,) = call(
        functools.partial(chip_sum_body, chips), "chip_sum", [struct((steps[0], width))], first
    )
    first = backward(paired([early] * filt, "filt"))
    *second, first[0] = lax.optimization_barrier((*second, first[0]))
    early, deep = call(
        functools.partial(chip_sum_body, chips),
        "chip_sum_rest",
        [struct((steps[1], width)), struct((deep_rows, width))],
        second,
        flops=HOLD,
    )
    second = backward(paired([early] * filt, "filt"))
    *first, second[0] = lax.optimization_barrier((*first, second[0]))
    sum_body = functools.partial(filt_sum_body, filt)
    first = call(
        sum_body, "filt_sum", struct((steps[0] + deep_rows, width)), (*first, deep), flops=HOLD
    )
    first = paired([first] * chips, "space", 2)
    *second, first[0] = lax.optimization_barrier((*second, first[0]))
    second = call(
        sum_body, "filt_sum_rest", struct((steps[1], width)), second, flops=HOLD
    )
    late, first[1] = lax.optimization_barrier((second, first[1]))
    second = paired([second, late] + [second] * (chips - 2), "space", 2)

    own = call(
        functools.partial(stack_body, sum(steps)),
        "stack",
        struct((chips, sum(steps) + deep_rows, width)),
        (*first, *second),
    )
    other = exchange(own, "space", 1)
    early_total = nx * ny * nz * space * filt
    deep_total = dx * dy * dz * space
    results = [struct((27, cin, width), F32), struct((27, filters, width), F32)]
    scales = (1.0 / math.sqrt(early_total), 1.0 / math.sqrt(deep_total))
    scales += ((*steps, deep_rows), 3 * cuts[0][1])
    scratch = [
        pltpu.VMEM((27, cin // 2, width), F32),
        pltpu.VMEM((27, filters // 2, width), F32),
        DMA((18,)),
    ]
    results = call(
        functools.partial(finish_body, True, *scales),
        "finish_own",
        results,
        (own,),
        scratch,
        outs=HBM,
    )
    grad_early, grad_deep = call(
        functools.partial(finish_body, False, *scales),
        "finish_other",
        [struct(value.shape, F32) for value in results],
        (other, *results),
        scratch,
        hbm=(1, 2),
        outs=HBM,
        alias=((1, 0), (2, 1)),
    )
    return (block_out, grad_early, jnp.swapaxes(grad_deep, 1, 2))


def solution(mesh):
    return jax.shard_map(
        shards,
        mesh=mesh,
        in_specs=(
            P("space", "filt", None, None),
            P(),
            P(None, None, "filt"),
            P("space", None, None, "filt"),
        ),
        out_specs=(P("space", None, None, "filt"), P(), P(None, None, "filt")),
        check_vma=False,
    )
```

```python
import functools
import math

import jax
import jax.numpy as jnp
from jax import lax
from jax.experimental import pallas as pl
from jax.experimental.pallas import tpu as pltpu
from jax.sharding import PartitionSpec as P

F32 = jnp.float32
BF16 = jnp.bfloat16
HOLD = 1 << 32
VMEM_LIMIT = 24 * 1024 * 1024
VMEM = pl.BlockSpec(memory_space=pltpu.VMEM)
HBM = pl.BlockSpec(memory_space=pltpu.HBM)
DMA = pltpu.SemaphoreType.DMA


def call(
    body, name, out_shape, operands, scratch=(), flops=0, moved=1 << 20, hbm=(), outs=VMEM, alias=()
):
    return pl.pallas_call(
        body,
        name=name,
        out_shape=out_shape,
        in_specs=[HBM if i in hbm else VMEM for i in range(len(operands))],
        out_specs=outs if isinstance(outs, list) else jax.tree.map(lambda _: outs, out_shape),
        scratch_shapes=list(scratch),
        input_output_aliases=dict(alias),
        compiler_params=pltpu.CompilerParams(vmem_limit_bytes=VMEM_LIMIT),
        cost_estimate=pl.CostEstimate(flops=flops, bytes_accessed=moved, transcendentals=0),
    )(*operands)


def struct(shape, dtype=BF16):
    return jax.ShapeDtypeStruct(shape, dtype)


def ceil_to(value, step):
    return -(-value // step) * step


def sigmoid(value):
    return 1.0 / (1.0 + jnp.exp(-value))


def is_even(axis):
    return lax.rem(lax.axis_index(axis), 2) == 0


def edges_body(edges, copied):
    copied[...] = edges[...]


def has_both(axis):
    here = lax.axis_index(axis)
    return (here > 0) & (here < lax.axis_size(axis) - 1)


def spread_body(center, yeven, yodd, copied, sides, near, far):
    copied[...] = center[...]
    nx, ny, _, _ = center.shape
    even = is_even("filt")
    beyond = jnp.where(has_both("filt"), yodd[...], jnp.zeros(yodd.shape, BF16))
    sides[:, 0:1] = jnp.where(even, beyond[:, 1:2], yeven[:, 1:2])
    sides[:, 1:2] = jnp.where(even, yeven[:, 0:1], beyond[:, 0:1])
    odd = lax.rem(lax.axis_index("space"), 2)
    for out, start in ((near, (1 - odd) * (nx - 3)), (far, odd * (nx - 3))):
        rows = pl.ds(start, 3)
        out[:, 0:1] = sides[rows, 0:1]
        out[:, 1 : ny + 1] = center[rows]
        out[:, ny + 1 :] = sides[rows, 1:2]


def fill_windows(field, windows):
    count, wide_y, _, cin = field.shape
    ny = wide_y - 2
    half = windows.shape[2] // ny
    for x in range(count):
        for group in range(4):
            plane = field[x, :, pl.ds(7 + group, half, stride=2), :]
            for b in range(3):
                windows[b, x, :, group * cin : (group + 1) * cin] = (
                    plane[b : b + ny].reshape(ny * half, cin).astype(BF16)
                )


def clear_ends(field, nz):
    count, wide_y, _, cin = field.shape
    field[:, :, 0:8] = jnp.zeros((count, wide_y, 8, cin), F32)
    field[:, :, 8 + nz : 16 + nz] = jnp.zeros((count, wide_y, 8, cin), F32)


def early_rows_of(windows, start, wide, ny, keep):
    rows = windows.shape[2]
    cout = wide.shape[2] // 2
    acc = jnp.zeros((2 * rows, 2 * cout), F32)
    for ab in range(9):
        a, b = ab // 3, ab % 3
        left = windows[b, pl.ds(start + a, 2)].reshape(2 * rows, windows.shape[3])
        acc = acc + jnp.dot(left, wide[ab], preferred_element_type=F32)
    sig = sigmoid(acc)
    slope = (sig * (1.0 + acc * (1.0 - sig)) * keep).reshape(2, rows, 2 * cout)
    act = acc * sig
    act = act[:rows] + act[rows:]
    act = act[:, :cout] + act[:, cout:]
    act = act.reshape(ny // 2, 2, rows // ny, cout)
    act = (act[:, 0] + act[:, 1]) * keep
    return slope, act.reshape(rows // 2, cout).astype(BF16)


def near_body(center, sides, near, w, windows, sg, pooled, wide, field):
    nx, ny, nz, cin = center.shape
    cout = w.shape[2]
    for ab in range(9):
        for group in range(4):
            for side in range(2):
                tap = group - side
                value = w[3 * ab + tap] if 0 <= tap <= 2 else jnp.zeros((cin, cout), BF16)
                wide[
                    ab, group * cin : (group + 1) * cin, side * cout : (side + 1) * cout
                ] = value
    odd = lax.rem(lax.axis_index("space"), 2)
    clear_ends(field, nz)
    cells = slice(8, 8 + nz)
    own = pl.ds(3 * odd, nx)
    field[own, 1 : ny + 1, cells] = center[...].astype(F32)
    field[own, 0:1, cells] = sides[:, 0:1].astype(F32)
    field[own, ny + 1 :, cells] = sides[:, 1:2].astype(F32)
    field[pl.ds((1 - odd) * nx, 3), :, cells] = near[...].astype(F32)
    fill_windows(field, windows)
    for chunk in range(nx // 2):
        slope, pool = early_rows_of(windows, 1 - odd + 2 * chunk, wide, ny, 0.125)
        sg[2 * chunk : 2 * chunk + 2] = slope
        pooled[chunk] = pool


def far_body(windows, far, wide, far_windows, sg, pooled, field, held):
    _, wide_y, nz, _ = far.shape
    odd = lax.rem(lax.axis_index("space"), 2)
    clear_ends(field, nz)
    inside = jnp.where(has_both("space"), 1.0, 0.0).astype(F32)
    field[:, :, 8 : 8 + nz] = far[...].astype(F32) * inside
    fill_windows(field, far_windows)
    for b in range(3):
        held[b, pl.ds(3 * odd, 3)] = far_windows[b]
        held[b, pl.ds(3 - 3 * odd, 3)] = windows[b, pl.ds(4 * odd, 3)]
    first = jnp.where(odd == 0, inside, 1.0)
    second = jnp.where(odd == 1, inside, 1.0)
    for chunk, flag in enumerate((first, second)):
        slope, pool = early_rows_of(held, 2 * chunk, wide, wide_y - 2, 0.125 * flag)
        sg[2 * chunk : 2 * chunk + 2] = slope
        pooled[chunk] = pool


def transpose_body(windows, far_windows, turned):
    rows = windows.shape[2]
    part = turned.shape[2] // 4
    odd = lax.rem(lax.axis_index("space"), 2)
    for source, first in ((windows, 3 * (1 - odd)), (far_windows, windows.shape[1] * odd)):
        for b in range(3):
            for x in range(source.shape[1]):
                value = source[b, x].T
                spot = pl.multiple_of((first + x) * rows, rows)
                for group in range(4):
                    for side in range(2):
                        row = (2 * group + side) * part
                        turned[
                            b, side, group * part : (group + 1) * part, pl.ds(spot, rows)
                        ] = value[row : row + part]


def roll_z(value, shift):
    size = value.shape[-2]
    rolled = pltpu.roll(value, shift % size, value.ndim - 2)
    spot = lax.broadcasted_iota(jnp.int32, value.shape, value.ndim - 2)
    edge = 0 if shift == 1 else size - 1
    return jnp.where(spot == edge, 0.0, rolled)


def deep_body(parts_n, *refs):
    far, near, refs = refs[:parts_n], refs[parts_n : 2 * parts_n], refs[2 * parts_n :]
    wt, cot, block_out, grad, windows = refs[:5]
    sends = refs[5 : parts_n + 5]
    field, wide, slopes, turned, terms = refs[parts_n + 5 :]
    nx, ny, nz, filters = cot.shape
    width = wt.shape[2]
    rows = ny * nz
    py = ny // parts_n
    mine = lax.axis_index("filt")
    for ab in range(9):
        for c in range(3):
            wide[ab, :, c * width : (c + 1) * width] = wt[
                ab, c * filters : (c + 1) * filters
            ]
    field[:, 0:1] = jnp.zeros((nx + 2, 1, nz, width), F32)
    field[:, ny + 1 : ny + 2] = jnp.zeros((nx + 2, 1, nz, width), F32)
    odd = lax.rem(lax.axis_index("space"), 2)
    for parts, first in ((near, 2 * (1 - odd)), (far, 2 * odd)):
        for j in range(parts_n):
            spot = lax.bitwise_xor(mine, j) * py + 1
            field[pl.ds(first, 2), pl.ds(spot, py)] = (
                parts[-j][...].astype(F32).reshape(2, py, nz, width)
            )
    for x in range(nx + 2):
        plane = field[x]
        for c in range(3):
            moved = plane if c == 1 else roll_z(plane, 1 - c)
            for b in range(3):
                windows[b, x, :, c * width : (c + 1) * width] = (
                    moved[b : b + ny].reshape(rows, width).astype(BF16)
                )
    slopes[:, 0:1] = jnp.zeros((nx, 1, nz, filters), F32)
    slopes[:, ny + 1 :] = jnp.zeros((nx, 1, nz, filters), F32)
    for x in range(nx):
        acc = jnp.zeros((rows, filters), F32)
        for ab in range(9):
            a, b = ab // 3, ab % 3
            acc = acc + lax.dot_general(
                windows[b, x + a], wide[ab], (((1,), (1,)), ((), ())), preferred_element_type=F32
            )
        sig = sigmoid(acc)
        block_out[x] = (acc * sig).reshape(ny, nz, filters).astype(BF16)
        slope = sig * (1.0 + acc * (1.0 - sig))
        value = (cot[x].astype(F32).reshape(rows, filters) * slope).astype(BF16)
        grad[x] = value
        slopes[x, 1 : ny + 1] = value.astype(F32).reshape(ny, nz, filters)
    for x in range(nx):
        plane = slopes[x]
        plane = jnp.concatenate([roll_z(plane, -1), plane, roll_z(plane, 1)], axis=2)
        for b in range(3):
            turned[b, x] = (
                plane[2 - b : 2 - b + ny].reshape(rows, 3 * filters).astype(BF16)
            )
    for r in range(nx + 2):
        total = jnp.zeros((rows, width), F32)
        for ab in range(9):
            a, b = ab // 3, ab % 3
            if 0 <= r - a < nx:
                total = total + jnp.dot(turned[b, r - a], wt[ab], preferred_element_type=F32)
        terms[r] = total.reshape(ny, nz, width)
    for j in range(parts_n):
        spot = lax.bitwise_xor(mine, j) * py
        value = terms[:, pl.ds(spot, py)]
        sends[j][...] = value.reshape(nx + 2, py * nz, width).astype(sends[j].dtype)


def deep_grad_body(windows, grad, theirs, mine, held):
    nx, rows, filters = grad.shape
    width = windows.shape[3] // 3
    turned = grad[...].reshape(nx * rows, filters).astype(F32).T.astype(BF16)
    chips, step, _ = mine.shape
    part = filters // 2
    total = 27 * part
    if chips * step > total:
        held[:, total:] = jnp.zeros((2, chips * step - total, width), F32)
    for ab in range(9):
        a, b = ab // 3, ab % 3
        value = jnp.dot(
            turned,
            windows[b, a : a + nx].reshape(nx * rows, 3 * width),
            preferred_element_type=F32,
        )
        for c in range(3):
            spot = (3 * ab + c) * part
            for side in range(2):
                held[side, spot : spot + part] = value[
                    side * part : (side + 1) * part, c * width : (c + 1) * width
                ]
    core = lax.rem(lax.axis_index("space"), 2)
    for q in range(chips):
        theirs[q] = held[1 - core, q * step : (q + 1) * step].astype(theirs.dtype)
        mine[q] = held[core, q * step : (q + 1) * step]


def early_grad_body(nz, taps, *refs):
    parts, (sg, far_sg, turned, out, grad, held, spread) = refs[:-7], refs[-7:]
    count, rows, wide = sg.shape
    total = parts[0][...]
    for part in parts[1:]:
        total = total + part[...].astype(F32)
    px, prow, _ = total.shape
    py = prow // nz
    total = jnp.concatenate([total, total], axis=2).reshape(px, py, 1, nz, wide)
    spread[...] = jnp.broadcast_to(total, (px, py, 2, nz, wide)).reshape(px, rows, wide)
    odd = lax.rem(lax.axis_index("space"), 2)
    for source, first in ((sg, count * (1 - odd)), (far_sg, count * odd)):
        for x in range(count):
            grad[first + x] = (spread[lax.div(first, 2) + x // 2] * source[x]).astype(BF16)
    early_grad_half(1 - odd, taps, grad, turned, out, held)


def early_grad_rest_body(own, taps, *refs):
    grad, turned, *deep, out, held = refs
    core = lax.rem(lax.axis_index("space"), 2)
    early_grad_half(core if own else 1 - core, taps, grad, turned, out, held)
    step = out.shape[1] - (deep[0].shape[1] if deep else 0)
    for ref in deep:
        out[:, step:] = ref[...].astype(out.dtype)


def early_grad_half(side, taps, grad, turned, out, held):
    ext, rows, wide = grad.shape
    width = wide // 2
    part = turned.shape[2] // 4
    right = grad[...].reshape(ext * rows, wide)
    for ab in range(*taps):
        a, b = ab // 3, ab % 3
        value = jnp.dot(
            turned[b, side, :, a * rows : (a + ext) * rows], right, preferred_element_type=F32
        )
        for c in range(3):
            spot = (3 * (ab - taps[0]) + c) * part
            held[spot : spot + part] = (
                value[c * part : (c + 1) * part, :width]
                + value[(c + 1) * part : (c + 2) * part, width:]
            )
    step = held.shape[0] // out.shape[0]
    for q in range(out.shape[0]):
        out[q, :step] = held[q * step : (q + 1) * step].astype(out.dtype)


def core_sum_body(mine, other, *outs):
    chip = lax.div(lax.axis_index("space"), 2)
    for j, out in enumerate(outs):
        q = lax.bitwise_xor(chip, j)
        out[...] = (mine[q] + other[q].astype(F32)).astype(out.dtype)


def chip_sum_body(count, *refs):
    others, outs = refs[:count], refs[count:]
    total = others[0][...]
    for ref in others[1:]:
        total = total + ref[...].astype(F32)
    row = 0
    for out in outs:
        size = out.shape[0]
        out[...] = total[row : row + size].astype(BF16)
        row += size


def filt_sum_body(count, *refs):
    parts, rest, out = refs[:count], refs[count:-1], refs[-1]
    values = [part[...].astype(F32) for part in backward(list(parts))]
    while len(values) > 1:
        values = [low + high for low, high in zip(values[::2], values[1::2])]
    size = values[0].shape[0]
    out[:size] = values[0].astype(BF16)
    for ref in rest:
        out[size:] = ref[...]


def stack_body(step, *refs):
    *parts, out = refs
    chips = out.shape[0]
    chip = lax.div(lax.axis_index("space"), 2)
    for j in range(chips):
        first, second = parts[j], parts[chips + j]
        q = lax.bitwise_xor(chip, j)
        cut = step - second.shape[0]
        out[q, :cut] = first[:cut]
        out[q, cut:step] = second[...]
        out[q, step:] = first[cut:]


def finish_body(own, early_scale, deep_scale, steps, cut, pieces, *refs):
    early, deep, early_held, deep_held, sem = refs[-5:]
    core = lax.rem(lax.axis_index("space"), 2)
    side = core if own else 1 - core
    copies = []
    first = 0
    for out, held, begin, end, step, scale in (
        (early, early_held, 0, cut, steps[0], early_scale),
        (early, early_held, cut, 27, steps[1], early_scale),
        (deep, deep_held, 0, 27, steps[2], deep_scale),
    ):
        part = held.shape[1]
        for tap in range(begin, end):
            row = (tap - begin) * part
            stop = row + part
            while row < stop:
                q, inner = row // step, row % step
                size = min(step - inner, stop - row)
                spot = part - (stop - row)
                held[tap, spot : spot + size] = (
                    pieces[q, first + inner : first + inner + size].astype(F32) * scale
                )
                row += size
            some = (end - begin) // 3
            if (tap + 1 - begin) % some == 0:
                taps = pl.ds(tap + 1 - some, some)
                copy = pltpu.make_async_copy(
                    held.at[taps], out.at[taps, pl.ds(side * part, part)], sem.at[len(copies)]
                )
                copy.start()
                copies.append(copy)
        first += step
    for copy in copies:
        copy.wait()


def paired(values, axis, step=1):
    count = lax.axis_size(axis)
    got = {
        j: lax.ppermute(values[j], axis, [(i, i ^ (step * j)) for i in range(count)])
        for j in reversed(range(1, len(values)))
    }
    return [values[0]] + [got[j] for j in range(1, len(values))]


def exchange(value, axis, step):
    return lax.ppermute(value, axis, [(i, i ^ step) for i in range(lax.axis_size(axis))])


def backward(values):
    return [values[0]] + values[:0:-1]


def swap(value, axis, first):
    count = lax.axis_size(axis)
    pairs = [(i, (i + 1) % count) for i in range(first, count, 2)]
    return lax.ppermute(value, axis, pairs + [(b, a) for a, b in pairs])


def shards(volume, w_early, w_deep, cotangent):
    nx, ny, nz, cin = volume.shape
    width = w_early.shape[2]
    filters = w_deep.shape[2]
    space = lax.axis_size("space")
    filt = lax.axis_size("filt")
    chips = space // 2
    half = nz // 2
    ext = nx + 6
    rows = ny * half
    edges = jnp.concatenate([volume[:, :1], volume[:, ny - 1 :]], axis=1)
    edges = call(edges_body, "edges", struct(edges.shape), (edges,), flops=1 << 32)
    yeven, yodd = swap(edges, "filt", 0), swap(edges, "filt", 1)
    rim = struct((3, ny + 2, nz, cin))
    volume, sides, near, far = call(
        spread_body,
        "spread",
        [struct(volume.shape), struct((nx, 2, nz, cin)), rim, rim],
        (volume, yeven, yodd),
        flops=HOLD,
        moved=1 << 24,
    )
    far = swap(far, "space", 1)
    near = swap(near, "space", 0)
    windows, sg, near_pooled, wide = call(
        near_body,
        "early_near",
        (
            struct((3, nx + 3, rows, 4 * cin)),
            struct((nx, rows, 2 * width), F32),
            struct((nx // 2, rows // 2, width)),
            struct((9, 4 * cin, 2 * width)),
        ),
        (volume, sides, near, w_early),
        [pltpu.VMEM((nx + 3, ny + 2, nz + 16, cin), F32)],
        flops=2 * nx * rows * 36 * cin * 2 * width,
    )
    near_parts = paired([near_pooled] * filt, "filt")
    far_windows, far_sg, pooled = call(
        far_body,
        "early_far",
        (
            struct((3, 3, rows, 4 * cin)),
            struct((nx, rows, 2 * width), F32),
            struct((nx // 2, rows // 2, width)),
        ),
        (windows, far, wide),
        [
            pltpu.VMEM((3, ny + 2, nz + 16, cin), F32),
            pltpu.VMEM((3, 6, rows, 4 * cin), BF16),
        ],
        flops=2 * nx * rows * 36 * cin * 2 * width,
    )
    parts = backward(paired([pooled] * filt, "filt"))
    near_parts = backward(near_parts)
    windows, *near_parts = lax.optimization_barrier((windows, *near_parts))
    turned = call(
        transpose_body,
        "turn_windows",
        struct((3, 2, 2 * cin, ext * rows)),
        (windows, far_windows),
        flops=1 << 30,
    )
    *parts, turned = lax.optimization_barrier((*parts, turned))
    dx, dy, dz, _ = cotangent.shape
    px = dx + 2
    prow = rows // 2
    deep = call(
        functools.partial(deep_body, filt),
        "deep_conv",
        [
            struct(cotangent.shape),
            struct((dx, dy * dz, filters)),
            struct((3, px, dy * dz, 3 * width)),
            struct((px, prow, width), F32),
        ]
        + [struct((px, prow, width))] * (filt - 1),
        (*parts, *near_parts, jnp.swapaxes(w_deep, 1, 2).reshape(9, 3 * filters, width), cotangent),
        [
            pltpu.VMEM((px, dy + 2, dz, width), F32),
            pltpu.VMEM((9, filters, 3 * width), BF16),
            pltpu.VMEM((dx, dy + 2, dz, filters), F32),
            pltpu.VMEM((3, dx, dy * dz, 3 * filters), BF16),
            pltpu.VMEM((px, dy, dz, width), F32),
        ],
        flops=4 * dx * dy * dz * 27 * width * filters,
    )
    block_out, grad, deep_windows = deep[:3]
    terms = paired(deep[3:], "filt")

    deep_rows = ceil_to(-(-27 * filters // space), 16)
    deep_first, deep_second = call(
        deep_grad_body,
        "deep_grad",
        [struct((chips, deep_rows, width)), struct((chips, deep_rows, width), F32)],
        (deep_windows, grad),
        [pltpu.VMEM((2, chips * deep_rows, width), F32)],
        flops=2 * dx * dy * dz * 27 * width * filters,
    )
    deep_first, terms[-1] = lax.optimization_barrier((deep_first, terms[-1]))
    cuts = ((0, 5), (5, 9))
    steps = [3 * (end - begin) * (cin // 2) // chips for begin, end in cuts]
    flops = 2 * (nx + 4) * rows * 18 * cin * 2 * width
    helds = [pltpu.VMEM((step * chips, width), F32) for step in steps]

    def core_sums(name, mine, theirs):
        size = mine.shape[1:]
        shapes = [struct(size, F32)] + [struct(size)] * (chips - 1)
        return list(call(core_sum_body, name, shapes, (mine, theirs)))

    theirs, grad = call(
        functools.partial(early_grad_body, half, cuts[0]),
        "early_grad",
        [struct((chips, steps[0], width)), struct((nx + 4, rows, 2 * width))],
        (*backward(terms), sg, far_sg, turned),
        [helds[0], pltpu.VMEM((px, rows, 2 * width), F32)],
        flops=flops,
    )
    theirs = exchange(theirs, "space", 1)
    mine = call(
        functools.partial(early_grad_rest_body, True, cuts[0]),
        "early_grad_own",
        struct((chips, steps[0], width), F32),
        (grad, turned),
        [helds[0]],
        flops=flops,
    )
    sums = core_sums("core_sum", mine, theirs)
    grad, sums[0] = lax.optimization_barrier((grad, sums[0]))
    first = backward(paired(sums, "space", 2))
    size = (chips, steps[1] + deep_rows, width)
    theirs = call(
        functools.partial(early_grad_rest_body, False, cuts[1]),
        "early_grad_rest",
        struct(size),
        (grad, turned, deep_first),
        [helds[1]],
        flops=flops,
    )
    theirs = exchange(theirs, "space", 1)
    mine = call(
        functools.partial(early_grad_rest_body, True, cuts[1]),
        "early_grad_rest_own",
        struct(size, F32),
        (grad, turned, deep_second),
        [helds[1]],
        flops=flops,
    )
    sums = core_sums("core_sum_rest", mine, theirs)
    *sums, first = lax.optimization_barrier((*sums, first))
    second = backward(paired(sums, "space", 2))
    (early,) = call(
        functools.partial(chip_sum_body, chips), "chip_sum", [struct((steps[0], width))], first
    )
    first = backward(paired([early] * filt, "filt"))
    *second, first[0] = lax.optimization_barrier((*second, first[0]))
    early, deep = call(
        functools.partial(chip_sum_body, chips),
        "chip_sum_rest",
        [struct((steps[1], width)), struct((deep_rows, width))],
        second,
        flops=HOLD,
    )
    second = backward(paired([early] * filt, "filt"))
    *first, second[0] = lax.optimization_barrier((*first, second[0]))
    sum_body = functools.partial(filt_sum_body, filt)
    first = call(
        sum_body, "filt_sum", struct((steps[0] + deep_rows, width)), (*first, deep), flops=HOLD
    )
    first = paired([first] * chips, "space", 2)
    *second, first[0] = lax.optimization_barrier((*second, first[0]))
    second = call(
        sum_body, "filt_sum_rest", struct((steps[1], width)), second, flops=HOLD
    )
    late, first[1] = lax.optimization_barrier((second, first[1]))
    second = paired([second, late] + [second] * (chips - 2), "space", 2)

    own = call(
        functools.partial(stack_body, sum(steps)),
        "stack",
        struct((chips, sum(steps) + deep_rows, width)),
        (*first, *second),
    )
    other = exchange(own, "space", 1)
    early_total = nx * ny * nz * space * filt
    deep_total = dx * dy * dz * space
    results = [struct((27, cin, width), F32), struct((27, filters, width), F32)]
    scales = (1.0 / math.sqrt(early_total), 1.0 / math.sqrt(deep_total))
    scales += ((*steps, deep_rows), 3 * cuts[0][1])
    scratch = [
        pltpu.VMEM((27, cin // 2, width), F32),
        pltpu.VMEM((27, filters // 2, width), F32),
        DMA((9,)),
    ]
    results = call(
        functools.partial(finish_body, True, *scales),
        "finish_own",
        results,
        (own,),
        scratch,
        outs=HBM,
    )
    grad_early, grad_deep = call(
        functools.partial(finish_body, False, *scales),
        "finish_other",
        [struct(value.shape, F32) for value in results],
        (other, *results),
        scratch,
        hbm=(1, 2),
        outs=HBM,
        alias=((1, 0), (2, 1)),
    )
    return (block_out, grad_early, jnp.swapaxes(grad_deep, 1, 2))


def solution(mesh):
    return jax.shard_map(
        shards,
        mesh=mesh,
        in_specs=(
            P("space", "filt", None, None),
            P(),
            P(None, None, "filt"),
            P("space", None, None, "filt"),
        ),
        out_specs=(P("space", None, None, "filt"), P(), P(None, None, "filt")),
        check_vma=False,
    )
```

```python
import functools
import math

import jax
import jax.numpy as jnp
from jax import lax
from jax.experimental import pallas as pl
from jax.experimental.pallas import tpu as pltpu
from jax.sharding import PartitionSpec as P

F32 = jnp.float32
BF16 = jnp.bfloat16
HOLD = 1 << 32
VMEM_LIMIT = 24 * 1024 * 1024
VMEM = pl.BlockSpec(memory_space=pltpu.VMEM)
HBM = pl.BlockSpec(memory_space=pltpu.HBM)
DMA = pltpu.SemaphoreType.DMA


def call(
    body, name, out_shape, operands, scratch=(), flops=0, moved=1 << 20, hbm=(), outs=VMEM, alias=()
):
    return pl.pallas_call(
        body,
        name=name,
        out_shape=out_shape,
        in_specs=[HBM if i in hbm else VMEM for i in range(len(operands))],
        out_specs=outs if isinstance(outs, list) else jax.tree.map(lambda _: outs, out_shape),
        scratch_shapes=list(scratch),
        input_output_aliases=dict(alias),
        compiler_params=pltpu.CompilerParams(vmem_limit_bytes=VMEM_LIMIT),
        cost_estimate=pl.CostEstimate(flops=flops, bytes_accessed=moved, transcendentals=0),
    )(*operands)


def struct(shape, dtype=BF16):
    return jax.ShapeDtypeStruct(shape, dtype)


def ceil_to(value, step):
    return -(-value // step) * step


def sigmoid(value):
    return 1.0 / (1.0 + jnp.exp(-value))


def is_even(axis):
    return lax.rem(lax.axis_index(axis), 2) == 0


def edges_body(edges, copied):
    copied[...] = edges[...]


def has_both(axis):
    here = lax.axis_index(axis)
    return (here > 0) & (here < lax.axis_size(axis) - 1)


def spread_body(center, yodd, yeven, copied, sides, near, far):
    copied[...] = center[...]
    nx, ny, _, _ = center.shape
    even = is_even("filt")
    beyond = jnp.where(has_both("filt"), yodd[...], jnp.zeros(yodd.shape, BF16))
    sides[:, 0:1] = jnp.where(even, beyond[:, 1:2], yeven[:, 1:2])
    sides[:, 1:2] = jnp.where(even, yeven[:, 0:1], beyond[:, 0:1])
    odd = lax.rem(lax.axis_index("space"), 2)
    for out, start in ((near, (1 - odd) * (nx - 3)), (far, odd * (nx - 3))):
        rows = pl.ds(start, 3)
        out[:, 0:1] = sides[rows, 0:1]
        out[:, 1 : ny + 1] = center[rows]
        out[:, ny + 1 :] = sides[rows, 1:2]


def fill_windows(field, windows):
    count, wide_y, _, cin = field.shape
    ny = wide_y - 2
    half = windows.shape[2] // ny
    for x in range(count):
        for group in range(4):
            plane = field[x, :, pl.ds(7 + group, half, stride=2), :]
            for b in range(3):
                windows[b, x, :, group * cin : (group + 1) * cin] = (
                    plane[b : b + ny].reshape(ny * half, cin).astype(BF16)
                )


def clear_ends(field, nz):
    count, wide_y, _, cin = field.shape
    field[:, :, 0:8] = jnp.zeros((count, wide_y, 8, cin), F32)
    field[:, :, 8 + nz : 16 + nz] = jnp.zeros((count, wide_y, 8, cin), F32)


def early_rows_of(windows, start, wide, ny, keep):
    rows = windows.shape[2]
    cout = wide.shape[2] // 2
    acc = jnp.zeros((2 * rows, 2 * cout), F32)
    for ab in range(9):
        a, b = ab // 3, ab % 3
        left = windows[b, pl.ds(start + a, 2)].reshape(2 * rows, windows.shape[3])
        acc = acc + jnp.dot(left, wide[ab], preferred_element_type=F32)
    sig = sigmoid(acc)
    slope = (sig * (1.0 + acc * (1.0 - sig)) * keep).reshape(2, rows, 2 * cout)
    act = acc * sig
    act = act[:rows] + act[rows:]
    act = act[:, :cout] + act[:, cout:]
    act = act.reshape(ny // 2, 2, rows // ny, cout)
    act = (act[:, 0] + act[:, 1]) * keep
    return slope, act.reshape(rows // 2, cout).astype(BF16)


def near_body(center, sides, near, w, windows, sg, pooled, wide, field):
    nx, ny, nz, cin = center.shape
    cout = w.shape[2]
    for ab in range(9):
        for group in range(4):
            for side in range(2):
                tap = group - side
                value = w[3 * ab + tap] if 0 <= tap <= 2 else jnp.zeros((cin, cout), BF16)
                wide[
                    ab, group * cin : (group + 1) * cin, side * cout : (side + 1) * cout
                ] = value
    odd = lax.rem(lax.axis_index("space"), 2)
    clear_ends(field, nz)
    cells = slice(8, 8 + nz)
    own = pl.ds(3 * odd, nx)
    field[own, 1 : ny + 1, cells] = center[...].astype(F32)
    field[own, 0:1, cells] = sides[:, 0:1].astype(F32)
    field[own, ny + 1 :, cells] = sides[:, 1:2].astype(F32)
    field[pl.ds((1 - odd) * nx, 3), :, cells] = near[...].astype(F32)
    fill_windows(field, windows)
    for chunk in range(nx // 2):
        slope, pool = early_rows_of(windows, 1 - odd + 2 * chunk, wide, ny, 0.125)
        sg[2 * chunk : 2 * chunk + 2] = slope
        pooled[chunk] = pool


def far_body(windows, far, wide, far_windows, sg, pooled, field, held):
    _, wide_y, nz, _ = far.shape
    odd = lax.rem(lax.axis_index("space"), 2)
    clear_ends(field, nz)
    inside = jnp.where(has_both("space"), 1.0, 0.0).astype(F32)
    field[:, :, 8 : 8 + nz] = far[...].astype(F32) * inside
    fill_windows(field, far_windows)
    for b in range(3):
        held[b, pl.ds(3 * odd, 3)] = far_windows[b]
        held[b, pl.ds(3 - 3 * odd, 3)] = windows[b, pl.ds(4 * odd, 3)]
    first = jnp.where(odd == 0, inside, 1.0)
    second = jnp.where(odd == 1, inside, 1.0)
    for chunk, flag in enumerate((first, second)):
        slope, pool = early_rows_of(held, 2 * chunk, wide, wide_y - 2, 0.125 * flag)
        sg[2 * chunk : 2 * chunk + 2] = slope
        pooled[chunk] = pool


def transpose_body(windows, far_windows, turned):
    rows = windows.shape[2]
    part = turned.shape[2] // 4
    odd = lax.rem(lax.axis_index("space"), 2)
    for source, first in ((windows, 3 * (1 - odd)), (far_windows, windows.shape[1] * odd)):
        for b in range(3):
            for x in range(source.shape[1]):
                value = source[b, x].T
                spot = pl.multiple_of((first + x) * rows, rows)
                for group in range(4):
                    for side in range(2):
                        row = (2 * group + side) * part
                        turned[
                            b, side, group * part : (group + 1) * part, pl.ds(spot, rows)
                        ] = value[row : row + part]


def roll_z(value, shift):
    size = value.shape[-2]
    rolled = pltpu.roll(value, shift % size, value.ndim - 2)
    spot = lax.broadcasted_iota(jnp.int32, value.shape, value.ndim - 2)
    edge = 0 if shift == 1 else size - 1
    return jnp.where(spot == edge, 0.0, rolled)


def deep_body(parts_n, *refs):
    far, near, refs = refs[:parts_n], refs[parts_n : 2 * parts_n], refs[2 * parts_n :]
    wt, cot, block_out, grad, windows = refs[:5]
    sends = refs[5 : parts_n + 5]
    field, wide, slopes, turned, terms = refs[parts_n + 5 :]
    nx, ny, nz, filters = cot.shape
    width = wt.shape[2]
    rows = ny * nz
    py = ny // parts_n
    mine = lax.axis_index("filt")
    for ab in range(9):
        for c in range(3):
            wide[ab, :, c * width : (c + 1) * width] = wt[
                ab, c * filters : (c + 1) * filters
            ]
    field[:, 0:1] = jnp.zeros((nx + 2, 1, nz, width), F32)
    field[:, ny + 1 : ny + 2] = jnp.zeros((nx + 2, 1, nz, width), F32)
    odd = lax.rem(lax.axis_index("space"), 2)
    for parts, first in ((near, 2 * (1 - odd)), (far, 2 * odd)):
        for j in range(parts_n):
            spot = lax.bitwise_xor(mine, j) * py + 1
            field[pl.ds(first, 2), pl.ds(spot, py)] = (
                parts[-j][...].astype(F32).reshape(2, py, nz, width)
            )
    for x in range(nx + 2):
        plane = field[x]
        for c in range(3):
            moved = plane if c == 1 else roll_z(plane, 1 - c)
            for b in range(3):
                windows[b, x, :, c * width : (c + 1) * width] = (
                    moved[b : b + ny].reshape(rows, width).astype(BF16)
                )
    slopes[:, 0:1] = jnp.zeros((nx, 1, nz, filters), F32)
    slopes[:, ny + 1 :] = jnp.zeros((nx, 1, nz, filters), F32)
    for x in range(nx):
        acc = jnp.zeros((rows, filters), F32)
        for ab in range(9):
            a, b = ab // 3, ab % 3
            acc = acc + lax.dot_general(
                windows[b, x + a], wide[ab], (((1,), (1,)), ((), ())), preferred_element_type=F32
            )
        sig = sigmoid(acc)
        block_out[x] = (acc * sig).reshape(ny, nz, filters).astype(BF16)
        slope = sig * (1.0 + acc * (1.0 - sig))
        value = (cot[x].astype(F32).reshape(rows, filters) * slope).astype(BF16)
        grad[x] = value
        slopes[x, 1 : ny + 1] = value.astype(F32).reshape(ny, nz, filters)
    for x in range(nx):
        plane = slopes[x]
        plane = jnp.concatenate([roll_z(plane, -1), plane, roll_z(plane, 1)], axis=2)
        for b in range(3):
            turned[b, x] = (
                plane[2 - b : 2 - b + ny].reshape(rows, 3 * filters).astype(BF16)
            )
    for r in range(nx + 2):
        total = jnp.zeros((rows, width), F32)
        for ab in range(9):
            a, b = ab // 3, ab % 3
            if 0 <= r - a < nx:
                total = total + jnp.dot(turned[b, r - a], wt[ab], preferred_element_type=F32)
        terms[r] = total.reshape(ny, nz, width)
    for j in range(parts_n):
        spot = lax.bitwise_xor(mine, j) * py
        value = terms[:, pl.ds(spot, py)]
        sends[j][...] = value.reshape(nx + 2, py * nz, width).astype(sends[j].dtype)


def deep_grad_body(windows, grad, theirs, mine, held):
    nx, rows, filters = grad.shape
    width = windows.shape[3] // 3
    turned = grad[...].reshape(nx * rows, filters).astype(F32).T.astype(BF16)
    chips, step, _ = mine.shape
    part = filters // 2
    total = 27 * part
    if chips * step > total:
        held[:, total:] = jnp.zeros((2, chips * step - total, width), F32)
    for ab in range(9):
        a, b = ab // 3, ab % 3
        value = jnp.dot(
            turned,
            windows[b, a : a + nx].reshape(nx * rows, 3 * width),
            preferred_element_type=F32,
        )
        for c in range(3):
            spot = (3 * ab + c) * part
            for side in range(2):
                held[side, spot : spot + part] = value[
                    side * part : (side + 1) * part, c * width : (c + 1) * width
                ]
    core = lax.rem(lax.axis_index("space"), 2)
    for q in range(chips):
        theirs[q] = held[1 - core, q * step : (q + 1) * step].astype(theirs.dtype)
        mine[q] = held[core, q * step : (q + 1) * step]


def early_grad_body(nz, taps, *refs):
    parts, (sg, far_sg, turned, out, grad, held, spread) = refs[:-7], refs[-7:]
    count, rows, wide = sg.shape
    total = parts[0][...]
    for part in parts[1:]:
        total = total + part[...].astype(F32)
    px, prow, _ = total.shape
    py = prow // nz
    total = jnp.concatenate([total, total], axis=2).reshape(px, py, 1, nz, wide)
    spread[...] = jnp.broadcast_to(total, (px, py, 2, nz, wide)).reshape(px, rows, wide)
    odd = lax.rem(lax.axis_index("space"), 2)
    for source, first in ((sg, count * (1 - odd)), (far_sg, count * odd)):
        for x in range(count):
            grad[first + x] = (spread[lax.div(first, 2) + x // 2] * source[x]).astype(BF16)
    early_grad_half(1 - odd, taps, grad, turned, out, held)


def early_grad_rest_body(own, taps, *refs):
    grad, turned, *deep, out, held = refs
    core = lax.rem(lax.axis_index("space"), 2)
    early_grad_half(core if own else 1 - core, taps, grad, turned, out, held)
    step = out.shape[1] - (deep[0].shape[1] if deep else 0)
    for ref in deep:
        out[:, step:] = ref[...].astype(out.dtype)


def early_grad_half(side, taps, grad, turned, out, held):
    ext, rows, wide = grad.shape
    width = wide // 2
    part = turned.shape[2] // 4
    right = grad[...].reshape(ext * rows, wide)
    for ab in range(*taps):
        a, b = ab // 3, ab % 3
        value = jnp.dot(
            turned[b, side, :, a * rows : (a + ext) * rows], right, preferred_element_type=F32
        )
        for c in range(3):
            spot = (3 * (ab - taps[0]) + c) * part
            held[spot : spot + part] = (
                value[c * part : (c + 1) * part, :width]
                + value[(c + 1) * part : (c + 2) * part, width:]
            )
    step = held.shape[0] // out.shape[0]
    for q in range(out.shape[0]):
        out[q, :step] = held[q * step : (q + 1) * step].astype(out.dtype)


def core_sum_body(mine, other, *outs):
    chip = lax.div(lax.axis_index("space"), 2)
    for j, out in enumerate(outs):
        q = lax.bitwise_xor(chip, j)
        out[...] = (mine[q] + other[q].astype(F32)).astype(out.dtype)


def chip_sum_body(count, *refs):
    others, outs = refs[:count], refs[count:]
    total = others[0][...]
    for ref in others[1:]:
        total = total + ref[...].astype(F32)
    row = 0
    for out in outs:
        size = out.shape[0]
        out[...] = total[row : row + size].astype(BF16)
        row += size


def filt_sum_body(count, *refs):
    parts, rest, out = refs[:count], refs[count:-1], refs[-1]
    values = [part[...].astype(F32) for part in backward(list(parts))]
    while len(values) > 1:
        values = [low + high for low, high in zip(values[::2], values[1::2])]
    size = values[0].shape[0]
    out[:size] = values[0].astype(BF16)
    for ref in rest:
        out[size:] = ref[...]


def stack_body(step, *refs):
    *parts, out = refs
    chips = out.shape[0]
    chip = lax.div(lax.axis_index("space"), 2)
    for j in range(chips):
        first, second = parts[j], parts[chips + j]
        q = lax.bitwise_xor(chip, j)
        cut = step - second.shape[0]
        out[q, :cut] = first[:cut]
        out[q, cut:step] = second[...]
        out[q, step:] = first[cut:]


def finish_body(own, early_scale, deep_scale, steps, cut, pieces, *refs):
    early, deep, early_held, deep_held, sem = refs[-5:]
    core = lax.rem(lax.axis_index("space"), 2)
    side = core if own else 1 - core
    copies = []
    first = 0
    for out, held, begin, end, step, scale in (
        (early, early_held, 0, cut, steps[0], early_scale),
        (early, early_held, cut, 27, steps[1], early_scale),
        (deep, deep_held, 0, 27, steps[2], deep_scale),
    ):
        part = held.shape[1]
        for tap in range(begin, end):
            row = (tap - begin) * part
            stop = row + part
            while row < stop:
                q, inner = row // step, row % step
                size = min(step - inner, stop - row)
                spot = part - (stop - row)
                held[tap, spot : spot + size] = (
                    pieces[q, first + inner : first + inner + size].astype(F32) * scale
                )
                row += size
            some = (end - begin) // 3
            if (tap + 1 - begin) % some == 0:
                taps = pl.ds(tap + 1 - some, some)
                copy = pltpu.make_async_copy(
                    held.at[taps], out.at[taps, pl.ds(side * part, part)], sem.at[len(copies)]
                )
                copy.start()
                copies.append(copy)
        first += step
    for copy in copies:
        copy.wait()


def paired(values, axis, step=1):
    count = lax.axis_size(axis)
    got = {
        j: lax.ppermute(values[j], axis, [(i, i ^ (step * j)) for i in range(count)])
        for j in reversed(range(1, len(values)))
    }
    return [values[0]] + [got[j] for j in range(1, len(values))]


def exchange(value, axis, step):
    return lax.ppermute(value, axis, [(i, i ^ step) for i in range(lax.axis_size(axis))])


def backward(values):
    return [values[0]] + values[:0:-1]


def swap(value, axis, first):
    count = lax.axis_size(axis)
    pairs = [(i, (i + 1) % count) for i in range(first, count, 2)]
    return lax.ppermute(value, axis, pairs + [(b, a) for a, b in pairs])


def shards(volume, w_early, w_deep, cotangent):
    nx, ny, nz, cin = volume.shape
    width = w_early.shape[2]
    filters = w_deep.shape[2]
    space = lax.axis_size("space")
    filt = lax.axis_size("filt")
    chips = space // 2
    half = nz // 2
    ext = nx + 6
    rows = ny * half
    edges = jnp.concatenate([volume[:, :1], volume[:, ny - 1 :]], axis=1)
    edges = call(edges_body, "edges", struct(edges.shape), (edges,), flops=1 << 32)
    yeven, yodd = swap(edges, "filt", 0), swap(edges, "filt", 1)
    rim = struct((3, ny + 2, nz, cin))
    volume, sides, near, far = call(
        spread_body,
        "spread",
        [struct(volume.shape), struct((nx, 2, nz, cin)), rim, rim],
        (volume, yodd, yeven),
        flops=HOLD,
        moved=1 << 24,
    )
    far = swap(far, "space", 1)
    near = swap(near, "space", 0)
    windows, sg, near_pooled, wide = call(
        near_body,
        "early_near",
        (
            struct((3, nx + 3, rows, 4 * cin)),
            struct((nx, rows, 2 * width), F32),
            struct((nx // 2, rows // 2, width)),
            struct((9, 4 * cin, 2 * width)),
        ),
        (volume, sides, near, w_early),
        [pltpu.VMEM((nx + 3, ny + 2, nz + 16, cin), F32)],
        flops=2 * nx * rows * 36 * cin * 2 * width,
    )
    near_parts = paired([near_pooled] * filt, "filt")
    far_windows, far_sg, pooled = call(
        far_body,
        "early_far",
        (
            struct((3, 3, rows, 4 * cin)),
            struct((nx, rows, 2 * width), F32),
            struct((nx // 2, rows // 2, width)),
        ),
        (windows, far, wide),
        [
            pltpu.VMEM((3, ny + 2, nz + 16, cin), F32),
            pltpu.VMEM((3, 6, rows, 4 * cin), BF16),
        ],
        flops=2 * nx * rows * 36 * cin * 2 * width,
    )
    parts = backward(paired([pooled] * filt, "filt"))
    near_parts = backward(near_parts)
    windows, *near_parts = lax.optimization_barrier((windows, *near_parts))
    turned = call(
        transpose_body,
        "turn_windows",
        struct((3, 2, 2 * cin, ext * rows)),
        (windows, far_windows),
        flops=1 << 30,
    )
    *parts, turned = lax.optimization_barrier((*parts, turned))
    dx, dy, dz, _ = cotangent.shape
    px = dx + 2
    prow = rows // 2
    deep = call(
        functools.partial(deep_body, filt),
        "deep_conv",
        [
            struct(cotangent.shape),
            struct((dx, dy * dz, filters)),
            struct((3, px, dy * dz, 3 * width)),
            struct((px, prow, width), F32),
        ]
        + [struct((px, prow, width))] * (filt - 1),
        (*parts, *near_parts, jnp.swapaxes(w_deep, 1, 2).reshape(9, 3 * filters, width), cotangent),
        [
            pltpu.VMEM((px, dy + 2, dz, width), F32),
            pltpu.VMEM((9, filters, 3 * width), BF16),
            pltpu.VMEM((dx, dy + 2, dz, filters), F32),
            pltpu.VMEM((3, dx, dy * dz, 3 * filters), BF16),
            pltpu.VMEM((px, dy, dz, width), F32),
        ],
        flops=4 * dx * dy * dz * 27 * width * filters,
    )
    block_out, grad, deep_windows = deep[:3]
    terms = paired(deep[3:], "filt")

    deep_rows = ceil_to(-(-27 * filters // space), 16)
    deep_first, deep_second = call(
        deep_grad_body,
        "deep_grad",
        [struct((chips, deep_rows, width)), struct((chips, deep_rows, width), F32)],
        (deep_windows, grad),
        [pltpu.VMEM((2, chips * deep_rows, width), F32)],
        flops=2 * dx * dy * dz * 27 * width * filters,
    )
    deep_first, terms[-1] = lax.optimization_barrier((deep_first, terms[-1]))
    cuts = ((0, 5), (5, 9))
    steps = [3 * (end - begin) * (cin // 2) // chips for begin, end in cuts]
    flops = 2 * (nx + 4) * rows * 18 * cin * 2 * width
    helds = [pltpu.VMEM((step * chips, width), F32) for step in steps]

    def core_sums(name, mine, theirs):
        size = mine.shape[1:]
        shapes = [struct(size, F32)] + [struct(size)] * (chips - 1)
        return list(call(core_sum_body, name, shapes, (mine, theirs)))

    theirs, grad = call(
        functools.partial(early_grad_body, half, cuts[0]),
        "early_grad",
        [struct((chips, steps[0], width)), struct((nx + 4, rows, 2 * width))],
        (*backward(terms), sg, far_sg, turned),
        [helds[0], pltpu.VMEM((px, rows, 2 * width), F32)],
        flops=flops,
    )
    theirs = exchange(theirs, "space", 1)
    mine = call(
        functools.partial(early_grad_rest_body, True, cuts[0]),
        "early_grad_own",
        struct((chips, steps[0], width), F32),
        (grad, turned),
        [helds[0]],
        flops=flops,
    )
    sums = core_sums("core_sum", mine, theirs)
    grad, sums[0] = lax.optimization_barrier((grad, sums[0]))
    first = backward(paired(sums, "space", 2))
    size = (chips, steps[1] + deep_rows, width)
    theirs = call(
        functools.partial(early_grad_rest_body, False, cuts[1]),
        "early_grad_rest",
        struct(size),
        (grad, turned, deep_first),
        [helds[1]],
        flops=flops,
    )
    theirs = exchange(theirs, "space", 1)
    mine = call(
        functools.partial(early_grad_rest_body, True, cuts[1]),
        "early_grad_rest_own",
        struct(size, F32),
        (grad, turned, deep_second),
        [helds[1]],
        flops=flops,
    )
    sums = core_sums("core_sum_rest", mine, theirs)
    *sums, first = lax.optimization_barrier((*sums, first))
    second = backward(paired(sums, "space", 2))
    (early,) = call(
        functools.partial(chip_sum_body, chips), "chip_sum", [struct((steps[0], width))], first
    )
    first = backward(paired([early] * filt, "filt"))
    *second, first[0] = lax.optimization_barrier((*second, first[0]))
    early, deep = call(
        functools.partial(chip_sum_body, chips),
        "chip_sum_rest",
        [struct((steps[1], width)), struct((deep_rows, width))],
        second,
        flops=HOLD,
    )
    second = backward(paired([early] * filt, "filt"))
    *first, second[0] = lax.optimization_barrier((*first, second[0]))
    sum_body = functools.partial(filt_sum_body, filt)
    first = call(
        sum_body, "filt_sum", struct((steps[0] + deep_rows, width)), (*first, deep), flops=HOLD
    )
    first = paired([first] * chips, "space", 2)
    *second, first[0] = lax.optimization_barrier((*second, first[0]))
    second = call(
        sum_body, "filt_sum_rest", struct((steps[1], width)), second, flops=HOLD
    )
    late, first[1] = lax.optimization_barrier((second, first[1]))
    second = paired([second, late] + [second] * (chips - 2), "space", 2)

    own = call(
        functools.partial(stack_body, sum(steps)),
        "stack",
        struct((chips, sum(steps) + deep_rows, width)),
        (*first, *second),
    )
    other = exchange(own, "space", 1)
    early_total = nx * ny * nz * space * filt
    deep_total = dx * dy * dz * space
    results = [struct((27, cin, width), F32), struct((27, filters, width), F32)]
    scales = (1.0 / math.sqrt(early_total), 1.0 / math.sqrt(deep_total))
    scales += ((*steps, deep_rows), 3 * cuts[0][1])
    scratch = [
        pltpu.VMEM((27, cin // 2, width), F32),
        pltpu.VMEM((27, filters // 2, width), F32),
        DMA((9,)),
    ]
    results = call(
        functools.partial(finish_body, True, *scales),
        "finish_own",
        results,
        (own,),
        scratch,
        outs=HBM,
    )
    grad_early, grad_deep = call(
        functools.partial(finish_body, False, *scales),
        "finish_other",
        [struct(value.shape, F32) for value in results],
        (other, *results),
        scratch,
        hbm=(1, 2),
        outs=HBM,
        alias=((1, 0), (2, 1)),
    )
    return (block_out, grad_early, jnp.swapaxes(grad_deep, 1, 2))


def solution(mesh):
    return jax.shard_map(
        shards,
        mesh=mesh,
        in_specs=(
            P("space", "filt", None, None),
            P(),
            P(None, None, "filt"),
            P("space", None, None, "filt"),
        ),
        out_specs=(P("space", None, None, "filt"), P(), P(None, None, "filt")),
        check_vma=False,
    )
```

```python
import functools
import math

import jax
import jax.numpy as jnp
from jax import lax
from jax.experimental import pallas as pl
from jax.experimental.pallas import tpu as pltpu
from jax.sharding import PartitionSpec as P

F32 = jnp.float32
BF16 = jnp.bfloat16
HOLD = 1 << 32
VMEM_LIMIT = 24 * 1024 * 1024
VMEM = pl.BlockSpec(memory_space=pltpu.VMEM)
HBM = pl.BlockSpec(memory_space=pltpu.HBM)
DMA = pltpu.SemaphoreType.DMA


def call(
    body, name, out_shape, operands, scratch=(), flops=0, moved=1 << 20, hbm=(), outs=VMEM, alias=()
):
    return pl.pallas_call(
        body,
        name=name,
        out_shape=out_shape,
        in_specs=[HBM if i in hbm else VMEM for i in range(len(operands))],
        out_specs=outs if isinstance(outs, list) else jax.tree.map(lambda _: outs, out_shape),
        scratch_shapes=list(scratch),
        input_output_aliases=dict(alias),
        compiler_params=pltpu.CompilerParams(vmem_limit_bytes=VMEM_LIMIT),
        cost_estimate=pl.CostEstimate(flops=flops, bytes_accessed=moved, transcendentals=0),
    )(*operands)


def struct(shape, dtype=BF16):
    return jax.ShapeDtypeStruct(shape, dtype)


def ceil_to(value, step):
    return -(-value // step) * step


def sigmoid(value):
    return 1.0 / (1.0 + jnp.exp(-value))


def is_even(axis):
    return lax.rem(lax.axis_index(axis), 2) == 0


def edges_body(edges, copied):
    copied[...] = edges[...]


def has_both(axis):
    here = lax.axis_index(axis)
    return (here > 0) & (here < lax.axis_size(axis) - 1)


def spread_body(center, yeven, yodd, copied, sides, near, far):
    copied[...] = center[...]
    nx, ny, _, _ = center.shape
    even = is_even("filt")
    beyond = jnp.where(has_both("filt"), yodd[...], jnp.zeros(yodd.shape, BF16))
    sides[:, 0:1] = jnp.where(even, beyond[:, 1:2], yeven[:, 1:2])
    sides[:, 1:2] = jnp.where(even, yeven[:, 0:1], beyond[:, 0:1])
    odd = lax.rem(lax.axis_index("space"), 2)
    for out, start in ((near, (1 - odd) * (nx - 3)), (far, odd * (nx - 3))):
        rows = pl.ds(start, 3)
        out[:, 0:1] = sides[rows, 0:1]
        out[:, 1 : ny + 1] = center[rows]
        out[:, ny + 1 :] = sides[rows, 1:2]


def fill_windows(field, windows):
    count, wide_y, _, cin = field.shape
    ny = wide_y - 2
    half = windows.shape[2] // ny
    for x in range(count):
        for group in range(4):
            plane = field[x, :, pl.ds(7 + group, half, stride=2), :]
            for b in range(3):
                windows[b, x, :, group * cin : (group + 1) * cin] = (
                    plane[b : b + ny].reshape(ny * half, cin).astype(BF16)
                )


def clear_ends(field, nz):
    count, wide_y, _, cin = field.shape
    field[:, :, 0:8] = jnp.zeros((count, wide_y, 8, cin), F32)
    field[:, :, 8 + nz : 16 + nz] = jnp.zeros((count, wide_y, 8, cin), F32)


def early_rows_of(row_of, rows, wide, ny, keep):
    cout = wide.shape[2] // 2
    acc = jnp.zeros((2 * rows, 2 * cout), F32)
    for ab in range(9):
        a, b = ab // 3, ab % 3
        left = jnp.concatenate([row_of(b, a), row_of(b, a + 1)], axis=0)
        acc = acc + jnp.dot(left, wide[ab], preferred_element_type=F32)
    sig = sigmoid(acc)
    slope = (sig * (1.0 + acc * (1.0 - sig)) * keep).reshape(2, rows, 2 * cout)
    act = acc * sig
    act = act[:rows] + act[rows:]
    act = act[:, :cout] + act[:, cout:]
    act = act.reshape(ny // 2, 2, rows // ny, cout)
    act = (act[:, 0] + act[:, 1]) * keep
    return slope, act.reshape(rows // 2, cout).astype(BF16)


def near_body(center, sides, near, w, windows, sg, pooled, wide, field):
    nx, ny, nz, cin = center.shape
    cout = w.shape[2]
    for ab in range(9):
        for group in range(4):
            for side in range(2):
                tap = group - side
                value = w[3 * ab + tap] if 0 <= tap <= 2 else jnp.zeros((cin, cout), BF16)
                wide[
                    ab, group * cin : (group + 1) * cin, side * cout : (side + 1) * cout
                ] = value
    odd = lax.rem(lax.axis_index("space"), 2)
    clear_ends(field, nz)
    cells = slice(8, 8 + nz)
    own = pl.ds(3 * odd, nx)
    field[own, 1 : ny + 1, cells] = center[...].astype(F32)
    field[own, 0:1, cells] = sides[:, 0:1].astype(F32)
    field[own, ny + 1 :, cells] = sides[:, 1:2].astype(F32)
    field[pl.ds((1 - odd) * nx, 3), :, cells] = near[...].astype(F32)
    fill_windows(field, windows)
    for chunk in range(nx // 2):
        start = 1 - odd + 2 * chunk
        slope, pool = early_rows_of(
            lambda b, i: windows[b, start + i], windows.shape[2], wide, ny, 0.125
        )
        sg[2 * chunk : 2 * chunk + 2] = slope
        pooled[chunk] = pool


def far_body(windows, far, wide, far_windows, sg, pooled, field):
    _, wide_y, nz, _ = far.shape
    rows = windows.shape[2]
    odd = lax.rem(lax.axis_index("space"), 2)
    clear_ends(field, nz)
    inside = jnp.where(has_both("space"), 1.0, 0.0).astype(F32)
    field[:, :, 8 : 8 + nz] = far[...].astype(F32) * inside
    fill_windows(field, far_windows)

    def rows_for(parity):
        for chunk in range(2):

            def row_of(b, i):
                spot = 2 * chunk + i
                if (spot < 3) == (parity == 0):
                    return far_windows[b, spot % 3]
                return windows[b, spot % 3 + 4 * parity]

            keep = 0.125 * inside if chunk == parity else 0.125
            slope, pool = early_rows_of(row_of, rows, wide, wide_y - 2, keep)
            sg[2 * chunk : 2 * chunk + 2] = slope
            pooled[chunk] = pool

    @pl.when(odd == 0)
    def _():
        rows_for(0)

    @pl.when(odd == 1)
    def _():
        rows_for(1)


def transpose_body(windows, far_windows, turned):
    rows = windows.shape[2]
    part = turned.shape[2] // 4
    odd = lax.rem(lax.axis_index("space"), 2)
    for source, first in ((windows, 3 * (1 - odd)), (far_windows, windows.shape[1] * odd)):
        for b in range(3):
            for x in range(source.shape[1]):
                value = source[b, x].T
                spot = pl.multiple_of((first + x) * rows, rows)
                for group in range(4):
                    for side in range(2):
                        row = (2 * group + side) * part
                        turned[
                            b, side, group * part : (group + 1) * part, pl.ds(spot, rows)
                        ] = value[row : row + part]


def roll_z(value, shift):
    size = value.shape[-2]
    rolled = pltpu.roll(value, shift % size, value.ndim - 2)
    spot = lax.broadcasted_iota(jnp.int32, value.shape, value.ndim - 2)
    edge = 0 if shift == 1 else size - 1
    return jnp.where(spot == edge, 0.0, rolled)


def deep_body(parts_n, *refs):
    far, near, refs = refs[:parts_n], refs[parts_n : 2 * parts_n], refs[2 * parts_n :]
    wt, cot, block_out, grad, windows = refs[:5]
    sends = refs[5 : parts_n + 5]
    field, wide, slopes, turned, terms = refs[parts_n + 5 :]
    nx, ny, nz, filters = cot.shape
    width = wt.shape[2]
    rows = ny * nz
    py = ny // parts_n
    mine = lax.axis_index("filt")
    for ab in range(9):
        for c in range(3):
            wide[ab, :, c * width : (c + 1) * width] = wt[
                ab, c * filters : (c + 1) * filters
            ]
    field[:, 0:1] = jnp.zeros((nx + 2, 1, nz, width), F32)
    field[:, ny + 1 : ny + 2] = jnp.zeros((nx + 2, 1, nz, width), F32)
    odd = lax.rem(lax.axis_index("space"), 2)
    for parts, first in ((near, 2 * (1 - odd)), (far, 2 * odd)):
        for j in range(parts_n):
            spot = lax.bitwise_xor(mine, j) * py + 1
            field[pl.ds(first, 2), pl.ds(spot, py)] = (
                parts[-j][...].astype(F32).reshape(2, py, nz, width)
            )
    for x in range(nx + 2):
        plane = field[x]
        for c in range(3):
            moved = plane if c == 1 else roll_z(plane, 1 - c)
            for b in range(3):
                windows[b, x, :, c * width : (c + 1) * width] = (
                    moved[b : b + ny].reshape(rows, width).astype(BF16)
                )
    slopes[:, 0:1] = jnp.zeros((nx, 1, nz, filters), F32)
    slopes[:, ny + 1 :] = jnp.zeros((nx, 1, nz, filters), F32)
    acc = jnp.zeros((nx * rows, filters), F32)
    for ab in range(9):
        a, b = ab // 3, ab % 3
        left = windows[b, a : a + nx].reshape(nx * rows, 3 * width)
        acc = acc + lax.dot_general(
            left, wide[ab], (((1,), (1,)), ((), ())), preferred_element_type=F32
        )
    sig = sigmoid(acc)
    block_out[...] = (acc * sig).reshape(nx, ny, nz, filters).astype(BF16)
    slope = sig * (1.0 + acc * (1.0 - sig))
    value = (cot[...].astype(F32).reshape(nx * rows, filters) * slope).astype(BF16)
    grad[...] = value.reshape(nx, rows, filters)
    slopes[:, 1 : ny + 1] = value.astype(F32).reshape(nx, ny, nz, filters)
    for x in range(nx):
        plane = slopes[x]
        plane = jnp.concatenate([roll_z(plane, -1), plane, roll_z(plane, 1)], axis=2)
        for b in range(3):
            turned[b, x] = (
                plane[2 - b : 2 - b + ny].reshape(rows, 3 * filters).astype(BF16)
            )
    shares = []
    for a in range(3):
        total = jnp.zeros((nx * rows, width), F32)
        for b in range(3):
            left = turned[b].reshape(nx * rows, 3 * filters)
            total = total + jnp.dot(left, wt[3 * a + b], preferred_element_type=F32)
        shares.append(total.reshape(nx, ny, nz, width))
    for r in range(nx + 2):
        terms[r] = sum(shares[a][r - a] for a in range(3) if 0 <= r - a < nx)
    for j in range(parts_n):
        spot = lax.bitwise_xor(mine, j) * py
        value = terms[:, pl.ds(spot, py)]
        sends[j][...] = value.reshape(nx + 2, py * nz, width).astype(sends[j].dtype)


def deep_grad_body(windows, grad, theirs, mine, held):
    nx, rows, filters = grad.shape
    width = windows.shape[3] // 3
    turned = grad[...].reshape(nx * rows, filters).astype(F32).T.astype(BF16)
    chips, step, _ = mine.shape
    part = filters // 2
    total = 27 * part
    if chips * step > total:
        held[:, total:] = jnp.zeros((2, chips * step - total, width), F32)
    for ab in range(9):
        a, b = ab // 3, ab % 3
        value = jnp.dot(
            turned,
            windows[b, a : a + nx].reshape(nx * rows, 3 * width),
            preferred_element_type=F32,
        )
        for c in range(3):
            spot = (3 * ab + c) * part
            for side in range(2):
                held[side, spot : spot + part] = value[
                    side * part : (side + 1) * part, c * width : (c + 1) * width
                ]
    core = lax.rem(lax.axis_index("space"), 2)
    for q in range(chips):
        theirs[q] = held[1 - core, q * step : (q + 1) * step].astype(theirs.dtype)
        mine[q] = held[core, q * step : (q + 1) * step]


def early_grad_body(nz, taps, *refs):
    parts, (sg, far_sg, turned, out, grad, held, spread) = refs[:-7], refs[-7:]
    count, rows, wide = sg.shape
    total = parts[0][...]
    for part in parts[1:]:
        total = total + part[...].astype(F32)
    px, prow, _ = total.shape
    py = prow // nz
    total = jnp.concatenate([total, total], axis=2).reshape(px, py, 1, nz, wide)
    spread[...] = jnp.broadcast_to(total, (px, py, 2, nz, wide)).reshape(px, rows, wide)
    odd = lax.rem(lax.axis_index("space"), 2)
    for source, first in ((sg, count * (1 - odd)), (far_sg, count * odd)):
        for x in range(count):
            grad[first + x] = (spread[lax.div(first, 2) + x // 2] * source[x]).astype(BF16)
    early_grad_half(1 - odd, taps, grad, turned, out, held)


def early_grad_rest_body(own, taps, *refs):
    grad, turned, *deep, out, held = refs
    core = lax.rem(lax.axis_index("space"), 2)
    early_grad_half(core if own else 1 - core, taps, grad, turned, out, held)
    step = out.shape[1] - (deep[0].shape[1] if deep else 0)
    for ref in deep:
        out[:, step:] = ref[...].astype(out.dtype)


def early_grad_half(side, taps, grad, turned, out, held):
    ext, rows, wide = grad.shape
    width = wide // 2
    part = turned.shape[2] // 4
    right = grad[...].reshape(ext * rows, wide)
    for ab in range(*taps):
        a, b = ab // 3, ab % 3
        value = jnp.dot(
            turned[b, side, :, a * rows : (a + ext) * rows], right, preferred_element_type=F32
        )
        for c in range(3):
            spot = (3 * (ab - taps[0]) + c) * part
            held[spot : spot + part] = (
                value[c * part : (c + 1) * part, :width]
                + value[(c + 1) * part : (c + 2) * part, width:]
            )
    step = held.shape[0] // out.shape[0]
    for q in range(out.shape[0]):
        out[q, :step] = held[q * step : (q + 1) * step].astype(out.dtype)


def core_sum_body(mine, other, *outs):
    chip = lax.div(lax.axis_index("space"), 2)
    for j, out in enumerate(outs):
        q = lax.bitwise_xor(chip, j)
        out[...] = (mine[q] + other[q].astype(F32)).astype(out.dtype)


def chip_sum_body(count, *refs):
    others, outs = refs[:count], refs[count:]
    total = others[0][...]
    for ref in others[1:]:
        total = total + ref[...].astype(F32)
    row = 0
    for out in outs:
        size = out.shape[0]
        out[...] = total[row : row + size].astype(BF16)
        row += size


def filt_sum_body(count, *refs):
    parts, rest, out = refs[:count], refs[count:-1], refs[-1]
    values = [part[...].astype(F32) for part in backward(list(parts))]
    while len(values) > 1:
        values = [low + high for low, high in zip(values[::2], values[1::2])]
    size = values[0].shape[0]
    out[:size] = values[0].astype(BF16)
    for ref in rest:
        out[size:] = ref[...]


def stack_body(step, *refs):
    *parts, out = refs
    chips = out.shape[0]
    chip = lax.div(lax.axis_index("space"), 2)
    for j in range(chips):
        first, second = parts[j], parts[chips + j]
        q = lax.bitwise_xor(chip, j)
        cut = step - second.shape[0]
        out[q, :cut] = first[:cut]
        out[q, cut:step] = second[...]
        out[q, step:] = first[cut:]


def finish_body(own, early_scale, deep_scale, steps, cut, pieces, *refs):
    early, deep, early_held, deep_held, sem = refs[-5:]
    core = lax.rem(lax.axis_index("space"), 2)
    side = core if own else 1 - core
    copies = []
    first = 0
    for out, held, begin, end, step, scale in (
        (early, early_held, 0, cut, steps[0], early_scale),
        (early, early_held, cut, 27, steps[1], early_scale),
        (deep, deep_held, 0, 27, steps[2], deep_scale),
    ):
        part = held.shape[1]
        for tap in range(begin, end):
            row = (tap - begin) * part
            stop = row + part
            while row < stop:
                q, inner = row // step, row % step
                size = min(step - inner, stop - row)
                spot = part - (stop - row)
                held[tap, spot : spot + size] = (
                    pieces[q, first + inner : first + inner + size].astype(F32) * scale
                )
                row += size
            some = (end - begin) // 3
            if (tap + 1 - begin) % some == 0:
                taps = pl.ds(tap + 1 - some, some)
                copy = pltpu.make_async_copy(
                    held.at[taps], out.at[taps, pl.ds(side * part, part)], sem.at[len(copies)]
                )
                copy.start()
                copies.append(copy)
        first += step
    for copy in copies:
        copy.wait()


def paired(values, axis, step=1):
    count = lax.axis_size(axis)
    got = {
        j: lax.ppermute(values[j], axis, [(i, i ^ (step * j)) for i in range(count)])
        for j in reversed(range(1, len(values)))
    }
    return [values[0]] + [got[j] for j in range(1, len(values))]


def exchange(value, axis, step):
    return lax.ppermute(value, axis, [(i, i ^ step) for i in range(lax.axis_size(axis))])


def backward(values):
    return [values[0]] + values[:0:-1]


def swap(value, axis, first):
    count = lax.axis_size(axis)
    pairs = [(i, (i + 1) % count) for i in range(first, count, 2)]
    return lax.ppermute(value, axis, pairs + [(b, a) for a, b in pairs])


def shards(volume, w_early, w_deep, cotangent):
    nx, ny, nz, cin = volume.shape
    width = w_early.shape[2]
    filters = w_deep.shape[2]
    space = lax.axis_size("space")
    filt = lax.axis_size("filt")
    chips = space // 2
    half = nz // 2
    ext = nx + 6
    rows = ny * half
    edges = jnp.concatenate([volume[:, :1], volume[:, ny - 1 :]], axis=1)
    edges = call(edges_body, "edges", struct(edges.shape), (edges,), flops=1 << 32)
    yeven, yodd = swap(edges, "filt", 0), swap(edges, "filt", 1)
    rim = struct((3, ny + 2, nz, cin))
    volume, sides, near, far = call(
        spread_body,
        "spread",
        [struct(volume.shape), struct((nx, 2, nz, cin)), rim, rim],
        (volume, yeven, yodd),
        flops=HOLD,
        moved=1 << 24,
    )
    far = swap(far, "space", 1)
    near = swap(near, "space", 0)
    windows, sg, near_pooled, wide = call(
        near_body,
        "early_near",
        (
            struct((3, nx + 3, rows, 4 * cin)),
            struct((nx, rows, 2 * width), F32),
            struct((nx // 2, rows // 2, width)),
            struct((9, 4 * cin, 2 * width)),
        ),
        (volume, sides, near, w_early),
        [pltpu.VMEM((nx + 3, ny + 2, nz + 16, cin), F32)],
        flops=2 * nx * rows * 36 * cin * 2 * width,
    )
    near_parts = paired([near_pooled] * filt, "filt")
    far_windows, far_sg, pooled = call(
        far_body,
        "early_far",
        (
            struct((3, 3, rows, 4 * cin)),
            struct((nx, rows, 2 * width), F32),
            struct((nx // 2, rows // 2, width)),
        ),
        (windows, far, wide),
        [
            pltpu.VMEM((3, ny + 2, nz + 16, cin), F32),
        ],
        flops=2 * nx * rows * 36 * cin * 2 * width,
    )
    parts = backward(paired([pooled] * filt, "filt"))
    near_parts = backward(near_parts)
    windows, *near_parts = lax.optimization_barrier((windows, *near_parts))
    turned = call(
        transpose_body,
        "turn_windows",
        struct((3, 2, 2 * cin, ext * rows)),
        (windows, far_windows),
        flops=1 << 30,
    )
    *parts, turned = lax.optimization_barrier((*parts, turned))
    dx, dy, dz, _ = cotangent.shape
    px = dx + 2
    prow = rows // 2
    deep = call(
        functools.partial(deep_body, filt),
        "deep_conv",
        [
            struct(cotangent.shape),
            struct((dx, dy * dz, filters)),
            struct((3, px, dy * dz, 3 * width)),
            struct((px, prow, width), F32),
        ]
        + [struct((px, prow, width))] * (filt - 1),
        (*parts, *near_parts, jnp.swapaxes(w_deep, 1, 2).reshape(9, 3 * filters, width), cotangent),
        [
            pltpu.VMEM((px, dy + 2, dz, width), F32),
            pltpu.VMEM((9, filters, 3 * width), BF16),
            pltpu.VMEM((dx, dy + 2, dz, filters), F32),
            pltpu.VMEM((3, dx, dy * dz, 3 * filters), BF16),
            pltpu.VMEM((px, dy, dz, width), F32),
        ],
        flops=4 * dx * dy * dz * 27 * width * filters,
    )
    block_out, grad, deep_windows = deep[:3]
    terms = paired(deep[3:], "filt")

    deep_rows = ceil_to(-(-27 * filters // space), 16)
    deep_first, deep_second = call(
        deep_grad_body,
        "deep_grad",
        [struct((chips, deep_rows, width)), struct((chips, deep_rows, width), F32)],
        (deep_windows, grad),
        [pltpu.VMEM((2, chips * deep_rows, width), F32)],
        flops=2 * dx * dy * dz * 27 * width * filters,
    )
    deep_first, terms[-1] = lax.optimization_barrier((deep_first, terms[-1]))
    cuts = ((0, 5), (5, 9))
    steps = [3 * (end - begin) * (cin // 2) // chips for begin, end in cuts]
    flops = 2 * (nx + 4) * rows * 18 * cin * 2 * width
    helds = [pltpu.VMEM((step * chips, width), F32) for step in steps]

    def core_sums(name, mine, theirs):
        size = mine.shape[1:]
        shapes = [struct(size, F32)] + [struct(size)] * (chips - 1)
        return list(call(core_sum_body, name, shapes, (mine, theirs)))

    theirs, grad = call(
        functools.partial(early_grad_body, half, cuts[0]),
        "early_grad",
        [struct((chips, steps[0], width)), struct((nx + 4, rows, 2 * width))],
        (*backward(terms), sg, far_sg, turned),
        [helds[0], pltpu.VMEM((px, rows, 2 * width), F32)],
        flops=flops,
    )
    theirs = exchange(theirs, "space", 1)
    mine = call(
        functools.partial(early_grad_rest_body, True, cuts[0]),
        "early_grad_own",
        struct((chips, steps[0], width), F32),
        (grad, turned),
        [helds[0]],
        flops=flops,
    )
    sums = core_sums("core_sum", mine, theirs)
    grad, sums[0] = lax.optimization_barrier((grad, sums[0]))
    first = backward(paired(sums, "space", 2))
    size = (chips, steps[1] + deep_rows, width)
    theirs = call(
        functools.partial(early_grad_rest_body, False, cuts[1]),
        "early_grad_rest",
        struct(size),
        (grad, turned, deep_first),
        [helds[1]],
        flops=flops,
    )
    theirs = exchange(theirs, "space", 1)
    mine = call(
        functools.partial(early_grad_rest_body, True, cuts[1]),
        "early_grad_rest_own",
        struct(size, F32),
        (grad, turned, deep_second),
        [helds[1]],
        flops=flops,
    )
    sums = core_sums("core_sum_rest", mine, theirs)
    *sums, first = lax.optimization_barrier((*sums, first))
    second = backward(paired(sums, "space", 2))
    (early,) = call(
        functools.partial(chip_sum_body, chips), "chip_sum", [struct((steps[0], width))], first
    )
    first = backward(paired([early] * filt, "filt"))
    *second, first[0] = lax.optimization_barrier((*second, first[0]))
    early, deep = call(
        functools.partial(chip_sum_body, chips),
        "chip_sum_rest",
        [struct((steps[1], width)), struct((deep_rows, width))],
        second,
        flops=HOLD,
    )
    second = backward(paired([early] * filt, "filt"))
    *first, second[0] = lax.optimization_barrier((*first, second[0]))
    sum_body = functools.partial(filt_sum_body, filt)
    first = call(
        sum_body, "filt_sum", struct((steps[0] + deep_rows, width)), (*first, deep), flops=HOLD
    )
    first = paired([first] * chips, "space", 2)
    *second, first[0] = lax.optimization_barrier((*second, first[0]))
    second = call(
        sum_body, "filt_sum_rest", struct((steps[1], width)), second, flops=HOLD
    )
    late, first[1] = lax.optimization_barrier((second, first[1]))
    second = paired([second, late] + [second] * (chips - 2), "space", 2)

    own = call(
        functools.partial(stack_body, sum(steps)),
        "stack",
        struct((chips, sum(steps) + deep_rows, width)),
        (*first, *second),
    )
    other = exchange(own, "space", 1)
    early_total = nx * ny * nz * space * filt
    deep_total = dx * dy * dz * space
    results = [struct((27, cin, width), F32), struct((27, filters, width), F32)]
    scales = (1.0 / math.sqrt(early_total), 1.0 / math.sqrt(deep_total))
    scales += ((*steps, deep_rows), 3 * cuts[0][1])
    scratch = [
        pltpu.VMEM((27, cin // 2, width), F32),
        pltpu.VMEM((27, filters // 2, width), F32),
        DMA((9,)),
    ]
    results = call(
        functools.partial(finish_body, True, *scales),
        "finish_own",
        results,
        (own,),
        scratch,
        outs=HBM,
    )
    grad_early, grad_deep = call(
        functools.partial(finish_body, False, *scales),
        "finish_other",
        [struct(value.shape, F32) for value in results],
        (other, *results),
        scratch,
        hbm=(1, 2),
        outs=HBM,
        alias=((1, 0), (2, 1)),
    )
    return (block_out, grad_early, jnp.swapaxes(grad_deep, 1, 2))


def solution(mesh):
    return jax.shard_map(
        shards,
        mesh=mesh,
        in_specs=(
            P("space", "filt", None, None),
            P(),
            P(None, None, "filt"),
            P("space", None, None, "filt"),
        ),
        out_specs=(P("space", None, None, "filt"), P(), P(None, None, "filt")),
        check_vma=False,
    )
```

```python
import functools
import math

import jax
import jax.numpy as jnp
from jax import lax
from jax.experimental import pallas as pl
from jax.experimental.pallas import tpu as pltpu
from jax.sharding import PartitionSpec as P

F32 = jnp.float32
BF16 = jnp.bfloat16
HOLD = 1 << 32
VMEM_LIMIT = 24 * 1024 * 1024
VMEM = pl.BlockSpec(memory_space=pltpu.VMEM)
HBM = pl.BlockSpec(memory_space=pltpu.HBM)
DMA = pltpu.SemaphoreType.DMA


def call(
    body, name, out_shape, operands, scratch=(), flops=0, moved=1 << 20, hbm=(), outs=VMEM, alias=()
):
    return pl.pallas_call(
        body,
        name=name,
        out_shape=out_shape,
        in_specs=[HBM if i in hbm else VMEM for i in range(len(operands))],
        out_specs=outs if isinstance(outs, list) else jax.tree.map(lambda _: outs, out_shape),
        scratch_shapes=list(scratch),
        input_output_aliases=dict(alias),
        compiler_params=pltpu.CompilerParams(vmem_limit_bytes=VMEM_LIMIT),
        cost_estimate=pl.CostEstimate(flops=flops, bytes_accessed=moved, transcendentals=0),
    )(*operands)


def struct(shape, dtype=BF16):
    return jax.ShapeDtypeStruct(shape, dtype)


def ceil_to(value, step):
    return -(-value // step) * step


def sigmoid(value):
    return 1.0 / (1.0 + jnp.exp(-value))


def is_even(axis):
    return lax.rem(lax.axis_index(axis), 2) == 0


def edges_body(edges, copied):
    copied[...] = edges[...]


def has_both(axis):
    here = lax.axis_index(axis)
    return (here > 0) & (here < lax.axis_size(axis) - 1)


def spread_body(center, yeven, yodd, copied, sides, near, far):
    copied[...] = center[...]
    nx, ny, _, _ = center.shape
    even = is_even("filt")
    beyond = jnp.where(has_both("filt"), yodd[...], jnp.zeros(yodd.shape, BF16))
    sides[:, 0:1] = jnp.where(even, beyond[:, 1:2], yeven[:, 1:2])
    sides[:, 1:2] = jnp.where(even, yeven[:, 0:1], beyond[:, 0:1])
    odd = lax.rem(lax.axis_index("space"), 2)
    for out, start in ((near, (1 - odd) * (nx - 3)), (far, odd * (nx - 3))):
        rows = pl.ds(start, 3)
        out[:, 0:1] = sides[rows, 0:1]
        out[:, 1 : ny + 1] = center[rows]
        out[:, ny + 1 :] = sides[rows, 1:2]


def fill_windows(field, windows):
    count, wide_y, _, cin = field.shape
    ny = wide_y - 2
    half = windows.shape[2] // ny
    for x in range(count):
        for group in range(4):
            plane = field[x, :, pl.ds(7 + group, half, stride=2), :]
            for b in range(3):
                windows[b, x, :, group * cin : (group + 1) * cin] = (
                    plane[b : b + ny].reshape(ny * half, cin).astype(BF16)
                )


def clear_ends(field, nz):
    count, wide_y, _, cin = field.shape
    field[:, :, 0:8] = jnp.zeros((count, wide_y, 8, cin), F32)
    field[:, :, 8 + nz : 16 + nz] = jnp.zeros((count, wide_y, 8, cin), F32)


def early_rows_of(windows, start, wide, ny, keep):
    rows = windows.shape[2]
    cout = wide.shape[2] // 2
    slopes, acts = [], []
    for row in range(2):
        acc = jnp.zeros((rows, 2 * cout), F32)
        for ab in range(9):
            a, b = ab // 3, ab % 3
            acc = acc + jnp.dot(
                windows[b, start + a + row], wide[ab], preferred_element_type=F32
            )
        sig = sigmoid(acc)
        slopes.append(sig * (1.0 + acc * (1.0 - sig)) * keep)
        act = acc * sig
        acts.append(act[:, :cout] + act[:, cout:])
    act = (acts[0] + acts[1]).reshape(ny // 2, 2, rows // ny, cout)
    act = (act[:, 0] + act[:, 1]) * keep
    return slopes, act.reshape(rows // 2, cout).astype(BF16)


def near_body(center, sides, near, w, windows, sg, pooled, wide, field):
    nx, ny, nz, cin = center.shape
    cout = w.shape[2]
    for ab in range(9):
        for group in range(4):
            for side in range(2):
                tap = group - side
                value = w[3 * ab + tap] if 0 <= tap <= 2 else jnp.zeros((cin, cout), BF16)
                wide[
                    ab, group * cin : (group + 1) * cin, side * cout : (side + 1) * cout
                ] = value
    odd = lax.rem(lax.axis_index("space"), 2)
    clear_ends(field, nz)
    cells = slice(8, 8 + nz)
    own = pl.ds(3 * odd, nx)
    field[own, 1 : ny + 1, cells] = center[...].astype(F32)
    field[own, 0:1, cells] = sides[:, 0:1].astype(F32)
    field[own, ny + 1 :, cells] = sides[:, 1:2].astype(F32)
    field[pl.ds((1 - odd) * nx, 3), :, cells] = near[...].astype(F32)
    fill_windows(field, windows)
    for chunk in range(nx // 2):
        slope, pool = early_rows_of(windows, 1 - odd + 2 * chunk, wide, ny, 0.125)
        for row in range(2):
            sg[2 * chunk + row] = slope[row]
        pooled[chunk] = pool


def far_body(windows, far, wide, far_windows, sg, pooled, field, held):
    _, wide_y, nz, _ = far.shape
    odd = lax.rem(lax.axis_index("space"), 2)
    clear_ends(field, nz)
    inside = jnp.where(has_both("space"), 1.0, 0.0).astype(F32)
    field[:, :, 8 : 8 + nz] = far[...].astype(F32) * inside
    fill_windows(field, far_windows)
    for b in range(3):
        held[b, pl.ds(3 * odd, 3)] = far_windows[b]
        held[b, pl.ds(3 - 3 * odd, 3)] = windows[b, pl.ds(4 * odd, 3)]
    first = jnp.where(odd == 0, inside, 1.0)
    second = jnp.where(odd == 1, inside, 1.0)
    for chunk, flag in enumerate((first, second)):
        slope, pool = early_rows_of(held, 2 * chunk, wide, wide_y - 2, 0.125 * flag)
        for row in range(2):
            sg[2 * chunk + row] = slope[row]
        pooled[chunk] = pool


def transpose_body(windows, far_windows, turned):
    rows = windows.shape[2]
    part = turned.shape[2] // 4
    odd = lax.rem(lax.axis_index("space"), 2)
    for source, first in ((windows, 3 * (1 - odd)), (far_windows, windows.shape[1] * odd)):
        for b in range(3):
            for x in range(source.shape[1]):
                value = source[b, x].T
                spot = pl.multiple_of((first + x) * rows, rows)
                for group in range(4):
                    for side in range(2):
                        row = (2 * group + side) * part
                        turned[
                            b, side, group * part : (group + 1) * part, pl.ds(spot, rows)
                        ] = value[row : row + part]


def roll_z(value, shift):
    size = value.shape[-2]
    rolled = pltpu.roll(value, shift % size, value.ndim - 2)
    spot = lax.broadcasted_iota(jnp.int32, value.shape, value.ndim - 2)
    edge = 0 if shift == 1 else size - 1
    return jnp.where(spot == edge, 0.0, rolled)


def deep_body(parts_n, *refs):
    far, near, refs = refs[:parts_n], refs[parts_n : 2 * parts_n], refs[2 * parts_n :]
    wt, cot, block_out, grad, windows = refs[:5]
    sends = refs[5 : parts_n + 5]
    field, wide, slopes, turned, terms = refs[parts_n + 5 :]
    nx, ny, nz, filters = cot.shape
    width = wt.shape[2]
    rows = ny * nz
    py = ny // parts_n
    mine = lax.axis_index("filt")
    for ab in range(9):
        for c in range(3):
            wide[ab, :, c * width : (c + 1) * width] = wt[
                ab, c * filters : (c + 1) * filters
            ]
    field[:, 0:1] = jnp.zeros((nx + 2, 1, nz, width), F32)
    field[:, ny + 1 : ny + 2] = jnp.zeros((nx + 2, 1, nz, width), F32)
    odd = lax.rem(lax.axis_index("space"), 2)
    for parts, first in ((near, 2 * (1 - odd)), (far, 2 * odd)):
        for j in range(parts_n):
            spot = lax.bitwise_xor(mine, j) * py + 1
            field[pl.ds(first, 2), pl.ds(spot, py)] = (
                parts[-j][...].astype(F32).reshape(2, py, nz, width)
            )
    for x in range(nx + 2):
        plane = field[x]
        for c in range(3):
            moved = plane if c == 1 else roll_z(plane, 1 - c)
            for b in range(3):
                windows[b, x, :, c * width : (c + 1) * width] = (
                    moved[b : b + ny].reshape(rows, width).astype(BF16)
                )
    slopes[:, 0:1] = jnp.zeros((nx, 1, nz, filters), F32)
    slopes[:, ny + 1 :] = jnp.zeros((nx, 1, nz, filters), F32)
    for x in range(nx):
        acc = jnp.zeros((rows, filters), F32)
        for ab in range(9):
            a, b = ab // 3, ab % 3
            acc = acc + lax.dot_general(
                windows[b, x + a], wide[ab], (((1,), (1,)), ((), ())), preferred_element_type=F32
            )
        sig = sigmoid(acc)
        block_out[x] = (acc * sig).reshape(ny, nz, filters).astype(BF16)
        slope = sig * (1.0 + acc * (1.0 - sig))
        value = (cot[x].astype(F32).reshape(rows, filters) * slope).astype(BF16)
        grad[x] = value
        slopes[x, 1 : ny + 1] = value.astype(F32).reshape(ny, nz, filters)
    for x in range(nx):
        plane = slopes[x]
        plane = jnp.concatenate([roll_z(plane, -1), plane, roll_z(plane, 1)], axis=2)
        for b in range(3):
            turned[b, x] = (
                plane[2 - b : 2 - b + ny].reshape(rows, 3 * filters).astype(BF16)
            )
    for r in range(nx + 2):
        total = jnp.zeros((rows, width), F32)
        for ab in range(9):
            a, b = ab // 3, ab % 3
            if 0 <= r - a < nx:
                total = total + jnp.dot(turned[b, r - a], wt[ab], preferred_element_type=F32)
        terms[r] = total.reshape(ny, nz, width)
    for j in range(parts_n):
        spot = lax.bitwise_xor(mine, j) * py
        value = terms[:, pl.ds(spot, py)]
        sends[j][...] = value.reshape(nx + 2, py * nz, width).astype(sends[j].dtype)


def deep_grad_body(windows, grad, theirs, mine, held):
    nx, rows, filters = grad.shape
    width = windows.shape[3] // 3
    turned = grad[...].reshape(nx * rows, filters).astype(F32).T.astype(BF16)
    chips, step, _ = mine.shape
    part = filters // 2
    total = 27 * part
    if chips * step > total:
        held[:, total:] = jnp.zeros((2, chips * step - total, width), F32)
    for ab in range(9):
        a, b = ab // 3, ab % 3
        value = jnp.dot(
            turned,
            windows[b, a : a + nx].reshape(nx * rows, 3 * width),
            preferred_element_type=F32,
        )
        for c in range(3):
            spot = (3 * ab + c) * part
            for side in range(2):
                held[side, spot : spot + part] = value[
                    side * part : (side + 1) * part, c * width : (c + 1) * width
                ]
    core = lax.rem(lax.axis_index("space"), 2)
    for q in range(chips):
        theirs[q] = held[1 - core, q * step : (q + 1) * step].astype(theirs.dtype)
        mine[q] = held[core, q * step : (q + 1) * step]


def early_grad_body(nz, taps, *refs):
    parts, (sg, far_sg, turned, out, grad, held, spread) = refs[:-7], refs[-7:]
    count, rows, wide = sg.shape
    total = parts[0][...]
    for part in parts[1:]:
        total = total + part[...].astype(F32)
    px, prow, _ = total.shape
    py = prow // nz
    total = jnp.concatenate([total, total], axis=2).reshape(px, py, 1, nz, wide)
    spread[...] = jnp.broadcast_to(total, (px, py, 2, nz, wide)).reshape(px, rows, wide)
    odd = lax.rem(lax.axis_index("space"), 2)
    for source, first in ((sg, count * (1 - odd)), (far_sg, count * odd)):
        for x in range(count):
            grad[first + x] = (spread[lax.div(first, 2) + x // 2] * source[x]).astype(BF16)
    early_grad_half(1 - odd, taps, grad, turned, out, held)


def early_grad_rest_body(own, taps, *refs):
    grad, turned, *deep, out, held = refs
    core = lax.rem(lax.axis_index("space"), 2)
    early_grad_half(core if own else 1 - core, taps, grad, turned, out, held)
    step = out.shape[1] - (deep[0].shape[1] if deep else 0)
    for ref in deep:
        out[:, step:] = ref[...].astype(out.dtype)


def early_grad_half(side, taps, grad, turned, out, held):
    ext, rows, wide = grad.shape
    width = wide // 2
    part = turned.shape[2] // 4
    right = grad[...].reshape(ext * rows, wide)
    for ab in range(*taps):
        a, b = ab // 3, ab % 3
        value = jnp.dot(
            turned[b, side, :, a * rows : (a + ext) * rows], right, preferred_element_type=F32
        )
        for c in range(3):
            spot = (3 * (ab - taps[0]) + c) * part
            held[spot : spot + part] = (
                value[c * part : (c + 1) * part, :width]
                + value[(c + 1) * part : (c + 2) * part, width:]
            )
    step = held.shape[0] // out.shape[0]
    for q in range(out.shape[0]):
        out[q, :step] = held[q * step : (q + 1) * step].astype(out.dtype)


def core_sum_body(mine, other, *outs):
    chip = lax.div(lax.axis_index("space"), 2)
    for j, out in enumerate(outs):
        q = lax.bitwise_xor(chip, j)
        out[...] = (mine[q] + other[q].astype(F32)).astype(out.dtype)


def chip_sum_body(count, *refs):
    others, outs = refs[:count], refs[count:]
    total = others[0][...]
    for ref in others[1:]:
        total = total + ref[...].astype(F32)
    row = 0
    for out in outs:
        size = out.shape[0]
        out[...] = total[row : row + size].astype(BF16)
        row += size


def filt_sum_body(count, *refs):
    parts, rest, out = refs[:count], refs[count:-1], refs[-1]
    values = [part[...].astype(F32) for part in backward(list(parts))]
    while len(values) > 1:
        values = [low + high for low, high in zip(values[::2], values[1::2])]
    size = values[0].shape[0]
    out[:size] = values[0].astype(BF16)
    for ref in rest:
        out[size:] = ref[...]


def stack_body(step, *refs):
    *parts, out = refs
    chips = out.shape[0]
    chip = lax.div(lax.axis_index("space"), 2)
    for j in range(chips):
        first, second = parts[j], parts[chips + j]
        q = lax.bitwise_xor(chip, j)
        cut = step - second.shape[0]
        out[q, :cut] = first[:cut]
        out[q, cut:step] = second[...]
        out[q, step:] = first[cut:]


def finish_body(own, early_scale, deep_scale, steps, cut, pieces, *refs):
    early, deep, early_held, deep_held, sem = refs[-5:]
    core = lax.rem(lax.axis_index("space"), 2)
    side = core if own else 1 - core
    copies = []
    first = 0
    for out, held, begin, end, step, scale in (
        (early, early_held, 0, cut, steps[0], early_scale),
        (early, early_held, cut, 27, steps[1], early_scale),
        (deep, deep_held, 0, 27, steps[2], deep_scale),
    ):
        part = held.shape[1]
        for tap in range(begin, end):
            row = (tap - begin) * part
            stop = row + part
            while row < stop:
                q, inner = row // step, row % step
                size = min(step - inner, stop - row)
                spot = part - (stop - row)
                held[tap, spot : spot + size] = (
                    pieces[q, first + inner : first + inner + size].astype(F32) * scale
                )
                row += size
            some = (end - begin) // 3
            if (tap + 1 - begin) % some == 0:
                taps = pl.ds(tap + 1 - some, some)
                copy = pltpu.make_async_copy(
                    held.at[taps], out.at[taps, pl.ds(side * part, part)], sem.at[len(copies)]
                )
                copy.start()
                copies.append(copy)
        first += step
    for copy in copies:
        copy.wait()


def paired(values, axis, step=1):
    count = lax.axis_size(axis)
    got = {
        j: lax.ppermute(values[j], axis, [(i, i ^ (step * j)) for i in range(count)])
        for j in reversed(range(1, len(values)))
    }
    return [values[0]] + [got[j] for j in range(1, len(values))]


def exchange(value, axis, step):
    return lax.ppermute(value, axis, [(i, i ^ step) for i in range(lax.axis_size(axis))])


def backward(values):
    return [values[0]] + values[:0:-1]


def swap(value, axis, first):
    count = lax.axis_size(axis)
    pairs = [(i, (i + 1) % count) for i in range(first, count, 2)]
    return lax.ppermute(value, axis, pairs + [(b, a) for a, b in pairs])


def shards(volume, w_early, w_deep, cotangent):
    nx, ny, nz, cin = volume.shape
    width = w_early.shape[2]
    filters = w_deep.shape[2]
    space = lax.axis_size("space")
    filt = lax.axis_size("filt")
    chips = space // 2
    half = nz // 2
    ext = nx + 6
    rows = ny * half
    edges = jnp.concatenate([volume[:, :1], volume[:, ny - 1 :]], axis=1)
    edges = call(edges_body, "edges", struct(edges.shape), (edges,), flops=1 << 32)
    yeven, yodd = swap(edges, "filt", 0), swap(edges, "filt", 1)
    rim = struct((3, ny + 2, nz, cin))
    volume, sides, near, far = call(
        spread_body,
        "spread",
        [struct(volume.shape), struct((nx, 2, nz, cin)), rim, rim],
        (volume, yeven, yodd),
        flops=HOLD,
        moved=1 << 24,
    )
    far = swap(far, "space", 1)
    near = swap(near, "space", 0)
    windows, sg, near_pooled, wide = call(
        near_body,
        "early_near",
        (
            struct((3, nx + 3, rows, 4 * cin)),
            struct((nx, rows, 2 * width), F32),
            struct((nx // 2, rows // 2, width)),
            struct((9, 4 * cin, 2 * width)),
        ),
        (volume, sides, near, w_early),
        [pltpu.VMEM((nx + 3, ny + 2, nz + 16, cin), F32)],
        flops=2 * nx * rows * 36 * cin * 2 * width,
    )
    near_parts = paired([near_pooled] * filt, "filt")
    far_windows, far_sg, pooled = call(
        far_body,
        "early_far",
        (
            struct((3, 3, rows, 4 * cin)),
            struct((nx, rows, 2 * width), F32),
            struct((nx // 2, rows // 2, width)),
        ),
        (windows, far, wide),
        [
            pltpu.VMEM((3, ny + 2, nz + 16, cin), F32),
            pltpu.VMEM((3, 6, rows, 4 * cin), BF16),
        ],
        flops=2 * nx * rows * 36 * cin * 2 * width,
    )
    parts = backward(paired([pooled] * filt, "filt"))
    near_parts = backward(near_parts)
    windows, *near_parts = lax.optimization_barrier((windows, *near_parts))
    turned = call(
        transpose_body,
        "turn_windows",
        struct((3, 2, 2 * cin, ext * rows)),
        (windows, far_windows),
        flops=1 << 30,
    )
    *parts, turned = lax.optimization_barrier((*parts, turned))
    dx, dy, dz, _ = cotangent.shape
    px = dx + 2
    prow = rows // 2
    deep = call(
        functools.partial(deep_body, filt),
        "deep_conv",
        [
            struct(cotangent.shape),
            struct((dx, dy * dz, filters)),
            struct((3, px, dy * dz, 3 * width)),
            struct((px, prow, width), F32),
        ]
        + [struct((px, prow, width))] * (filt - 1),
        (*parts, *near_parts, jnp.swapaxes(w_deep, 1, 2).reshape(9, 3 * filters, width), cotangent),
        [
            pltpu.VMEM((px, dy + 2, dz, width), F32),
            pltpu.VMEM((9, filters, 3 * width), BF16),
            pltpu.VMEM((dx, dy + 2, dz, filters), F32),
            pltpu.VMEM((3, dx, dy * dz, 3 * filters), BF16),
            pltpu.VMEM((px, dy, dz, width), F32),
        ],
        flops=4 * dx * dy * dz * 27 * width * filters,
    )
    block_out, grad, deep_windows = deep[:3]
    terms = paired(deep[3:], "filt")

    deep_rows = ceil_to(-(-27 * filters // space), 16)
    deep_first, deep_second = call(
        deep_grad_body,
        "deep_grad",
        [struct((chips, deep_rows, width)), struct((chips, deep_rows, width), F32)],
        (deep_windows, grad),
        [pltpu.VMEM((2, chips * deep_rows, width), F32)],
        flops=2 * dx * dy * dz * 27 * width * filters,
    )
    deep_first, terms[-1] = lax.optimization_barrier((deep_first, terms[-1]))
    cuts = ((0, 5), (5, 9))
    steps = [3 * (end - begin) * (cin // 2) // chips for begin, end in cuts]
    flops = 2 * (nx + 4) * rows * 18 * cin * 2 * width
    helds = [pltpu.VMEM((step * chips, width), F32) for step in steps]

    def core_sums(name, mine, theirs):
        size = mine.shape[1:]
        shapes = [struct(size, F32)] + [struct(size)] * (chips - 1)
        return list(call(core_sum_body, name, shapes, (mine, theirs)))

    theirs, grad = call(
        functools.partial(early_grad_body, half, cuts[0]),
        "early_grad",
        [struct((chips, steps[0], width)), struct((nx + 4, rows, 2 * width))],
        (*backward(terms), sg, far_sg, turned),
        [helds[0], pltpu.VMEM((px, rows, 2 * width), F32)],
        flops=flops,
    )
    theirs = exchange(theirs, "space", 1)
    mine = call(
        functools.partial(early_grad_rest_body, True, cuts[0]),
        "early_grad_own",
        struct((chips, steps[0], width), F32),
        (grad, turned),
        [helds[0]],
        flops=flops,
    )
    sums = core_sums("core_sum", mine, theirs)
    grad, sums[0] = lax.optimization_barrier((grad, sums[0]))
    first = backward(paired(sums, "space", 2))
    size = (chips, steps[1] + deep_rows, width)
    theirs = call(
        functools.partial(early_grad_rest_body, False, cuts[1]),
        "early_grad_rest",
        struct(size),
        (grad, turned, deep_first),
        [helds[1]],
        flops=flops,
    )
    theirs = exchange(theirs, "space", 1)
    mine = call(
        functools.partial(early_grad_rest_body, True, cuts[1]),
        "early_grad_rest_own",
        struct(size, F32),
        (grad, turned, deep_second),
        [helds[1]],
        flops=flops,
    )
    sums = core_sums("core_sum_rest", mine, theirs)
    *sums, first = lax.optimization_barrier((*sums, first))
    second = backward(paired(sums, "space", 2))
    (early,) = call(
        functools.partial(chip_sum_body, chips), "chip_sum", [struct((steps[0], width))], first
    )
    first = backward(paired([early] * filt, "filt"))
    *second, first[0] = lax.optimization_barrier((*second, first[0]))
    early, deep = call(
        functools.partial(chip_sum_body, chips),
        "chip_sum_rest",
        [struct((steps[1], width)), struct((deep_rows, width))],
        second,
        flops=HOLD,
    )
    second = backward(paired([early] * filt, "filt"))
    *first, second[0] = lax.optimization_barrier((*first, second[0]))
    sum_body = functools.partial(filt_sum_body, filt)
    first = call(
        sum_body, "filt_sum", struct((steps[0] + deep_rows, width)), (*first, deep), flops=HOLD
    )
    first = paired([first] * chips, "space", 2)
    *second, first[0] = lax.optimization_barrier((*second, first[0]))
    second = call(
        sum_body, "filt_sum_rest", struct((steps[1], width)), second, flops=HOLD
    )
    late, first[1] = lax.optimization_barrier((second, first[1]))
    second = paired([second, late] + [second] * (chips - 2), "space", 2)

    own = call(
        functools.partial(stack_body, sum(steps)),
        "stack",
        struct((chips, sum(steps) + deep_rows, width)),
        (*first, *second),
    )
    other = exchange(own, "space", 1)
    early_total = nx * ny * nz * space * filt
    deep_total = dx * dy * dz * space
    results = [struct((27, cin, width), F32), struct((27, filters, width), F32)]
    scales = (1.0 / math.sqrt(early_total), 1.0 / math.sqrt(deep_total))
    scales += ((*steps, deep_rows), 3 * cuts[0][1])
    scratch = [
        pltpu.VMEM((27, cin // 2, width), F32),
        pltpu.VMEM((27, filters // 2, width), F32),
        DMA((9,)),
    ]
    results = call(
        functools.partial(finish_body, True, *scales),
        "finish_own",
        results,
        (own,),
        scratch,
        outs=HBM,
    )
    grad_early, grad_deep = call(
        functools.partial(finish_body, False, *scales),
        "finish_other",
        [struct(value.shape, F32) for value in results],
        (other, *results),
        scratch,
        hbm=(1, 2),
        outs=HBM,
        alias=((1, 0), (2, 1)),
    )
    return (block_out, grad_early, jnp.swapaxes(grad_deep, 1, 2))


def solution(mesh):
    return jax.shard_map(
        shards,
        mesh=mesh,
        in_specs=(
            P("space", "filt", None, None),
            P(),
            P(None, None, "filt"),
            P("space", None, None, "filt"),
        ),
        out_specs=(P("space", None, None, "filt"), P(), P(None, None, "filt")),
        check_vma=False,
    )
```

```python
import functools
import math

import jax
import jax.numpy as jnp
from jax import lax
from jax.experimental import pallas as pl
from jax.experimental.pallas import tpu as pltpu
from jax.sharding import PartitionSpec as P

F32 = jnp.float32
BF16 = jnp.bfloat16
HOLD = 1 << 32
VMEM_LIMIT = 24 * 1024 * 1024
VMEM = pl.BlockSpec(memory_space=pltpu.VMEM)
HBM = pl.BlockSpec(memory_space=pltpu.HBM)
DMA = pltpu.SemaphoreType.DMA


def call(
    body, name, out_shape, operands, scratch=(), flops=0, moved=1 << 20, hbm=(), outs=VMEM, alias=()
):
    return pl.pallas_call(
        body,
        name=name,
        out_shape=out_shape,
        in_specs=[HBM if i in hbm else VMEM for i in range(len(operands))],
        out_specs=outs if isinstance(outs, list) else jax.tree.map(lambda _: outs, out_shape),
        scratch_shapes=list(scratch),
        input_output_aliases=dict(alias),
        compiler_params=pltpu.CompilerParams(vmem_limit_bytes=VMEM_LIMIT),
        cost_estimate=pl.CostEstimate(flops=flops, bytes_accessed=moved, transcendentals=0),
    )(*operands)


def struct(shape, dtype=BF16):
    return jax.ShapeDtypeStruct(shape, dtype)


def ceil_to(value, step):
    return -(-value // step) * step


def sigmoid(value):
    return 1.0 / (1.0 + jnp.exp(-value))


def is_even(axis):
    return lax.rem(lax.axis_index(axis), 2) == 0


def edges_body(edges, copied):
    copied[...] = edges[...]


def has_both(axis):
    here = lax.axis_index(axis)
    return (here > 0) & (here < lax.axis_size(axis) - 1)


def spread_body(center, yeven, yodd, copied, sides, near, far):
    copied[...] = center[...]
    nx, ny, _, _ = center.shape
    even = is_even("filt")
    beyond = jnp.where(has_both("filt"), yodd[...], jnp.zeros(yodd.shape, BF16))
    sides[:, 0:1] = jnp.where(even, beyond[:, 1:2], yeven[:, 1:2])
    sides[:, 1:2] = jnp.where(even, yeven[:, 0:1], beyond[:, 0:1])
    odd = lax.rem(lax.axis_index("space"), 2)
    for out, start in ((near, (1 - odd) * (nx - 3)), (far, odd * (nx - 3))):
        rows = pl.ds(start, 3)
        out[:, 0:1] = sides[rows, 0:1]
        out[:, 1 : ny + 1] = center[rows]
        out[:, ny + 1 :] = sides[rows, 1:2]


def fill_windows(field, windows):
    count, wide_y, _, cin = field.shape
    ny = wide_y - 2
    half = windows.shape[2] // ny
    for x in range(count):
        for group in range(4):
            plane = field[x, :, pl.ds(7 + group, half, stride=2), :]
            for b in range(3):
                windows[b, x, :, group * cin : (group + 1) * cin] = (
                    plane[b : b + ny].reshape(ny * half, cin).astype(BF16)
                )


def clear_ends(field, nz):
    count, wide_y, _, cin = field.shape
    field[:, :, 0:8] = jnp.zeros((count, wide_y, 8, cin), F32)
    field[:, :, 8 + nz : 16 + nz] = jnp.zeros((count, wide_y, 8, cin), F32)


def early_rows_of(windows, start, wide, ny, keep):
    rows = windows.shape[2]
    cout = wide.shape[2] // 2
    acc = jnp.zeros((2 * rows, 2 * cout), F32)
    for ab in range(9):
        a, b = ab // 3, ab % 3
        left = windows[b, pl.ds(start + a, 2)].reshape(2 * rows, windows.shape[3])
        acc = acc + jnp.dot(left, wide[ab], preferred_element_type=F32)
    sig = sigmoid(acc)
    slope = (sig * (1.0 + acc * (1.0 - sig)) * keep).reshape(2, rows, 2 * cout)
    act = acc * sig
    act = act[:rows] + act[rows:]
    act = act[:, :cout] + act[:, cout:]
    act = act.reshape(ny // 2, 2, rows // ny, cout)
    act = (act[:, 0] + act[:, 1]) * keep
    return slope, act.reshape(rows // 2, cout).astype(BF16)


def near_body(center, sides, near, w, windows, sg, pooled, wide, field):
    nx, ny, nz, cin = center.shape
    cout = w.shape[2]
    for ab in range(9):
        for group in range(4):
            for side in range(2):
                tap = group - side
                value = w[3 * ab + tap] if 0 <= tap <= 2 else jnp.zeros((cin, cout), BF16)
                wide[
                    ab, group * cin : (group + 1) * cin, side * cout : (side + 1) * cout
                ] = value
    odd = lax.rem(lax.axis_index("space"), 2)
    clear_ends(field, nz)
    cells = slice(8, 8 + nz)
    own = pl.ds(3 * odd, nx)
    field[own, 1 : ny + 1, cells] = center[...].astype(F32)
    field[own, 0:1, cells] = sides[:, 0:1].astype(F32)
    field[own, ny + 1 :, cells] = sides[:, 1:2].astype(F32)
    field[pl.ds((1 - odd) * nx, 3), :, cells] = near[...].astype(F32)
    fill_windows(field, windows)
    for chunk in range(nx // 2):
        slope, pool = early_rows_of(windows, 1 - odd + 2 * chunk, wide, ny, 0.125)
        sg[2 * chunk : 2 * chunk + 2] = slope
        pooled[chunk] = pool


def far_body(windows, far, wide, far_windows, sg, pooled, field, held):
    _, wide_y, nz, _ = far.shape
    odd = lax.rem(lax.axis_index("space"), 2)
    clear_ends(field, nz)
    inside = jnp.where(has_both("space"), 1.0, 0.0).astype(F32)
    field[:, :, 8 : 8 + nz] = far[...].astype(F32) * inside
    fill_windows(field, far_windows)
    for b in range(3):
        held[b, pl.ds(3 * odd, 3)] = far_windows[b]
        held[b, pl.ds(3 - 3 * odd, 3)] = windows[b, pl.ds(4 * odd, 3)]
    first = jnp.where(odd == 0, inside, 1.0)
    second = jnp.where(odd == 1, inside, 1.0)
    for chunk, flag in enumerate((first, second)):
        slope, pool = early_rows_of(held, 2 * chunk, wide, wide_y - 2, 0.125 * flag)
        sg[2 * chunk : 2 * chunk + 2] = slope
        pooled[chunk] = pool


def transpose_body(windows, far_windows, turned):
    rows = windows.shape[2]
    part = turned.shape[2] // 4
    odd = lax.rem(lax.axis_index("space"), 2)
    for source, first in ((windows, 3 * (1 - odd)), (far_windows, windows.shape[1] * odd)):
        for b in range(3):
            for x in range(source.shape[1]):
                value = source[b, x].T
                spot = pl.multiple_of((first + x) * rows, rows)
                for group in range(4):
                    for side in range(2):
                        row = (2 * group + side) * part
                        turned[
                            b, side, group * part : (group + 1) * part, pl.ds(spot, rows)
                        ] = value[row : row + part]


def roll_z(value, shift):
    size = value.shape[-2]
    rolled = pltpu.roll(value, shift % size, value.ndim - 2)
    spot = lax.broadcasted_iota(jnp.int32, value.shape, value.ndim - 2)
    edge = 0 if shift == 1 else size - 1
    return jnp.where(spot == edge, 0.0, rolled)


def deep_body(parts_n, *refs):
    far, near, refs = refs[:parts_n], refs[parts_n : 2 * parts_n], refs[2 * parts_n :]
    wt, cot, block_out, grad, windows = refs[:5]
    sends = refs[5 : parts_n + 5]
    field, wide, slopes, turned, terms = refs[parts_n + 5 :]
    nx, ny, nz, filters = cot.shape
    width = wt.shape[2]
    rows = ny * nz
    py = ny // parts_n
    mine = lax.axis_index("filt")
    for ab in range(9):
        for c in range(3):
            wide[ab, :, c * width : (c + 1) * width] = wt[
                ab, c * filters : (c + 1) * filters
            ]
    field[:, 0:1] = jnp.zeros((nx + 2, 1, nz, width), F32)
    field[:, ny + 1 : ny + 2] = jnp.zeros((nx + 2, 1, nz, width), F32)
    odd = lax.rem(lax.axis_index("space"), 2)
    for parts, first in ((near, 2 * (1 - odd)), (far, 2 * odd)):
        for j in range(parts_n):
            spot = lax.bitwise_xor(mine, j) * py + 1
            field[pl.ds(first, 2), pl.ds(spot, py)] = (
                parts[-j][...].astype(F32).reshape(2, py, nz, width)
            )
    for x in range(nx + 2):
        plane = field[x]
        for c in range(3):
            moved = plane if c == 1 else roll_z(plane, 1 - c)
            for b in range(3):
                windows[b, x, :, c * width : (c + 1) * width] = (
                    moved[b : b + ny].reshape(rows, width).astype(BF16)
                )
    slopes[:, 0:1] = jnp.zeros((nx, 1, nz, filters), F32)
    slopes[:, ny + 1 :] = jnp.zeros((nx, 1, nz, filters), F32)
    for x in range(nx):
        acc = jnp.zeros((rows, filters), F32)
        for ab in range(9):
            a, b = ab // 3, ab % 3
            acc = acc + lax.dot_general(
                windows[b, x + a], wide[ab], (((1,), (1,)), ((), ())), preferred_element_type=F32
            )
        sig = sigmoid(acc)
        block_out[x] = (acc * sig).reshape(ny, nz, filters).astype(BF16)
        slope = sig * (1.0 + acc * (1.0 - sig))
        value = (cot[x].astype(F32).reshape(rows, filters) * slope).astype(BF16)
        grad[x] = value
        slopes[x, 1 : ny + 1] = value.astype(F32).reshape(ny, nz, filters)
    for x in range(nx):
        plane = slopes[x]
        plane = jnp.concatenate([roll_z(plane, -1), plane, roll_z(plane, 1)], axis=2)
        for b in range(3):
            turned[b, x] = (
                plane[2 - b : 2 - b + ny].reshape(rows, 3 * filters).astype(BF16)
            )
    for r in range(nx + 2):
        total = jnp.zeros((rows, width), F32)
        for ab in range(9):
            a, b = ab // 3, ab % 3
            if 0 <= r - a < nx:
                total = total + jnp.dot(turned[b, r - a], wt[ab], preferred_element_type=F32)
        terms[r] = total.reshape(ny, nz, width)
    for j in range(parts_n):
        spot = lax.bitwise_xor(mine, j) * py
        value = terms[:, pl.ds(spot, py)]
        sends[j][...] = value.reshape(nx + 2, py * nz, width).astype(sends[j].dtype)


def deep_grad_body(windows, grad, theirs, mine, held):
    nx, rows, filters = grad.shape
    width = windows.shape[3] // 3
    turned = grad[...].reshape(nx * rows, filters).astype(F32).T.astype(BF16)
    chips, step, _ = mine.shape
    part = filters // 2
    total = 27 * part
    if chips * step > total:
        held[:, total:] = jnp.zeros((2, chips * step - total, width), F32)
    for ab in range(9):
        a, b = ab // 3, ab % 3
        value = jnp.dot(
            turned,
            windows[b, a : a + nx].reshape(nx * rows, 3 * width),
            preferred_element_type=F32,
        )
        for c in range(3):
            spot = (3 * ab + c) * part
            for side in range(2):
                held[side, spot : spot + part] = value[
                    side * part : (side + 1) * part, c * width : (c + 1) * width
                ]
    core = lax.rem(lax.axis_index("space"), 2)
    for q in range(chips):
        theirs[q] = held[1 - core, q * step : (q + 1) * step].astype(theirs.dtype)
        mine[q] = held[core, q * step : (q + 1) * step]


def early_grad_body(nz, taps, *refs):
    parts, (sg, far_sg, turned, out, grad, held, spread) = refs[:-7], refs[-7:]
    count, rows, wide = sg.shape
    total = parts[0][...]
    for part in parts[1:]:
        total = total + part[...].astype(F32)
    px, prow, _ = total.shape
    py = prow // nz
    total = jnp.concatenate([total, total], axis=2).reshape(px, py, 1, nz, wide)
    spread[...] = jnp.broadcast_to(total, (px, py, 2, nz, wide)).reshape(px, rows, wide)
    odd = lax.rem(lax.axis_index("space"), 2)
    for source, first in ((sg, count * (1 - odd)), (far_sg, count * odd)):
        for x in range(count):
            grad[first + x] = (spread[lax.div(first, 2) + x // 2] * source[x]).astype(BF16)
    early_grad_half(1 - odd, taps, grad, turned, out, held)


def early_grad_rest_body(own, taps, *refs):
    grad, turned, *deep, out, held = refs
    core = lax.rem(lax.axis_index("space"), 2)
    early_grad_half(core if own else 1 - core, taps, grad, turned, out, held)
    step = out.shape[1] - (deep[0].shape[1] if deep else 0)
    for ref in deep:
        out[:, step:] = ref[...].astype(out.dtype)


def early_grad_half(side, taps, grad, turned, out, held):
    ext, rows, wide = grad.shape
    width = wide // 2
    part = turned.shape[2] // 4
    right = grad[...].reshape(ext * rows, wide)
    for ab in range(*taps):
        a, b = ab // 3, ab % 3
        value = jnp.dot(
            turned[b, side, :, a * rows : (a + ext) * rows], right, preferred_element_type=F32
        )
        for c in range(3):
            spot = (3 * (ab - taps[0]) + c) * part
            held[spot : spot + part] = (
                value[c * part : (c + 1) * part, :width]
                + value[(c + 1) * part : (c + 2) * part, width:]
            )
    step = held.shape[0] // out.shape[0]
    for q in range(out.shape[0]):
        out[q, :step] = held[q * step : (q + 1) * step].astype(out.dtype)


def core_sum_body(mine, other, *outs):
    chip = lax.div(lax.axis_index("space"), 2)
    for j, out in enumerate(outs):
        q = lax.bitwise_xor(chip, j)
        out[...] = (mine[q] + other[q].astype(F32)).astype(out.dtype)


def chip_sum_body(count, *refs):
    others, outs = refs[:count], refs[count:]
    total = others[0][...]
    for ref in others[1:]:
        total = total + ref[...].astype(F32)
    row = 0
    for out in outs:
        size = out.shape[0]
        out[...] = total[row : row + size].astype(BF16)
        row += size


def filt_sum_body(count, *refs):
    parts, rest, out = refs[:count], refs[count:-1], refs[-1]
    values = [part[...].astype(F32) for part in backward(list(parts))]
    while len(values) > 1:
        values = [low + high for low, high in zip(values[::2], values[1::2])]
    size = values[0].shape[0]
    out[:size] = values[0].astype(BF16)
    for ref in rest:
        out[size:] = ref[...]


def stack_body(step, *refs):
    *parts, out = refs
    chips = out.shape[0]
    chip = lax.div(lax.axis_index("space"), 2)
    for j in range(chips):
        first, second = parts[j], parts[chips + j]
        q = lax.bitwise_xor(chip, j)
        cut = step - second.shape[0]
        out[q, :cut] = first[:cut]
        out[q, cut:step] = second[...]
        out[q, step:] = first[cut:]


def finish_body(own, early_scale, deep_scale, steps, cut, pieces, *refs):
    early, deep, early_held, deep_held, sem = refs[-5:]
    core = lax.rem(lax.axis_index("space"), 2)
    side = core if own else 1 - core
    copies = []
    first = 0
    for out, held, begin, end, step, scale in (
        (early, early_held, 0, cut, steps[0], early_scale),
        (early, early_held, cut, 27, steps[1], early_scale),
        (deep, deep_held, 0, 27, steps[2], deep_scale),
    ):
        part = held.shape[1]
        for tap in range(begin, end):
            row = (tap - begin) * part
            stop = row + part
            while row < stop:
                q, inner = row // step, row % step
                size = min(step - inner, stop - row)
                spot = part - (stop - row)
                held[tap, spot : spot + size] = (
                    pieces[q, first + inner : first + inner + size].astype(F32) * scale
                )
                row += size
            some = (end - begin) // 3
            if (tap + 1 - begin) % some == 0:
                taps = pl.ds(tap + 1 - some, some)
                copy = pltpu.make_async_copy(
                    held.at[taps], out.at[taps, pl.ds(side * part, part)], sem.at[len(copies)]
                )
                copy.start()
                copies.append(copy)
        first += step
    for copy in copies:
        copy.wait()


def paired(values, axis, step=1):
    count = lax.axis_size(axis)
    got = {
        j: lax.ppermute(values[j], axis, [(i, i ^ (step * j)) for i in range(count)])
        for j in reversed(range(1, len(values)))
    }
    return [values[0]] + [got[j] for j in range(1, len(values))]


def exchange(value, axis, step):
    return lax.ppermute(value, axis, [(i, i ^ step) for i in range(lax.axis_size(axis))])


def backward(values):
    return [values[0]] + values[:0:-1]


def swap(value, axis, first):
    count = lax.axis_size(axis)
    pairs = [(i, (i + 1) % count) for i in range(first, count, 2)]
    return lax.ppermute(value, axis, pairs + [(b, a) for a, b in pairs])


def shards(volume, w_early, w_deep, cotangent):
    nx, ny, nz, cin = volume.shape
    width = w_early.shape[2]
    filters = w_deep.shape[2]
    space = lax.axis_size("space")
    filt = lax.axis_size("filt")
    chips = space // 2
    half = nz // 2
    ext = nx + 6
    rows = ny * half
    edges = jnp.concatenate([volume[:, :1], volume[:, ny - 1 :]], axis=1)
    edges = call(edges_body, "edges", struct(edges.shape), (edges,), flops=1 << 32)
    yeven, yodd = swap(edges, "filt", 0), swap(edges, "filt", 1)
    rim = struct((3, ny + 2, nz, cin))
    volume, sides, near, far = call(
        spread_body,
        "spread",
        [struct(volume.shape), struct((nx, 2, nz, cin)), rim, rim],
        (volume, yeven, yodd),
        flops=HOLD,
        moved=1 << 24,
    )
    far = swap(far, "space", 1)
    near = swap(near, "space", 0)
    windows, sg, near_pooled, wide = call(
        near_body,
        "early_near",
        (
            struct((3, nx + 3, rows, 4 * cin)),
            struct((nx, rows, 2 * width), F32),
            struct((nx // 2, rows // 2, width)),
            struct((9, 4 * cin, 2 * width)),
        ),
        (volume, sides, near, w_early),
        [pltpu.VMEM((nx + 3, ny + 2, nz + 16, cin), F32)],
        flops=2 * nx * rows * 36 * cin * 2 * width,
    )
    near_parts = paired([near_pooled] * filt, "filt")
    far_windows, far_sg, pooled = call(
        far_body,
        "early_far",
        (
            struct((3, 3, rows, 4 * cin)),
            struct((nx, rows, 2 * width), F32),
            struct((nx // 2, rows // 2, width)),
        ),
        (windows, far, wide),
        [
            pltpu.VMEM((3, ny + 2, nz + 16, cin), F32),
            pltpu.VMEM((3, 6, rows, 4 * cin), BF16),
        ],
        flops=2 * nx * rows * 36 * cin * 2 * width,
    )
    parts = backward(paired([pooled] * filt, "filt"))
    near_parts = backward(near_parts)
    windows, *near_parts = lax.optimization_barrier((windows, *near_parts))
    turned = call(
        transpose_body,
        "turn_windows",
        struct((3, 2, 2 * cin, ext * rows)),
        (windows, far_windows),
        flops=1 << 30,
    )
    *parts, turned = lax.optimization_barrier((*parts, turned))
    dx, dy, dz, _ = cotangent.shape
    px = dx + 2
    prow = rows // 2
    deep = call(
        functools.partial(deep_body, filt),
        "deep_conv",
        [
            struct(cotangent.shape),
            struct((dx, dy * dz, filters)),
            struct((3, px, dy * dz, 3 * width)),
            struct((px, prow, width), F32),
        ]
        + [struct((px, prow, width))] * (filt - 1),
        (*parts, *near_parts, jnp.swapaxes(w_deep, 1, 2).reshape(9, 3 * filters, width), cotangent),
        [
            pltpu.VMEM((px, dy + 2, dz, width), F32),
            pltpu.VMEM((9, filters, 3 * width), BF16),
            pltpu.VMEM((dx, dy + 2, dz, filters), F32),
            pltpu.VMEM((3, dx, dy * dz, 3 * filters), BF16),
            pltpu.VMEM((px, dy, dz, width), F32),
        ],
        flops=4 * dx * dy * dz * 27 * width * filters,
    )
    block_out, grad, deep_windows = deep[:3]
    terms = paired(deep[3:], "filt")

    deep_rows = ceil_to(-(-27 * filters // space), 16)
    deep_first, deep_second = call(
        deep_grad_body,
        "deep_grad",
        [struct((chips, deep_rows, width)), struct((chips, deep_rows, width), F32)],
        (deep_windows, grad),
        [pltpu.VMEM((2, chips * deep_rows, width), F32)],
        flops=2 * dx * dy * dz * 27 * width * filters,
    )
    deep_first, terms[-1] = lax.optimization_barrier((deep_first, terms[-1]))
    cuts = ((0, 4), (4, 9))
    steps = [3 * (end - begin) * (cin // 2) // chips for begin, end in cuts]
    flops = 2 * (nx + 4) * rows * 18 * cin * 2 * width
    helds = [pltpu.VMEM((step * chips, width), F32) for step in steps]

    def core_sums(name, mine, theirs):
        size = mine.shape[1:]
        shapes = [struct(size, F32)] + [struct(size)] * (chips - 1)
        return list(call(core_sum_body, name, shapes, (mine, theirs)))

    theirs, grad = call(
        functools.partial(early_grad_body, half, cuts[0]),
        "early_grad",
        [struct((chips, steps[0], width)), struct((nx + 4, rows, 2 * width))],
        (*backward(terms), sg, far_sg, turned),
        [helds[0], pltpu.VMEM((px, rows, 2 * width), F32)],
        flops=flops,
    )
    theirs = exchange(theirs, "space", 1)
    mine = call(
        functools.partial(early_grad_rest_body, True, cuts[0]),
        "early_grad_own",
        struct((chips, steps[0], width), F32),
        (grad, turned),
        [helds[0]],
        flops=flops,
    )
    sums = core_sums("core_sum", mine, theirs)
    grad, sums[0] = lax.optimization_barrier((grad, sums[0]))
    first = backward(paired(sums, "space", 2))
    size = (chips, steps[1] + deep_rows, width)
    theirs = call(
        functools.partial(early_grad_rest_body, False, cuts[1]),
        "early_grad_rest",
        struct(size),
        (grad, turned, deep_first),
        [helds[1]],
        flops=flops,
    )
    theirs = exchange(theirs, "space", 1)
    mine = call(
        functools.partial(early_grad_rest_body, True, cuts[1]),
        "early_grad_rest_own",
        struct(size, F32),
        (grad, turned, deep_second),
        [helds[1]],
        flops=flops,
    )
    sums = core_sums("core_sum_rest", mine, theirs)
    *sums, first = lax.optimization_barrier((*sums, first))
    second = backward(paired(sums, "space", 2))
    (early,) = call(
        functools.partial(chip_sum_body, chips), "chip_sum", [struct((steps[0], width))], first
    )
    first = backward(paired([early] * filt, "filt"))
    *second, first[0] = lax.optimization_barrier((*second, first[0]))
    early, deep = call(
        functools.partial(chip_sum_body, chips),
        "chip_sum_rest",
        [struct((steps[1], width)), struct((deep_rows, width))],
        second,
        flops=HOLD,
    )
    second = backward(paired([early] * filt, "filt"))
    *first, second[0] = lax.optimization_barrier((*first, second[0]))
    sum_body = functools.partial(filt_sum_body, filt)
    first = call(
        sum_body, "filt_sum", struct((steps[0] + deep_rows, width)), (*first, deep), flops=HOLD
    )
    first = paired([first] * chips, "space", 2)
    *second, first[0] = lax.optimization_barrier((*second, first[0]))
    second = call(
        sum_body, "filt_sum_rest", struct((steps[1], width)), second, flops=HOLD
    )
    late, first[1] = lax.optimization_barrier((second, first[1]))
    second = paired([second, late] + [second] * (chips - 2), "space", 2)

    own = call(
        functools.partial(stack_body, sum(steps)),
        "stack",
        struct((chips, sum(steps) + deep_rows, width)),
        (*first, *second),
    )
    other = exchange(own, "space", 1)
    early_total = nx * ny * nz * space * filt
    deep_total = dx * dy * dz * space
    results = [struct((27, cin, width), F32), struct((27, filters, width), F32)]
    scales = (1.0 / math.sqrt(early_total), 1.0 / math.sqrt(deep_total))
    scales += ((*steps, deep_rows), 3 * cuts[0][1])
    scratch = [
        pltpu.VMEM((27, cin // 2, width), F32),
        pltpu.VMEM((27, filters // 2, width), F32),
        DMA((9,)),
    ]
    results = call(
        functools.partial(finish_body, True, *scales),
        "finish_own",
        results,
        (own,),
        scratch,
        outs=HBM,
    )
    grad_early, grad_deep = call(
        functools.partial(finish_body, False, *scales),
        "finish_other",
        [struct(value.shape, F32) for value in results],
        (other, *results),
        scratch,
        hbm=(1, 2),
        outs=HBM,
        alias=((1, 0), (2, 1)),
    )
    return (block_out, grad_early, jnp.swapaxes(grad_deep, 1, 2))


def solution(mesh):
    return jax.shard_map(
        shards,
        mesh=mesh,
        in_specs=(
            P("space", "filt", None, None),
            P(),
            P(None, None, "filt"),
            P("space", None, None, "filt"),
        ),
        out_specs=(P("space", None, None, "filt"), P(), P(None, None, "filt")),
        check_vma=False,
    )
```
